32 devices in a mesh: grp: 2 (over x), scan: 16 (over z, y, core).
Axes of the slice: x: 2, y: 2, z: 4, core: 2. Of those that a mesh axis runs over, the one named last changes fastest.
Arguments:
- object_tiles: float32 [32, 2, 512, 512], P(('grp', 'scan')), parts along dimension 0, may hold values from -5 to 5
- probe: float32 [4, 2, 256, 256], replicated, may hold values from -5 to 5
- positions: int32 [32, 6, 2], P(('grp', 'scan')), parts along dimension 0, may hold values from 0 to 3840, as said below
- frames: float32 [32, 6, 256, 256], P(('grp', 'scan')), parts along dimension 0, may hold values from 0.5 to 8
- counts: int32 [32], P(('grp', 'scan')), parts along dimension 0, may hold values from 1 to 6
Outputs:
- object_new: float32 [32, 2, 512, 512], P(('grp', 'scan')), parts along dimension 0
The draws below stay inside these ranges and needn't reach their ends.
There are 2 independent parts, one for each index of `grp`. The reference program is written for one: setup_inputs(seed, part) draws one part's arguments, and reference() takes and returns one part's arrays. A program takes and returns all parts, laid end to end along the dimension named above; an argument that names none is the same for every part. Nothing has to cross between parts.
Inputs may be any that keep to these rules, and one draw needn't show every extreme that they name: `positions`: A frame of device k starts inside tile k: its row lies in [(k // 8) * 512, (k // 8 + 1) * 512) and its column in [(k % 8) * 512, (k % 8 + 1) * 512); every frame lies inside the 1024 x 4096 region. The last dimension holds row then column.
All inputs are finite; a program needn't handle non-finite values.
Results may differ from the reference program's by a relative error of at most 0.0012.
Values sent between devices are 32-bit elements; how exact they have to be, the bound alone decides.
No kernel may reach another device: no remote copies, remote signals or barrier semaphores. Data moves between devices by JAX's collectives and lax.ppermute only.
A program may use at most 64 MiB of HBM per device.

```python
import math
import jax
import jax.numpy as jnp
from jax import lax

FRAME = 256
MODES = 4
TCOLS = 8
TILE = 512
CAP = 6
N_SCAN = 16


def draw_positions(key, part):
    key = jax.random.fold_in(key, 11)
    key_rows, key_cols = jax.random.split(key)
    tile_rows = N_SCAN // TCOLS
    device = jnp.arange(N_SCAN, dtype=jnp.int32)
    tile_row = device // TCOLS
    tile_col = device % TCOLS
    row_span = jnp.where(tile_row == tile_rows - 1, TILE - FRAME + 1, TILE)
    col_span = jnp.where(tile_col == TCOLS - 1, TILE - FRAME + 1, TILE)
    row_draw = jax.random.randint(key_rows, (N_SCAN, CAP), 0, 2 ** 30) % row_span[:, None]
    col_draw = jax.random.randint(key_cols, (N_SCAN, CAP), 0, 2 ** 30) % col_span[:, None]
    rows_all = tile_row[:, None] * TILE + row_draw
    cols_all = tile_col[:, None] * TILE + col_draw
    rows_all = rows_all.at[N_SCAN - 1, 0].set(tile_rows * TILE - FRAME).at[0, 0].set(0)
    cols_all = cols_all.at[N_SCAN - 1, 0].set(TCOLS * TILE - FRAME).at[0, 0].set(0)
    return jnp.stack([rows_all, cols_all], axis=-1).astype(jnp.int32)


def draw_counts(key, part):
    key = jax.random.fold_in(key, 12)
    key_base, key_dense, key_forced = jax.random.split(key, 3)
    base_count = jax.random.randint(key_base, (N_SCAN,), 1, 3)
    dense_flag = jax.random.randint(key_dense, (N_SCAN,), 0, 4) == 0
    forced_device = jax.random.randint(key_forced, (), 0, N_SCAN)
    busy = dense_flag | (jnp.arange(N_SCAN, dtype=jnp.int32) == forced_device)
    return jnp.where(busy, CAP, base_count).astype(jnp.int32)


def block_scale(stream_key, shape, cuts, smallest, largest):
    level, own = 1.0, jax.random.fold_in(stream_key, 6)
    for axis_at, parts in cuts:
        heights = jnp.exp(jax.random.uniform(jax.random.fold_in(own, axis_at), (parts,), jnp.float32, smallest / len(cuts), largest / len(cuts)))
        level = level * jnp.repeat(heights, shape[axis_at] // parts).reshape([-1 if axis == axis_at else 1 for axis in range(len(shape))])
    return level


def scatter_about(own_key, shape, width, reach, cuts=(), kind=jnp.bfloat16):
    entries = width * jax.random.normal(own_key, shape, jnp.float32)
    if cuts:
        entries = entries * block_scale(own_key, shape, cuts, -0.22, 0.18)
    return jnp.clip(entries, -reach, reach).astype(kind)


def setup_inputs(seed: int = 0, part: int = 0) -> dict:
    arg_keys = jax.random.split(jax.random.key(seed), 6)
    part_keys = jax.random.split(jax.random.fold_in(arg_keys[5], part), 6)
    object_tiles = scatter_about(part_keys[0], (N_SCAN, 2, TILE, TILE), 0.7, 5.0, ((0, 16),), jnp.float32)
    probe = scatter_about(arg_keys[1], (MODES, 2, FRAME, FRAME), 0.7, 5.0, (), jnp.float32)
    positions = draw_positions(jax.random.fold_in(jax.random.fold_in(arg_keys[5], part), 71), part)
    frames = jnp.clip(jnp.exp(math.log(8.0) - 2.7725887 * jax.random.uniform(part_keys[3], (N_SCAN, CAP, FRAME, FRAME), jnp.float32) ** block_scale(part_keys[3], (N_SCAN, CAP, FRAME, FRAME), ((0, 16),), -0.2, 0.2)), 0.5, 8.0)
    counts = draw_counts(jax.random.fold_in(jax.random.fold_in(arg_keys[5], part), 71), part)
    return dict(object_tiles=object_tiles, probe=probe, positions=positions, frames=frames, counts=counts)


def dft_tables(frame_len):
    index = jnp.arange(frame_len, dtype=jnp.int32)
    phase = (index[:, None] * index[None, :] % frame_len).astype(jnp.float32) * (2.0 * math.pi / frame_len)
    cosine = jnp.cos(phase)
    sine = jnp.sin(phase)
    forward = jnp.concatenate([jnp.concatenate([cosine, -sine], axis=1), jnp.concatenate([sine, cosine], axis=1)], axis=0)
    inverse = jnp.concatenate([jnp.concatenate([cosine, sine], axis=1), jnp.concatenate([-sine, cosine], axis=1)], axis=0)
    return (forward.astype(jnp.bfloat16), inverse.astype(jnp.bfloat16))

def flip_planes(values):
    mode_count, row_len, double_width = values.shape
    return values.reshape(mode_count, row_len, 2, row_len).transpose(0, 3, 2, 1).reshape(mode_count, row_len, double_width)

def table_pass(values, table):
    mode_count, row_len, double_width = values.shape
    product = jnp.dot(values.reshape(mode_count * row_len, double_width).astype(jnp.float32), table.astype(jnp.float32))
    return flip_planes(product.reshape(mode_count, row_len, double_width))

def frame_gradient(patch, measured, probe, forward, inverse):
    frame_len = patch.shape[-1]
    probe_real = probe[:, 0]
    probe_imag = probe[:, 1]
    exit_real = probe_real * patch[0] - probe_imag * patch[1]
    exit_imag = probe_real * patch[1] + probe_imag * patch[0]
    exit_wave = jnp.concatenate([exit_real, exit_imag], axis=2).astype(jnp.bfloat16)
    half_field = table_pass(exit_wave, forward).astype(jnp.bfloat16)
    far_field = table_pass(half_field, forward) / frame_len
    far_real = far_field[:, :, :frame_len]
    far_imag = far_field[:, :, frame_len:]
    intensity = lax.optimization_barrier(jnp.sum(far_real * far_real + far_imag * far_imag, axis=0))
    amp_ratio = jnp.sqrt(measured) / jnp.sqrt(jnp.maximum(intensity, 1.0))
    factor = jnp.concatenate([1.0 - amp_ratio, 1.0 - amp_ratio], axis=1)
    residual_field = (far_field * factor[None]).astype(jnp.bfloat16)
    half_back = table_pass(residual_field, inverse).astype(jnp.bfloat16)
    back_field = table_pass(half_back, inverse) / frame_len
    back_real = back_field[:, :, :frame_len]
    back_imag = back_field[:, :, frame_len:]
    grad_real = lax.optimization_barrier(jnp.sum(probe_real * back_real + probe_imag * back_imag, axis=0))
    grad_imag = lax.optimization_barrier(jnp.sum(probe_real * back_imag - probe_imag * back_real, axis=0))
    return jnp.stack([grad_real, grad_imag])

def reference(object_tiles, probe, positions, frames, counts):
    tile_rows = N_SCAN // TCOLS
    image = object_tiles.reshape(tile_rows, TCOLS, 2, TILE, TILE).transpose(2, 0, 3, 1, 4).reshape(2, tile_rows * TILE, TCOLS * TILE)
    forward, inverse = dft_tables(FRAME)
    probe_power = lax.optimization_barrier(jnp.sum(probe * probe, axis=(0, 1)))
    live_mask = (jnp.arange(CAP, dtype=jnp.int32)[None, :] < counts[:, None]).astype(jnp.float32).reshape(-1)
    flat_positions = positions.reshape(N_SCAN * CAP, 2)
    flat_frames = frames.reshape(N_SCAN * CAP, FRAME, FRAME)
    anchor = jnp.zeros((), jnp.int32)

    def advance(carry, item):
        gradient, illumination = carry
        where_at, measured, weight = item
        row_at = where_at[0].astype(jnp.int32)
        col_at = where_at[1].astype(jnp.int32)
        patch = lax.dynamic_slice(image, (anchor, row_at, col_at), (2, FRAME, FRAME))
        piece = frame_gradient(patch, measured, probe, forward, inverse) * weight
        current = lax.dynamic_slice(gradient, (anchor, row_at, col_at), (2, FRAME, FRAME))
        gradient = lax.dynamic_update_slice(gradient, current + piece, (anchor, row_at, col_at))
        lit = lax.dynamic_slice(illumination, (row_at, col_at), (FRAME, FRAME))
        illumination = lax.dynamic_update_slice(illumination, lit + probe_power * weight, (row_at, col_at))
        return ((gradient, illumination), None)
    start = (jnp.zeros(image.shape, jnp.float32), jnp.zeros(image.shape[1:], jnp.float32))
    (gradient, illumination), _ = lax.scan(advance, start, (flat_positions, flat_frames, live_mask))
    updated = image - gradient / (illumination + 1.0)[None]
    return updated.reshape(2, tile_rows, TILE, TCOLS, TILE).transpose(1, 3, 0, 2, 4).reshape(N_SCAN, 2, TILE, TILE)
```

```python
import functools
import math

import jax
import jax.numpy as jnp
import numpy as np
from jax import lax
from jax.experimental import pallas as pl
from jax.experimental.pallas import tpu as pltpu
from jax.sharding import PartitionSpec as P

TCOLS = 8
LANES = 128
ROW_ALIGN = 8
SIZES = (64, 128, 192, 256, 384, 512, 768, 1024, 1536)
VMEM_LIMIT = 56 * 1024 * 1024
F32 = jnp.float32
BF16 = jnp.bfloat16


def dft_tables(frame_len):
    index = np.arange(frame_len, dtype=np.int64)
    phase = (index[:, None] * index[None, :] % frame_len).astype(np.float64) * (2.0 * math.pi / frame_len)
    cosine, sine = np.cos(phase), np.sin(phase)
    forward = np.block([[cosine, -sine], [sine, cosine]])
    inverse = np.block([[cosine, sine], [-sine, cosine]])
    return jnp.asarray(forward, F32).astype(BF16), jnp.asarray(inverse, F32).astype(BF16)


def shifted(array, axis, by):
    peers = lax.axis_size(axis)
    pairs = [(i, i + by) for i in range(peers) if 0 <= i + by < peers]
    return lax.ppermute(array, axis, pairs)


def any_spec():
    return pl.BlockSpec(memory_space=pl.ANY)


def smem_spec():
    return pl.BlockSpec(memory_space=pltpu.SMEM)


def roll_lanes(block, by):
    return pltpu.roll(block, by, axis=1)


def taken_from(blocks, by):
    lane = lax.broadcasted_iota(jnp.int32, blocks[0].shape, 1)
    rolled = [roll_lanes(block, lax.rem(LANES - by, LANES)) for block in blocks]
    return [jnp.where(lane < LANES - by, one, two) for one, two in zip(rolled[:-1], rolled[1:])]


def put_into(blocks, by):
    lane = lax.broadcasted_iota(jnp.int32, blocks[0].shape, 1)
    rolled = [roll_lanes(block, by) for block in blocks]
    none = jnp.zeros_like(blocks[0])
    return [jnp.where(lane >= by, one, two) for one, two in zip(rolled + [none], [none] + rolled)]


def run_copies(copies):
    for copy in copies:
        copy.start()
    for copy in copies:
        copy.wait()


def block_copies(pairs, sems):
    return [pltpu.make_async_copy(source, target, sems.at[at]) for at, (source, target) in enumerate(pairs)]


def lanes_of(block):
    return pl.ds(block * LANES, LANES)


def side_by_side(parts):
    return jnp.concatenate(parts, axis=1)


def halves(array):
    return [array[:, :LANES], array[:, LANES:]]


def cut_kernel(slots, tile, strip, packed, band, sems):
    frame = strip.shape[-1]
    extent = tile.shape[-1]
    cap = slots.shape[1]
    across = frame // LANES
    own_blocks = extent // LANES
    top = pl.ds(0, frame)

    @pl.when(slots[5, 0] > 0)
    def _():
        run_copies(block_copies(
            [(tile.at[:, top, lanes_of(b)], band.at[:, b]) for b in range(own_blocks)]
            + [(strip.at[:, top, lanes_of(b)], band.at[:, own_blocks + b]) for b in range(across)], sems))

        def one(slot, carry):
            col, below, place = slots[1, slot], slots[2, slot], slots[3, slot]

            @pl.when(below > 0)
            def _():
                first = col // LANES
                at = pl.ds(pl.multiple_of(place, ROW_ALIGN), frame)
                for plane in range(2):
                    cut = taken_from([band[plane, first + b] for b in range(across + 1)], lax.rem(col, LANES))
                    packed[at, pl.ds(plane * frame, frame)] = side_by_side(cut)

            return carry

        lax.fori_loop(0, cap, one, 0)


def cut_pieces(slots, tile, strip, rows):
    frame = strip.shape[-1]
    extent = tile.shape[-1]
    blocks = (extent + frame) // LANES
    return pl.pallas_call(
        cut_kernel,
        out_shape=jax.ShapeDtypeStruct((rows + frame, 2 * frame), F32),
        in_specs=[smem_spec(), any_spec(), any_spec()],
        out_specs=pl.BlockSpec(memory_space=pltpu.VMEM),
        scratch_shapes=[pltpu.VMEM((2, blocks, frame, LANES), F32), pltpu.SemaphoreType.DMA((blocks,))],
        compiler_params=pltpu.CompilerParams(vmem_limit_bytes=VMEM_LIMIT),
        name="cut_pieces",
    )(slots, tile, strip)


def frames_kernel(slots, tile, strip, received, frames, probe, forward, inverse,
                  main_out, strip_out, packed_out,
                  band, total, held, field, piece, sems):
    frame = strip.shape[-1]
    extent = tile.shape[-1]
    modes = probe.shape[0]
    rows = received.shape[0]
    across = frame // LANES
    own_blocks = extent // LANES
    all_rows = pl.ds(0, extent)
    run_copies(block_copies(
        [(tile.at[:, :, lanes_of(b)], band.at[:, b, all_rows]) for b in range(own_blocks)]
        + [(strip.at[:, :, lanes_of(b)], band.at[:, own_blocks + b, all_rows]) for b in range(across)]
        + [(received.at[:, lanes_of(b)], held.at[b, pl.ds(frame, rows)]) for b in range(2 * across)], sems))
    total[...] = jnp.zeros_like(total)
    row_index = lax.broadcasted_iota(jnp.int32, (frame, LANES), 0)
    scale = 1.0 / frame

    def one(slot, carry):
        row, col, below, place = slots[0, slot], slots[1, slot], slots[2, slot], slots[3, slot]
        inside = frame - below
        first, by = col // LANES, lax.rem(col, LANES)
        patch = []
        for plane in range(2):
            own = taken_from([band[plane, first + b, pl.ds(row, frame), :] for b in range(across + 1)], by)
            other = [held[plane * across + b, pl.ds(place + below, frame), :] for b in range(across)]
            patch.append(side_by_side([jnp.where(row_index < inside, a, b) for a, b in zip(own, other)]))
        intensity = jnp.zeros((frame, frame), F32)
        for mode in range(modes):
            probe_real, probe_imag = probe[mode, 0], probe[mode, 1]
            wave = side_by_side(
                [probe_real * patch[0] - probe_imag * patch[1], probe_real * patch[1] + probe_imag * patch[0]]
            ).astype(BF16)
            half = jnp.dot(wave, forward[...], preferred_element_type=F32).astype(BF16)
            half = jnp.concatenate([half[:, :frame], half[:, frame:]], axis=0)
            far = jnp.dot(inverse[...], half, preferred_element_type=F32) * scale
            field[mode] = far
            intensity += far[:frame] * far[:frame] + far[frame:] * far[frame:]
        factor = 1.0 - jnp.sqrt(frames[slot]) / jnp.sqrt(jnp.maximum(intensity, 1.0))
        grad_real = jnp.zeros((frame, frame), F32)
        grad_imag = jnp.zeros((frame, frame), F32)
        for mode in range(modes):
            residual = side_by_side([field[mode, :frame] * factor, field[mode, frame:] * factor]).astype(BF16)
            half = jnp.dot(residual, inverse[...], preferred_element_type=F32).astype(BF16)
            half = jnp.concatenate([half[:, :frame], half[:, frame:]], axis=0)
            back = jnp.dot(forward[...], half, preferred_element_type=F32) * scale
            probe_real, probe_imag = probe[mode, 0], probe[mode, 1]
            grad_real += probe_real * back[:frame] + probe_imag * back[frame:]
            grad_imag += probe_real * back[frame:] - probe_imag * back[:frame]
        grads = [halves(grad_real), halves(grad_imag)]
        for plane in range(2):
            for b, moved in enumerate(put_into(grads[plane], by)):
                at = (plane, first + b, pl.ds(row, frame), slice(None))
                total[at] = total[at] + moved

        @pl.when(below > 0)
        def _():
            at = pl.ds(pl.multiple_of(place, ROW_ALIGN), frame)
            for b, part in enumerate(grads[0] + grads[1]):
                piece[b, pl.ds(0, frame), :] = part
                packed_out[at, lanes_of(b)] = piece[b, pl.ds(inside, frame), :]

        return carry

    lax.fori_loop(0, slots[4, 0], one, 0)
    run_copies(block_copies(
        [(total.at[:, b, all_rows], main_out.at[:, :, lanes_of(b)]) for b in range(own_blocks)]
        + [(total.at[:, own_blocks + b, all_rows], strip_out.at[:, :, lanes_of(b)]) for b in range(across)], sems))


def frames_gradient(slots, tile, strip, received, frames, probe, forward, inverse):
    frame = strip.shape[-1]
    extent = tile.shape[-1]
    modes = probe.shape[0]
    rows = received.shape[0]
    tall = extent + frame
    blocks = tall // LANES
    across = frame // LANES
    vmem = pl.BlockSpec(memory_space=pltpu.VMEM)
    return pl.pallas_call(
        frames_kernel,
        out_shape=(
            jax.ShapeDtypeStruct((2, extent, extent), F32),
            jax.ShapeDtypeStruct((2, extent, frame), F32),
            jax.ShapeDtypeStruct((rows + frame, 2 * frame), F32),
        ),
        in_specs=[smem_spec(), any_spec(), any_spec(), any_spec(), vmem, vmem, vmem, vmem],
        out_specs=(any_spec(), any_spec(), vmem),
        scratch_shapes=[
            pltpu.VMEM((2, blocks, tall, LANES), F32),
            pltpu.VMEM((2, blocks, tall, LANES), F32),
            pltpu.VMEM((2 * across, rows + 2 * frame, LANES), F32),
            pltpu.VMEM((modes, 2 * frame, frame), F32),
            pltpu.VMEM((2 * across, 2 * frame, LANES), F32),
            pltpu.SemaphoreType.DMA((blocks + 2 * across,)),
        ],
        compiler_params=pltpu.CompilerParams(vmem_limit_bytes=VMEM_LIMIT),
        name="frames_gradient",
    )(slots, tile, strip, received, frames, probe, forward, inverse)


def light_kernel(own, left, up, corner, probe, light, total):
    modes, _, frame, _ = probe.shape
    extent = light.shape[0]
    across = frame // LANES
    total[...] = jnp.zeros_like(total)
    power = jnp.zeros((frame, frame), F32)
    for mode in range(modes):
        power += probe[mode, 0] * probe[mode, 0] + probe[mode, 1] * probe[mode, 1]
    for table, down, right in ((own, 0, 0), (left, 0, 1), (up, 1, 0), (corner, 1, 1)):

        def one(slot, carry, table=table, down=down, right=right):
            row = table[0, slot] + frame - down * extent
            col = table[1, slot] + frame - right * extent

            @pl.when((row > 0) & (col > 0))
            def _():
                for b, moved in enumerate(put_into(halves(power), lax.rem(col, LANES))):
                    at = (col // LANES + b, pl.ds(row, frame), slice(None))
                    total[at] = total[at] + moved

            return carry

        lax.fori_loop(0, table[4, 0], one, 0)
    for b in range(extent // LANES):
        light[:, lanes_of(b)] = total[across + b, pl.ds(frame, extent), :]


def light_plane(tables, probe, extent):
    frame = probe.shape[-1]
    tall = extent + 2 * frame
    return pl.pallas_call(
        light_kernel,
        out_shape=jax.ShapeDtypeStruct((extent, extent), F32),
        in_specs=[smem_spec()] * 4 + [pl.BlockSpec(memory_space=pltpu.VMEM)],
        out_specs=pl.BlockSpec(memory_space=pltpu.VMEM),
        scratch_shapes=[pltpu.VMEM((tall // LANES, tall, LANES), F32)],
        compiler_params=pltpu.CompilerParams(vmem_limit_bytes=VMEM_LIMIT),
        name="light_plane",
    )(*tables, probe)


def join_kernel(slots, pieces, main, strip, main_out, strip_out, band, held, sems):
    frame = strip.shape[-1]
    extent = main.shape[-1]
    cap = slots.shape[1]
    rows = pieces.shape[0]
    across = frame // LANES
    own_blocks = extent // LANES
    top = pl.ds(0, frame)
    row_index = lax.broadcasted_iota(jnp.int32, (frame, LANES), 0)

    @pl.when(slots[5, 0] > 0)
    def _():
        run_copies(block_copies(
            [(main.at[:, top, lanes_of(b)], band.at[:, b]) for b in range(own_blocks)]
            + [(strip.at[:, top, lanes_of(b)], band.at[:, own_blocks + b]) for b in range(across)]
            + [(pieces.at[:, lanes_of(b)], held.at[b, pl.ds(0, rows)]) for b in range(2 * across)], sems))

        def one(slot, carry):
            col, below, place = slots[1, slot], slots[2, slot], slots[3, slot]

            @pl.when(below > 0)
            def _():
                first = col // LANES
                at = pl.ds(pl.multiple_of(place, ROW_ALIGN), frame)
                for plane in range(2):
                    got = [jnp.where(row_index < below, held[plane * across + b, at, :], 0.0) for b in range(across)]
                    for b, moved in enumerate(put_into(got, lax.rem(col, LANES))):
                        band[plane, first + b] = band[plane, first + b] + moved

            return carry

        lax.fori_loop(0, cap, one, 0)
        run_copies(block_copies(
            [(band.at[:, b], main_out.at[:, top, lanes_of(b)]) for b in range(own_blocks)]
            + [(band.at[:, own_blocks + b], strip_out.at[:, top, lanes_of(b)]) for b in range(across)], sems))


def join_pieces(slots, pieces, main, strip):
    frame = strip.shape[-1]
    extent = main.shape[-1]
    blocks = (extent + frame) // LANES
    across = frame // LANES
    return pl.pallas_call(
        join_kernel,
        out_shape=(jax.ShapeDtypeStruct(main.shape, F32), jax.ShapeDtypeStruct(strip.shape, F32)),
        in_specs=[smem_spec(), any_spec(), any_spec(), any_spec()],
        out_specs=(any_spec(), any_spec()),
        input_output_aliases={2: 0, 3: 1},
        scratch_shapes=[
            pltpu.VMEM((2, blocks, frame, LANES), F32),
            pltpu.VMEM((2 * across, pieces.shape[0] + frame, LANES), F32),
            pltpu.SemaphoreType.DMA((blocks + 2 * across,)),
        ],
        compiler_params=pltpu.CompilerParams(vmem_limit_bytes=VMEM_LIMIT),
        name="join_pieces",
    )(slots, pieces, main, strip)


def slot_table(meta, cap, extent, frame):
    count = meta[2 * cap]
    live = jnp.arange(cap, dtype=jnp.int32) < count
    row, col = meta[:cap], meta[cap:2 * cap]
    below = jnp.where(live, jnp.maximum(row + frame - extent, 0), 0)
    padded = (below + ROW_ALIGN - 1) // ROW_ALIGN * ROW_ALIGN
    place = jnp.cumsum(padded) - padded
    needed = jnp.sum(padded)
    full = lambda value: jnp.full((cap,), value, jnp.int32)
    return jnp.stack([row, col, below, place, full(count), full(needed)]), needed


def body(object_tiles, probe, positions, frames, counts):
    tile = object_tiles[0]
    extent = tile.shape[-1]
    frame = frames.shape[-1]
    cap = frames.shape[1]
    peers = lax.axis_size("scan")
    device = lax.axis_index("scan")
    tile_row = device // TCOLS
    corner_at = jnp.stack([tile_row * extent, device % TCOLS * extent])
    offsets = (positions[0] - corner_at[None, :]).astype(jnp.int32)
    meta = jnp.concatenate([offsets[:, 0], offsets[:, 1], counts[:1]]).astype(jnp.int32)
    meta_up = shifted(meta, "scan", TCOLS)
    meta_left = shifted(meta, "scan", 1)
    meta_corner = shifted(meta_up, "scan", 1)
    strip = shifted(tile[:, :, :frame], "scan", -1)
    own, own_needs = slot_table(meta, cap, extent, frame)
    up, up_needs = slot_table(meta_up, cap, extent, frame)
    left, _ = slot_table(meta_left, cap, extent, frame)
    corner, _ = slot_table(meta_corner, cap, extent, frame)
    forward, inverse = dft_tables(frame)
    light = light_plane((own, left, up, corner), probe, extent)

    rows = cap * frame
    sizes = jnp.asarray(SIZES, jnp.int32)

    def exchange(packed, upward):
        def sender(size, pairs):
            def run(data):
                if size == 0:
                    return jnp.zeros((rows, 2 * frame), F32)
                moved = lax.ppermute(data[:size], "scan", pairs)
                return jnp.pad(moved, ((0, rows - size), (0, 0)))
            return run

        result = None
        for phase in range(2):
            uppers = [k for k in range(peers - TCOLS) if k // TCOLS % 2 == phase]
            if not uppers:
                continue
            pairs = [(k + TCOLS, k) if upward else (k, k + TCOLS) for k in uppers]
            is_upper = tile_row % 2 == phase
            needed = jnp.where(is_upper, own_needs, up_needs)
            choice = jnp.where(needed > 0, 1 + jnp.sum(needed > sizes), 0)
            moved = lax.switch(choice, [sender(size, pairs) for size in (0,) + SIZES], packed)
            receives = is_upper if upward else ~is_upper
            result = moved if result is None else jnp.where(receives, moved, result)
        return result

    packed = cut_pieces(up, tile, strip, rows)
    received = exchange(packed, True)
    main, right, packed_grad = frames_gradient(own, tile, strip, received, frames[0], probe, forward, inverse)
    pieces = exchange(packed_grad, False)
    main, right = join_pieces(up, pieces, main, right)
    from_left = shifted(right, "scan", 1)
    gradient = main.at[:, :, :frame].add(from_left)
    return (tile - gradient / (light + 1.0)[None])[None]


def solution(mesh):
    return jax.shard_map(
        body,
        mesh=mesh,
        in_specs=(
            P(("grp", "scan"), None, None, None),
            P(),
            P(("grp", "scan"), None, None),
            P(("grp", "scan"), None, None, None),
            P(("grp", "scan")),
        ),
        out_specs=P(("grp", "scan"), None, None, None),
        check_vma=False,
    )
```

```python
import math

import jax
import jax.numpy as jnp
import numpy as np
from jax import lax
from jax.experimental import pallas as pl
from jax.experimental.pallas import tpu as pltpu
from jax.sharding import PartitionSpec as P

TCOLS = 8
LANES = 128
ROW_ALIGN = 8
CHUNK = 64
SIZES = (32, 64, 96, 128, 160, 192, 224, 256, 320, 384, 448, 512, 640, 768)
VMEM_LIMIT = 56 * 1024 * 1024
F32 = jnp.float32
BF16 = jnp.bfloat16

ROW, COL, BELOW, PLACE = 0, 8, 16, 24
COUNT, NEEDED, CHOICE = 32, 33, 34
TABLE = 64


def dft_tables(frame_len):
    index = np.arange(frame_len, dtype=np.int64)
    phase = (index[:, None] * index[None, :] % frame_len).astype(np.float64) * (2.0 * math.pi / frame_len)
    cosine, sine = np.cos(phase), np.sin(phase)
    forward = np.block([[cosine, -sine], [sine, cosine]])
    inverse = np.block([[cosine, sine], [-sine, cosine]])
    return jnp.asarray(forward, F32).astype(BF16), jnp.asarray(inverse, F32).astype(BF16)


def shifted(array, axis, by):
    peers = lax.axis_size(axis)
    pairs = [(i, i + by) for i in range(peers) if 0 <= i + by < peers]
    return lax.ppermute(array, axis, pairs)


def any_spec():
    return pl.BlockSpec(memory_space=pl.ANY)


def smem_spec():
    return pl.BlockSpec(memory_space=pltpu.SMEM)


def vmem_spec():
    return pl.BlockSpec(memory_space=pltpu.VMEM)


def params():
    return pltpu.CompilerParams(vmem_limit_bytes=VMEM_LIMIT)


def taken_from(blocks, by):
    lane = lax.broadcasted_iota(jnp.int32, blocks[0].shape, 1)
    rolled = [pltpu.roll(block, lax.rem(LANES - by, LANES), axis=1) for block in blocks]
    return [jnp.where(lane < LANES - by, one, two) for one, two in zip(rolled[:-1], rolled[1:])]


def put_into(blocks, by):
    lane = lax.broadcasted_iota(jnp.int32, blocks[0].shape, 1)
    rolled = [pltpu.roll(block, by, axis=1) for block in blocks]
    none = jnp.zeros_like(blocks[0])
    return [jnp.where(lane >= by, one, two) for one, two in zip(rolled + [none], [none] + rolled)]


def start_all(pairs, sems, first=0):
    copies = [pltpu.make_async_copy(source, target, sems.at[first + at]) for at, (source, target) in enumerate(pairs)]
    for copy in copies:
        copy.start()
    return copies


def wait_all(copies):
    for copy in copies:
        copy.wait()


def lanes_of(block):
    return pl.ds(block * LANES, LANES)


def side_by_side(parts):
    return jnp.concatenate(parts, axis=1)


def halves(array):
    return [array[:, :LANES], array[:, LANES:]]


def is_band(table):
    return table[CHOICE] > len(SIZES)


def band_places(blocks, frame):
    for at in range(2 * blocks):
        group, lane = divmod(at, 4)
        yield at // blocks, at % blocks, pl.ds(group * frame, frame), lanes_of(lane)


def copy_out_rows(table, packed, out, sems):
    chunks = jnp.where(is_band(table), out.shape[0], table[NEEDED])
    chunks = (chunks + CHUNK - 1) // CHUNK

    def copy(chunk):
        at = pl.ds(pl.multiple_of(chunk * CHUNK, CHUNK), CHUNK)
        return pltpu.make_async_copy(packed.at[at], out.at[at], sems.at[chunk])

    def begin(chunk, carry):
        copy(chunk).start()
        return carry

    def end(chunk, carry):
        copy(chunk).wait()
        return carry

    lax.fori_loop(0, chunks, begin, 0)
    lax.fori_loop(0, chunks, end, 0)


def table_kernel(extent, frame, positions, counts, table):
    cap = positions.shape[1]
    count = counts[0]
    total = jnp.int32(0)
    for at in range(TABLE):
        table[at] = 0
    for slot in range(cap):
        row = lax.rem(positions[0, slot, 0], extent)
        col = lax.rem(positions[0, slot, 1], extent)
        below = jnp.where(slot < count, jnp.maximum(row + (frame - extent), 0), 0)
        table[ROW + slot] = row
        table[COL + slot] = col
        table[BELOW + slot] = below
        table[PLACE + slot] = total
        total = total + (below + ROW_ALIGN - 1) // ROW_ALIGN * ROW_ALIGN
    choice = jnp.where(total > 0, 1, 0)
    for size in SIZES:
        choice = choice + jnp.where(total > size, 1, 0)
    table[COUNT] = count
    table[NEEDED] = total
    table[CHOICE] = choice


def slot_table(positions, counts, extent, frame):
    return pl.pallas_call(
        lambda *refs: table_kernel(extent, frame, *refs),
        out_shape=jax.ShapeDtypeStruct((TABLE,), jnp.int32),
        in_specs=[smem_spec(), smem_spec()],
        out_specs=smem_spec(),
        name="slot_table",
    )(positions, counts)


def cut_kernel(cap, table, tile, strip, out, band, packed, sems):
    frame = strip.shape[-1]
    extent = tile.shape[-1]
    across = frame // LANES
    own_blocks = extent // LANES
    top = pl.ds(0, frame)

    @pl.when(table[NEEDED] > 0)
    def _():
        wait_all(start_all(
            [(tile.at[:, top, lanes_of(b)], band.at[:, b]) for b in range(own_blocks)]
            + [(strip.at[:, :, lanes_of(b)], band.at[:, own_blocks + b]) for b in range(across)], sems))

        def one(slot, carry):
            col, below, place = table[COL + slot], table[BELOW + slot], table[PLACE + slot]

            @pl.when(below > 0)
            def _():
                first = col // LANES
                at = pl.ds(pl.multiple_of(place, ROW_ALIGN), frame)
                for plane in range(2):
                    cut = taken_from([band[plane, first + b] for b in range(across + 1)], lax.rem(col, LANES))
                    packed[at, pl.ds(plane * frame, frame)] = side_by_side(cut)

            return carry

        @pl.when(is_band(table))
        def _():
            for plane, b, at, lanes in band_places(own_blocks + across, frame):
                packed[at, lanes] = band[plane, b]

        @pl.when(jnp.logical_not(is_band(table)))
        def _():
            lax.fori_loop(0, cap, one, 0)

        copy_out_rows(table, packed, out, sems)


def cut_pieces(table, tile, strip, cap):
    frame = strip.shape[-1]
    extent = tile.shape[-1]
    blocks = (extent + frame) // LANES
    rows = SIZES[-1]
    return pl.pallas_call(
        lambda *refs: cut_kernel(cap, *refs),
        out_shape=jax.ShapeDtypeStruct((rows, 2 * frame), F32),
        in_specs=[smem_spec(), any_spec(), any_spec()],
        out_specs=any_spec(),
        scratch_shapes=[
            pltpu.VMEM((2, blocks, frame, LANES), F32),
            pltpu.VMEM((rows + frame, 2 * frame), F32),
            pltpu.SemaphoreType.DMA((rows // CHUNK,)),
        ],
        compiler_params=params(),
        name="cut_pieces",
    )(table, tile, strip)


def frame_step(patch, measured, probe, forward, inverse, field):
    modes, _, frame, _ = probe.shape
    scale = 1.0 / frame
    intensity = jnp.zeros((frame, frame), F32)
    for mode in range(modes):
        probe_real, probe_imag = probe[mode, 0], probe[mode, 1]
        wave = side_by_side(
            [probe_real * patch[0] - probe_imag * patch[1], probe_real * patch[1] + probe_imag * patch[0]]
        ).astype(BF16)
        half = jnp.dot(wave, forward[...], preferred_element_type=F32).astype(BF16)
        half = jnp.concatenate([half[:, :frame], half[:, frame:]], axis=0)
        far = jnp.dot(inverse[...], half, preferred_element_type=F32) * scale
        field[mode] = far
        intensity += far[:frame] * far[:frame] + far[frame:] * far[frame:]
    factor = 1.0 - jnp.sqrt(measured) / jnp.sqrt(jnp.maximum(intensity, 1.0))
    grad_real = jnp.zeros((frame, frame), F32)
    grad_imag = jnp.zeros((frame, frame), F32)
    for mode in range(modes):
        residual = side_by_side([field[mode, :frame] * factor, field[mode, frame:] * factor]).astype(BF16)
        half = jnp.dot(residual, inverse[...], preferred_element_type=F32).astype(BF16)
        half = jnp.concatenate([half[:, :frame], half[:, frame:]], axis=0)
        back = jnp.dot(forward[...], half, preferred_element_type=F32) * scale
        probe_real, probe_imag = probe[mode, 0], probe[mode, 1]
        grad_real += probe_real * back[:frame] + probe_imag * back[frame:]
        grad_imag += probe_real * back[frame:] - probe_imag * back[:frame]
    return [halves(grad_real), halves(grad_imag)]


def window(band, plane, row, col, frame):
    return taken_from(
        [band[plane, col // LANES + b, pl.ds(row, frame), :] for b in range(frame // LANES + 1)], lax.rem(col, LANES)
    )


def add_window(total, lead, parts, row, col, frame):
    for b, moved in enumerate(put_into(parts, lax.rem(col, LANES))):
        at = lead + (col // LANES + b, pl.ds(row, frame), slice(None))
        total[at] = total[at] + moved


def band_copies(tile, strip_top, strip_low, band, frame):
    extent = tile.shape[-1]
    across = frame // LANES
    own_blocks = extent // LANES
    return (
        [(tile.at[:, :, lanes_of(b)], band.at[:, b, pl.ds(0, extent)]) for b in range(own_blocks)]
        + [(strip_top.at[:, :, lanes_of(b)], band.at[:, own_blocks + b, pl.ds(0, frame)]) for b in range(across)]
        + [(strip_low.at[:, :, lanes_of(b)], band.at[:, own_blocks + b, pl.ds(frame, extent - frame)])
           for b in range(across)]
    )


def inner_kernel(own, left, up, corner, tile, strip_top, strip_low, frames, probe_in, tables_in, total_out, light_out,
                 band, total, light, measured, probe, tables, field, sems, frame_sems):
    cap, frame, _ = frames.shape
    extent = tile.shape[-1]
    modes = probe.shape[0]
    across = frame // LANES
    own_blocks = extent // LANES
    probe_copy = start_all([(probe_in, probe)], sems)

    def frame_copy(slot):
        return pltpu.make_async_copy(frames.at[slot], measured.at[slot], frame_sems.at[slot])

    def inner(slot):
        return jnp.logical_and(slot < own[COUNT], own[BELOW + slot] == 0)

    for slot in range(cap):
        @pl.when(inner(slot))
        def _():
            frame_copy(slot).start()

    rest = start_all([(tables_in, tables)] + band_copies(tile, strip_top, strip_low, band, frame), sems, 1)
    total[...] = jnp.zeros_like(total)
    inside = (pl.ds(across, own_blocks), pl.ds(frame, extent), slice(None))
    light[inside] = jnp.zeros((own_blocks, extent, LANES), F32)
    wait_all(probe_copy)
    power = jnp.zeros((frame, frame), F32)
    for mode in range(modes):
        power += probe[mode, 0] * probe[mode, 0] + probe[mode, 1] * probe[mode, 1]
    power = halves(power)
    for table, down, right in ((own, 0, 0), (left, 0, 1), (up, 1, 0), (corner, 1, 1)):

        def lit(slot, carry, table=table, down=down, right=right):
            row = table[ROW + slot] + frame - down * extent
            col = table[COL + slot] + frame - right * extent

            @pl.when((row > 0) & (col > 0))
            def _():
                add_window(light, (), power, row, col, frame)

            return carry

        lax.fori_loop(0, table[COUNT], lit, 0)
    light_copy = start_all([(light.at[inside[0], inside[1]], light_out)], sems)
    wait_all(rest)

    def one(slot, carry):
        @pl.when(inner(slot))
        def _():
            row, col = own[ROW + slot], own[COL + slot]
            patch = [side_by_side(window(band, plane, row, col, frame)) for plane in range(2)]
            frame_copy(slot).wait()
            grads = frame_step(patch, measured[slot], probe, tables.at[0], tables.at[1], field)
            for plane in range(2):
                add_window(total, (plane,), grads[plane], row, col, frame)

        return carry

    lax.fori_loop(0, own[COUNT], one, 0)
    wait_all(start_all([(total, total_out)], sems, 1))
    wait_all(light_copy)


def kernel_cost(frames, modes, frame):
    flops = frames * modes * 4 * 2 * frame * 2 * frame * 2 * frame
    return pl.CostEstimate(flops=flops, bytes_accessed=16 * 1024 * 1024, transcendentals=0)


def inner_frames(own, left, up, corner, tile, strip_top, strip_low, frames, probe, tables):
    cap, frame, _ = frames.shape
    extent = tile.shape[-1]
    modes = probe.shape[0]
    blocks = (extent + frame) // LANES
    wide = extent + 2 * frame
    return pl.pallas_call(
        inner_kernel,
        out_shape=(
            jax.ShapeDtypeStruct((2, blocks, extent, LANES), F32),
            jax.ShapeDtypeStruct((extent // LANES, extent, LANES), F32),
        ),
        in_specs=[smem_spec()] * 4 + [any_spec()] * 6,
        out_specs=(any_spec(), any_spec()),
        scratch_shapes=[
            pltpu.VMEM((2, blocks, extent, LANES), F32),
            pltpu.VMEM((2, blocks, extent, LANES), F32),
            pltpu.VMEM((wide // LANES, wide, LANES), F32),
            pltpu.VMEM((cap, frame, frame), F32),
            pltpu.VMEM(probe.shape, F32),
            pltpu.VMEM(tables.shape, BF16),
            pltpu.VMEM((modes, 2 * frame, frame), F32),
            pltpu.SemaphoreType.DMA((blocks + 2 * (frame // LANES) + 2,)),
            pltpu.SemaphoreType.DMA((cap,)),
        ],
        compiler_params=params(),
        cost_estimate=kernel_cost(cap, modes, frame),
        name="inner_frames",
    )(own, left, up, corner, tile, strip_top, strip_low, frames, probe, tables)


def outer_kernel(own, tile, strip_top, strip_low, frames, probe_in, tables_in, received, total_in, total_out, packed_out,
                 band, total, held, packed, piece, measured, probe, tables, field, sems, frame_sems, held_sems, chunk_sems):
    cap, frame, _ = frames.shape
    extent = tile.shape[-1]
    across = frame // LANES
    blocks = band.shape[1]
    rows = received.shape[0]
    whole = is_band(own)

    def frame_copy(slot):
        return pltpu.make_async_copy(frames.at[slot], measured.at[slot], frame_sems.at[slot])

    def source_row(slot):
        return jnp.minimum(own[PLACE + slot], rows - frame)

    def held_copies(slot):
        at = pl.ds(pl.multiple_of(source_row(slot), ROW_ALIGN), frame)
        return [
            pltpu.make_async_copy(received.at[at, lanes_of(b)], held.at[slot, b, pl.ds(frame, frame)], held_sems.at[slot, b])
            for b in range(2 * across)
        ]

    def outer(slot):
        return own[BELOW + slot] > 0

    @pl.when(own[NEEDED] > 0)
    def _():
        first = start_all([(probe_in, probe), (tables_in, tables)]
                          + band_copies(tile, strip_top, strip_low, band, frame), sems)
        for slot in range(cap):
            @pl.when(outer(slot))
            def _():
                frame_copy(slot).start()

                @pl.when(jnp.logical_not(whole))
                def _():
                    for copy in held_copies(slot):
                        copy.start()

        last = start_all([(total_in, total.at[:, :, pl.ds(0, extent)])], sems, len(first))
        total[:, :, pl.ds(extent, frame), :] = jnp.zeros((2, blocks, frame, LANES), F32)
        first_outer = jnp.int32(cap)
        for slot in reversed(range(cap)):
            first_outer = jnp.where(outer(slot), slot, first_outer)
        wait_all(first)

        @pl.when(whole)
        def _():
            wait_all(start_all(
                [(received.at[at, lanes], band.at[plane, b, pl.ds(extent, frame)])
                 for plane, b, at, lanes in band_places(blocks, frame)], sems))

        row_index = lax.broadcasted_iota(jnp.int32, (frame, LANES), 0)

        def one(slot, carry):
            @pl.when(outer(slot))
            def _():
                row, col, below, place = own[ROW + slot], own[COL + slot], own[BELOW + slot], own[PLACE + slot]
                inside = jnp.where(whole, frame, frame - below)

                @pl.when(jnp.logical_not(whole))
                def _():
                    for copy in held_copies(slot):
                        copy.wait()

                patch = []
                at = pl.ds(below + place - source_row(slot), frame)
                for plane in range(2):
                    mine = window(band, plane, row, col, frame)
                    other = [held[slot, plane * across + b, at, :] for b in range(across)]
                    patch.append(side_by_side([jnp.where(row_index < inside, a, b) for a, b in zip(mine, other)]))
                frame_copy(slot).wait()
                grads = frame_step(patch, measured[slot], probe, tables.at[0], tables.at[1], field)

                @pl.when(slot == first_outer)
                def _():
                    wait_all(last)

                for plane in range(2):
                    add_window(total, (plane,), grads[plane], row, col, frame)

                @pl.when(jnp.logical_not(whole))
                def _():
                    target = pl.ds(pl.multiple_of(place, ROW_ALIGN), frame)
                    for b, part in enumerate(grads[0] + grads[1]):
                        piece[b, pl.ds(0, frame), :] = part
                        packed[target, lanes_of(b)] = piece[b, pl.ds(frame - below, frame), :]

            return carry

        lax.fori_loop(0, own[COUNT], one, 0)

        @pl.when(whole)
        def _():
            for plane, b, at, lanes in band_places(blocks, frame):
                packed[at, lanes] = total[plane, b, pl.ds(extent, frame), :]

        end = start_all([(total.at[:, :, pl.ds(0, extent)], total_out)], sems)
        copy_out_rows(own, packed, packed_out, chunk_sems)
        wait_all(end)


def outer_frames(own, tile, strip_top, strip_low, frames, probe, tables, received, total):
    cap, frame, _ = frames.shape
    extent = tile.shape[-1]
    modes = probe.shape[0]
    tall = extent + frame
    blocks = tall // LANES
    across = frame // LANES
    rows = received.shape[0]
    return pl.pallas_call(
        outer_kernel,
        out_shape=(
            jax.ShapeDtypeStruct(total.shape, F32),
            jax.ShapeDtypeStruct(received.shape, F32),
        ),
        in_specs=[smem_spec()] + [any_spec()] * 8,
        out_specs=(any_spec(), any_spec()),
        input_output_aliases={8: 0},
        scratch_shapes=[
            pltpu.VMEM((2, blocks, tall, LANES), F32),
            pltpu.VMEM((2, blocks, tall, LANES), F32),
            pltpu.VMEM((cap, 2 * across, 3 * frame, LANES), F32),
            pltpu.VMEM((rows + frame, 2 * frame), F32),
            pltpu.VMEM((2 * across, 2 * frame, LANES), F32),
            pltpu.VMEM((cap, frame, frame), F32),
            pltpu.VMEM(probe.shape, F32),
            pltpu.VMEM(tables.shape, BF16),
            pltpu.VMEM((modes, 2 * frame, frame), F32),
            pltpu.SemaphoreType.DMA((2 * blocks + 3,)),
            pltpu.SemaphoreType.DMA((cap,)),
            pltpu.SemaphoreType.DMA((cap, 2 * across)),
            pltpu.SemaphoreType.DMA((rows // CHUNK,)),
        ],
        compiler_params=params(),
        cost_estimate=kernel_cost(cap, modes, frame),
        name="outer_frames",
    )(own, tile, strip_top, strip_low, frames, probe, tables, received, total)


def join_kernel(cap, frame, table, pieces, total_in, total_out, band, held, sems):
    blocks = band.shape[1]
    across = frame // LANES
    rows = pieces.shape[0]
    whole = is_band(table)
    top = pl.ds(0, frame)

    @pl.when(table[NEEDED] > 0)
    def _():
        wait_all(start_all(
            [(total_in.at[:, :, top], band)]
            + [(pieces.at[:, lanes_of(b)], held.at[b, pl.ds(0, rows)]) for b in range(2 * across)], sems))
        row_index = lax.broadcasted_iota(jnp.int32, (frame, LANES), 0)

        def one(slot, carry):
            col, below, place = table[COL + slot], table[BELOW + slot], table[PLACE + slot]

            @pl.when(below > 0)
            def _():
                at = pl.ds(pl.multiple_of(place, ROW_ALIGN), frame)
                for plane in range(2):
                    got = [jnp.where(row_index < below, held[plane * across + b, at, :], 0.0) for b in range(across)]
                    add_window(band, (plane,), got, 0, col, frame)

            return carry

        @pl.when(whole)
        def _():
            for at in range(2 * blocks):
                group, lane = divmod(at, 4)
                band[at // blocks, at % blocks] = band[at // blocks, at % blocks] + held[lane, pl.ds(group * frame, frame), :]

        @pl.when(jnp.logical_not(whole))
        def _():
            lax.fori_loop(0, cap, one, 0)

        wait_all(start_all([(band, total_out.at[:, :, top])], sems))


def join_pieces(table, pieces, total, cap):
    rows, double = pieces.shape
    frame = double // 2
    blocks = total.shape[1]
    across = frame // LANES
    return pl.pallas_call(
        lambda *refs: join_kernel(cap, frame, *refs),
        out_shape=jax.ShapeDtypeStruct(total.shape, F32),
        in_specs=[smem_spec(), any_spec(), any_spec()],
        out_specs=any_spec(),
        input_output_aliases={2: 0},
        scratch_shapes=[
            pltpu.VMEM((2, blocks, frame, LANES), F32),
            pltpu.VMEM((2 * across, rows + frame, LANES), F32),
            pltpu.SemaphoreType.DMA((2 * across + 1,)),
        ],
        compiler_params=params(),
        name="join_pieces",
    )(table, pieces, total)


def final_kernel(tops, tile, total, light, top, low, out):
    across = top.shape[1]
    step = pl.program_id(0)
    for b in range(total.shape[1]):
        below = 1.0 / (light[b] + 1.0)
        for plane in range(2):
            grad = total[plane, b]
            if b < across:
                grad = grad + jnp.where(step < tops, top[plane, b], low[plane, b])
            out[plane, :, lanes_of(b)] = tile[plane, :, lanes_of(b)] - grad * below


def final_update(tile, total, light, top, low):
    extent = tile.shape[-1]
    blocks = extent // LANES
    across, height = top.shape[1], top.shape[2]
    tall = 128
    tops = height // tall
    return pl.pallas_call(
        lambda *refs: final_kernel(tops, *refs),
        grid=(extent // tall,),
        out_shape=jax.ShapeDtypeStruct(tile.shape, F32),
        in_specs=[
            pl.BlockSpec((2, tall, extent), lambda i: (0, i, 0)),
            pl.BlockSpec((2, blocks, tall, LANES), lambda i: (0, 0, i, 0)),
            pl.BlockSpec((blocks, tall, LANES), lambda i: (0, i, 0)),
            pl.BlockSpec((2, across, tall, LANES), lambda i: (0, 0, jnp.minimum(i, tops - 1), 0)),
            pl.BlockSpec((2, across, tall, LANES), lambda i: (0, 0, jnp.maximum(i - tops, 0), 0)),
        ],
        out_specs=pl.BlockSpec((2, tall, extent), lambda i: (0, i, 0)),
        compiler_params=params(),
        name="final_update",
    )(tile, total, light, top, low)


def body(object_tiles, probe, positions, frames, counts):
    tile = object_tiles[0]
    extent = tile.shape[-1]
    frame = frames.shape[-1]
    cap = frames.shape[1]
    peers = lax.axis_size("scan")
    tile_row = lax.axis_index("scan") // TCOLS
    rows = SIZES[-1]
    tables = jnp.stack(dft_tables(frame))

    own = slot_table(positions, counts, extent, frame)
    up = shifted(own, "scan", TCOLS)
    left = shifted(own, "scan", 1)
    corner = shifted(own, "scan", TCOLS + 1)
    strip_top = shifted(tile[:, :frame, :frame], "scan", -1)
    strip_low = shifted(tile[:, frame:, :frame], "scan", -1)
    left, corner, up, strip_top = lax.optimization_barrier((left, corner, up, strip_top))

    def exchange(packed, upward, beside):
        def sender(size, pairs, meanwhile):
            def run(data):
                moved = jnp.zeros((rows, 2 * frame), F32)
                if size:
                    got = lax.ppermute(data[:size], "scan", pairs)
                    moved = got if size == rows else jnp.pad(got, ((0, rows - size), (0, 0)))
                return moved, meanwhile()
            return run

        result, others = None, None
        for phase in range(2):
            uppers = [k for k in range(peers - TCOLS) if k // TCOLS % 2 == phase]
            if not uppers:
                continue
            pairs = [(k + TCOLS, k) if upward else (k, k + TCOLS) for k in uppers]
            is_upper = tile_row % 2 == phase
            choice = jnp.where(is_upper, own[CHOICE], up[CHOICE])
            meanwhile = beside if result is None else lambda: ()
            branches = [sender(size, pairs, meanwhile) for size in (0,) + SIZES + (rows,)]
            moved, done = lax.switch(choice, branches, packed)
            receives = is_upper if upward else jnp.logical_not(is_upper)
            result = moved if result is None else jnp.where(receives, moved, result)
            others = done if others is None else others
        return result, others

    packed = cut_pieces(up, tile, strip_top, cap)
    received, (total, light) = exchange(
        packed, True, lambda: inner_frames(own, left, up, corner, tile, strip_top, strip_low, frames[0], probe, tables)
    )
    total, packed_grad = outer_frames(own, tile, strip_top, strip_low, frames[0], probe, tables, received, total)
    own_blocks = extent // LANES
    left_low = shifted(total[:, own_blocks:, frame:], "scan", 1)
    pieces, _ = exchange(packed_grad, False, lambda: ())
    total = join_pieces(up, pieces, total, cap)
    left_top = shifted(total[:, own_blocks:, :frame], "scan", 1)
    return final_update(tile, total, light, left_top, left_low)[None]


def solution(mesh):
    return jax.shard_map(
        body,
        mesh=mesh,
        in_specs=(
            P(("grp", "scan"), None, None, None),
            P(),
            P(("grp", "scan"), None, None),
            P(("grp", "scan"), None, None, None),
            P(("grp", "scan")),
        ),
        out_specs=P(("grp", "scan"), None, None, None),
        check_vma=False,
    )
```

```python
import math

import jax
import jax.numpy as jnp
import numpy as np
from jax import lax
from jax.experimental import pallas as pl
from jax.experimental.pallas import tpu as pltpu
from jax.sharding import PartitionSpec as P

TCOLS = 8
LANES = 128
ROW_ALIGN = 8
CHUNK = 64
SIZES = (32, 64, 96, 128, 160, 192, 224, 256, 320, 384, 448, 512, 640, 768)
VMEM_LIMIT = 56 * 1024 * 1024
F32 = jnp.float32
BF16 = jnp.bfloat16

ROW, COL, BELOW, PLACE = 0, 8, 16, 24
COUNT, NEEDED, CHOICE = 32, 33, 34
TABLE = 64


def dft_tables(frame):
    near = np.arange(frame // 2, dtype=np.int64)
    blocks = []
    for odd in range(2):
        phase = (near[:, None] * (2 * near[None, :] + odd) % frame).astype(np.float64) * (2.0 * math.pi / frame)
        c, s = np.cos(phase), np.sin(phase)
        ahead = np.block([[c, -s], [s, c]])
        back = np.block([[c.T, s.T], [-s.T, c.T]])
        blocks.append((ahead, ahead.T, back, back.T))
    order = np.zeros((frame, frame))
    order[2 * near, near] = 1.0
    order[2 * near + 1, near + frame // 2] = 1.0
    tables = [blocks[odd][kind] for kind in range(4) for odd in range(2)] + [order]
    return jnp.asarray(np.stack(tables), F32).astype(BF16)


def shifted(array, axis, by):
    peers = lax.axis_size(axis)
    pairs = [(i, i + by) for i in range(peers) if 0 <= i + by < peers]
    return lax.ppermute(array, axis, pairs)


def any_spec():
    return pl.BlockSpec(memory_space=pl.ANY)


def smem_spec():
    return pl.BlockSpec(memory_space=pltpu.SMEM)


def vmem_spec():
    return pl.BlockSpec(memory_space=pltpu.VMEM)


def params():
    return pltpu.CompilerParams(vmem_limit_bytes=VMEM_LIMIT)


def taken_from(blocks, by):
    lane = lax.broadcasted_iota(jnp.int32, blocks[0].shape, 1)
    rolled = [pltpu.roll(block, lax.rem(LANES - by, LANES), axis=1) for block in blocks]
    return [jnp.where(lane < LANES - by, one, two) for one, two in zip(rolled[:-1], rolled[1:])]


def put_into(blocks, by):
    lane = lax.broadcasted_iota(jnp.int32, blocks[0].shape, 1)
    rolled = [pltpu.roll(block, by, axis=1) for block in blocks]
    none = jnp.zeros_like(blocks[0])
    return [jnp.where(lane >= by, one, two) for one, two in zip(rolled + [none], [none] + rolled)]


def start_all(pairs, sems, first=0):
    copies = [pltpu.make_async_copy(source, target, sems.at[first + at]) for at, (source, target) in enumerate(pairs)]
    for copy in copies:
        copy.start()
    return copies


def wait_all(copies):
    for copy in copies:
        copy.wait()


def lanes_of(block):
    return pl.ds(block * LANES, LANES)


def side_by_side(parts):
    return jnp.concatenate(parts, axis=1)


def halves(array):
    return [array[:, :LANES], array[:, LANES:]]


def is_band(table):
    return table[CHOICE] > len(SIZES)


def band_places(blocks, frame):
    for at in range(2 * blocks):
        group, lane = divmod(at, 4)
        yield at // blocks, at % blocks, pl.ds(group * frame, frame), lanes_of(lane)


def copy_out_rows(table, packed, out, sems):
    chunks = jnp.where(is_band(table), out.shape[0], table[NEEDED])
    chunks = (chunks + CHUNK - 1) // CHUNK

    def copy(chunk):
        at = pl.ds(pl.multiple_of(chunk * CHUNK, CHUNK), CHUNK)
        return pltpu.make_async_copy(packed.at[at], out.at[at], sems.at[chunk])

    def begin(chunk, carry):
        copy(chunk).start()
        return carry

    def end(chunk, carry):
        copy(chunk).wait()
        return carry

    lax.fori_loop(0, chunks, begin, 0)
    lax.fori_loop(0, chunks, end, 0)


def table_kernel(extent, frame, positions, counts, table):
    cap = positions.shape[1]
    count = counts[0]
    total = jnp.int32(0)
    for at in range(TABLE):
        table[at] = 0
    for slot in range(cap):
        row = lax.rem(positions[0, slot, 0], extent)
        col = lax.rem(positions[0, slot, 1], extent)
        below = jnp.where(slot < count, jnp.maximum(row + (frame - extent), 0), 0)
        table[ROW + slot] = row
        table[COL + slot] = col
        table[BELOW + slot] = below
        table[PLACE + slot] = total
        total = total + (below + ROW_ALIGN - 1) // ROW_ALIGN * ROW_ALIGN
    choice = jnp.where(total > 0, 1, 0)
    for size in SIZES:
        choice = choice + jnp.where(total > size, 1, 0)
    table[COUNT] = count
    table[NEEDED] = total
    table[CHOICE] = choice


def slot_table(positions, counts, extent, frame):
    return pl.pallas_call(
        lambda *refs: table_kernel(extent, frame, *refs),
        out_shape=jax.ShapeDtypeStruct((TABLE,), jnp.int32),
        in_specs=[smem_spec(), smem_spec()],
        out_specs=smem_spec(),
        name="slot_table",
    )(positions, counts)


def cut_kernel(cap, table, own, parity, tile, strip, out, first, second, band, packed, sems):
    frame = strip.shape[-1]
    extent = tile.shape[-1]
    across = frame // LANES
    own_blocks = extent // LANES
    top = pl.ds(0, frame)
    first[0] = jnp.where(parity[0] == 0, own[CHOICE], table[CHOICE])
    second[0] = jnp.where(parity[0] == 1, own[CHOICE], table[CHOICE])

    @pl.when(table[NEEDED] > 0)
    def _():
        wait_all(start_all(
            [(tile.at[:, top, lanes_of(b)], band.at[:, b]) for b in range(own_blocks)]
            + [(strip.at[:, :, lanes_of(b)], band.at[:, own_blocks + b]) for b in range(across)], sems))

        def one(slot, carry):
            col, below, place = table[COL + slot], table[BELOW + slot], table[PLACE + slot]

            @pl.when(below > 0)
            def _():
                first = col // LANES
                at = pl.ds(pl.multiple_of(place, ROW_ALIGN), frame)
                for plane in range(2):
                    cut = taken_from([band[plane, first + b] for b in range(across + 1)], lax.rem(col, LANES))
                    packed[at, pl.ds(plane * frame, frame)] = side_by_side(cut)

            return carry

        @pl.when(is_band(table))
        def _():
            for plane, b, at, lanes in band_places(own_blocks + across, frame):
                packed[at, lanes] = band[plane, b]

        @pl.when(jnp.logical_not(is_band(table)))
        def _():
            lax.fori_loop(0, cap, one, 0)

        copy_out_rows(table, packed, out, sems)


def cut_pieces(table, own, parity, tile, strip, cap):
    frame = strip.shape[-1]
    extent = tile.shape[-1]
    blocks = (extent + frame) // LANES
    rows = SIZES[-1]
    return pl.pallas_call(
        lambda *refs: cut_kernel(cap, *refs),
        out_shape=(
            jax.ShapeDtypeStruct((rows, 2 * frame), F32),
            jax.ShapeDtypeStruct((1,), jnp.int32),
            jax.ShapeDtypeStruct((1,), jnp.int32),
        ),
        in_specs=[smem_spec(), smem_spec(), smem_spec(), any_spec(), any_spec()],
        out_specs=(any_spec(), smem_spec(), smem_spec()),
        scratch_shapes=[
            pltpu.VMEM((2, blocks, frame, LANES), F32),
            pltpu.VMEM((rows + frame, 2 * frame), F32),
            pltpu.SemaphoreType.DMA((rows // CHUNK,)),
        ],
        compiler_params=params(),
        name="cut_pieces",
    )(table, own, parity, tile, strip)


def dot(one, two):
    return jnp.dot(one, two, preferred_element_type=F32)


def stacked(parts):
    return jnp.concatenate(parts, axis=0)


def sums(array, axis):
    half = array.shape[axis] // 2
    near = lax.slice_in_dim(array, 0, half, axis=axis)
    far = lax.slice_in_dim(array, half, 2 * half, axis=axis)
    return near + far, near - far


def quarters(real, imag):
    half = real.shape[1] // 2
    return stacked([side_by_side([real[:, :half], imag[:, :half]]), side_by_side([real[:, half:], imag[:, half:]])])


def frame_step(patch, amplitude, probe, tables, field):
    modes, _, frame, _ = probe.shape
    half = frame // 2
    lit = [jnp.zeros((half, frame), F32), jnp.zeros((half, frame), F32)]
    for mode in range(modes):
        probe_real, probe_imag = probe[mode, 0], probe[mode, 1]
        real = sums(probe_real * patch[0] - probe_imag * patch[1], 1)
        imag = sums(probe_real * patch[1] + probe_imag * patch[0], 1)
        across = [sums(dot(side_by_side([real[odd], imag[odd]]).astype(BF16), tables[odd]), 0) for odd in range(2)]
        for odd in range(2):
            far = dot(tables[2 + odd], quarters(across[0][odd], across[1][odd]).astype(BF16))
            field[mode, odd] = far
            lit[odd] += far[:half] * far[:half] + far[half:] * far[half:]
    factors = []
    for odd in range(2):
        factor = 1.0 / frame - amplitude[odd] * lax.rsqrt(jnp.maximum(lit[odd], float(frame * frame)))
        factors.append(stacked([factor, factor]))
    grad_real = jnp.zeros((frame, frame), F32)
    grad_imag = jnp.zeros((frame, frame), F32)
    for mode in range(modes):
        rest = [(field[mode, odd] * factors[odd]).astype(BF16) for odd in range(2)]
        moved = []
        for odd in range(2):
            lanes = slice(odd * half, odd * half + half)
            moved.append(dot(
                stacked([side_by_side([part[:half, lanes], part[half:, lanes]]) for part in rest]), tables[4 + odd]))
        near, far = moved[0] + moved[1], moved[0] - moved[1]
        even = dot(tables[6], quarters(near[:half], far[:half]).astype(BF16))
        odd = dot(tables[7], quarters(near[half:], far[half:]).astype(BF16))
        near, far = even + odd, even - odd
        back_real = stacked([near[:half], far[:half]])
        back_imag = stacked([near[half:], far[half:]])
        probe_real, probe_imag = probe[mode, 0], probe[mode, 1]
        grad_real += probe_real * back_real + probe_imag * back_imag
        grad_imag += probe_real * back_imag - probe_imag * back_real
    return [halves(grad_real * (1.0 / frame)), halves(grad_imag * (1.0 / frame))]


def ordered_amplitude(measured, slot, order):
    frame = measured.shape[2]
    parts = []
    for odd in range(2):
        root = jnp.sqrt(side_by_side(
            [measured[slot, b, pl.ds(odd, frame // 2, stride=2), :] for b in range(measured.shape[1])]))
        high = root.astype(BF16)
        low = (root - high.astype(F32)).astype(BF16)
        parts.append(dot(high, order) + dot(low, order))
    return parts


def window(band, plane, row, col, frame):
    return taken_from(
        [band[plane, col // LANES + b, pl.ds(row, frame), :] for b in range(frame // LANES + 1)], lax.rem(col, LANES)
    )


def add_window(total, lead, parts, row, col, frame):
    for b, moved in enumerate(put_into(parts, lax.rem(col, LANES))):
        at = lead + (col // LANES + b, pl.ds(row, frame), slice(None))
        total[at] = total[at] + moved


def band_copies(tile, strip_top, strip_low, band, frame):
    extent = tile.shape[-1]
    across = frame // LANES
    own_blocks = extent // LANES
    return (
        [(tile.at[:, :, lanes_of(b)], band.at[:, b, pl.ds(0, extent)]) for b in range(own_blocks)]
        + [(strip_top.at[:, :, lanes_of(b)], band.at[:, own_blocks + b, pl.ds(0, frame)]) for b in range(across)]
        + [(strip_low.at[:, :, lanes_of(b)], band.at[:, own_blocks + b, pl.ds(frame, extent - frame)])
           for b in range(across)]
    )


def kernel_cost(frames, modes, frame):
    return pl.CostEstimate(
        flops=frames * modes * 4 * 4 * frame ** 3, bytes_accessed=16 * 1024 * 1024, transcendentals=0)


def frames_kernel(own, tile, strip_top, strip_low, frames, probe_in, tables_in, received, total_out, low_out, packed_out,
                  band, total, held, packed, piece, measured, probe, tables, field,
                  sems, frame_sems, held_sems, chunk_sems):
    cap, frame, _ = frames.shape
    extent = tile.shape[-1]
    across = frame // LANES
    blocks = band.shape[1]
    own_blocks = extent // LANES
    rows = received.shape[0]
    whole = is_band(own)

    def frame_copies(slot):
        return [pltpu.make_async_copy(frames.at[slot, :, lanes_of(b)], measured.at[slot, b], frame_sems.at[slot, b])
                for b in range(across)]

    def source_row(slot):
        return jnp.minimum(own[PLACE + slot], rows - frame)

    def held_copies(slot):
        at = pl.ds(pl.multiple_of(source_row(slot), ROW_ALIGN), frame)
        return [
            pltpu.make_async_copy(received.at[at, lanes_of(b)], held.at[slot, b, pl.ds(frame, frame)], held_sems.at[slot, b])
            for b in range(2 * across)
        ]

    def split(slot):
        return jnp.logical_and(own[BELOW + slot] > 0, jnp.logical_not(whole))

    first = start_all(band_copies(tile, strip_top, strip_low, band, frame) + [(probe_in, probe), (tables_in, tables)], sems)
    for slot in range(cap):
        @pl.when(slot < own[COUNT])
        def _():
            for copy in frame_copies(slot):
                copy.start()

        @pl.when(split(slot))
        def _():
            for copy in held_copies(slot):
                copy.start()

    total[...] = jnp.zeros_like(total)
    wait_all(first)

    @pl.when(whole)
    def _():
        wait_all(start_all(
            [(received.at[at, lanes], band.at[plane, b, pl.ds(extent, frame)])
             for plane, b, at, lanes in band_places(blocks, frame)], sems))

    row_index = lax.broadcasted_iota(jnp.int32, (frame, LANES), 0)

    def one(slot, carry):
        row, col, below, place = own[ROW + slot], own[COL + slot], own[BELOW + slot], own[PLACE + slot]
        inside = jnp.where(whole, frame, frame - below)

        @pl.when(split(slot))
        def _():
            for copy in held_copies(slot):
                copy.wait()

        patch = []
        at = pl.ds(jnp.where(whole, 0, below + place - source_row(slot)), frame)
        for plane in range(2):
            mine = window(band, plane, row, col, frame)
            other = [held[slot, plane * across + b, at, :] for b in range(across)]
            patch.append(side_by_side([jnp.where(row_index < inside, a, b) for a, b in zip(mine, other)]))
        for copy in frame_copies(slot):
            copy.wait()
        grads = frame_step(patch, ordered_amplitude(measured, slot, tables[8]), probe, tables, field)
        for plane in range(2):
            add_window(total, (plane,), grads[plane], row, col, frame)

        @pl.when(split(slot))
        def _():
            target = pl.ds(pl.multiple_of(place, ROW_ALIGN), frame)
            for b, part in enumerate(grads[0] + grads[1]):
                piece[b, pl.ds(0, frame), :] = part
                packed[target, lanes_of(b)] = piece[b, pl.ds(frame - below, frame), :]

        return carry

    lax.fori_loop(0, own[COUNT], one, 0)

    @pl.when(whole)
    def _():
        for plane, b, at, lanes in band_places(blocks, frame):
            packed[at, lanes] = total[plane, b, pl.ds(extent, frame), :]

    end = start_all([
        (total.at[:, :, pl.ds(0, extent)], total_out),
        (total.at[:, pl.ds(own_blocks, across), pl.ds(frame, extent - frame)], low_out),
    ], sems)

    @pl.when(own[NEEDED] > 0)
    def _():
        copy_out_rows(own, packed, packed_out, chunk_sems)

    wait_all(end)


def frames_gradient(own, tile, strip_top, strip_low, frames, probe, tables, received):
    cap, frame, _ = frames.shape
    extent = tile.shape[-1]
    modes = probe.shape[0]
    tall = extent + frame
    blocks = tall // LANES
    across = frame // LANES
    rows = received.shape[0]
    return pl.pallas_call(
        frames_kernel,
        out_shape=(
            jax.ShapeDtypeStruct((2, blocks, extent, LANES), F32),
            jax.ShapeDtypeStruct((2, across, extent - frame, LANES), F32),
            jax.ShapeDtypeStruct(received.shape, F32),
        ),
        in_specs=[smem_spec()] + [any_spec()] * 7,
        out_specs=(any_spec(), any_spec(), any_spec()),
        scratch_shapes=[
            pltpu.VMEM((2, blocks, tall, LANES), F32),
            pltpu.VMEM((2, blocks, tall, LANES), F32),
            pltpu.VMEM((cap, 2 * across, 3 * frame, LANES), F32),
            pltpu.VMEM((rows + frame, 2 * frame), F32),
            pltpu.VMEM((2 * across, 2 * frame, LANES), F32),
            pltpu.VMEM((cap, across, frame, LANES), F32),
            pltpu.VMEM(probe.shape, F32),
            pltpu.VMEM(tables.shape, BF16),
            pltpu.VMEM((modes, 2, frame, frame), F32),
            pltpu.SemaphoreType.DMA((2 * blocks + 2,)),
            pltpu.SemaphoreType.DMA((cap, across)),
            pltpu.SemaphoreType.DMA((cap, 2 * across)),
            pltpu.SemaphoreType.DMA((rows // CHUNK,)),
        ],
        compiler_params=params(),
        cost_estimate=kernel_cost(cap, modes, frame),
        name="frames_gradient",
    )(own, tile, strip_top, strip_low, frames, probe, tables, received)


def light_kernel(own, left, up, corner, probe, light_out, light, sem):
    modes, _, frame, _ = probe.shape
    own_blocks, extent, _ = light_out.shape
    across = frame // LANES
    inside = (pl.ds(across, own_blocks), pl.ds(frame, extent), slice(None))
    light[inside] = jnp.zeros((own_blocks, extent, LANES), F32)
    power = jnp.zeros((frame, frame), F32)
    for mode in range(modes):
        power += probe[mode, 0] * probe[mode, 0] + probe[mode, 1] * probe[mode, 1]
    power = halves(power)
    for table, down, right in ((own, 0, 0), (left, 0, 1), (up, 1, 0), (corner, 1, 1)):

        def lit(slot, carry, table=table, down=down, right=right):
            row = table[ROW + slot] + frame - down * extent
            col = table[COL + slot] + frame - right * extent

            @pl.when((row > 0) & (col > 0))
            def _():
                add_window(light, (), power, row, col, frame)

            return carry

        lax.fori_loop(0, table[COUNT], lit, 0)
    copy = pltpu.make_async_copy(light.at[inside[0], inside[1]], light_out, sem)
    copy.start()
    copy.wait()


def light_plane(own, left, up, corner, probe, extent):
    frame = probe.shape[-1]
    wide = extent + 2 * frame
    return pl.pallas_call(
        light_kernel,
        out_shape=jax.ShapeDtypeStruct((extent // LANES, extent, LANES), F32),
        in_specs=[smem_spec()] * 4 + [vmem_spec()],
        out_specs=any_spec(),
        scratch_shapes=[pltpu.VMEM((wide // LANES, wide, LANES), F32), pltpu.SemaphoreType.DMA],
        compiler_params=params(),
        cost_estimate=pl.CostEstimate(flops=0, bytes_accessed=12 * 1024 * 1024, transcendentals=0),
        name="light_plane",
    )(own, left, up, corner, probe)


def join_kernel(cap, frame, table, pieces, total_in, total_out, top_out, band, held, sems):
    blocks = band.shape[1]
    right = pl.ds(blocks - frame // LANES, frame // LANES)
    across = frame // LANES
    rows = pieces.shape[0]
    whole = is_band(table)
    top = pl.ds(0, frame)

    @pl.when(table[NEEDED] > 0)
    def _():
        wait_all(start_all(
            [(total_in.at[:, :, top], band)]
            + [(pieces.at[:, lanes_of(b)], held.at[b, pl.ds(0, rows)]) for b in range(2 * across)], sems))
        row_index = lax.broadcasted_iota(jnp.int32, (frame, LANES), 0)

        def one(slot, carry):
            col, below, place = table[COL + slot], table[BELOW + slot], table[PLACE + slot]

            @pl.when(below > 0)
            def _():
                at = pl.ds(pl.multiple_of(place, ROW_ALIGN), frame)
                for plane in range(2):
                    got = [jnp.where(row_index < below, held[plane * across + b, at, :], 0.0) for b in range(across)]
                    add_window(band, (plane,), got, 0, col, frame)

            return carry

        @pl.when(whole)
        def _():
            for at in range(2 * blocks):
                group, lane = divmod(at, 4)
                band[at // blocks, at % blocks] = band[at // blocks, at % blocks] + held[lane, pl.ds(group * frame, frame), :]

        @pl.when(jnp.logical_not(whole))
        def _():
            lax.fori_loop(0, cap, one, 0)

        wait_all(start_all([(band.at[:, right], top_out), (band, total_out.at[:, :, top])], sems))

    @pl.when(table[NEEDED] == 0)
    def _():
        wait_all(start_all([(total_in.at[:, right, top], top_out)], sems))


def join_pieces(table, pieces, total, cap):
    rows, double = pieces.shape
    frame = double // 2
    blocks = total.shape[1]
    across = frame // LANES
    return pl.pallas_call(
        lambda *refs: join_kernel(cap, frame, *refs),
        out_shape=(jax.ShapeDtypeStruct(total.shape, F32), jax.ShapeDtypeStruct((2, across, frame, LANES), F32)),
        in_specs=[smem_spec(), any_spec(), any_spec()],
        out_specs=(any_spec(), any_spec()),
        input_output_aliases={2: 0},
        scratch_shapes=[
            pltpu.VMEM((2, blocks, frame, LANES), F32),
            pltpu.VMEM((2 * across, rows + frame, LANES), F32),
            pltpu.SemaphoreType.DMA((2 * across + 1,)),
        ],
        compiler_params=params(),
        name="join_pieces",
    )(table, pieces, total)


def final_kernel(tops, tile, total, light, top, low, out):
    across = top.shape[1]
    step = pl.program_id(0)
    for b in range(total.shape[1]):
        below = 1.0 / (light[b] + 1.0)
        for plane in range(2):
            grad = total[plane, b]
            if b < across:
                grad = grad + jnp.where(step < tops, top[plane, b], low[plane, b])
            out[plane, :, lanes_of(b)] = tile[plane, :, lanes_of(b)] - grad * below


def final_update(tile, total, light, top, low):
    extent = tile.shape[-1]
    blocks = extent // LANES
    across, height = top.shape[1], top.shape[2]
    tall = 128
    tops = height // tall
    return pl.pallas_call(
        lambda *refs: final_kernel(tops, *refs),
        grid=(extent // tall,),
        out_shape=jax.ShapeDtypeStruct(tile.shape, F32),
        in_specs=[
            pl.BlockSpec((2, tall, extent), lambda i: (0, i, 0)),
            pl.BlockSpec((2, blocks, tall, LANES), lambda i: (0, 0, i, 0)),
            pl.BlockSpec((blocks, tall, LANES), lambda i: (0, i, 0)),
            pl.BlockSpec((2, across, tall, LANES), lambda i: (0, 0, jnp.minimum(i, tops - 1), 0)),
            pl.BlockSpec((2, across, tall, LANES), lambda i: (0, 0, jnp.maximum(i - tops, 0), 0)),
        ],
        out_specs=pl.BlockSpec((2, tall, extent), lambda i: (0, i, 0)),
        compiler_params=params(),
        name="final_update",
    )(tile, total, light, top, low)


def body(object_tiles, probe, positions, frames, counts):
    tile = object_tiles[0]
    extent = tile.shape[-1]
    frame = frames.shape[-1]
    cap = frames.shape[1]
    peers = lax.axis_size("scan")
    tile_row = lax.axis_index("scan") // TCOLS
    rows = SIZES[-1]
    tables = dft_tables(frame)
    parity = (tile_row % 2).reshape(1)

    own = slot_table(positions, counts, extent, frame)
    up = shifted(own, "scan", TCOLS)
    own, later = lax.optimization_barrier((own, tile))
    strip_top = shifted(later[:, :frame, :frame], "scan", -1)
    strip_low = shifted(later[:, frame:, :frame], "scan", -1)
    left = shifted(own, "scan", 1)
    corner = shifted(own, "scan", TCOLS + 1)
    left, corner, up, strip_top = lax.optimization_barrier((left, corner, up, strip_top))
    packed, *choices = cut_pieces(up, own, parity, tile, strip_top, cap)

    def exchange(packed, upward):
        def sender(size, pairs):
            def run(data):
                if not size:
                    return jnp.zeros((rows, 2 * frame), F32)
                got = lax.ppermute(data[:size], "scan", pairs)
                return got if size == rows else jnp.pad(got, ((0, rows - size), (0, 0)))
            return run

        result = None
        for phase in range(2):
            uppers = [k for k in range(peers - TCOLS) if k // TCOLS % 2 == phase]
            if not uppers:
                continue
            pairs = [(k + TCOLS, k) if upward else (k, k + TCOLS) for k in uppers]
            branches = [sender(size, pairs) for size in (0,) + SIZES + (rows,)]
            moved = lax.switch(choices[phase].reshape(()), branches, packed)
            receives = (tile_row % 2 == phase) if upward else (tile_row % 2 != phase)
            result = moved if result is None else jnp.where(receives, moved, result)
        return result

    received = exchange(packed, True)
    total, low, packed_grad = frames_gradient(own, tile, strip_top, strip_low, frames[0], probe, tables, received)
    pieces = exchange(packed_grad, False)
    total, pieces, low = lax.optimization_barrier((total, pieces, low))
    left_low = shifted(low, "scan", 1)
    total, top = join_pieces(up, pieces, total, cap)
    left_top = shifted(top, "scan", 1)
    total, left, corner = lax.optimization_barrier((total, left, corner))
    light = light_plane(own, left, up, corner, probe, extent)
    return final_update(tile, total, light, left_top, left_low)[None]


def solution(mesh):
    return jax.shard_map(
        body,
        mesh=mesh,
        in_specs=(
            P(("grp", "scan"), None, None, None),
            P(),
            P(("grp", "scan"), None, None),
            P(("grp", "scan"), None, None, None),
            P(("grp", "scan")),
        ),
        out_specs=P(("grp", "scan"), None, None, None),
        check_vma=False,
    )
```

```python
import math

import jax
import jax.numpy as jnp
import numpy as np
from jax import lax
from jax.experimental import pallas as pl
from jax.experimental.pallas import tpu as pltpu
from jax.sharding import PartitionSpec as P

TCOLS = 8
LANES = 128
ROW_ALIGN = 8
CHUNK = 64
SIZES = (32, 64, 96, 128, 160, 192, 224, 256, 320, 384, 448, 512, 640, 768, 960, 1344)
VMEM_LIMIT = 56 * 1024 * 1024
F32 = jnp.float32
BF16 = jnp.bfloat16

KEEP = 160
ROW, COL, NEAR, FAR, PLACE, SHOT = 0, 8, 16, 24, 32, 40
COUNT, KEPT, LENT, FORTH, BACK = 48, 49, 50, 51, 52
TABLE = 64

ACTIVE, AT_ROW, AT_COL, LO, HI, START, PIECE, SHIFT, ROLE = range(9)


def dft_tables(frame):
    near = np.arange(frame // 2, dtype=np.int64)
    blocks = []
    for odd in range(2):
        phase = (near[:, None] * (2 * near[None, :] + odd) % frame).astype(np.float64) * (2.0 * math.pi / frame)
        c, s = np.cos(phase), np.sin(phase)
        ahead = np.block([[c, -s], [s, c]])
        back = np.block([[c.T, s.T], [-s.T, c.T]])
        blocks.append((ahead, ahead.T, back, back.T))
    order = np.zeros((frame, frame))
    order[2 * near, near] = 1.0
    order[2 * near + 1, near + frame // 2] = 1.0
    tables = [blocks[odd][kind] for kind in range(4) for odd in range(2)] + [order]
    return jnp.asarray(np.stack(tables), F32).astype(BF16)


def shifted(array, axis, by):
    peers = lax.axis_size(axis)
    pairs = [(i, i + by) for i in range(peers) if 0 <= i + by < peers]
    return lax.ppermute(array, axis, pairs)


def any_spec():
    return pl.BlockSpec(memory_space=pl.ANY)


def smem_spec():
    return pl.BlockSpec(memory_space=pltpu.SMEM)


def vmem_spec():
    return pl.BlockSpec(memory_space=pltpu.VMEM)


def params():
    return pltpu.CompilerParams(vmem_limit_bytes=VMEM_LIMIT)


def taken_from(blocks, by):
    lane = lax.broadcasted_iota(jnp.int32, blocks[0].shape, 1)
    rolled = [pltpu.roll(block, lax.rem(LANES - by, LANES), axis=1) for block in blocks]
    return [jnp.where(lane < LANES - by, one, two) for one, two in zip(rolled[:-1], rolled[1:])]


def put_into(blocks, by):
    lane = lax.broadcasted_iota(jnp.int32, blocks[0].shape, 1)
    rolled = [pltpu.roll(block, by, axis=1) for block in blocks]
    none = jnp.zeros_like(blocks[0])
    return [jnp.where(lane >= by, one, two) for one, two in zip(rolled + [none], [none] + rolled)]


def start_all(pairs, sems, first=0):
    copies = [pltpu.make_async_copy(source, target, sems.at[first + at]) for at, (source, target) in enumerate(pairs)]
    for copy in copies:
        copy.start()
    return copies


def wait_all(copies):
    for copy in copies:
        copy.wait()


def lanes_of(block):
    return pl.ds(block * LANES, LANES)


def side_by_side(parts):
    return jnp.concatenate(parts, axis=1)


def halves(array):
    return [array[:, :LANES], array[:, LANES:]]


def copy_out_rows(needed, packed, out, sems):
    chunks = (needed + CHUNK - 1) // CHUNK

    def copy(chunk):
        at = pl.ds(pl.multiple_of(chunk * CHUNK, CHUNK), CHUNK)
        return pltpu.make_async_copy(packed.at[at], out.at[at], sems.at[chunk])

    def begin(chunk, carry):
        copy(chunk).start()
        return carry

    def end(chunk, carry):
        copy(chunk).wait()
        return carry

    lax.fori_loop(0, chunks, begin, 0)
    lax.fori_loop(0, chunks, end, 0)


def up_to(value, step):
    return (value + step - 1) // step * step


def size_choice(needed):
    choice = jnp.where(needed > 0, 1, 0)
    for size in SIZES:
        choice = choice + jnp.where(needed > size, 1, 0)
    return choice


def table_kernel(extent, frame, positions, counts, table):
    cap = positions.shape[2]
    count = counts[0]
    kept, lent, shots = jnp.int32(0), jnp.int32(0), jnp.int32(0)
    for at in range(TABLE):
        table[at] = 0
    for slot in range(cap):
        row = lax.rem(positions[0, 0, slot], extent)
        col = lax.rem(positions[0, 1, slot], extent)
        below = jnp.where(slot < count, jnp.maximum(row + (frame - extent), 0), 0)
        stays = below <= KEEP
        near = jnp.where(stays, below, 0)
        far = jnp.where(stays, 0, frame - below)
        table[ROW + slot] = row
        table[COL + slot] = col
        table[NEAR + slot] = near
        table[FAR + slot] = far
        table[PLACE + slot] = jnp.where(stays, kept, lent)
        table[SHOT + slot] = shots
        kept = kept + up_to(near, ROW_ALIGN)
        lent = lent + up_to(far, ROW_ALIGN)
        shots = shots + jnp.where(stays, 0, frame // 2)
    for slot in range(cap):
        table[SHOT + slot] = table[SHOT + slot] + lent
    table[COUNT] = count
    table[KEPT] = kept
    table[LENT] = lent
    table[FORTH] = jnp.maximum(kept, lent + shots)
    table[BACK] = jnp.maximum(kept, lent)


def slot_table(positions, counts, extent, frame):
    return pl.pallas_call(
        lambda *refs: table_kernel(extent, frame, *refs),
        out_shape=jax.ShapeDtypeStruct((TABLE,), jnp.int32),
        in_specs=[smem_spec(), smem_spec()],
        out_specs=smem_spec(),
        name="slot_table",
    )(jnp.swapaxes(positions, 1, 2), counts)


def cut_kernel(phase, own, up, parity, tile, strip, frames, out, forth, back, band, packed, sems, chunk_sems):
    cap, frame, _ = frames.shape
    extent = tile.shape[-1]
    across = frame // LANES
    own_blocks = extent // LANES
    upper = parity[0] == phase
    forth[0] = size_choice(jnp.where(upper, own[FORTH], up[FORTH]))
    back[0] = size_choice(jnp.where(upper, own[BACK], up[BACK]))
    lends = jnp.logical_and(upper, own[LENT] > 0)
    gives = jnp.logical_and(jnp.logical_not(upper), up[KEPT] > 0)

    def cut(col, row, place):
        at = pl.ds(pl.multiple_of(place, ROW_ALIGN), frame)
        for plane in range(2):
            packed[at, pl.ds(plane * frame, frame)] = side_by_side(window(band, (plane,), row, col, frame))

    @pl.when(jnp.logical_or(lends, gives))
    def _():
        base = jnp.where(upper, extent - frame, 0)
        rows = pl.ds(pl.multiple_of(base, ROW_ALIGN), frame)
        wait_all(start_all(
            [(tile.at[:, rows, lanes_of(b)], band.at[:, b, pl.ds(0, frame)]) for b in range(own_blocks)]
            + [(strip.at[:, rows, lanes_of(b)], band.at[:, own_blocks + b, pl.ds(0, frame)]) for b in range(across)], sems))

        def one(slot, carry):
            @pl.when(jnp.logical_and(upper, own[FAR + slot] > 0))
            def _():
                cut(own[COL + slot], own[ROW + slot] - (extent - frame), own[PLACE + slot])

            @pl.when(jnp.logical_and(gives, up[NEAR + slot] > 0))
            def _():
                cut(up[COL + slot], 0, up[PLACE + slot])

            return carry

        lax.fori_loop(0, cap, one, 0)

        def shots(slot):
            at = pl.ds(pl.multiple_of(own[SHOT + slot], ROW_ALIGN), frame // 2)
            return [pltpu.make_async_copy(frames.at[slot, pl.ds(part * frame // 2, frame // 2)],
                                          packed.at[at, pl.ds(part * frame, frame)], sems.at[2 * slot + part])
                    for part in range(2)]

        for wait in range(2):
            for slot in range(cap):
                @pl.when(jnp.logical_and(lends, own[FAR + slot] > 0))
                def _():
                    for copy in shots(slot):
                        if wait:
                            copy.wait()
                        else:
                            copy.start()

        copy_out_rows(jnp.where(upper, own[FORTH], up[KEPT]), packed, out, chunk_sems)


def cut_pieces(phase, own, up, parity, tile, strip, frames):
    cap, frame, _ = frames.shape
    extent = tile.shape[-1]
    blocks = (extent + frame) // LANES
    rows = SIZES[-1]
    return pl.pallas_call(
        lambda *refs: cut_kernel(phase, *refs),
        out_shape=(
            jax.ShapeDtypeStruct((rows, 2 * frame), F32),
            jax.ShapeDtypeStruct((1,), jnp.int32),
            jax.ShapeDtypeStruct((1,), jnp.int32),
        ),
        in_specs=[smem_spec(), smem_spec(), smem_spec(), any_spec(), any_spec(), any_spec()],
        out_specs=(any_spec(), smem_spec(), smem_spec()),
        scratch_shapes=[
            pltpu.VMEM((2, blocks, 2 * frame, LANES), F32),
            pltpu.VMEM((rows + frame, 2 * frame), F32),
            pltpu.SemaphoreType.DMA((max(blocks, 2 * cap),)),
            pltpu.SemaphoreType.DMA((rows // CHUNK,)),
        ],
        compiler_params=params(),
        name="cut_pieces",
    )(own, up, parity, tile, strip, frames)


def dot(one, two):
    return jnp.dot(one, two, preferred_element_type=F32)


def stacked(parts):
    return jnp.concatenate(parts, axis=0)


def sums(array, axis):
    half = array.shape[axis] // 2
    near = lax.slice_in_dim(array, 0, half, axis=axis)
    far = lax.slice_in_dim(array, half, 2 * half, axis=axis)
    return near + far, near - far


def quarters(real, imag):
    half = real.shape[1] // 2
    return stacked([side_by_side([real[:, :half], imag[:, :half]]), side_by_side([real[:, half:], imag[:, half:]])])


def frame_step(patch, amplitude, probe, tables, field):
    modes, _, frame, _ = probe.shape
    half = frame // 2
    lit = [jnp.zeros((half, frame), F32), jnp.zeros((half, frame), F32)]
    for mode in range(modes):
        probe_real, probe_imag = probe[mode, 0], probe[mode, 1]
        real = sums(probe_real * patch[0] - probe_imag * patch[1], 1)
        imag = sums(probe_real * patch[1] + probe_imag * patch[0], 1)
        across = [sums(dot(side_by_side([real[odd], imag[odd]]).astype(BF16), tables[odd]), 0) for odd in range(2)]
        for odd in range(2):
            far = dot(tables[2 + odd], quarters(across[0][odd], across[1][odd]).astype(BF16))
            field[mode, odd] = far
            lit[odd] += far[:half] * far[:half] + far[half:] * far[half:]
    factors = []
    for odd in range(2):
        factor = 1.0 / frame - amplitude[odd] * lax.rsqrt(jnp.maximum(lit[odd], float(frame * frame)))
        factors.append(stacked([factor, factor]))
    grad_real = jnp.zeros((frame, frame), F32)
    grad_imag = jnp.zeros((frame, frame), F32)
    for mode in range(modes):
        rest = [(field[mode, odd] * factors[odd]).astype(BF16) for odd in range(2)]
        moved = []
        for odd in range(2):
            lanes = slice(odd * half, odd * half + half)
            moved.append(dot(
                stacked([side_by_side([part[:half, lanes], part[half:, lanes]]) for part in rest]), tables[4 + odd]))
        near, far = moved[0] + moved[1], moved[0] - moved[1]
        even = dot(tables[6], quarters(near[:half], far[:half]).astype(BF16))
        odd = dot(tables[7], quarters(near[half:], far[half:]).astype(BF16))
        near, far = even + odd, even - odd
        back_real = stacked([near[:half], far[:half]])
        back_imag = stacked([near[half:], far[half:]])
        probe_real, probe_imag = probe[mode, 0], probe[mode, 1]
        grad_real += probe_real * back_real + probe_imag * back_imag
        grad_imag += probe_real * back_imag - probe_imag * back_real
    return [halves(grad_real * (1.0 / frame)), halves(grad_imag * (1.0 / frame))]


def ordered_amplitude(measured, slot, order):
    frame = measured.shape[2]
    parts = []
    for odd in range(2):
        root = jnp.sqrt(side_by_side(
            [measured[slot, b, pl.ds(odd, frame // 2, stride=2), :] for b in range(measured.shape[1])]))
        high = root.astype(BF16)
        low = (root - high.astype(F32)).astype(BF16)
        parts.append(dot(high, order) + dot(low, order))
    return parts


def window(band, lead, row, col, frame):
    return taken_from(
        [band[lead + (col // LANES + b, pl.ds(row, frame), slice(None))] for b in range(frame // LANES + 1)],
        lax.rem(col, LANES),
    )


def add_window(total, lead, parts, row, col, frame):
    for b, moved in enumerate(put_into(parts, lax.rem(col, LANES))):
        at = lead + (col // LANES + b, pl.ds(row, frame), slice(None))
        total[at] = total[at] + moved


def kernel_cost(frames, modes, frame):
    return pl.CostEstimate(
        flops=frames * modes * 4 * 4 * frame ** 3, bytes_accessed=16 * 1024 * 1024, transcendentals=0)


def frames_kernel(phases, own, up, parity, tile, strip, frames, probe_in, tables_in, as_upper, as_lower, total_out, *rest):
    packed_outs = rest[:phases]
    band, total, held, packed, piece, measured, probe, tables, field, work, sems, shot_sems, held_sems, chunk_sems = rest[phases:]
    cap, frame, _ = frames.shape
    extent = tile.shape[-1]
    across = frame // LANES
    own_blocks = extent // LANES
    half = frame // 2
    own_rows = pl.ds(frame, extent)

    first = start_all(
        [(tile.at[:, :, lanes_of(b)], band.at[:, b, own_rows]) for b in range(own_blocks)]
        + [(strip.at[:, :, lanes_of(b)], band.at[:, own_blocks + b, own_rows]) for b in range(across)]
        + [(probe_in, probe), (tables_in, tables)], sems)

    def mine(slot):
        return jnp.logical_and(slot < own[COUNT], own[FAR + slot] == 0)

    def borrowed(slot):
        return up[FAR + slot] > 0

    def shot_copies(slot, task, lent):
        if not lent:
            return [pltpu.make_async_copy(frames.at[slot, :, lanes_of(b)], measured.at[task, b], shot_sems.at[task, b])
                    for b in range(across)]
        at = pl.ds(pl.multiple_of(up[SHOT + slot], ROW_ALIGN), half)
        return [
            pltpu.make_async_copy(as_lower.at[at, lanes_of(part * across + b)],
                                  measured.at[task, b, pl.ds(part * half, half)], shot_sems.at[task, part * across + b])
            for part in range(2) for b in range(across)
        ]

    def held_copies(slot, task, lent):
        source, table = (as_lower, up) if lent else (as_upper, own)
        at = pl.ds(pl.multiple_of(table[PLACE + slot], ROW_ALIGN), frame)
        return [
            pltpu.make_async_copy(source.at[at, lanes_of(b)], held.at[task, b, pl.ds(frame, frame)], held_sems.at[task, b])
            for b in range(2 * across)
        ]

    def for_tasks(wait):
        for slot in range(cap):
            def run(copies):
                for copy in copies:
                    if wait:
                        copy.wait()
                    else:
                        copy.start()

            @pl.when(mine(slot))
            def _():
                run(shot_copies(slot, slot, False))

            @pl.when(own[NEAR + slot] > 0)
            def _():
                run(held_copies(slot, slot, False))

            @pl.when(borrowed(slot))
            def _():
                run(shot_copies(slot, cap + slot, True))
                run(held_copies(slot, cap + slot, True))

    for_tasks(False)
    for slot in range(cap):
        near = own[NEAR + slot]
        for field_at, value in (
            (ACTIVE, mine(slot).astype(jnp.int32)), (AT_ROW, own[ROW + slot] + frame), (AT_COL, own[COL + slot]),
            (LO, frame - near), (HI, frame), (START, near), (PIECE, own[PLACE + slot]), (SHIFT, frame - near), (ROLE, 0),
        ):
            work[slot, field_at] = value
        for field_at, value in (
            (ACTIVE, borrowed(slot).astype(jnp.int32)), (AT_ROW, up[ROW + slot] + frame - extent), (AT_COL, up[COL + slot]),
            (LO, 0), (HI, up[FAR + slot]), (START, frame), (PIECE, up[PLACE + slot]), (SHIFT, 0), (ROLE, 1),
        ):
            work[cap + slot, field_at] = value
    total[...] = jnp.zeros_like(total)
    wait_all(first)
    for_tasks(True)
    row_index = lax.broadcasted_iota(jnp.int32, (frame, LANES), 0)

    def one(task, carry):
        @pl.when(work[task, ACTIVE] > 0)
        def _():
            row, col, start = work[task, AT_ROW], work[task, AT_COL], work[task, START]
            lo, hi = work[task, LO], work[task, HI]
            theirs = jnp.logical_and(row_index >= lo, row_index < hi)
            patch = []
            for plane in range(2):
                near = window(band, (plane,), row, col, frame)
                other = [held[task, plane * across + b, pl.ds(start, frame), :] for b in range(across)]
                patch.append(side_by_side([jnp.where(theirs, b, a) for a, b in zip(near, other)]))
            grads = frame_step(patch, ordered_amplitude(measured, task, tables[8]), probe, tables, field)
            for plane in range(2):
                add_window(total, (plane,), grads[plane], row, col, frame)

            @pl.when(lo < hi)
            def _():
                target = pl.ds(pl.multiple_of(work[task, PIECE], ROW_ALIGN), frame)
                source = pl.ds(work[task, SHIFT], frame)
                for b, part in enumerate(grads[0] + grads[1]):
                    piece[b, pl.ds(0, frame), :] = part
                    packed[work[task, ROLE], target, lanes_of(b)] = piece[b, source, :]

        return carry

    lax.fori_loop(0, 2 * cap, one, 0)
    end = start_all([(total.at[:, :, own_rows], total_out)], sems)
    for phase in range(phases):
        upper = parity[0] == phase
        role = jnp.where(upper, 0, 1)
        copy_out_rows(jnp.where(upper, own[KEPT], up[LENT]), packed.at[role], packed_outs[phase], chunk_sems)
    wait_all(end)


def frames_gradient(phases, own, up, parity, tile, strip, frames, probe, tables, as_upper, as_lower):
    cap, frame, _ = frames.shape
    extent = tile.shape[-1]
    modes = probe.shape[0]
    tall = extent + 2 * frame
    blocks = (extent + frame) // LANES
    across = frame // LANES
    rows = as_upper.shape[0]
    kept_rows = cap * KEEP
    return pl.pallas_call(
        lambda *refs: frames_kernel(phases, *refs),
        out_shape=(jax.ShapeDtypeStruct((2, blocks, extent, LANES), F32),)
        + (jax.ShapeDtypeStruct(as_upper.shape, F32),) * phases,
        in_specs=[smem_spec()] * 3 + [any_spec()] * 7,
        out_specs=(any_spec(),) * (1 + phases),
        scratch_shapes=[
            pltpu.VMEM((2, blocks, tall, LANES), F32),
            pltpu.VMEM((2, blocks, tall, LANES), F32),
            pltpu.VMEM((2 * cap, 2 * across, 2 * frame, LANES), F32),
            pltpu.VMEM((2, kept_rows + frame, 2 * frame), F32),
            pltpu.VMEM((2 * across, 2 * frame, LANES), F32),
            pltpu.VMEM((2 * cap, across, frame, LANES), F32),
            pltpu.VMEM(probe.shape, F32),
            pltpu.VMEM(tables.shape, BF16),
            pltpu.VMEM((modes, 2, frame, frame), F32),
            pltpu.SMEM((2 * cap, 16), jnp.int32),
            pltpu.SemaphoreType.DMA((blocks + 2,)),
            pltpu.SemaphoreType.DMA((2 * cap, 2 * across)),
            pltpu.SemaphoreType.DMA((2 * cap, 2 * across)),
            pltpu.SemaphoreType.DMA((rows // CHUNK,)),
        ],
        compiler_params=params(),
        cost_estimate=kernel_cost(cap, modes, frame),
        name="frames_gradient",
    )(own, up, parity, tile, strip, frames, probe, tables, as_upper, as_lower)


def light_kernel(own, up, beside, probe, light_out, light, sem):
    modes, _, frame, _ = probe.shape
    own_blocks, extent, _ = light_out.shape
    across = frame // LANES
    inside = (pl.ds(across, own_blocks), pl.ds(frame, extent), slice(None))
    light[inside] = jnp.zeros((own_blocks, extent, LANES), F32)
    power = jnp.zeros((frame, frame), F32)
    for mode in range(modes):
        power += probe[mode, 0] * probe[mode, 0] + probe[mode, 1] * probe[mode, 1]
    power = halves(power)
    for table, lead, down, right in ((own, 0, 0, 0), (beside, 0, 0, 1), (up, 0, 1, 0), (beside, TABLE, 1, 1)):

        def lit(slot, carry, table=table, lead=lead, down=down, right=right):
            row = table[lead + ROW + slot] + frame - down * extent
            col = table[lead + COL + slot] + frame - right * extent

            @pl.when((row > 0) & (col > 0))
            def _():
                add_window(light, (), power, row, col, frame)

            return carry

        lax.fori_loop(0, table[lead + COUNT], lit, 0)
    copy = pltpu.make_async_copy(light.at[inside[0], inside[1]], light_out, sem)
    copy.start()
    copy.wait()


def light_plane(own, up, beside, probe, extent):
    frame = probe.shape[-1]
    wide = extent + 2 * frame
    return pl.pallas_call(
        light_kernel,
        out_shape=jax.ShapeDtypeStruct((extent // LANES, extent, LANES), F32),
        in_specs=[smem_spec()] * 3 + [vmem_spec()],
        out_specs=any_spec(),
        scratch_shapes=[pltpu.VMEM((wide // LANES, wide, LANES), F32), pltpu.SemaphoreType.DMA],
        compiler_params=params(),
        cost_estimate=pl.CostEstimate(flops=0, bytes_accessed=12 * 1024 * 1024, transcendentals=0),
        name="light_plane",
    )(own, up, beside, probe)


def join_kernel(frame, own, up, as_upper, as_lower, total_in, total_out, right_out, band, held, sems):
    blocks = band.shape[1]
    extent = total_in.shape[2]
    across = frame // LANES
    rows = held.shape[1] - frame
    cap = rows // KEEP
    own_rows = pl.ds(0, extent)
    right = pl.ds(blocks - across, across)
    anything = jnp.logical_or(own[LENT] > 0, up[KEPT] > 0)

    @pl.when(anything)
    def _():
        whole = start_all([(total_in, band.at[:, :, own_rows])], sems)
        row_index = lax.broadcasted_iota(jnp.int32, (frame, LANES), 0)
        for number, (table, needed, field, pieces) in enumerate(
                ((own, own[LENT], FAR, as_upper), (up, up[KEPT], NEAR, as_lower))):

            @pl.when(needed > 0)
            def _(table=table, needed=needed, field=field, pieces=pieces):
                chunks = (needed + CHUNK - 1) // CHUNK

                def copies(chunk):
                    at = pl.ds(pl.multiple_of(chunk * CHUNK, CHUNK), CHUNK)
                    return [pltpu.make_async_copy(pieces.at[at, lanes_of(b)], held.at[b, at], sems.at[1 + chunk * 2 * across + b])
                            for b in range(2 * across)]

                def begin(chunk, carry):
                    for copy in copies(chunk):
                        copy.start()
                    return carry

                def end(chunk, carry):
                    for copy in copies(chunk):
                        copy.wait()
                    return carry

                lax.fori_loop(0, chunks, begin, 0)
                lax.fori_loop(0, chunks, end, 0)

            if not number:
                wait_all(whole)

            def one(slot, carry, table=table, field=field):
                col, height = table[COL + slot], table[field + slot]

                @pl.when(height > 0)
                def _():
                    row = table[ROW + slot] if field == FAR else 0
                    at = pl.ds(pl.multiple_of(table[PLACE + slot], ROW_ALIGN), frame)
                    for plane in range(2):
                        got = [jnp.where(row_index < height, held[plane * across + b, at, :], 0.0) for b in range(across)]
                        add_window(band, (plane,), got, row, col, frame)

                return carry

            lax.fori_loop(0, cap, one, 0)

        wait_all(start_all([(band.at[:, right, own_rows], right_out), (band.at[:, :, own_rows], total_out)], sems))

    @pl.when(jnp.logical_not(anything))
    def _():
        wait_all(start_all([(total_in.at[:, right], band.at[:, right, own_rows])], sems))
        wait_all(start_all([(band.at[:, right, own_rows], right_out)], sems))


def join_pieces(own, up, as_upper, as_lower, total, cap):
    frame = as_upper.shape[1] // 2
    _, blocks, extent, _ = total.shape
    across = frame // LANES
    rows = cap * KEEP
    return pl.pallas_call(
        lambda *refs: join_kernel(frame, *refs),
        out_shape=(jax.ShapeDtypeStruct(total.shape, F32), jax.ShapeDtypeStruct((2, across, extent, LANES), F32)),
        in_specs=[smem_spec(), smem_spec(), any_spec(), any_spec(), any_spec()],
        out_specs=(any_spec(), any_spec()),
        input_output_aliases={4: 0},
        scratch_shapes=[
            pltpu.VMEM((2, blocks, extent + frame, LANES), F32),
            pltpu.VMEM((2 * across, rows + frame, LANES), F32),
            pltpu.SemaphoreType.DMA((1 + rows // CHUNK * 2 * across,)),
        ],
        compiler_params=params(),
        name="join_pieces",
    )(own, up, as_upper, as_lower, total)


def final_kernel(tile, total, light, left, out):
    across = left.shape[1]
    for b in range(total.shape[1]):
        below = 1.0 / (light[b] + 1.0)
        for plane in range(2):
            grad = total[plane, b]
            if b < across:
                grad = grad + left[plane, b]
            out[plane, :, lanes_of(b)] = tile[plane, :, lanes_of(b)] - grad * below


def final_update(tile, total, light, left):
    extent = tile.shape[-1]
    blocks = extent // LANES
    across = left.shape[1]
    tall = 128
    return pl.pallas_call(
        final_kernel,
        grid=(extent // tall,),
        out_shape=jax.ShapeDtypeStruct(tile.shape, F32),
        in_specs=[
            pl.BlockSpec((2, tall, extent), lambda i: (0, i, 0)),
            pl.BlockSpec((2, blocks, tall, LANES), lambda i: (0, 0, i, 0)),
            pl.BlockSpec((blocks, tall, LANES), lambda i: (0, i, 0)),
            pl.BlockSpec((2, across, tall, LANES), lambda i: (0, 0, i, 0)),
        ],
        out_specs=pl.BlockSpec((2, tall, extent), lambda i: (0, i, 0)),
        compiler_params=params(),
        name="final_update",
    )(tile, total, light, left)


def body(object_tiles, probe, positions, frames, counts):
    tile = object_tiles[0]
    extent = tile.shape[-1]
    frame = frames.shape[-1]
    cap = frames.shape[1]
    peers = lax.axis_size("scan")
    tile_row = lax.axis_index("scan") // TCOLS
    phases = min(2, peers // TCOLS - 1)
    tables = dft_tables(frame)
    parity = (tile_row % 2).reshape(1)
    even = tile_row % 2 == 0

    own = slot_table(positions, counts, extent, frame)
    up = shifted(own, "scan", TCOLS)
    strip = shifted(tile[:, :, :frame], "scan", -1)
    beside = shifted(jnp.concatenate([own, up]), "scan", 1)
    beside, up, strip = lax.optimization_barrier((beside, up, strip))

    def exchange(phase, packed, choice):
        uppers = [k for k in range(peers - TCOLS) if k // TCOLS % 2 == phase]
        pairs = [(k, k + TCOLS) for k in uppers] + [(k + TCOLS, k) for k in uppers]

        def sender(size):
            def run(data):
                return lax.dynamic_update_slice(data, lax.ppermute(data[:size], "scan", pairs), (0, 0))
            return run

        branches = [lambda data: data] + [sender(size) for size in SIZES]
        return lax.switch(choice.reshape(()), branches, packed)

    def by_role(arrays):
        if len(arrays) == 1:
            return arrays[0], arrays[0]
        return jnp.where(even, arrays[0], arrays[1]), jnp.where(even, arrays[1], arrays[0])

    cuts = [cut_pieces(phase, own, up, parity, tile, strip, frames[0]) for phase in range(phases)]
    received = by_role([exchange(phase, cut[0], cut[1]) for phase, cut in enumerate(cuts)])
    total, *packed = frames_gradient(phases, own, up, parity, tile, strip, frames[0], probe, tables, *received)
    returned = by_role([exchange(phase, packed[phase], cut[2]) for phase, cut in enumerate(cuts)])
    total, right = join_pieces(own, up, *returned, total, cap)
    left = shifted(right, "scan", 1)
    total, beside = lax.optimization_barrier((total, beside))
    light = light_plane(own, up, beside, probe, extent)
    return final_update(tile, total, light, left)[None]


def solution(mesh):
    return jax.shard_map(
        body,
        mesh=mesh,
        in_specs=(
            P(("grp", "scan"), None, None, None),
            P(),
            P(("grp", "scan"), None, None),
            P(("grp", "scan"), None, None, None),
            P(("grp", "scan")),
        ),
        out_specs=P(("grp", "scan"), None, None, None),
        check_vma=False,
    )
```

```python
import math

import jax
import jax.numpy as jnp
import numpy as np
from jax import lax
from jax.experimental import pallas as pl
from jax.experimental.pallas import tpu as pltpu
from jax.sharding import PartitionSpec as P

TCOLS = 8
LANES = 128
ROW_ALIGN = 8
CHUNK = 64
STEP = 32
TILE_ROWS = 16
SIZES = (32, 64, 96, 128, 160, 192, 224, 256, 320, 384, 448, 512, 640, 768, 960, 1344)
MIB = 1024 * 1024
F32 = jnp.float32
BF16 = jnp.bfloat16

KEEP = 160
ROW, COL, NEAR, FAR, PLACE, SHOT = 0, 8, 16, 24, 32, 40
COUNT, KEPT, LENT, FORTH, BACK = 48, 49, 50, 51, 52
TABLE = 64

ACTIVE, AT_ROW, AT_COL, LO, HI, START, PIECE, SHIFT, ROLE = range(9)


def dft_tables(frame):
    near = np.arange(frame // 2, dtype=np.int64)
    blocks = []
    for odd in range(2):
        phase = (near[:, None] * (2 * near[None, :] + odd) % frame).astype(np.float64) * (2.0 * math.pi / frame)
        c, s = np.cos(phase), np.sin(phase)
        ahead = np.block([[c, -s], [s, c]])
        back = np.block([[c.T, s.T], [-s.T, c.T]])
        blocks.append((ahead, ahead.T, back, back.T))
    order = np.zeros((frame, frame))
    order[2 * near, near] = 1.0
    order[2 * near + 1, near + frame // 2] = 1.0
    tables = [blocks[odd][kind] for kind in range(4) for odd in range(2)] + [order]
    return jnp.asarray(np.stack(tables), F32).astype(BF16)


def shifted(array, axis, by):
    peers = lax.axis_size(axis)
    pairs = [(i, i + by) for i in range(peers) if 0 <= i + by < peers]
    return lax.ppermute(array, axis, pairs)


def any_spec():
    return pl.BlockSpec(memory_space=pl.ANY)


def smem_spec():
    return pl.BlockSpec(memory_space=pltpu.SMEM)


def vmem_spec():
    return pl.BlockSpec(memory_space=pltpu.VMEM)


def params(mebibytes):
    return pltpu.CompilerParams(vmem_limit_bytes=mebibytes * MIB)


def taken_from(blocks, by):
    lane = lax.broadcasted_iota(jnp.int32, blocks[0].shape, 1)
    rolled = [pltpu.roll(block, lax.rem(LANES - by, LANES), axis=1) for block in blocks]
    return [jnp.where(lane < LANES - by, one, two) for one, two in zip(rolled[:-1], rolled[1:])]


def put_into(blocks, by):
    lane = lax.broadcasted_iota(jnp.int32, blocks[0].shape, 1)
    rolled = [pltpu.roll(block, by, axis=1) for block in blocks]
    none = jnp.zeros_like(blocks[0])
    return [jnp.where(lane >= by, one, two) for one, two in zip(rolled + [none], [none] + rolled)]


def start_all(pairs, sems, first=0):
    copies = [pltpu.make_async_copy(source, target, sems.at[first + at]) for at, (source, target) in enumerate(pairs)]
    for copy in copies:
        copy.start()
    return copies


def wait_all(copies):
    for copy in copies:
        copy.wait()


def lanes_of(block):
    return pl.ds(block * LANES, LANES)


def side_by_side(parts):
    return jnp.concatenate(parts, axis=1)


def halves(array):
    return [array[:, :LANES], array[:, LANES:]]


def copy_out_rows(needed, packed, out, sems):
    chunks = (needed + CHUNK - 1) // CHUNK

    def copy(chunk):
        at = pl.ds(pl.multiple_of(chunk * CHUNK, CHUNK), CHUNK)
        return pltpu.make_async_copy(packed.at[at], out.at[at], sems.at[chunk])

    def begin(chunk, carry):
        copy(chunk).start()
        return carry

    def end(chunk, carry):
        copy(chunk).wait()
        return carry

    lax.fori_loop(0, chunks, begin, 0)
    lax.fori_loop(0, chunks, end, 0)


def up_to(value, step):
    return (value + step - 1) // step * step


def size_choice(needed):
    choice = jnp.where(needed > 0, 1, 0)
    for size in SIZES:
        choice = choice + jnp.where(needed > size, 1, 0)
    return choice


def table_kernel(extent, frame, positions, counts, table):
    cap = positions.shape[2]
    count = counts[0]
    kept, lent, shots = jnp.int32(0), jnp.int32(0), jnp.int32(0)
    for at in range(TABLE):
        table[at] = 0
    for slot in range(cap):
        row = lax.rem(positions[0, 0, slot], extent)
        col = lax.rem(positions[0, 1, slot], extent)
        below = jnp.where(slot < count, jnp.maximum(row + (frame - extent), 0), 0)
        stays = below <= KEEP
        near = jnp.where(stays, below, 0)
        far = jnp.where(stays, 0, frame - below)
        table[ROW + slot] = row
        table[COL + slot] = col
        table[NEAR + slot] = near
        table[FAR + slot] = far
        table[PLACE + slot] = jnp.where(stays, kept, lent)
        table[SHOT + slot] = shots
        kept = kept + up_to(near, ROW_ALIGN)
        lent = lent + up_to(far, ROW_ALIGN)
        shots = shots + jnp.where(stays, 0, frame // 2)
    for slot in range(cap):
        table[SHOT + slot] = table[SHOT + slot] + lent
    table[COUNT] = count
    table[KEPT] = kept
    table[LENT] = lent
    table[FORTH] = jnp.maximum(kept, lent + shots)
    table[BACK] = jnp.maximum(kept, lent)


def slot_table(positions, counts, extent, frame):
    return pl.pallas_call(
        lambda *refs: table_kernel(extent, frame, *refs),
        out_shape=jax.ShapeDtypeStruct((TABLE,), jnp.int32),
        in_specs=[smem_spec(), smem_spec()],
        out_specs=smem_spec(),
        name="slot_table",
    )(jnp.swapaxes(positions, 1, 2), counts)


def cut_kernel(phase, own, up, parity, tile, strip, frames, out, forth, back, band, packed, sems, chunk_sems):
    cap, frame, _ = frames.shape
    extent = tile.shape[-1]
    across = frame // LANES
    own_blocks = extent // LANES
    upper = parity[0] == phase
    forth[0] = size_choice(jnp.where(upper, own[FORTH], up[FORTH]))
    back[0] = size_choice(jnp.where(upper, own[BACK], up[BACK]))
    lends = jnp.logical_and(upper, own[LENT] > 0)
    gives = jnp.logical_and(jnp.logical_not(upper), up[KEPT] > 0)

    def cut(col, row, place):
        at = pl.ds(pl.multiple_of(place, ROW_ALIGN), frame)
        for plane in range(2):
            packed[at, pl.ds(plane * frame, frame)] = side_by_side(window(band, (plane,), row, col, frame, across))

    @pl.when(jnp.logical_or(lends, gives))
    def _():
        base = jnp.where(upper, extent - frame, 0)
        rows = pl.ds(pl.multiple_of(base, ROW_ALIGN), frame)
        wait_all(start_all(
            [(tile.at[:, rows, lanes_of(b)], band.at[:, b, pl.ds(0, frame)]) for b in range(own_blocks)]
            + [(strip.at[:, rows, lanes_of(b)], band.at[:, own_blocks + b, pl.ds(0, frame)]) for b in range(across)], sems))

        def one(slot, carry):
            @pl.when(jnp.logical_and(upper, own[FAR + slot] > 0))
            def _():
                cut(own[COL + slot], own[ROW + slot] - (extent - frame), own[PLACE + slot])

            @pl.when(jnp.logical_and(gives, up[NEAR + slot] > 0))
            def _():
                cut(up[COL + slot], 0, up[PLACE + slot])

            return carry

        lax.fori_loop(0, cap, one, 0)

        def shots(slot):
            at = pl.ds(pl.multiple_of(own[SHOT + slot], ROW_ALIGN), frame // 2)
            return [pltpu.make_async_copy(frames.at[slot, pl.ds(part * frame // 2, frame // 2)],
                                          packed.at[at, pl.ds(part * frame, frame)], sems.at[2 * slot + part])
                    for part in range(2)]

        for wait in range(2):
            for slot in range(cap):
                @pl.when(jnp.logical_and(lends, own[FAR + slot] > 0))
                def _():
                    for copy in shots(slot):
                        if wait:
                            copy.wait()
                        else:
                            copy.start()

        copy_out_rows(jnp.where(upper, own[FORTH], up[KEPT]), packed, out, chunk_sems)


def cut_pieces(phase, own, up, parity, tile, strip, frames):
    cap, frame, _ = frames.shape
    extent = tile.shape[-1]
    blocks = (extent + frame) // LANES
    rows = SIZES[-1]
    return pl.pallas_call(
        lambda *refs: cut_kernel(phase, *refs),
        out_shape=(
            jax.ShapeDtypeStruct((rows, 2 * frame), F32),
            jax.ShapeDtypeStruct((1,), jnp.int32),
            jax.ShapeDtypeStruct((1,), jnp.int32),
        ),
        in_specs=[smem_spec(), smem_spec(), smem_spec(), any_spec(), any_spec(), any_spec()],
        out_specs=(any_spec(), smem_spec(), smem_spec()),
        scratch_shapes=[
            pltpu.VMEM((2, blocks, 2 * frame, LANES), F32),
            pltpu.VMEM((rows + frame, 2 * frame), F32),
            pltpu.SemaphoreType.DMA((max(blocks, 2 * cap),)),
            pltpu.SemaphoreType.DMA((rows // CHUNK,)),
        ],
        compiler_params=params(9),
        name="cut_pieces",
    )(own, up, parity, tile, strip, frames)


def dot(one, two):
    return jnp.dot(one, two, preferred_element_type=F32)


def stacked(parts):
    return jnp.concatenate(parts, axis=0)


def lane_parts(array):
    half = array.shape[1] // 2
    return array[:, :half], array[:, half:]


def wave_stage(mode, probe, patch, waves):
    frame = probe.shape[2]
    for at in range(0, frame, STEP):
        rows = pl.ds(at, STEP)
        probe_real, probe_imag = probe[mode, 0, rows], probe[mode, 1, rows]
        patch_real, patch_imag = patch[0, rows], patch[1, rows]
        parts = [lane_parts(part) for part in (
            probe_real * patch_real - probe_imag * patch_imag, probe_real * patch_imag + probe_imag * patch_real)]
        waves[0, mode, rows] = side_by_side([near + far for near, far in parts]).astype(BF16)
        waves[1, mode, rows] = side_by_side([near - far for near, far in parts]).astype(BF16)


def rows_dot(mode, source, tables, first, product):
    for odd in range(2):
        product[odd, mode] = dot(source[odd, mode], tables[first + odd])


def columns_dot(mode, tables, first, source, product):
    for odd in range(2):
        product[odd, mode] = dot(tables[first + odd], source[odd, mode])


def half_stage(mode, product, halfway):
    half = product.shape[2] // 2
    for at in range(0, half, TILE_ROWS):
        near, far = pl.ds(at, TILE_ROWS), pl.ds(half + at, TILE_ROWS)
        upper = [product[odd, mode, near] for odd in range(2)]
        lower = [product[odd, mode, far] for odd in range(2)]
        for odd in range(2):
            mixed = [a + b if not odd else a - b for a, b in zip(upper, lower)]
            real, imag = zip(*[lane_parts(part) for part in mixed])
            halfway[odd, mode, near] = side_by_side(real).astype(BF16)
            halfway[odd, mode, far] = side_by_side(imag).astype(BF16)


def residual_stage(modes, frame, field, amplitude, waves):
    half = frame // 2
    for odd in range(2):
        for at in range(0, half, TILE_ROWS):
            near, far = pl.ds(at, TILE_ROWS), pl.ds(half + at, TILE_ROWS)
            real = [field[odd, mode, near] for mode in range(modes)]
            imag = [field[odd, mode, far] for mode in range(modes)]
            lit = sum(a * a + b * b for a, b in zip(real, imag))
            factor = 1.0 / frame - amplitude[odd, near] * lax.rsqrt(jnp.maximum(lit, float(frame * frame)))
            target = pl.ds(odd * half + at, TILE_ROWS)
            for mode in range(modes):
                parts = [lane_parts(real[mode] * factor), lane_parts(imag[mode] * factor)]
                for column in range(2):
                    waves[column, mode, target] = side_by_side([part[column] for part in parts]).astype(BF16)


def back_stage(mode, product, halfway):
    half = product.shape[2] // 2
    for odd in range(2):
        for at in range(0, half, TILE_ROWS):
            rows = pl.ds(odd * half + at, TILE_ROWS)
            even_part, odd_part = product[0, mode, rows], product[1, mode, rows]
            near, far = lane_parts(even_part + odd_part), lane_parts(even_part - odd_part)
            halfway[odd, mode, pl.ds(at, TILE_ROWS)] = side_by_side([near[0], far[0]]).astype(BF16)
            halfway[odd, mode, pl.ds(half + at, TILE_ROWS)] = side_by_side([near[1], far[1]]).astype(BF16)


def gradient_stage(some_modes, first, product, probe, piece):
    frame = probe.shape[2]
    half = frame // 2
    across = frame // LANES
    for at in range(0, half, TILE_ROWS):
        rows = [pl.ds(at, TILE_ROWS), pl.ds(half + at, TILE_ROWS)]
        grads = [[0.0, 0.0], [0.0, 0.0]]
        for mode in some_modes:
            mixed = [(product[0, mode, part], product[1, mode, part]) for part in rows]
            for side in range(2):
                back_real, back_imag = [a + b if not side else a - b for a, b in mixed]
                probe_real, probe_imag = probe[mode, 0, rows[side]], probe[mode, 1, rows[side]]
                grads[side][0] += probe_real * back_real + probe_imag * back_imag
                grads[side][1] += probe_real * back_imag - probe_imag * back_real
        for side in range(2):
            for plane in range(2):
                grad = grads[side][plane] * (1.0 / frame)
                for b in range(across):
                    where = (plane * across + b, rows[side], slice(None))
                    part = grad[:, b * LANES:(b + 1) * LANES]
                    piece[where] = part if first else piece[where] + part


def frame_step(patch, amplitude, probe, tables, waves, halfway, product, field, piece):
    modes, _, frame, _ = probe.shape
    for step in range(modes + 1):
        if step < modes:
            wave_stage(step, probe, patch, waves)
            rows_dot(step, waves, tables, 0, product)
        if step:
            half_stage(step - 1, product, halfway)
            columns_dot(step - 1, tables, 2, halfway, field)
    residual_stage(modes, frame, field, amplitude, waves)
    for step in range(modes + 1):
        if step < modes:
            rows_dot(step, waves, tables, 4, product)
        if step:
            back_stage(step - 1, product, halfway)
            columns_dot(step - 1, tables, 6, halfway, field)
        if step and step % 2 == 0:
            gradient_stage((step - 2, step - 1), step == 2, field, probe, piece)


def ordered_amplitude(measured, task, order, amplitude):
    frame = measured.shape[2]
    for odd in range(2):
        root = jnp.sqrt(side_by_side(
            [measured[task, b, pl.ds(odd, frame // 2, stride=2), :] for b in range(measured.shape[1])]))
        high = root.astype(BF16)
        low = (root - high.astype(F32)).astype(BF16)
        amplitude[odd] = dot(high, order) + dot(low, order)


def window(band, lead, row, col, height, across):
    return taken_from(
        [band[lead + (col // LANES + b, pl.ds(row, height), slice(None))] for b in range(across + 1)],
        lax.rem(col, LANES),
    )


def add_window(total, lead, parts, row, col, frame):
    for b, moved in enumerate(put_into(parts, lax.rem(col, LANES))):
        at = lead + (col // LANES + b, pl.ds(row, frame), slice(None))
        total[at] = total[at] + moved


def kernel_cost(frames, modes, frame):
    return pl.CostEstimate(
        flops=frames * modes * 4 * 4 * frame ** 3, bytes_accessed=16 * 1024 * 1024, transcendentals=0)


def frames_kernel(phases, own, up, parity, tile, strip, frames, probe_in, tables_in, as_upper, as_lower, total_out, *rest):
    packed_outs = rest[:phases]
    (band, total, held, packed, piece, measured, probe, tables, patch, amplitude, waves, halfway, product, field, work,
     sems, shot_sems, held_sems, chunk_sems) = rest[phases:]
    cap, frame, _ = frames.shape
    extent = tile.shape[-1]
    across = frame // LANES
    own_blocks = extent // LANES
    half = frame // 2
    own_rows = pl.ds(frame, extent)

    first = start_all(
        [(tile.at[:, :, lanes_of(b)], band.at[:, b, own_rows]) for b in range(own_blocks)]
        + [(strip.at[:, :, lanes_of(b)], band.at[:, own_blocks + b, own_rows]) for b in range(across)]
        + [(probe_in, probe), (tables_in, tables)], sems)

    def mine(slot):
        return jnp.logical_and(slot < own[COUNT], own[FAR + slot] == 0)

    def borrowed(slot):
        return up[FAR + slot] > 0

    def shot_copies(slot, task, lent):
        if not lent:
            return [pltpu.make_async_copy(frames.at[slot, :, lanes_of(b)], measured.at[task, b], shot_sems.at[task, b])
                    for b in range(across)]
        at = pl.ds(pl.multiple_of(up[SHOT + slot], ROW_ALIGN), half)
        return [
            pltpu.make_async_copy(as_lower.at[at, lanes_of(part * across + b)],
                                  measured.at[task, b, pl.ds(part * half, half)], shot_sems.at[task, part * across + b])
            for part in range(2) for b in range(across)
        ]

    def held_copies(slot, task, lent):
        source, table = (as_lower, up) if lent else (as_upper, own)
        at = pl.ds(pl.multiple_of(table[PLACE + slot], ROW_ALIGN), frame)
        return [
            pltpu.make_async_copy(source.at[at, lanes_of(b)], held.at[task, b, pl.ds(frame, frame)], held_sems.at[task, b])
            for b in range(2 * across)
        ]

    def for_tasks(wait):
        for slot in range(cap):
            def run(copies):
                for copy in copies:
                    if wait:
                        copy.wait()
                    else:
                        copy.start()

            @pl.when(mine(slot))
            def _():
                run(shot_copies(slot, slot, False))

            @pl.when(own[NEAR + slot] > 0)
            def _():
                run(held_copies(slot, slot, False))

            @pl.when(borrowed(slot))
            def _():
                run(shot_copies(slot, cap + slot, True))
                run(held_copies(slot, cap + slot, True))

    for_tasks(False)
    for slot in range(cap):
        near = own[NEAR + slot]
        for field_at, value in (
            (ACTIVE, mine(slot).astype(jnp.int32)), (AT_ROW, own[ROW + slot] + frame), (AT_COL, own[COL + slot]),
            (LO, frame - near), (HI, frame), (START, near), (PIECE, own[PLACE + slot]), (SHIFT, frame - near), (ROLE, 0),
        ):
            work[slot, field_at] = value
        for field_at, value in (
            (ACTIVE, borrowed(slot).astype(jnp.int32)), (AT_ROW, up[ROW + slot] + frame - extent), (AT_COL, up[COL + slot]),
            (LO, 0), (HI, up[FAR + slot]), (START, frame), (PIECE, up[PLACE + slot]), (SHIFT, 0), (ROLE, 1),
        ):
            work[cap + slot, field_at] = value
    total[...] = jnp.zeros_like(total)
    wait_all(first)
    for_tasks(True)
    row_index = lax.broadcasted_iota(jnp.int32, (STEP, LANES), 0)

    def one(task, carry):
        @pl.when(work[task, ACTIVE] > 0)
        def _():
            row, col, start = work[task, AT_ROW], work[task, AT_COL], work[task, START]
            lo, hi = work[task, LO], work[task, HI]
            for at in range(0, frame, STEP):
                theirs = jnp.logical_and(row_index >= lo - at, row_index < hi - at)
                for plane in range(2):
                    near = window(band, (plane,), row + at, col, STEP, across)
                    other = [held[task, plane * across + b, pl.ds(start + at, STEP), :] for b in range(across)]
                    patch[plane, pl.ds(at, STEP)] = side_by_side([jnp.where(theirs, b, a) for a, b in zip(near, other)])
            ordered_amplitude(measured, task, tables[8], amplitude)
            frame_step(patch, amplitude, probe, tables, waves, halfway, product, field, piece)
            for at in range(0, frame, STEP):
                for plane in range(2):
                    parts = [piece[plane * across + b, pl.ds(at, STEP), :] for b in range(across)]
                    add_window(total, (plane,), parts, row + at, col, STEP)

            @pl.when(lo < hi)
            def _():
                target = pl.ds(pl.multiple_of(work[task, PIECE], ROW_ALIGN), frame)
                source = pl.ds(work[task, SHIFT], frame)
                for b in range(2 * across):
                    packed[work[task, ROLE], target, lanes_of(b)] = piece[b, source, :]

        return carry

    lax.fori_loop(0, 2 * cap, one, 0)
    end = start_all([(total.at[:, :, own_rows], total_out)], sems)
    for phase in range(phases):
        upper = parity[0] == phase
        role = jnp.where(upper, 0, 1)
        copy_out_rows(jnp.where(upper, own[KEPT], up[LENT]), packed.at[role], packed_outs[phase], chunk_sems)
    wait_all(end)


def frames_gradient(phases, own, up, parity, tile, strip, frames, probe, tables, as_upper, as_lower):
    cap, frame, _ = frames.shape
    extent = tile.shape[-1]
    modes = probe.shape[0]
    tall = extent + 2 * frame
    blocks = (extent + frame) // LANES
    across = frame // LANES
    rows = as_upper.shape[0]
    kept_rows = cap * KEEP
    return pl.pallas_call(
        lambda *refs: frames_kernel(phases, *refs),
        out_shape=(jax.ShapeDtypeStruct((2, blocks, extent, LANES), F32),)
        + (jax.ShapeDtypeStruct(as_upper.shape, F32),) * phases,
        in_specs=[smem_spec()] * 3 + [any_spec()] * 7,
        out_specs=(any_spec(),) * (1 + phases),
        scratch_shapes=[
            pltpu.VMEM((2, blocks, tall, LANES), F32),
            pltpu.VMEM((2, blocks, tall, LANES), F32),
            pltpu.VMEM((2 * cap, 2 * across, 2 * frame, LANES), F32),
            pltpu.VMEM((2, kept_rows + frame, 2 * frame), F32),
            pltpu.VMEM((2 * across, 2 * frame, LANES), F32),
            pltpu.VMEM((2 * cap, across, frame, LANES), F32),
            pltpu.VMEM(probe.shape, F32),
            pltpu.VMEM(tables.shape, BF16),
            pltpu.VMEM((2, frame, frame), F32),
            pltpu.VMEM((2, frame // 2, frame), F32),
            pltpu.VMEM((2, modes, frame, frame), BF16),
            pltpu.VMEM((2, modes, frame, frame), BF16),
            pltpu.VMEM((2, modes, frame, frame), F32),
            pltpu.VMEM((2, modes, frame, frame), F32),
            pltpu.SMEM((2 * cap, 16), jnp.int32),
            pltpu.SemaphoreType.DMA((blocks + 2,)),
            pltpu.SemaphoreType.DMA((2 * cap, 2 * across)),
            pltpu.SemaphoreType.DMA((2 * cap, 2 * across)),
            pltpu.SemaphoreType.DMA((rows // CHUNK,)),
        ],
        compiler_params=params(47),
        cost_estimate=kernel_cost(cap, modes, frame),
        name="frames_gradient",
    )(own, up, parity, tile, strip, frames, probe, tables, as_upper, as_lower)


def light_kernel(own, up, beside, probe, light_out, light, sem):
    modes, _, frame, _ = probe.shape
    own_blocks, extent, _ = light_out.shape
    across = frame // LANES
    inside = (pl.ds(across, own_blocks), pl.ds(frame, extent), slice(None))
    light[inside] = jnp.zeros((own_blocks, extent, LANES), F32)
    power = jnp.zeros((frame, frame), F32)
    for mode in range(modes):
        power += probe[mode, 0] * probe[mode, 0] + probe[mode, 1] * probe[mode, 1]
    power = halves(power)
    for table, lead, down, right in ((own, 0, 0, 0), (beside, 0, 0, 1), (up, 0, 1, 0), (beside, TABLE, 1, 1)):

        def lit(slot, carry, table=table, lead=lead, down=down, right=right):
            row = table[lead + ROW + slot] + frame - down * extent
            col = table[lead + COL + slot] + frame - right * extent

            @pl.when((row > 0) & (col > 0))
            def _():
                add_window(light, (), power, row, col, frame)

            return carry

        lax.fori_loop(0, table[lead + COUNT], lit, 0)
    copy = pltpu.make_async_copy(light.at[inside[0], inside[1]], light_out, sem)
    copy.start()
    copy.wait()


def light_plane(own, up, beside, probe, extent):
    frame = probe.shape[-1]
    wide = extent + 2 * frame
    return pl.pallas_call(
        light_kernel,
        out_shape=jax.ShapeDtypeStruct((extent // LANES, extent, LANES), F32),
        in_specs=[smem_spec()] * 3 + [vmem_spec()],
        out_specs=any_spec(),
        scratch_shapes=[pltpu.VMEM((wide // LANES, wide, LANES), F32), pltpu.SemaphoreType.DMA],
        compiler_params=params(9),
        cost_estimate=pl.CostEstimate(flops=0, bytes_accessed=12 * 1024 * 1024, transcendentals=0),
        name="light_plane",
    )(own, up, beside, probe)


def join_kernel(frame, own, up, as_upper, as_lower, total_in, total_out, right_out, band, held, sems):
    blocks = band.shape[1]
    extent = total_in.shape[2]
    across = frame // LANES
    rows = held.shape[1] - frame
    cap = rows // KEEP
    own_rows = pl.ds(0, extent)
    right = pl.ds(blocks - across, across)
    anything = jnp.logical_or(own[LENT] > 0, up[KEPT] > 0)

    @pl.when(anything)
    def _():
        whole = start_all([(total_in, band.at[:, :, own_rows])], sems)
        row_index = lax.broadcasted_iota(jnp.int32, (frame, LANES), 0)
        for number, (table, needed, field, pieces) in enumerate(
                ((own, own[LENT], FAR, as_upper), (up, up[KEPT], NEAR, as_lower))):

            @pl.when(needed > 0)
            def _(table=table, needed=needed, field=field, pieces=pieces):
                chunks = (needed + CHUNK - 1) // CHUNK

                def copies(chunk):
                    at = pl.ds(pl.multiple_of(chunk * CHUNK, CHUNK), CHUNK)
                    return [pltpu.make_async_copy(pieces.at[at, lanes_of(b)], held.at[b, at], sems.at[1 + chunk * 2 * across + b])
                            for b in range(2 * across)]

                def begin(chunk, carry):
                    for copy in copies(chunk):
                        copy.start()
                    return carry

                def end(chunk, carry):
                    for copy in copies(chunk):
                        copy.wait()
                    return carry

                lax.fori_loop(0, chunks, begin, 0)
                lax.fori_loop(0, chunks, end, 0)

            if not number:
                wait_all(whole)

            def one(slot, carry, table=table, field=field):
                col, height = table[COL + slot], table[field + slot]

                @pl.when(height > 0)
                def _():
                    row = table[ROW + slot] if field == FAR else 0
                    at = pl.ds(pl.multiple_of(table[PLACE + slot], ROW_ALIGN), frame)
                    for plane in range(2):
                        got = [jnp.where(row_index < height, held[plane * across + b, at, :], 0.0) for b in range(across)]
                        add_window(band, (plane,), got, row, col, frame)

                return carry

            lax.fori_loop(0, cap, one, 0)

        wait_all(start_all([(band.at[:, right, own_rows], right_out), (band.at[:, :, own_rows], total_out)], sems))

    @pl.when(jnp.logical_not(anything))
    def _():
        wait_all(start_all([(total_in.at[:, right], band.at[:, right, own_rows])], sems))
        wait_all(start_all([(band.at[:, right, own_rows], right_out)], sems))


def join_pieces(own, up, as_upper, as_lower, total, cap):
    frame = as_upper.shape[1] // 2
    _, blocks, extent, _ = total.shape
    across = frame // LANES
    rows = cap * KEEP
    return pl.pallas_call(
        lambda *refs: join_kernel(frame, *refs),
        out_shape=(jax.ShapeDtypeStruct(total.shape, F32), jax.ShapeDtypeStruct((2, across, extent, LANES), F32)),
        in_specs=[smem_spec(), smem_spec(), any_spec(), any_spec(), any_spec()],
        out_specs=(any_spec(), any_spec()),
        input_output_aliases={4: 0},
        scratch_shapes=[
            pltpu.VMEM((2, blocks, extent + frame, LANES), F32),
            pltpu.VMEM((2 * across, rows + frame, LANES), F32),
            pltpu.SemaphoreType.DMA((1 + rows // CHUNK * 2 * across,)),
        ],
        compiler_params=params(10),
        name="join_pieces",
    )(own, up, as_upper, as_lower, total)


def final_kernel(tile, total, light, left, out):
    across = left.shape[1]
    for b in range(total.shape[1]):
        below = 1.0 / (light[b] + 1.0)
        for plane in range(2):
            grad = total[plane, b]
            if b < across:
                grad = grad + left[plane, b]
            out[plane, :, lanes_of(b)] = tile[plane, :, lanes_of(b)] - grad * below


def final_update(tile, total, light, left):
    extent = tile.shape[-1]
    blocks = extent // LANES
    across = left.shape[1]
    tall = 128
    return pl.pallas_call(
        final_kernel,
        grid=(extent // tall,),
        out_shape=jax.ShapeDtypeStruct(tile.shape, F32),
        in_specs=[
            pl.BlockSpec((2, tall, extent), lambda i: (0, i, 0)),
            pl.BlockSpec((2, blocks, tall, LANES), lambda i: (0, 0, i, 0)),
            pl.BlockSpec((blocks, tall, LANES), lambda i: (0, i, 0)),
            pl.BlockSpec((2, across, tall, LANES), lambda i: (0, 0, i, 0)),
        ],
        out_specs=pl.BlockSpec((2, tall, extent), lambda i: (0, i, 0)),
        compiler_params=params(8),
        name="final_update",
    )(tile, total, light, left)


def body(object_tiles, probe, positions, frames, counts):
    tile = object_tiles[0]
    extent = tile.shape[-1]
    frame = frames.shape[-1]
    cap = frames.shape[1]
    peers = lax.axis_size("scan")
    tile_row = lax.axis_index("scan") // TCOLS
    phases = min(2, peers // TCOLS - 1)
    tables = dft_tables(frame)
    parity = (tile_row % 2).reshape(1)
    even = tile_row % 2 == 0

    own = slot_table(positions, counts, extent, frame)
    up = shifted(own, "scan", TCOLS)
    strip = shifted(tile[:, :, :frame], "scan", -1)
    beside = shifted(jnp.concatenate([own, up]), "scan", 1)
    beside, up, strip = lax.optimization_barrier((beside, up, strip))

    def exchange(phase, packed, choice):
        uppers = [k for k in range(peers - TCOLS) if k // TCOLS % 2 == phase]
        pairs = [(k, k + TCOLS) for k in uppers] + [(k + TCOLS, k) for k in uppers]

        def sender(size):
            def run(data):
                return lax.dynamic_update_slice(data, lax.ppermute(data[:size], "scan", pairs), (0, 0))
            return run

        branches = [lambda data: data] + [sender(size) for size in SIZES]
        return lax.switch(choice.reshape(()), branches, packed)

    def by_role(arrays):
        if len(arrays) == 1:
            return arrays[0], arrays[0]
        return jnp.where(even, arrays[0], arrays[1]), jnp.where(even, arrays[1], arrays[0])

    cuts = [cut_pieces(phase, own, up, parity, tile, strip, frames[0]) for phase in range(phases)]
    received = by_role([exchange(phase, cut[0], cut[1]) for phase, cut in enumerate(cuts)])
    total, *packed = frames_gradient(phases, own, up, parity, tile, strip, frames[0], probe, tables, *received)
    returned = by_role([exchange(phase, packed[phase], cut[2]) for phase, cut in enumerate(cuts)])
    total, right = join_pieces(own, up, *returned, total, cap)
    left = shifted(right, "scan", 1)
    total, beside = lax.optimization_barrier((total, beside))
    light = light_plane(own, up, beside, probe, extent)
    return final_update(tile, total, light, left)[None]


def solution(mesh):
    return jax.shard_map(
        body,
        mesh=mesh,
        in_specs=(
            P(("grp", "scan"), None, None, None),
            P(),
            P(("grp", "scan"), None, None),
            P(("grp", "scan"), None, None, None),
            P(("grp", "scan")),
        ),
        out_specs=P(("grp", "scan"), None, None, None),
        check_vma=False,
    )
```

```python
import math

import jax
import jax.numpy as jnp
import numpy as np
from jax import lax
from jax.experimental import pallas as pl
from jax.experimental.pallas import tpu as pltpu
from jax.sharding import PartitionSpec as P

TCOLS = 8
LANES = 128
ROW_ALIGN = 8
CHUNK = 64
STEP = 32
TILE_ROWS = 16
SIZES = (32, 64, 96, 128, 160, 192, 224, 256, 320, 384, 448, 512, 640, 768, 960, 1344)
MIB = 1024 * 1024
F32 = jnp.float32
BF16 = jnp.bfloat16

KEEP = 160
ROW, COL, NEAR, FAR, PLACE, SHOT = 0, 8, 16, 24, 32, 40
COUNT, KEPT, LENT, FORTH, BACK = 48, 49, 50, 51, 52
TABLE = 64

ACTIVE, AT_ROW, AT_COL, LO, HI, START, PIECE, SHIFT, ROLE = range(9)


def dft_tables(frame):
    near = np.arange(frame // 2, dtype=np.int64)
    blocks = []
    for odd in range(2):
        phase = (near[:, None] * (2 * near[None, :] + odd) % frame).astype(np.float64) * (2.0 * math.pi / frame)
        c, s = np.cos(phase), np.sin(phase)
        ahead = np.block([[c, -s], [s, c]])
        back = np.block([[c.T, s.T], [-s.T, c.T]])
        blocks.append((ahead, ahead.T, back, back.T))
    order = np.zeros((frame, frame))
    order[2 * near, near] = 1.0
    order[2 * near + 1, near + frame // 2] = 1.0
    tables = [blocks[odd][kind] for kind in range(4) for odd in range(2)] + [order]
    return jnp.asarray(np.stack(tables), F32).astype(BF16)


def shifted(array, axis, by):
    peers = lax.axis_size(axis)
    pairs = [(i, i + by) for i in range(peers) if 0 <= i + by < peers]
    return lax.ppermute(array, axis, pairs)


def any_spec():
    return pl.BlockSpec(memory_space=pl.ANY)


def hbm_spec():
    return pl.BlockSpec(memory_space=pltpu.HBM)


def smem_spec():
    return pl.BlockSpec(memory_space=pltpu.SMEM)


def vmem_spec():
    return pl.BlockSpec(memory_space=pltpu.VMEM)


def params(mebibytes):
    return pltpu.CompilerParams(vmem_limit_bytes=mebibytes * MIB)


def taken_from(blocks, by):
    lane = lax.broadcasted_iota(jnp.int32, blocks[0].shape, 1)
    rolled = [pltpu.roll(block, lax.rem(LANES - by, LANES), axis=1) for block in blocks]
    return [jnp.where(lane < LANES - by, one, two) for one, two in zip(rolled[:-1], rolled[1:])]


def put_into(blocks, by):
    lane = lax.broadcasted_iota(jnp.int32, blocks[0].shape, 1)
    rolled = [pltpu.roll(block, by, axis=1) for block in blocks]
    none = jnp.zeros_like(blocks[0])
    return [jnp.where(lane >= by, one, two) for one, two in zip(rolled + [none], [none] + rolled)]


def start_all(pairs, sems, first=0):
    copies = [pltpu.make_async_copy(source, target, sems.at[first + at]) for at, (source, target) in enumerate(pairs)]
    for copy in copies:
        copy.start()
    return copies


def wait_all(copies):
    for copy in copies:
        copy.wait()


def lanes_of(block):
    return pl.ds(block * LANES, LANES)


def side_by_side(parts):
    return jnp.concatenate(parts, axis=1)


def halves(array):
    return [array[:, :LANES], array[:, LANES:]]


def copy_out_rows(needed, packed, out, sems):
    chunks = (needed + CHUNK - 1) // CHUNK

    def copy(chunk):
        at = pl.ds(pl.multiple_of(chunk * CHUNK, CHUNK), CHUNK)
        return pltpu.make_async_copy(packed.at[at], out.at[at], sems.at[chunk])

    def begin(chunk, carry):
        copy(chunk).start()
        return carry

    def end(chunk, carry):
        copy(chunk).wait()
        return carry

    lax.fori_loop(0, chunks, begin, 0)
    lax.fori_loop(0, chunks, end, 0)


def up_to(value, step):
    return (value + step - 1) // step * step


def size_choice(needed):
    choice = jnp.where(needed > 0, 1, 0)
    for size in SIZES:
        choice = choice + jnp.where(needed > size, 1, 0)
    return choice


def prep_kernel(positions, counts, tile, table, edge, middle, sems):
    cap = positions.shape[2]
    extent = tile.shape[-1]
    frame = edge.shape[-1]
    count = counts[0]
    lanes = pl.ds(0, frame)
    copies = start_all([
        (tile.at[:, pl.ds(0, KEEP), lanes], edge.at[:, pl.ds(0, KEEP)]),
        (tile.at[:, pl.ds(KEEP + extent - frame, frame - KEEP), lanes], edge.at[:, pl.ds(KEEP, frame - KEEP)]),
        (tile.at[:, pl.ds(KEEP, extent - frame), lanes], middle),
    ], sems)
    kept, lent, shots = jnp.int32(0), jnp.int32(0), jnp.int32(0)
    for at in range(TABLE):
        table[at] = 0
    for slot in range(cap):
        row = lax.rem(positions[0, 0, slot], extent)
        col = lax.rem(positions[0, 1, slot], extent)
        below = jnp.where(slot < count, jnp.maximum(row + (frame - extent), 0), 0)
        stays = below <= KEEP
        near = jnp.where(stays, below, 0)
        far = jnp.where(stays, 0, frame - below)
        table[ROW + slot] = row
        table[COL + slot] = col
        table[NEAR + slot] = near
        table[FAR + slot] = far
        table[PLACE + slot] = jnp.where(stays, kept, lent)
        table[SHOT + slot] = shots
        kept = kept + up_to(near, ROW_ALIGN)
        lent = lent + up_to(far, ROW_ALIGN)
        shots = shots + jnp.where(stays, 0, frame // 2)
    for slot in range(cap):
        table[SHOT + slot] = table[SHOT + slot] + lent
    table[COUNT] = count
    table[KEPT] = kept
    table[LENT] = lent
    table[FORTH] = jnp.maximum(kept, lent + shots)
    table[BACK] = jnp.maximum(kept, lent)
    wait_all(copies)


def prepare(positions, counts, tile, frame):
    extent = tile.shape[-1]
    return pl.pallas_call(
        prep_kernel,
        out_shape=(
            jax.ShapeDtypeStruct((TABLE,), jnp.int32),
            jax.ShapeDtypeStruct((2, frame, frame), F32),
            jax.ShapeDtypeStruct((2, extent - frame, frame), F32),
        ),
        in_specs=[smem_spec(), smem_spec(), hbm_spec()],
        out_specs=(smem_spec(), vmem_spec(), vmem_spec()),
        scratch_shapes=[pltpu.SemaphoreType.DMA((3,))],
        compiler_params=params(4),
        name="prepare",
    )(jnp.swapaxes(positions, 1, 2), counts, tile)


def cut_kernel(phase, own, up, parity, tile, edge, frames, out, forth, back, band, packed, sems, chunk_sems):
    cap, frame, _ = frames.shape
    extent = tile.shape[-1]
    across = frame // LANES
    own_blocks = extent // LANES
    upper = parity[0] == phase
    forth[0] = size_choice(jnp.where(upper, own[FORTH], up[FORTH]))
    back[0] = size_choice(jnp.where(upper, own[BACK], up[BACK]))
    lends = jnp.logical_and(upper, own[LENT] > 0)
    gives = jnp.logical_and(jnp.logical_not(upper), up[KEPT] > 0)

    def cut(col, row, place):
        at = pl.ds(pl.multiple_of(place, ROW_ALIGN), frame)
        for plane in range(2):
            packed[at, pl.ds(plane * frame, frame)] = side_by_side(window(band, (plane,), row, col, frame, across))

    @pl.when(jnp.logical_or(lends, gives))
    def _():
        base = jnp.where(upper, extent - frame, 0)
        rows = pl.ds(pl.multiple_of(base, ROW_ALIGN), frame)
        wait_all(start_all(
            [(tile.at[:, rows, lanes_of(b)], band.at[:, b, pl.ds(0, frame)]) for b in range(own_blocks)]
            + [(edge.at[:, :, lanes_of(b)], band.at[:, own_blocks + b, pl.ds(0, frame)]) for b in range(across)], sems))

        def one(slot, carry):
            @pl.when(jnp.logical_and(upper, own[FAR + slot] > 0))
            def _():
                cut(own[COL + slot], own[ROW + slot] - (extent - frame), own[PLACE + slot])

            @pl.when(jnp.logical_and(gives, up[NEAR + slot] > 0))
            def _():
                cut(up[COL + slot], 0, up[PLACE + slot])

            return carry

        lax.fori_loop(0, cap, one, 0)

        def shots(slot):
            at = pl.ds(pl.multiple_of(own[SHOT + slot], ROW_ALIGN), frame // 2)
            return [pltpu.make_async_copy(frames.at[slot, pl.ds(part * frame // 2, frame // 2)],
                                          packed.at[at, pl.ds(part * frame, frame)], sems.at[2 * slot + part])
                    for part in range(2)]

        for wait in range(2):
            for slot in range(cap):
                @pl.when(jnp.logical_and(lends, own[FAR + slot] > 0))
                def _():
                    for copy in shots(slot):
                        if wait:
                            copy.wait()
                        else:
                            copy.start()

        copy_out_rows(jnp.where(upper, own[FORTH], up[KEPT]), packed, out, chunk_sems)


def cut_pieces(phase, own, up, parity, tile, edge, frames):
    cap, frame, _ = frames.shape
    extent = tile.shape[-1]
    blocks = (extent + frame) // LANES
    rows = SIZES[-1]
    return pl.pallas_call(
        lambda *refs: cut_kernel(phase, *refs),
        out_shape=(
            jax.ShapeDtypeStruct((rows, 2 * frame), F32),
            jax.ShapeDtypeStruct((1,), jnp.int32),
            jax.ShapeDtypeStruct((1,), jnp.int32),
        ),
        in_specs=[smem_spec(), smem_spec(), smem_spec(), hbm_spec(), hbm_spec(), hbm_spec()],
        out_specs=(hbm_spec(), smem_spec(), smem_spec()),
        scratch_shapes=[
            pltpu.VMEM((2, blocks, 2 * frame, LANES), F32),
            pltpu.VMEM((rows + frame, 2 * frame), F32),
            pltpu.SemaphoreType.DMA((max(blocks, 2 * cap),)),
            pltpu.SemaphoreType.DMA((rows // CHUNK,)),
        ],
        compiler_params=params(9),
        name="cut_pieces",
    )(own, up, parity, tile, edge, frames)


def dot(one, two):
    return jnp.dot(one, two, preferred_element_type=F32)


def stacked(parts):
    return jnp.concatenate(parts, axis=0)


def lane_parts(array):
    half = array.shape[1] // 2
    return array[:, :half], array[:, half:]


def wave_stage(mode, probe, patch, waves):
    frame = probe.shape[2]
    for at in range(0, frame, STEP):
        rows = pl.ds(at, STEP)
        probe_real, probe_imag = probe[mode, 0, rows], probe[mode, 1, rows]
        patch_real, patch_imag = patch[0, rows], patch[1, rows]
        parts = [lane_parts(part) for part in (
            probe_real * patch_real - probe_imag * patch_imag, probe_real * patch_imag + probe_imag * patch_real)]
        waves[0, mode, rows] = side_by_side([near + far for near, far in parts]).astype(BF16)
        waves[1, mode, rows] = side_by_side([near - far for near, far in parts]).astype(BF16)


def rows_dot(mode, source, tables, first, product):
    for odd in range(2):
        product[odd, mode] = dot(source[odd, mode], tables[first + odd])


def columns_dot(mode, tables, first, source, product):
    for odd in range(2):
        product[odd, mode] = dot(tables[first + odd], source[odd, mode])


def half_stage(mode, product, halfway):
    half = product.shape[2] // 2
    for at in range(0, half, TILE_ROWS):
        near, far = pl.ds(at, TILE_ROWS), pl.ds(half + at, TILE_ROWS)
        upper = [product[odd, mode, near] for odd in range(2)]
        lower = [product[odd, mode, far] for odd in range(2)]
        for odd in range(2):
            mixed = [a + b if not odd else a - b for a, b in zip(upper, lower)]
            real, imag = zip(*[lane_parts(part) for part in mixed])
            halfway[odd, mode, near] = side_by_side(real).astype(BF16)
            halfway[odd, mode, far] = side_by_side(imag).astype(BF16)


def residual_stage(modes, frame, field, amplitude, waves):
    half = frame // 2
    for odd in range(2):
        for at in range(0, half, TILE_ROWS):
            near, far = pl.ds(at, TILE_ROWS), pl.ds(half + at, TILE_ROWS)
            real = [field[odd, mode, near] for mode in range(modes)]
            imag = [field[odd, mode, far] for mode in range(modes)]
            lit = sum(a * a + b * b for a, b in zip(real, imag))
            factor = 1.0 / frame - amplitude[odd, near] * lax.rsqrt(jnp.maximum(lit, float(frame * frame)))
            target = pl.ds(odd * half + at, TILE_ROWS)
            for mode in range(modes):
                parts = [lane_parts(real[mode] * factor), lane_parts(imag[mode] * factor)]
                for column in range(2):
                    waves[column, mode, target] = side_by_side([part[column] for part in parts]).astype(BF16)


def back_stage(mode, product, halfway):
    half = product.shape[2] // 2
    for odd in range(2):
        for at in range(0, half, TILE_ROWS):
            rows = pl.ds(odd * half + at, TILE_ROWS)
            even_part, odd_part = product[0, mode, rows], product[1, mode, rows]
            near, far = lane_parts(even_part + odd_part), lane_parts(even_part - odd_part)
            halfway[odd, mode, pl.ds(at, TILE_ROWS)] = side_by_side([near[0], far[0]]).astype(BF16)
            halfway[odd, mode, pl.ds(half + at, TILE_ROWS)] = side_by_side([near[1], far[1]]).astype(BF16)


def gradient_stage(some_modes, first, product, probe, piece):
    frame = probe.shape[2]
    half = frame // 2
    across = frame // LANES
    for at in range(0, half, TILE_ROWS):
        rows = [pl.ds(at, TILE_ROWS), pl.ds(half + at, TILE_ROWS)]
        grads = [[0.0, 0.0], [0.0, 0.0]]
        for mode in some_modes:
            mixed = [(product[0, mode, part], product[1, mode, part]) for part in rows]
            for side in range(2):
                back_real, back_imag = [a + b if not side else a - b for a, b in mixed]
                probe_real, probe_imag = probe[mode, 0, rows[side]], probe[mode, 1, rows[side]]
                grads[side][0] += probe_real * back_real + probe_imag * back_imag
                grads[side][1] += probe_real * back_imag - probe_imag * back_real
        for side in range(2):
            for plane in range(2):
                grad = grads[side][plane] * (1.0 / frame)
                for b in range(across):
                    where = (plane * across + b, rows[side], slice(None))
                    part = grad[:, b * LANES:(b + 1) * LANES]
                    piece[where] = part if first else piece[where] + part


def frame_step(patch, amplitude, probe, tables, waves, halfway, product, field, piece):
    modes, _, frame, _ = probe.shape
    for step in range(modes + 1):
        if step < modes:
            wave_stage(step, probe, patch, waves)
            rows_dot(step, waves, tables, 0, product)
        if step:
            half_stage(step - 1, product, halfway)
            columns_dot(step - 1, tables, 2, halfway, field)
    residual_stage(modes, frame, field, amplitude, waves)
    for step in range(modes + 1):
        if step < modes:
            rows_dot(step, waves, tables, 4, product)
        if step:
            back_stage(step - 1, product, halfway)
            columns_dot(step - 1, tables, 6, halfway, field)
        if step and step % 2 == 0:
            gradient_stage((step - 2, step - 1), step == 2, field, probe, piece)


def ordered_amplitude(measured, task, order, amplitude):
    frame = measured.shape[2]
    for odd in range(2):
        root = jnp.sqrt(side_by_side(
            [measured[task, b, pl.ds(odd, frame // 2, stride=2), :] for b in range(measured.shape[1])]))
        high = root.astype(BF16)
        low = (root - high.astype(F32)).astype(BF16)
        amplitude[odd] = dot(high, order) + dot(low, order)


def window(band, lead, row, col, height, across):
    return taken_from(
        [band[lead + (col // LANES + b, pl.ds(row, height), slice(None))] for b in range(across + 1)],
        lax.rem(col, LANES),
    )


def add_window(total, lead, parts, row, col, frame):
    for b, moved in enumerate(put_into(parts, lax.rem(col, LANES))):
        at = lead + (col // LANES + b, pl.ds(row, frame), slice(None))
        total[at] = total[at] + moved


def kernel_cost(frames, modes, frame):
    return pl.CostEstimate(
        flops=frames * modes * 4 * 4 * frame ** 3, bytes_accessed=16 * 1024 * 1024, transcendentals=0)


def frames_kernel(phases, own, up, parity, tile, edge, middle, frames, probe_in, tables_in, as_upper, as_lower, total_out, *rest):
    packed_outs = rest[:phases]
    (band, total, held, packed, piece, measured, probe, tables, patch, amplitude, waves, halfway, product, field, work,
     sems, shot_sems, held_sems, chunk_sems) = rest[phases:]
    cap, frame, _ = frames.shape
    extent = tile.shape[-1]
    across = frame // LANES
    own_blocks = extent // LANES
    half = frame // 2
    own_rows = pl.ds(frame, extent)

    first = start_all(
        [(tile.at[:, :, lanes_of(b)], band.at[:, b, own_rows]) for b in range(own_blocks)]
        + [(source.at[:, pl.ds(at, height), lanes_of(b)], band.at[:, own_blocks + b, pl.ds(frame + target, height)])
           for source, at, height, target in (
               (edge, 0, KEEP, 0), (middle, 0, extent - frame, KEEP), (edge, KEEP, frame - KEEP, KEEP + extent - frame))
           for b in range(across)]
        + [(probe_in, probe), (tables_in, tables)], sems)

    def mine(slot):
        return jnp.logical_and(slot < own[COUNT], own[FAR + slot] == 0)

    def borrowed(slot):
        return up[FAR + slot] > 0

    def shot_copies(slot, task, lent):
        if not lent:
            return [pltpu.make_async_copy(frames.at[slot, :, lanes_of(b)], measured.at[task, b], shot_sems.at[task, b])
                    for b in range(across)]
        at = pl.ds(pl.multiple_of(up[SHOT + slot], ROW_ALIGN), half)
        return [
            pltpu.make_async_copy(as_lower.at[at, lanes_of(part * across + b)],
                                  measured.at[task, b, pl.ds(part * half, half)], shot_sems.at[task, part * across + b])
            for part in range(2) for b in range(across)
        ]

    def held_copies(slot, task, lent):
        source, table = (as_lower, up) if lent else (as_upper, own)
        at = pl.ds(pl.multiple_of(table[PLACE + slot], ROW_ALIGN), frame)
        return [
            pltpu.make_async_copy(source.at[at, lanes_of(b)], held.at[task, b, pl.ds(frame, frame)], held_sems.at[task, b])
            for b in range(2 * across)
        ]

    def for_tasks(wait):
        for slot in range(cap):
            def run(copies):
                for copy in copies:
                    if wait:
                        copy.wait()
                    else:
                        copy.start()

            @pl.when(mine(slot))
            def _():
                run(shot_copies(slot, slot, False))

            @pl.when(own[NEAR + slot] > 0)
            def _():
                run(held_copies(slot, slot, False))

            @pl.when(borrowed(slot))
            def _():
                run(shot_copies(slot, cap + slot, True))
                run(held_copies(slot, cap + slot, True))

    for_tasks(False)
    for slot in range(cap):
        near = own[NEAR + slot]
        for field_at, value in (
            (ACTIVE, mine(slot).astype(jnp.int32)), (AT_ROW, own[ROW + slot] + frame), (AT_COL, own[COL + slot]),
            (LO, frame - near), (HI, frame), (START, near), (PIECE, own[PLACE + slot]), (SHIFT, frame - near), (ROLE, 0),
        ):
            work[slot, field_at] = value
        for field_at, value in (
            (ACTIVE, borrowed(slot).astype(jnp.int32)), (AT_ROW, up[ROW + slot] + frame - extent), (AT_COL, up[COL + slot]),
            (LO, 0), (HI, up[FAR + slot]), (START, frame), (PIECE, up[PLACE + slot]), (SHIFT, 0), (ROLE, 1),
        ):
            work[cap + slot, field_at] = value
    total[...] = jnp.zeros_like(total)
    wait_all(first)
    for_tasks(True)
    row_index = lax.broadcasted_iota(jnp.int32, (STEP, LANES), 0)

    def one(task, carry):
        @pl.when(work[task, ACTIVE] > 0)
        def _():
            row, col, start = work[task, AT_ROW], work[task, AT_COL], work[task, START]
            lo, hi = work[task, LO], work[task, HI]
            for at in range(0, frame, STEP):
                theirs = jnp.logical_and(row_index >= lo - at, row_index < hi - at)
                for plane in range(2):
                    near = window(band, (plane,), row + at, col, STEP, across)
                    other = [held[task, plane * across + b, pl.ds(start + at, STEP), :] for b in range(across)]
                    patch[plane, pl.ds(at, STEP)] = side_by_side([jnp.where(theirs, b, a) for a, b in zip(near, other)])
            ordered_amplitude(measured, task, tables[8], amplitude)
            frame_step(patch, amplitude, probe, tables, waves, halfway, product, field, piece)
            for at in range(0, frame, STEP):
                for plane in range(2):
                    parts = [piece[plane * across + b, pl.ds(at, STEP), :] for b in range(across)]
                    add_window(total, (plane,), parts, row + at, col, STEP)

            @pl.when(lo < hi)
            def _():
                target = pl.ds(pl.multiple_of(work[task, PIECE], ROW_ALIGN), frame)
                source = pl.ds(work[task, SHIFT], frame)
                for b in range(2 * across):
                    packed[work[task, ROLE], target, lanes_of(b)] = piece[b, source, :]

        return carry

    lax.fori_loop(0, 2 * cap, one, 0)
    end = start_all([(total.at[:, :, own_rows], total_out)], sems)
    for phase in range(phases):
        upper = parity[0] == phase
        role = jnp.where(upper, 0, 1)
        copy_out_rows(jnp.where(upper, own[KEPT], up[LENT]), packed.at[role], packed_outs[phase], chunk_sems)
    wait_all(end)


def frames_gradient(phases, own, up, parity, tile, edge, middle, frames, probe, tables, as_upper, as_lower):
    cap, frame, _ = frames.shape
    extent = tile.shape[-1]
    modes = probe.shape[0]
    tall = extent + 2 * frame
    blocks = (extent + frame) // LANES
    across = frame // LANES
    rows = as_upper.shape[0]
    kept_rows = cap * KEEP
    return pl.pallas_call(
        lambda *refs: frames_kernel(phases, *refs),
        out_shape=(jax.ShapeDtypeStruct((2, blocks, extent, LANES), F32),)
        + (jax.ShapeDtypeStruct(as_upper.shape, F32),) * phases,
        in_specs=[smem_spec()] * 3 + [hbm_spec()] * 8,
        out_specs=(hbm_spec(),) * (1 + phases),
        scratch_shapes=[
            pltpu.VMEM((2, blocks, tall, LANES), F32),
            pltpu.VMEM((2, blocks, tall, LANES), F32),
            pltpu.VMEM((2 * cap, 2 * across, 2 * frame, LANES), F32),
            pltpu.VMEM((2, kept_rows + frame, 2 * frame), F32),
            pltpu.VMEM((2 * across, 2 * frame, LANES), F32),
            pltpu.VMEM((2 * cap, across, frame, LANES), F32),
            pltpu.VMEM(probe.shape, F32),
            pltpu.VMEM(tables.shape, BF16),
            pltpu.VMEM((2, frame, frame), F32),
            pltpu.VMEM((2, frame // 2, frame), F32),
            pltpu.VMEM((2, modes, frame, frame), BF16),
            pltpu.VMEM((2, modes, frame, frame), BF16),
            pltpu.VMEM((2, modes, frame, frame), F32),
            pltpu.VMEM((2, modes, frame, frame), F32),
            pltpu.SMEM((2 * cap, 16), jnp.int32),
            pltpu.SemaphoreType.DMA((blocks + 2 * across + 2,)),
            pltpu.SemaphoreType.DMA((2 * cap, 2 * across)),
            pltpu.SemaphoreType.DMA((2 * cap, 2 * across)),
            pltpu.SemaphoreType.DMA((rows // CHUNK,)),
        ],
        compiler_params=params(47),
        cost_estimate=kernel_cost(cap, modes, frame),
        name="frames_gradient",
    )(own, up, parity, tile, edge, middle, frames, probe, tables, as_upper, as_lower)


def light_kernel(own, up, beside, probe, light_out, light, sem):
    modes, _, frame, _ = probe.shape
    own_blocks, extent, _ = light_out.shape
    across = frame // LANES
    inside = (pl.ds(across, own_blocks), pl.ds(frame, extent), slice(None))
    light[inside] = jnp.zeros((own_blocks, extent, LANES), F32)
    power = jnp.zeros((frame, frame), F32)
    for mode in range(modes):
        power += probe[mode, 0] * probe[mode, 0] + probe[mode, 1] * probe[mode, 1]
    power = halves(power)
    for table, lead, down, right in ((own, 0, 0, 0), (beside, 0, 0, 1), (up, 0, 1, 0), (beside, TABLE, 1, 1)):

        def lit(slot, carry, table=table, lead=lead, down=down, right=right):
            row = table[lead + ROW + slot] + frame - down * extent
            col = table[lead + COL + slot] + frame - right * extent

            @pl.when((row > 0) & (col > 0))
            def _():
                add_window(light, (), power, row, col, frame)

            return carry

        lax.fori_loop(0, table[lead + COUNT], lit, 0)
    copy = pltpu.make_async_copy(light.at[inside[0], inside[1]], light_out, sem)
    copy.start()
    copy.wait()


def light_plane(own, up, beside, probe, extent):
    frame = probe.shape[-1]
    wide = extent + 2 * frame
    return pl.pallas_call(
        light_kernel,
        out_shape=jax.ShapeDtypeStruct((extent // LANES, extent, LANES), F32),
        in_specs=[smem_spec()] * 3 + [vmem_spec()],
        out_specs=any_spec(),
        scratch_shapes=[pltpu.VMEM((wide // LANES, wide, LANES), F32), pltpu.SemaphoreType.DMA],
        compiler_params=params(9),
        cost_estimate=pl.CostEstimate(flops=0, bytes_accessed=12 * 1024 * 1024, transcendentals=0),
        name="light_plane",
    )(own, up, beside, probe)


def join_kernel(frame, own, up, as_upper, as_lower, total_in, total_out, right_out, band, held, sems):
    blocks = band.shape[1]
    extent = total_in.shape[2]
    across = frame // LANES
    rows = held.shape[1] - frame
    cap = rows // KEEP
    own_rows = pl.ds(0, extent)
    right = pl.ds(blocks - across, across)
    anything = jnp.logical_or(own[LENT] > 0, up[KEPT] > 0)

    @pl.when(anything)
    def _():
        whole = start_all([(total_in, band.at[:, :, own_rows])], sems)
        row_index = lax.broadcasted_iota(jnp.int32, (frame, LANES), 0)
        for number, (table, needed, field, pieces) in enumerate(
                ((own, own[LENT], FAR, as_upper), (up, up[KEPT], NEAR, as_lower))):

            @pl.when(needed > 0)
            def _(table=table, needed=needed, field=field, pieces=pieces):
                chunks = (needed + CHUNK - 1) // CHUNK

                def copies(chunk):
                    at = pl.ds(pl.multiple_of(chunk * CHUNK, CHUNK), CHUNK)
                    return [pltpu.make_async_copy(pieces.at[at, lanes_of(b)], held.at[b, at], sems.at[1 + chunk * 2 * across + b])
                            for b in range(2 * across)]

                def begin(chunk, carry):
                    for copy in copies(chunk):
                        copy.start()
                    return carry

                def end(chunk, carry):
                    for copy in copies(chunk):
                        copy.wait()
                    return carry

                lax.fori_loop(0, chunks, begin, 0)
                lax.fori_loop(0, chunks, end, 0)

            if not number:
                wait_all(whole)

            def one(slot, carry, table=table, field=field):
                col, height = table[COL + slot], table[field + slot]

                @pl.when(height > 0)
                def _():
                    row = table[ROW + slot] if field == FAR else 0
                    at = pl.ds(pl.multiple_of(table[PLACE + slot], ROW_ALIGN), frame)
                    for plane in range(2):
                        got = [jnp.where(row_index < height, held[plane * across + b, at, :], 0.0) for b in range(across)]
                        add_window(band, (plane,), got, row, col, frame)

                return carry

            lax.fori_loop(0, cap, one, 0)

        wait_all(start_all([(band.at[:, right, own_rows], right_out), (band.at[:, :, own_rows], total_out)], sems))

    @pl.when(jnp.logical_not(anything))
    def _():
        wait_all(start_all([(total_in.at[:, right], band.at[:, right, own_rows])], sems))
        wait_all(start_all([(band.at[:, right, own_rows], right_out)], sems))


def join_pieces(own, up, as_upper, as_lower, total, cap):
    frame = as_upper.shape[1] // 2
    _, blocks, extent, _ = total.shape
    across = frame // LANES
    rows = cap * KEEP
    return pl.pallas_call(
        lambda *refs: join_kernel(frame, *refs),
        out_shape=(jax.ShapeDtypeStruct(total.shape, F32), jax.ShapeDtypeStruct((2, across, extent, LANES), F32)),
        in_specs=[smem_spec(), smem_spec(), hbm_spec(), hbm_spec(), hbm_spec()],
        out_specs=(hbm_spec(), any_spec()),
        input_output_aliases={4: 0},
        scratch_shapes=[
            pltpu.VMEM((2, blocks, extent + frame, LANES), F32),
            pltpu.VMEM((2 * across, rows + frame, LANES), F32),
            pltpu.SemaphoreType.DMA((1 + rows // CHUNK * 2 * across,)),
        ],
        compiler_params=params(10),
        name="join_pieces",
    )(own, up, as_upper, as_lower, total)


def final_kernel(tile, total, light, left, out):
    across = left.shape[1]
    for b in range(total.shape[1]):
        below = 1.0 / (light[b] + 1.0)
        for plane in range(2):
            grad = total[plane, b]
            if b < across:
                grad = grad + left[plane, b]
            out[plane, :, lanes_of(b)] = tile[plane, :, lanes_of(b)] - grad * below


def final_update(tile, total, light, left):
    extent = tile.shape[-1]
    blocks = extent // LANES
    across = left.shape[1]
    tall = 128
    return pl.pallas_call(
        final_kernel,
        grid=(extent // tall,),
        out_shape=jax.ShapeDtypeStruct(tile.shape, F32),
        in_specs=[
            pl.BlockSpec((2, tall, extent), lambda i: (0, i, 0)),
            pl.BlockSpec((2, blocks, tall, LANES), lambda i: (0, 0, i, 0)),
            pl.BlockSpec((blocks, tall, LANES), lambda i: (0, i, 0)),
            pl.BlockSpec((2, across, tall, LANES), lambda i: (0, 0, i, 0)),
        ],
        out_specs=pl.BlockSpec((2, tall, extent), lambda i: (0, i, 0)),
        compiler_params=params(8),
        name="final_update",
    )(tile, total, light, left)


def body(object_tiles, probe, positions, frames, counts):
    tile = object_tiles[0]
    extent = tile.shape[-1]
    frame = frames.shape[-1]
    cap = frames.shape[1]
    peers = lax.axis_size("scan")
    tile_row = lax.axis_index("scan") // TCOLS
    phases = min(2, peers // TCOLS - 1)
    tables = dft_tables(frame)
    parity = (tile_row % 2).reshape(1)
    even = tile_row % 2 == 0

    own, edge, middle = prepare(positions, counts, tile, frame)
    up = shifted(own, "scan", TCOLS)
    edge = shifted(edge, "scan", -1)
    middle = shifted(middle, "scan", -1)
    beside = shifted(jnp.concatenate([own, up]), "scan", 1)

    def exchange(phase, packed, choice):
        uppers = [k for k in range(peers - TCOLS) if k // TCOLS % 2 == phase]
        pairs = [(k, k + TCOLS) for k in uppers] + [(k + TCOLS, k) for k in uppers]

        def sender(size):
            def run(data):
                return lax.dynamic_update_slice(data, lax.ppermute(data[:size], "scan", pairs), (0, 0))
            return run

        branches = [lambda data: data] + [sender(size) for size in SIZES]
        return lax.switch(choice.reshape(()), branches, packed)

    def by_role(arrays):
        if len(arrays) == 1:
            return arrays[0], arrays[0]
        return jnp.where(even, arrays[0], arrays[1]), jnp.where(even, arrays[1], arrays[0])

    cuts = [cut_pieces(phase, own, up, parity, tile, edge, frames[0]) for phase in range(phases)]
    received = by_role([exchange(phase, cut[0], cut[1]) for phase, cut in enumerate(cuts)])
    received, beside = lax.optimization_barrier((received, beside))
    total, *packed = frames_gradient(phases, own, up, parity, tile, edge, middle, frames[0], probe, tables, *received)
    returned = by_role([exchange(phase, packed[phase], cut[2]) for phase, cut in enumerate(cuts)])
    total, right = join_pieces(own, up, *returned, total, cap)
    left = shifted(right, "scan", 1)
    total, beside = lax.optimization_barrier((total, beside))
    light = light_plane(own, up, beside, probe, extent)
    return final_update(tile, total, light, left)[None]


def solution(mesh):
    return jax.shard_map(
        body,
        mesh=mesh,
        in_specs=(
            P(("grp", "scan"), None, None, None),
            P(),
            P(("grp", "scan"), None, None),
            P(("grp", "scan"), None, None, None),
            P(("grp", "scan")),
        ),
        out_specs=P(("grp", "scan"), None, None, None),
        check_vma=False,
    )
```

```python
import math

import jax
import jax.numpy as jnp
import numpy as np
from jax import lax
from jax.experimental import pallas as pl
from jax.experimental.pallas import tpu as pltpu
from jax.sharding import PartitionSpec as P

TCOLS = 8
LANES = 128
ROW_ALIGN = 8
CHUNK = 64
STEP = 32
TILE_ROWS = 16
SIZES = (32, 64, 96, 128, 160, 192, 224, 256, 320, 384, 448, 512, 640, 768, 960, 1344)
MIB = 1024 * 1024
F32 = jnp.float32
BF16 = jnp.bfloat16

KEEP = 160
ROW, COL, NEAR, FAR, PLACE, SHOT = 0, 8, 16, 24, 32, 40
COUNT, KEPT, LENT, FORTH, BACK = 48, 49, 50, 51, 52
TABLE = 64

ACTIVE, AT_ROW, AT_COL, LO, HI, START, PIECE, SHIFT, ROLE = range(9)


def dft_tables(frame):
    near = np.arange(frame // 2, dtype=np.int64)
    blocks = []
    for odd in range(2):
        phase = (near[:, None] * (2 * near[None, :] + odd) % frame).astype(np.float64) * (2.0 * math.pi / frame)
        c, s = np.cos(phase), np.sin(phase)
        ahead = np.block([[c, -s], [s, c]])
        back = np.block([[c.T, s.T], [-s.T, c.T]])
        blocks.append((ahead, ahead.T, back, back.T))
    order = np.zeros((frame, frame))
    order[2 * near, near] = 1.0
    order[2 * near + 1, near + frame // 2] = 1.0
    tables = [blocks[odd][kind] for kind in range(4) for odd in range(2)] + [order]
    return jnp.asarray(np.stack(tables), F32).astype(BF16)


def shifted(array, axis, by):
    peers = lax.axis_size(axis)
    pairs = [(i, i + by) for i in range(peers) if 0 <= i + by < peers]
    return lax.ppermute(array, axis, pairs)


def any_spec():
    return pl.BlockSpec(memory_space=pl.ANY)


def hbm_spec():
    return pl.BlockSpec(memory_space=pltpu.HBM)


def smem_spec():
    return pl.BlockSpec(memory_space=pltpu.SMEM)


def vmem_spec():
    return pl.BlockSpec(memory_space=pltpu.VMEM)


def params(mebibytes):
    return pltpu.CompilerParams(vmem_limit_bytes=mebibytes * MIB)


def taken_from(blocks, by):
    lane = lax.broadcasted_iota(jnp.int32, blocks[0].shape, 1)
    rolled = [pltpu.roll(block, lax.rem(LANES - by, LANES), axis=1) for block in blocks]
    return [jnp.where(lane < LANES - by, one, two) for one, two in zip(rolled[:-1], rolled[1:])]


def put_into(blocks, by):
    lane = lax.broadcasted_iota(jnp.int32, blocks[0].shape, 1)
    rolled = [pltpu.roll(block, by, axis=1) for block in blocks]
    none = jnp.zeros_like(blocks[0])
    return [jnp.where(lane >= by, one, two) for one, two in zip(rolled + [none], [none] + rolled)]


def start_all(pairs, sems, first=0):
    copies = [pltpu.make_async_copy(source, target, sems.at[first + at]) for at, (source, target) in enumerate(pairs)]
    for copy in copies:
        copy.start()
    return copies


def wait_all(copies):
    for copy in copies:
        copy.wait()


def lanes_of(block):
    return pl.ds(block * LANES, LANES)


def side_by_side(parts):
    return jnp.concatenate(parts, axis=1)


def halves(array):
    return [array[:, :LANES], array[:, LANES:]]


def copy_out_rows(needed, packed, out, sems):
    chunks = (needed + CHUNK - 1) // CHUNK

    def copy(chunk):
        at = pl.ds(pl.multiple_of(chunk * CHUNK, CHUNK), CHUNK)
        return pltpu.make_async_copy(packed.at[at], out.at[at], sems.at[chunk])

    def begin(chunk, carry):
        copy(chunk).start()
        return carry

    def end(chunk, carry):
        copy(chunk).wait()
        return carry

    lax.fori_loop(0, chunks, begin, 0)
    lax.fori_loop(0, chunks, end, 0)


def up_to(value, step):
    return (value + step - 1) // step * step


def size_choice(needed):
    choice = jnp.where(needed > 0, 1, 0)
    for size in SIZES:
        choice = choice + jnp.where(needed > size, 1, 0)
    return choice


def prep_kernel(positions, counts, tile, table, edge, middle, sems):
    cap = positions.shape[2]
    extent = tile.shape[-1]
    frame = edge.shape[-1]
    count = counts[0]
    lanes = pl.ds(0, frame)
    copies = start_all([
        (tile.at[:, pl.ds(0, KEEP), lanes], edge.at[:, pl.ds(0, KEEP)]),
        (tile.at[:, pl.ds(KEEP + extent - frame, frame - KEEP), lanes], edge.at[:, pl.ds(KEEP, frame - KEEP)]),
        (tile.at[:, pl.ds(KEEP, extent - frame), lanes], middle),
    ], sems)
    kept, lent, shots = jnp.int32(0), jnp.int32(0), jnp.int32(0)
    for at in range(TABLE):
        table[at] = 0
    for slot in range(cap):
        row = lax.rem(positions[0, 0, slot], extent)
        col = lax.rem(positions[0, 1, slot], extent)
        below = jnp.where(slot < count, jnp.maximum(row + (frame - extent), 0), 0)
        stays = below <= KEEP
        near = jnp.where(stays, below, 0)
        far = jnp.where(stays, 0, frame - below)
        table[ROW + slot] = row
        table[COL + slot] = col
        table[NEAR + slot] = near
        table[FAR + slot] = far
        table[PLACE + slot] = jnp.where(stays, kept, lent)
        table[SHOT + slot] = shots
        kept = kept + up_to(near, ROW_ALIGN)
        lent = lent + up_to(far, ROW_ALIGN)
        shots = shots + jnp.where(stays, 0, frame // 2)
    for slot in range(cap):
        table[SHOT + slot] = table[SHOT + slot] + lent
    table[COUNT] = count
    table[KEPT] = kept
    table[LENT] = lent
    table[FORTH] = jnp.maximum(kept, lent + shots)
    table[BACK] = jnp.maximum(kept, lent)
    wait_all(copies)


def prepare(positions, counts, tile, frame):
    extent = tile.shape[-1]
    return pl.pallas_call(
        prep_kernel,
        out_shape=(
            jax.ShapeDtypeStruct((TABLE,), jnp.int32),
            jax.ShapeDtypeStruct((2, frame, frame), F32),
            jax.ShapeDtypeStruct((2, extent - frame, frame), F32),
        ),
        in_specs=[smem_spec(), smem_spec(), hbm_spec()],
        out_specs=(smem_spec(), vmem_spec(), vmem_spec()),
        scratch_shapes=[pltpu.SemaphoreType.DMA((3,))],
        compiler_params=params(62),
        name="prepare",
    )(jnp.swapaxes(positions, 1, 2), counts, tile)


def cut_kernel(phase, own, up, parity, tile, edge, frames, out, forth, back, band, packed, sems, chunk_sems):
    cap, frame, _ = frames.shape
    extent = tile.shape[-1]
    across = frame // LANES
    own_blocks = extent // LANES
    upper = parity[0] == phase
    forth[0] = size_choice(jnp.where(upper, own[FORTH], up[FORTH]))
    back[0] = size_choice(jnp.where(upper, own[BACK], up[BACK]))
    lends = jnp.logical_and(upper, own[LENT] > 0)
    gives = jnp.logical_and(jnp.logical_not(upper), up[KEPT] > 0)

    def cut(col, row, place):
        at = pl.ds(pl.multiple_of(place, ROW_ALIGN), frame)
        for plane in range(2):
            packed[at, pl.ds(plane * frame, frame)] = side_by_side(window(band, (plane,), row, col, frame, across))

    @pl.when(jnp.logical_or(lends, gives))
    def _():
        base = jnp.where(upper, extent - frame, 0)
        rows = pl.ds(pl.multiple_of(base, ROW_ALIGN), frame)
        wait_all(start_all(
            [(tile.at[:, rows, lanes_of(b)], band.at[:, b, pl.ds(0, frame)]) for b in range(own_blocks)]
            + [(edge.at[:, :, lanes_of(b)], band.at[:, own_blocks + b, pl.ds(0, frame)]) for b in range(across)], sems))

        def one(slot, carry):
            @pl.when(jnp.logical_and(upper, own[FAR + slot] > 0))
            def _():
                cut(own[COL + slot], own[ROW + slot] - (extent - frame), own[PLACE + slot])

            @pl.when(jnp.logical_and(gives, up[NEAR + slot] > 0))
            def _():
                cut(up[COL + slot], 0, up[PLACE + slot])

            return carry

        lax.fori_loop(0, cap, one, 0)

        def shots(slot):
            at = pl.ds(pl.multiple_of(own[SHOT + slot], ROW_ALIGN), frame // 2)
            return [pltpu.make_async_copy(frames.at[slot, pl.ds(part * frame // 2, frame // 2)],
                                          packed.at[at, pl.ds(part * frame, frame)], sems.at[2 * slot + part])
                    for part in range(2)]

        for wait in range(2):
            for slot in range(cap):
                @pl.when(jnp.logical_and(lends, own[FAR + slot] > 0))
                def _():
                    for copy in shots(slot):
                        if wait:
                            copy.wait()
                        else:
                            copy.start()

        copy_out_rows(jnp.where(upper, own[FORTH], up[KEPT]), packed, out, chunk_sems)


def cut_pieces(phase, own, up, parity, tile, edge, frames):
    cap, frame, _ = frames.shape
    extent = tile.shape[-1]
    blocks = (extent + frame) // LANES
    rows = SIZES[-1]
    return pl.pallas_call(
        lambda *refs: cut_kernel(phase, *refs),
        out_shape=(
            jax.ShapeDtypeStruct((rows, 2 * frame), F32),
            jax.ShapeDtypeStruct((1,), jnp.int32),
            jax.ShapeDtypeStruct((1,), jnp.int32),
        ),
        in_specs=[smem_spec(), smem_spec(), smem_spec(), hbm_spec(), hbm_spec(), hbm_spec()],
        out_specs=(hbm_spec(), smem_spec(), smem_spec()),
        scratch_shapes=[
            pltpu.VMEM((2, blocks, 2 * frame, LANES), F32),
            pltpu.VMEM((rows + frame, 2 * frame), F32),
            pltpu.SemaphoreType.DMA((max(blocks, 2 * cap),)),
            pltpu.SemaphoreType.DMA((rows // CHUNK,)),
        ],
        compiler_params=params(60),
        name="cut_pieces",
    )(own, up, parity, tile, edge, frames)


def dot(one, two):
    return jnp.dot(one, two, preferred_element_type=F32)


def stacked(parts):
    return jnp.concatenate(parts, axis=0)


def lane_parts(array):
    half = array.shape[1] // 2
    return array[:, :half], array[:, half:]


def wave_stage(mode, probe, patch, waves):
    frame = probe.shape[2]
    for at in range(0, frame, STEP):
        rows = pl.ds(at, STEP)
        probe_real, probe_imag = probe[mode, 0, rows], probe[mode, 1, rows]
        patch_real, patch_imag = patch[0, rows], patch[1, rows]
        parts = [lane_parts(part) for part in (
            probe_real * patch_real - probe_imag * patch_imag, probe_real * patch_imag + probe_imag * patch_real)]
        waves[0, mode, rows] = side_by_side([near + far for near, far in parts]).astype(BF16)
        waves[1, mode, rows] = side_by_side([near - far for near, far in parts]).astype(BF16)


def rows_dot(mode, source, tables, first, product):
    for odd in range(2):
        product[odd, mode] = dot(source[odd, mode], tables[first + odd])


def columns_dot(mode, tables, first, source, product):
    for odd in range(2):
        product[odd, mode] = dot(tables[first + odd], source[odd, mode])


def half_stage(mode, product, halfway):
    half = product.shape[2] // 2
    for at in range(0, half, TILE_ROWS):
        near, far = pl.ds(at, TILE_ROWS), pl.ds(half + at, TILE_ROWS)
        upper = [product[odd, mode, near] for odd in range(2)]
        lower = [product[odd, mode, far] for odd in range(2)]
        for odd in range(2):
            mixed = [a + b if not odd else a - b for a, b in zip(upper, lower)]
            real, imag = zip(*[lane_parts(part) for part in mixed])
            halfway[odd, mode, near] = side_by_side(real).astype(BF16)
            halfway[odd, mode, far] = side_by_side(imag).astype(BF16)


def residual_stage(modes, frame, field, amplitude, waves):
    half = frame // 2
    for odd in range(2):
        for at in range(0, half, TILE_ROWS):
            near, far = pl.ds(at, TILE_ROWS), pl.ds(half + at, TILE_ROWS)
            real = [field[odd, mode, near] for mode in range(modes)]
            imag = [field[odd, mode, far] for mode in range(modes)]
            lit = sum(a * a + b * b for a, b in zip(real, imag))
            factor = 1.0 / frame - amplitude[odd, near] * lax.rsqrt(jnp.maximum(lit, float(frame * frame)))
            target = pl.ds(odd * half + at, TILE_ROWS)
            for mode in range(modes):
                parts = [lane_parts(real[mode] * factor), lane_parts(imag[mode] * factor)]
                for column in range(2):
                    waves[column, mode, target] = side_by_side([part[column] for part in parts]).astype(BF16)


def back_stage(mode, product, halfway):
    half = product.shape[2] // 2
    for odd in range(2):
        for at in range(0, half, TILE_ROWS):
            rows = pl.ds(odd * half + at, TILE_ROWS)
            even_part, odd_part = product[0, mode, rows], product[1, mode, rows]
            near, far = lane_parts(even_part + odd_part), lane_parts(even_part - odd_part)
            halfway[odd, mode, pl.ds(at, TILE_ROWS)] = side_by_side([near[0], far[0]]).astype(BF16)
            halfway[odd, mode, pl.ds(half + at, TILE_ROWS)] = side_by_side([near[1], far[1]]).astype(BF16)


def gradient_stage(some_modes, first, product, probe, piece):
    frame = probe.shape[2]
    half = frame // 2
    across = frame // LANES
    for at in range(0, half, TILE_ROWS):
        rows = [pl.ds(at, TILE_ROWS), pl.ds(half + at, TILE_ROWS)]
        grads = [[0.0, 0.0], [0.0, 0.0]]
        for mode in some_modes:
            mixed = [(product[0, mode, part], product[1, mode, part]) for part in rows]
            for side in range(2):
                back_real, back_imag = [a + b if not side else a - b for a, b in mixed]
                probe_real, probe_imag = probe[mode, 0, rows[side]], probe[mode, 1, rows[side]]
                grads[side][0] += probe_real * back_real + probe_imag * back_imag
                grads[side][1] += probe_real * back_imag - probe_imag * back_real
        for side in range(2):
            for plane in range(2):
                grad = grads[side][plane] * (1.0 / frame)
                for b in range(across):
                    where = (plane * across + b, rows[side], slice(None))
                    part = grad[:, b * LANES:(b + 1) * LANES]
                    piece[where] = part if first else piece[where] + part


def frame_step(patch, amplitude, probe, tables, waves, halfway, product, field, piece):
    modes, _, frame, _ = probe.shape
    for step in range(modes + 1):
        if step < modes:
            wave_stage(step, probe, patch, waves)
            rows_dot(step, waves, tables, 0, product)
        if step:
            half_stage(step - 1, product, halfway)
            columns_dot(step - 1, tables, 2, halfway, field)
    residual_stage(modes, frame, field, amplitude, waves)
    for step in range(modes + 1):
        if step < modes:
            rows_dot(step, waves, tables, 4, product)
        if step:
            back_stage(step - 1, product, halfway)
            columns_dot(step - 1, tables, 6, halfway, field)
        if step and step % 2 == 0:
            gradient_stage((step - 2, step - 1), step == 2, field, probe, piece)


def ordered_amplitude(measured, task, order, amplitude):
    frame = measured.shape[2]
    for odd in range(2):
        root = jnp.sqrt(side_by_side(
            [measured[task, b, pl.ds(odd, frame // 2, stride=2), :] for b in range(measured.shape[1])]))
        high = root.astype(BF16)
        low = (root - high.astype(F32)).astype(BF16)
        amplitude[odd] = dot(high, order) + dot(low, order)


def window(band, lead, row, col, height, across):
    return taken_from(
        [band[lead + (col // LANES + b, pl.ds(row, height), slice(None))] for b in range(across + 1)],
        lax.rem(col, LANES),
    )


def add_window(total, lead, parts, row, col, frame):
    for b, moved in enumerate(put_into(parts, lax.rem(col, LANES))):
        at = lead + (col // LANES + b, pl.ds(row, frame), slice(None))
        total[at] = total[at] + moved


def kernel_cost(frames, modes, frame):
    return pl.CostEstimate(
        flops=frames * modes * 4 * 4 * frame ** 3, bytes_accessed=16 * 1024 * 1024, transcendentals=0)


def frames_kernel(phases, own, up, parity, tile, edge, middle, frames, probe_in, tables_in, as_upper, as_lower, total_out, *rest):
    packed_outs = rest[:phases]
    (band, total, held, packed, piece, measured, probe, tables, patch, amplitude, waves, halfway, product, field, work,
     sems, shot_sems, held_sems, chunk_sems) = rest[phases:]
    cap, frame, _ = frames.shape
    extent = tile.shape[-1]
    across = frame // LANES
    own_blocks = extent // LANES
    half = frame // 2
    own_rows = pl.ds(frame, extent)

    first = start_all(
        [(tile.at[:, :, lanes_of(b)], band.at[:, b, own_rows]) for b in range(own_blocks)]
        + [(source.at[:, pl.ds(at, height), lanes_of(b)], band.at[:, own_blocks + b, pl.ds(frame + target, height)])
           for source, at, height, target in (
               (edge, 0, KEEP, 0), (middle, 0, extent - frame, KEEP), (edge, KEEP, frame - KEEP, KEEP + extent - frame))
           for b in range(across)]
        + [(probe_in, probe), (tables_in, tables)], sems)

    def mine(slot):
        return jnp.logical_and(slot < own[COUNT], own[FAR + slot] == 0)

    def borrowed(slot):
        return up[FAR + slot] > 0

    def shot_copies(slot, task, lent):
        if not lent:
            return [pltpu.make_async_copy(frames.at[slot, :, lanes_of(b)], measured.at[task, b], shot_sems.at[task, b])
                    for b in range(across)]
        at = pl.ds(pl.multiple_of(up[SHOT + slot], ROW_ALIGN), half)
        return [
            pltpu.make_async_copy(as_lower.at[at, lanes_of(part * across + b)],
                                  measured.at[task, b, pl.ds(part * half, half)], shot_sems.at[task, part * across + b])
            for part in range(2) for b in range(across)
        ]

    def held_copies(slot, task, lent):
        source, table = (as_lower, up) if lent else (as_upper, own)
        at = pl.ds(pl.multiple_of(table[PLACE + slot], ROW_ALIGN), frame)
        return [
            pltpu.make_async_copy(source.at[at, lanes_of(b)], held.at[task, b, pl.ds(frame, frame)], held_sems.at[task, b])
            for b in range(2 * across)
        ]

    def for_tasks(wait):
        for slot in range(cap):
            def run(copies):
                for copy in copies:
                    if wait:
                        copy.wait()
                    else:
                        copy.start()

            @pl.when(mine(slot))
            def _():
                run(shot_copies(slot, slot, False))

            @pl.when(own[NEAR + slot] > 0)
            def _():
                run(held_copies(slot, slot, False))

            @pl.when(borrowed(slot))
            def _():
                run(shot_copies(slot, cap + slot, True))
                run(held_copies(slot, cap + slot, True))

    for_tasks(False)
    for slot in range(cap):
        near = own[NEAR + slot]
        for field_at, value in (
            (ACTIVE, mine(slot).astype(jnp.int32)), (AT_ROW, own[ROW + slot] + frame), (AT_COL, own[COL + slot]),
            (LO, frame - near), (HI, frame), (START, near), (PIECE, own[PLACE + slot]), (SHIFT, frame - near), (ROLE, 0),
        ):
            work[slot, field_at] = value
        for field_at, value in (
            (ACTIVE, borrowed(slot).astype(jnp.int32)), (AT_ROW, up[ROW + slot] + frame - extent), (AT_COL, up[COL + slot]),
            (LO, 0), (HI, up[FAR + slot]), (START, frame), (PIECE, up[PLACE + slot]), (SHIFT, 0), (ROLE, 1),
        ):
            work[cap + slot, field_at] = value
    total[...] = jnp.zeros_like(total)
    wait_all(first)
    for_tasks(True)
    row_index = lax.broadcasted_iota(jnp.int32, (STEP, LANES), 0)

    def one(task, carry):
        @pl.when(work[task, ACTIVE] > 0)
        def _():
            row, col, start = work[task, AT_ROW], work[task, AT_COL], work[task, START]
            lo, hi = work[task, LO], work[task, HI]
            for at in range(0, frame, STEP):
                theirs = jnp.logical_and(row_index >= lo - at, row_index < hi - at)
                for plane in range(2):
                    near = window(band, (plane,), row + at, col, STEP, across)
                    other = [held[task, plane * across + b, pl.ds(start + at, STEP), :] for b in range(across)]
                    patch[plane, pl.ds(at, STEP)] = side_by_side([jnp.where(theirs, b, a) for a, b in zip(near, other)])
            ordered_amplitude(measured, task, tables[8], amplitude)
            frame_step(patch, amplitude, probe, tables, waves, halfway, product, field, piece)
            for at in range(0, frame, STEP):
                for plane in range(2):
                    parts = [piece[plane * across + b, pl.ds(at, STEP), :] for b in range(across)]
                    add_window(total, (plane,), parts, row + at, col, STEP)

            @pl.when(lo < hi)
            def _():
                target = pl.ds(pl.multiple_of(work[task, PIECE], ROW_ALIGN), frame)
                source = pl.ds(work[task, SHIFT], frame)
                for b in range(2 * across):
                    packed[work[task, ROLE], target, lanes_of(b)] = piece[b, source, :]

        return carry

    lax.fori_loop(0, 2 * cap, one, 0)
    end = start_all([(total.at[:, :, own_rows], total_out)], sems)
    for phase in range(phases):
        upper = parity[0] == phase
        role = jnp.where(upper, 0, 1)
        copy_out_rows(jnp.where(upper, own[KEPT], up[LENT]), packed.at[role], packed_outs[phase], chunk_sems)
    wait_all(end)


def frames_gradient(phases, own, up, parity, tile, edge, middle, frames, probe, tables, as_upper, as_lower):
    cap, frame, _ = frames.shape
    extent = tile.shape[-1]
    modes = probe.shape[0]
    tall = extent + 2 * frame
    blocks = (extent + frame) // LANES
    across = frame // LANES
    rows = as_upper.shape[0]
    kept_rows = cap * KEEP
    return pl.pallas_call(
        lambda *refs: frames_kernel(phases, *refs),
        out_shape=(jax.ShapeDtypeStruct((2, blocks, extent, LANES), F32),)
        + (jax.ShapeDtypeStruct(as_upper.shape, F32),) * phases,
        in_specs=[smem_spec()] * 3 + [hbm_spec()] * 8,
        out_specs=(hbm_spec(),) * (1 + phases),
        scratch_shapes=[
            pltpu.VMEM((2, blocks, tall, LANES), F32),
            pltpu.VMEM((2, blocks, tall, LANES), F32),
            pltpu.VMEM((2 * cap, 2 * across, 2 * frame, LANES), F32),
            pltpu.VMEM((2, kept_rows + frame, 2 * frame), F32),
            pltpu.VMEM((2 * across, 2 * frame, LANES), F32),
            pltpu.VMEM((2 * cap, across, frame, LANES), F32),
            pltpu.VMEM(probe.shape, F32),
            pltpu.VMEM(tables.shape, BF16),
            pltpu.VMEM((2, frame, frame), F32),
            pltpu.VMEM((2, frame // 2, frame), F32),
            pltpu.VMEM((2, modes, frame, frame), BF16),
            pltpu.VMEM((2, modes, frame, frame), BF16),
            pltpu.VMEM((2, modes, frame, frame), F32),
            pltpu.VMEM((2, modes, frame, frame), F32),
            pltpu.SMEM((2 * cap, 16), jnp.int32),
            pltpu.SemaphoreType.DMA((blocks + 2 * across + 2,)),
            pltpu.SemaphoreType.DMA((2 * cap, 2 * across)),
            pltpu.SemaphoreType.DMA((2 * cap, 2 * across)),
            pltpu.SemaphoreType.DMA((rows // CHUNK,)),
        ],
        compiler_params=params(55),
        cost_estimate=kernel_cost(cap, modes, frame),
        name="frames_gradient",
    )(own, up, parity, tile, edge, middle, frames, probe, tables, as_upper, as_lower)


def light_kernel(own, up, beside, probe, light_out, light, sem):
    modes, _, frame, _ = probe.shape
    own_blocks, extent, _ = light_out.shape
    across = frame // LANES
    inside = (pl.ds(across, own_blocks), pl.ds(frame, extent), slice(None))
    light[inside] = jnp.zeros((own_blocks, extent, LANES), F32)
    power = jnp.zeros((frame, frame), F32)
    for mode in range(modes):
        power += probe[mode, 0] * probe[mode, 0] + probe[mode, 1] * probe[mode, 1]
    power = halves(power)
    for table, lead, down, right in ((own, 0, 0, 0), (beside, 0, 0, 1), (up, 0, 1, 0), (beside, TABLE, 1, 1)):

        def lit(slot, carry, table=table, lead=lead, down=down, right=right):
            row = table[lead + ROW + slot] + frame - down * extent
            col = table[lead + COL + slot] + frame - right * extent

            @pl.when((row > 0) & (col > 0))
            def _():
                add_window(light, (), power, row, col, frame)

            return carry

        lax.fori_loop(0, table[lead + COUNT], lit, 0)
    copy = pltpu.make_async_copy(light.at[inside[0], inside[1]], light_out, sem)
    copy.start()
    copy.wait()


def light_plane(own, up, beside, probe, extent):
    frame = probe.shape[-1]
    wide = extent + 2 * frame
    return pl.pallas_call(
        light_kernel,
        out_shape=jax.ShapeDtypeStruct((extent // LANES, extent, LANES), F32),
        in_specs=[smem_spec()] * 3 + [vmem_spec()],
        out_specs=any_spec(),
        scratch_shapes=[pltpu.VMEM((wide // LANES, wide, LANES), F32), pltpu.SemaphoreType.DMA],
        compiler_params=params(9),
        cost_estimate=pl.CostEstimate(flops=0, bytes_accessed=12 * 1024 * 1024, transcendentals=0),
        name="light_plane",
    )(own, up, beside, probe)


def join_kernel(frame, own, up, as_upper, as_lower, total_in, total_out, right_out, band, held, sems):
    blocks = band.shape[1]
    extent = total_in.shape[2]
    across = frame // LANES
    rows = held.shape[1] - frame
    cap = rows // KEEP
    own_rows = pl.ds(0, extent)
    right = pl.ds(blocks - across, across)
    anything = jnp.logical_or(own[LENT] > 0, up[KEPT] > 0)

    @pl.when(anything)
    def _():
        whole = start_all([(total_in, band.at[:, :, own_rows])], sems)
        row_index = lax.broadcasted_iota(jnp.int32, (frame, LANES), 0)
        for number, (table, needed, field, pieces) in enumerate(
                ((own, own[LENT], FAR, as_upper), (up, up[KEPT], NEAR, as_lower))):

            @pl.when(needed > 0)
            def _(table=table, needed=needed, field=field, pieces=pieces):
                chunks = (needed + CHUNK - 1) // CHUNK

                def copies(chunk):
                    at = pl.ds(pl.multiple_of(chunk * CHUNK, CHUNK), CHUNK)
                    return [pltpu.make_async_copy(pieces.at[at, lanes_of(b)], held.at[b, at], sems.at[1 + chunk * 2 * across + b])
                            for b in range(2 * across)]

                def begin(chunk, carry):
                    for copy in copies(chunk):
                        copy.start()
                    return carry

                def end(chunk, carry):
                    for copy in copies(chunk):
                        copy.wait()
                    return carry

                lax.fori_loop(0, chunks, begin, 0)
                lax.fori_loop(0, chunks, end, 0)

            if not number:
                wait_all(whole)

            def one(slot, carry, table=table, field=field):
                col, height = table[COL + slot], table[field + slot]

                @pl.when(height > 0)
                def _():
                    row = table[ROW + slot] if field == FAR else 0
                    at = pl.ds(pl.multiple_of(table[PLACE + slot], ROW_ALIGN), frame)
                    for plane in range(2):
                        got = [jnp.where(row_index < height, held[plane * across + b, at, :], 0.0) for b in range(across)]
                        add_window(band, (plane,), got, row, col, frame)

                return carry

            lax.fori_loop(0, cap, one, 0)

        wait_all(start_all([(band.at[:, right, own_rows], right_out), (band.at[:, :, own_rows], total_out)], sems))

    @pl.when(jnp.logical_not(anything))
    def _():
        wait_all(start_all([(total_in.at[:, right], band.at[:, right, own_rows])], sems))
        wait_all(start_all([(band.at[:, right, own_rows], right_out)], sems))


def join_pieces(own, up, as_upper, as_lower, total, cap):
    frame = as_upper.shape[1] // 2
    _, blocks, extent, _ = total.shape
    across = frame // LANES
    rows = cap * KEEP
    return pl.pallas_call(
        lambda *refs: join_kernel(frame, *refs),
        out_shape=(jax.ShapeDtypeStruct(total.shape, F32), jax.ShapeDtypeStruct((2, across, extent, LANES), F32)),
        in_specs=[smem_spec(), smem_spec(), hbm_spec(), hbm_spec(), hbm_spec()],
        out_specs=(hbm_spec(), any_spec()),
        input_output_aliases={4: 0},
        scratch_shapes=[
            pltpu.VMEM((2, blocks, extent + frame, LANES), F32),
            pltpu.VMEM((2 * across, rows + frame, LANES), F32),
            pltpu.SemaphoreType.DMA((1 + rows // CHUNK * 2 * across,)),
        ],
        compiler_params=params(56),
        name="join_pieces",
    )(own, up, as_upper, as_lower, total)


def final_kernel(tile, total, light, left, out):
    across = left.shape[1]
    for b in range(total.shape[1]):
        below = 1.0 / (light[b] + 1.0)
        for plane in range(2):
            grad = total[plane, b]
            if b < across:
                grad = grad + left[plane, b]
            out[plane, :, lanes_of(b)] = tile[plane, :, lanes_of(b)] - grad * below


def final_update(tile, total, light, left):
    extent = tile.shape[-1]
    blocks = extent // LANES
    across = left.shape[1]
    tall = 128
    return pl.pallas_call(
        final_kernel,
        grid=(extent // tall,),
        out_shape=jax.ShapeDtypeStruct(tile.shape, F32),
        in_specs=[
            pl.BlockSpec((2, tall, extent), lambda i: (0, i, 0)),
            pl.BlockSpec((2, blocks, tall, LANES), lambda i: (0, 0, i, 0)),
            pl.BlockSpec((blocks, tall, LANES), lambda i: (0, i, 0)),
            pl.BlockSpec((2, across, tall, LANES), lambda i: (0, 0, i, 0)),
        ],
        out_specs=pl.BlockSpec((2, tall, extent), lambda i: (0, i, 0)),
        compiler_params=params(8),
        name="final_update",
    )(tile, total, light, left)


def body(object_tiles, probe, positions, frames, counts):
    tile = object_tiles[0]
    extent = tile.shape[-1]
    frame = frames.shape[-1]
    cap = frames.shape[1]
    peers = lax.axis_size("scan")
    tile_row = lax.axis_index("scan") // TCOLS
    phases = min(2, peers // TCOLS - 1)
    tables = dft_tables(frame)
    parity = (tile_row % 2).reshape(1)
    even = tile_row % 2 == 0

    own, edge, middle = prepare(positions, counts, tile, frame)
    up = shifted(own, "scan", TCOLS)
    edge = shifted(edge, "scan", -1)
    middle = shifted(middle, "scan", -1)
    beside = shifted(jnp.concatenate([own, up]), "scan", 1)

    def exchange(phase, packed, choice):
        uppers = [k for k in range(peers - TCOLS) if k // TCOLS % 2 == phase]
        pairs = [(k, k + TCOLS) for k in uppers] + [(k + TCOLS, k) for k in uppers]

        def sender(size):
            def run(data):
                return lax.dynamic_update_slice(data, lax.ppermute(data[:size], "scan", pairs), (0, 0))
            return run

        branches = [lambda data: data] + [sender(size) for size in SIZES]
        return lax.switch(choice.reshape(()), branches, packed)

    def by_role(arrays):
        if len(arrays) == 1:
            return arrays[0], arrays[0]
        return jnp.where(even, arrays[0], arrays[1]), jnp.where(even, arrays[1], arrays[0])

    cuts = [cut_pieces(phase, own, up, parity, tile, edge, frames[0]) for phase in range(phases)]
    received = by_role([exchange(phase, cut[0], cut[1]) for phase, cut in enumerate(cuts)])
    received, beside = lax.optimization_barrier((received, beside))
    total, *packed = frames_gradient(phases, own, up, parity, tile, edge, middle, frames[0], probe, tables, *received)
    returned = by_role([exchange(phase, packed[phase], cut[2]) for phase, cut in enumerate(cuts)])
    total, right = join_pieces(own, up, *returned, total, cap)
    left = shifted(right, "scan", 1)
    total, beside = lax.optimization_barrier((total, beside))
    light = light_plane(own, up, beside, probe, extent)
    return final_update(tile, total, light, left)[None]


def solution(mesh):
    return jax.shard_map(
        body,
        mesh=mesh,
        in_specs=(
            P(("grp", "scan"), None, None, None),
            P(),
            P(("grp", "scan"), None, None),
            P(("grp", "scan"), None, None, None),
            P(("grp", "scan")),
        ),
        out_specs=P(("grp", "scan"), None, None, None),
        check_vma=False,
    )
```

```python
import math

import jax
import jax.numpy as jnp
import numpy as np
from jax import lax
from jax.experimental import pallas as pl
from jax.experimental.pallas import tpu as pltpu
from jax.sharding import PartitionSpec as P

TCOLS = 8
LANES = 128
ROW_ALIGN = 8
CHUNK = 64
STEP = 32
TILE_ROWS = 16
SIZES = (32, 64, 96, 128, 160, 192, 224, 256, 320, 384, 448, 512, 640, 768, 960, 1344)
MIB = 1024 * 1024
F32 = jnp.float32
BF16 = jnp.bfloat16

KEEP = 160
ROW, COL, NEAR, FAR, PLACE, SHOT = 0, 8, 16, 24, 32, 40
COUNT, KEPT, LENT, FORTH, BACK = 48, 49, 50, 51, 52
TABLE = 64

ACTIVE, AT_ROW, AT_COL, LO, HI, START, PIECE, SHIFT, ROLE = range(9)


def dft_tables(frame):
    near = np.arange(frame // 2, dtype=np.int64)
    blocks = []
    for odd in range(2):
        phase = (near[:, None] * (2 * near[None, :] + odd) % frame).astype(np.float64) * (2.0 * math.pi / frame)
        c, s = np.cos(phase), np.sin(phase)
        ahead = np.block([[c, -s], [s, c]])
        back = np.block([[c.T, s.T], [-s.T, c.T]])
        blocks.append((ahead, ahead.T, back, back.T))
    order = np.zeros((frame, frame))
    order[2 * near, near] = 1.0
    order[2 * near + 1, near + frame // 2] = 1.0
    tables = [blocks[odd][kind] for kind in range(4) for odd in range(2)] + [order]
    return jnp.asarray(np.stack(tables), F32).astype(BF16)


def shifted(array, axis, by):
    peers = lax.axis_size(axis)
    pairs = [(i, i + by) for i in range(peers) if 0 <= i + by < peers]
    return lax.ppermute(array, axis, pairs)


def any_spec():
    return pl.BlockSpec(memory_space=pl.ANY)


def hbm_spec():
    return pl.BlockSpec(memory_space=pltpu.HBM)


def smem_spec():
    return pl.BlockSpec(memory_space=pltpu.SMEM)


def vmem_spec():
    return pl.BlockSpec(memory_space=pltpu.VMEM)


def params(mebibytes):
    return pltpu.CompilerParams(vmem_limit_bytes=mebibytes * MIB)


def taken_from(blocks, by):
    lane = lax.broadcasted_iota(jnp.int32, blocks[0].shape, 1)
    rolled = [pltpu.roll(block, lax.rem(LANES - by, LANES), axis=1) for block in blocks]
    return [jnp.where(lane < LANES - by, one, two) for one, two in zip(rolled[:-1], rolled[1:])]


def put_into(blocks, by):
    lane = lax.broadcasted_iota(jnp.int32, blocks[0].shape, 1)
    rolled = [pltpu.roll(block, by, axis=1) for block in blocks]
    none = jnp.zeros_like(blocks[0])
    return [jnp.where(lane >= by, one, two) for one, two in zip(rolled + [none], [none] + rolled)]


def start_all(pairs, sems, first=0):
    copies = [pltpu.make_async_copy(source, target, sems.at[first + at]) for at, (source, target) in enumerate(pairs)]
    for copy in copies:
        copy.start()
    return copies


def wait_all(copies):
    for copy in copies:
        copy.wait()


def lanes_of(block):
    return pl.ds(block * LANES, LANES)


def side_by_side(parts):
    return jnp.concatenate(parts, axis=1)


def halves(array):
    return [array[:, :LANES], array[:, LANES:]]


def copy_out_rows(needed, packed, out, sems):
    chunks = (needed + CHUNK - 1) // CHUNK

    def copy(chunk):
        at = pl.ds(pl.multiple_of(chunk * CHUNK, CHUNK), CHUNK)
        return pltpu.make_async_copy(packed.at[at], out.at[at], sems.at[chunk])

    def begin(chunk, carry):
        copy(chunk).start()
        return carry

    def end(chunk, carry):
        copy(chunk).wait()
        return carry

    lax.fori_loop(0, chunks, begin, 0)
    lax.fori_loop(0, chunks, end, 0)


def up_to(value, step):
    return (value + step - 1) // step * step


def size_choice(needed):
    choice = jnp.where(needed > 0, 1, 0)
    for size in SIZES:
        choice = choice + jnp.where(needed > size, 1, 0)
    return choice


def prep_kernel(positions, counts, tile, table, edge, middle, sems):
    cap = positions.shape[2]
    extent = tile.shape[-1]
    frame = edge.shape[-1]
    count = counts[0]
    lanes = pl.ds(0, frame)
    copies = start_all([
        (tile.at[:, pl.ds(0, KEEP), lanes], edge.at[:, pl.ds(0, KEEP)]),
        (tile.at[:, pl.ds(KEEP + extent - frame, frame - KEEP), lanes], edge.at[:, pl.ds(KEEP, frame - KEEP)]),
        (tile.at[:, pl.ds(KEEP, extent - frame), lanes], middle),
    ], sems)
    kept, lent, shots = jnp.int32(0), jnp.int32(0), jnp.int32(0)
    for at in range(TABLE):
        table[at] = 0
    for slot in range(cap):
        row = lax.rem(positions[0, 0, slot], extent)
        col = lax.rem(positions[0, 1, slot], extent)
        below = jnp.where(slot < count, jnp.maximum(row + (frame - extent), 0), 0)
        stays = below <= KEEP
        near = jnp.where(stays, below, 0)
        far = jnp.where(stays, 0, frame - below)
        table[ROW + slot] = row
        table[COL + slot] = col
        table[NEAR + slot] = near
        table[FAR + slot] = far
        table[PLACE + slot] = jnp.where(stays, kept, lent)
        table[SHOT + slot] = shots
        kept = kept + up_to(near, ROW_ALIGN)
        lent = lent + up_to(far, ROW_ALIGN)
        shots = shots + jnp.where(stays, 0, frame // 2)
    for slot in range(cap):
        table[SHOT + slot] = table[SHOT + slot] + lent
    table[COUNT] = count
    table[KEPT] = kept
    table[LENT] = lent
    table[FORTH] = jnp.maximum(kept, lent + shots)
    table[BACK] = jnp.maximum(kept, lent)
    wait_all(copies)


def prepare(positions, counts, tile, frame):
    extent = tile.shape[-1]
    return pl.pallas_call(
        prep_kernel,
        out_shape=(
            jax.ShapeDtypeStruct((TABLE,), jnp.int32),
            jax.ShapeDtypeStruct((2, frame, frame), F32),
            jax.ShapeDtypeStruct((2, extent - frame, frame), F32),
        ),
        in_specs=[smem_spec(), smem_spec(), hbm_spec()],
        out_specs=(smem_spec(), vmem_spec(), vmem_spec()),
        scratch_shapes=[pltpu.SemaphoreType.DMA((3,))],
        compiler_params=params(62),
        name="prepare",
    )(jnp.swapaxes(positions, 1, 2), counts, tile)


def cut_kernel(phase, own, up, parity, tile, edge, frames, out, forth, back, band, packed, sems, chunk_sems):
    cap, frame, _ = frames.shape
    extent = tile.shape[-1]
    across = frame // LANES
    own_blocks = extent // LANES
    upper = parity[0] == phase
    forth[0] = size_choice(jnp.where(upper, own[FORTH], up[FORTH]))
    back[0] = size_choice(jnp.where(upper, own[BACK], up[BACK]))
    lends = jnp.logical_and(upper, own[LENT] > 0)
    gives = jnp.logical_and(jnp.logical_not(upper), up[KEPT] > 0)

    def cut(col, row, place):
        at = pl.ds(pl.multiple_of(place, ROW_ALIGN), frame)
        for plane in range(2):
            packed[at, pl.ds(plane * frame, frame)] = side_by_side(window(band, (plane,), row, col, frame, across))

    @pl.when(jnp.logical_or(lends, gives))
    def _():
        base = jnp.where(upper, extent - frame, 0)
        rows = pl.ds(pl.multiple_of(base, ROW_ALIGN), frame)
        wait_all(start_all(
            [(tile.at[:, rows, lanes_of(b)], band.at[:, b, pl.ds(0, frame)]) for b in range(own_blocks)]
            + [(edge.at[:, :, lanes_of(b)], band.at[:, own_blocks + b, pl.ds(0, frame)]) for b in range(across)], sems))

        def one(slot, carry):
            @pl.when(jnp.logical_and(upper, own[FAR + slot] > 0))
            def _():
                cut(own[COL + slot], own[ROW + slot] - (extent - frame), own[PLACE + slot])

            @pl.when(jnp.logical_and(gives, up[NEAR + slot] > 0))
            def _():
                cut(up[COL + slot], 0, up[PLACE + slot])

            return carry

        lax.fori_loop(0, cap, one, 0)

        def shots(slot):
            at = pl.ds(pl.multiple_of(own[SHOT + slot], ROW_ALIGN), frame // 2)
            return [pltpu.make_async_copy(frames.at[slot, pl.ds(part * frame // 2, frame // 2)],
                                          packed.at[at, pl.ds(part * frame, frame)], sems.at[2 * slot + part])
                    for part in range(2)]

        for wait in range(2):
            for slot in range(cap):
                @pl.when(jnp.logical_and(lends, own[FAR + slot] > 0))
                def _():
                    for copy in shots(slot):
                        if wait:
                            copy.wait()
                        else:
                            copy.start()

        copy_out_rows(jnp.where(upper, own[FORTH], up[KEPT]), packed, out, chunk_sems)


def cut_pieces(phase, own, up, parity, tile, edge, frames):
    cap, frame, _ = frames.shape
    extent = tile.shape[-1]
    blocks = (extent + frame) // LANES
    rows = SIZES[-1]
    return pl.pallas_call(
        lambda *refs: cut_kernel(phase, *refs),
        out_shape=(
            jax.ShapeDtypeStruct((rows, 2 * frame), F32),
            jax.ShapeDtypeStruct((1,), jnp.int32),
            jax.ShapeDtypeStruct((1,), jnp.int32),
        ),
        in_specs=[smem_spec(), smem_spec(), smem_spec(), hbm_spec(), hbm_spec(), hbm_spec()],
        out_specs=(hbm_spec(), smem_spec(), smem_spec()),
        scratch_shapes=[
            pltpu.VMEM((2, blocks, 2 * frame, LANES), F32),
            pltpu.VMEM((rows + frame, 2 * frame), F32),
            pltpu.SemaphoreType.DMA((max(blocks, 2 * cap),)),
            pltpu.SemaphoreType.DMA((rows // CHUNK,)),
        ],
        compiler_params=params(60),
        name="cut_pieces",
    )(own, up, parity, tile, edge, frames)


def dot(one, two):
    return jnp.dot(one, two, preferred_element_type=F32)


def stacked(parts):
    return jnp.concatenate(parts, axis=0)


def lane_parts(array):
    half = array.shape[1] // 2
    return array[:, :half], array[:, half:]


def wave_stage(mode, probe, patch, waves):
    frame = probe.shape[2]
    for at in range(0, frame, STEP):
        rows = pl.ds(at, STEP)
        probe_real, probe_imag = probe[mode, 0, rows], probe[mode, 1, rows]
        patch_real, patch_imag = patch[0, rows], patch[1, rows]
        parts = [lane_parts(part) for part in (
            probe_real * patch_real - probe_imag * patch_imag, probe_real * patch_imag + probe_imag * patch_real)]
        waves[0, mode, rows] = side_by_side([near + far for near, far in parts]).astype(BF16)
        waves[1, mode, rows] = side_by_side([near - far for near, far in parts]).astype(BF16)


def rows_dot(mode, source, tables, first, product):
    for odd in range(2):
        product[odd, mode] = dot(source[odd, mode], tables[first + odd])


def columns_dot(mode, tables, first, source, product):
    for odd in range(2):
        product[odd, mode] = dot(tables[first + odd], source[odd, mode])


def half_stage(mode, product, halfway):
    half = product.shape[2] // 2
    for at in range(0, half, TILE_ROWS):
        near, far = pl.ds(at, TILE_ROWS), pl.ds(half + at, TILE_ROWS)
        upper = [product[odd, mode, near] for odd in range(2)]
        lower = [product[odd, mode, far] for odd in range(2)]
        for odd in range(2):
            mixed = [a + b if not odd else a - b for a, b in zip(upper, lower)]
            real, imag = zip(*[lane_parts(part) for part in mixed])
            halfway[odd, mode, near] = side_by_side(real).astype(BF16)
            halfway[odd, mode, far] = side_by_side(imag).astype(BF16)


def residual_stage(modes, frame, field, amplitude, waves):
    half = frame // 2
    for odd in range(2):
        for at in range(0, half, TILE_ROWS):
            near, far = pl.ds(at, TILE_ROWS), pl.ds(half + at, TILE_ROWS)
            real = [field[odd, mode, near] for mode in range(modes)]
            imag = [field[odd, mode, far] for mode in range(modes)]
            lit = sum(a * a + b * b for a, b in zip(real, imag))
            factor = 1.0 / frame - amplitude[odd, near] * lax.rsqrt(jnp.maximum(lit, float(frame * frame)))
            target = pl.ds(odd * half + at, TILE_ROWS)
            for mode in range(modes):
                parts = [lane_parts(real[mode] * factor), lane_parts(imag[mode] * factor)]
                for column in range(2):
                    waves[column, mode, target] = side_by_side([part[column] for part in parts]).astype(BF16)


def back_stage(mode, product, halfway):
    half = product.shape[2] // 2
    for odd in range(2):
        for at in range(0, half, TILE_ROWS):
            rows = pl.ds(odd * half + at, TILE_ROWS)
            even_part, odd_part = product[0, mode, rows], product[1, mode, rows]
            near, far = lane_parts(even_part + odd_part), lane_parts(even_part - odd_part)
            halfway[odd, mode, pl.ds(at, TILE_ROWS)] = side_by_side([near[0], far[0]]).astype(BF16)
            halfway[odd, mode, pl.ds(half + at, TILE_ROWS)] = side_by_side([near[1], far[1]]).astype(BF16)


def gradient_stage(some_modes, first, product, probe, piece):
    frame = probe.shape[2]
    half = frame // 2
    across = frame // LANES
    for at in range(0, half, TILE_ROWS):
        rows = [pl.ds(at, TILE_ROWS), pl.ds(half + at, TILE_ROWS)]
        grads = [[0.0, 0.0], [0.0, 0.0]]
        for mode in some_modes:
            mixed = [(product[0, mode, part], product[1, mode, part]) for part in rows]
            for side in range(2):
                back_real, back_imag = [a + b if not side else a - b for a, b in mixed]
                probe_real, probe_imag = probe[mode, 0, rows[side]], probe[mode, 1, rows[side]]
                grads[side][0] += probe_real * back_real + probe_imag * back_imag
                grads[side][1] += probe_real * back_imag - probe_imag * back_real
        for side in range(2):
            for plane in range(2):
                grad = grads[side][plane] * (1.0 / frame)
                for b in range(across):
                    where = (plane * across + b, rows[side], slice(None))
                    part = grad[:, b * LANES:(b + 1) * LANES]
                    piece[where] = part if first else piece[where] + part


def frame_step(patch, amplitude, probe, tables, waves, halfway, product, field, piece):
    modes, _, frame, _ = probe.shape
    for step in range(modes + 1):
        if step < modes:
            wave_stage(step, probe, patch, waves)
            rows_dot(step, waves, tables, 0, product)
        if step:
            half_stage(step - 1, product, halfway)
            columns_dot(step - 1, tables, 2, halfway, field)
    residual_stage(modes, frame, field, amplitude, waves)
    for step in range(modes + 1):
        if step < modes:
            rows_dot(step, waves, tables, 4, product)
        if step:
            back_stage(step - 1, product, halfway)
            columns_dot(step - 1, tables, 6, halfway, field)
        if step and step % 2 == 0:
            gradient_stage((step - 2, step - 1), step == 2, field, probe, piece)


def ordered_amplitude(measured, task, order, amplitude):
    frame = measured.shape[2]
    for odd in range(2):
        root = jnp.sqrt(side_by_side(
            [measured[task, b, pl.ds(odd, frame // 2, stride=2), :] for b in range(measured.shape[1])]))
        high = root.astype(BF16)
        low = (root - high.astype(F32)).astype(BF16)
        amplitude[odd] = dot(high, order) + dot(low, order)


def window(band, lead, row, col, height, across):
    return taken_from(
        [band[lead + (col // LANES + b, pl.ds(row, height), slice(None))] for b in range(across + 1)],
        lax.rem(col, LANES),
    )


def add_window(total, lead, parts, row, col, frame):
    for b, moved in enumerate(put_into(parts, lax.rem(col, LANES))):
        at = lead + (col // LANES + b, pl.ds(row, frame), slice(None))
        total[at] = total[at] + moved


def kernel_cost(frames, modes, frame):
    return pl.CostEstimate(
        flops=frames * modes * 4 * 4 * frame ** 3, bytes_accessed=16 * 1024 * 1024, transcendentals=0)


def frames_kernel(phases, own, up, parity, tile, edge, middle, frames, probe_in, tables_in, as_upper, as_lower, total_out, *rest):
    packed_outs = rest[:phases]
    (band, total, held, packed, piece, measured, probe, tables, patch, amplitude, waves, halfway, product, field, work,
     sems, shot_sems, held_sems, chunk_sems) = rest[phases:]
    cap, frame, _ = frames.shape
    extent = tile.shape[-1]
    across = frame // LANES
    own_blocks = extent // LANES
    half = frame // 2
    own_rows = pl.ds(frame, extent)

    first = start_all(
        [(tile.at[:, :, lanes_of(b)], band.at[:, b, own_rows]) for b in range(own_blocks)]
        + [(source.at[:, pl.ds(at, height), lanes_of(b)], band.at[:, own_blocks + b, pl.ds(frame + target, height)])
           for source, at, height, target in (
               (edge, 0, KEEP, 0), (middle, 0, extent - frame, KEEP), (edge, KEEP, frame - KEEP, KEEP + extent - frame))
           for b in range(across)]
        + [(probe_in, probe), (tables_in, tables)], sems)

    def mine(slot):
        return jnp.logical_and(slot < own[COUNT], own[FAR + slot] == 0)

    def borrowed(slot):
        return up[FAR + slot] > 0

    def shot_copies(slot, task, lent):
        if not lent:
            return [pltpu.make_async_copy(frames.at[slot, :, lanes_of(b)], measured.at[task, b], shot_sems.at[task, b])
                    for b in range(across)]
        at = pl.ds(pl.multiple_of(up[SHOT + slot], ROW_ALIGN), half)
        return [
            pltpu.make_async_copy(as_lower.at[at, lanes_of(part * across + b)],
                                  measured.at[task, b, pl.ds(part * half, half)], shot_sems.at[task, part * across + b])
            for part in range(2) for b in range(across)
        ]

    def held_copies(slot, task, lent):
        source, table = (as_lower, up) if lent else (as_upper, own)
        at = pl.ds(pl.multiple_of(table[PLACE + slot], ROW_ALIGN), frame)
        return [
            pltpu.make_async_copy(source.at[at, lanes_of(b)], held.at[task, b, pl.ds(frame, frame)], held_sems.at[task, b])
            for b in range(2 * across)
        ]

    def for_tasks(wait):
        for slot in range(cap):
            def run(copies):
                for copy in copies:
                    if wait:
                        copy.wait()
                    else:
                        copy.start()

            @pl.when(mine(slot))
            def _():
                run(shot_copies(slot, slot, False))

            @pl.when(own[NEAR + slot] > 0)
            def _():
                run(held_copies(slot, slot, False))

            @pl.when(borrowed(slot))
            def _():
                run(shot_copies(slot, cap + slot, True))
                run(held_copies(slot, cap + slot, True))

    for_tasks(False)
    for slot in range(cap):
        near = own[NEAR + slot]
        for field_at, value in (
            (ACTIVE, mine(slot).astype(jnp.int32)), (AT_ROW, own[ROW + slot] + frame), (AT_COL, own[COL + slot]),
            (LO, frame - near), (HI, frame), (START, near), (PIECE, own[PLACE + slot]), (SHIFT, frame - near), (ROLE, 0),
        ):
            work[slot, field_at] = value
        for field_at, value in (
            (ACTIVE, borrowed(slot).astype(jnp.int32)), (AT_ROW, up[ROW + slot] + frame - extent), (AT_COL, up[COL + slot]),
            (LO, 0), (HI, up[FAR + slot]), (START, frame), (PIECE, up[PLACE + slot]), (SHIFT, 0), (ROLE, 1),
        ):
            work[cap + slot, field_at] = value
    total[...] = jnp.zeros_like(total)
    wait_all(first)
    for_tasks(True)
    row_index = lax.broadcasted_iota(jnp.int32, (STEP, LANES), 0)

    def one(task, carry):
        @pl.when(work[task, ACTIVE] > 0)
        def _():
            row, col, start = work[task, AT_ROW], work[task, AT_COL], work[task, START]
            lo, hi = work[task, LO], work[task, HI]
            for at in range(0, frame, STEP):
                theirs = jnp.logical_and(row_index >= lo - at, row_index < hi - at)
                for plane in range(2):
                    near = window(band, (plane,), row + at, col, STEP, across)
                    other = [held[task, plane * across + b, pl.ds(start + at, STEP), :] for b in range(across)]
                    patch[plane, pl.ds(at, STEP)] = side_by_side([jnp.where(theirs, b, a) for a, b in zip(near, other)])
            ordered_amplitude(measured, task, tables[8], amplitude)
            frame_step(patch, amplitude, probe, tables, waves, halfway, product, field, piece)
            for at in range(0, frame, STEP):
                for plane in range(2):
                    parts = [piece[plane * across + b, pl.ds(at, STEP), :] for b in range(across)]
                    add_window(total, (plane,), parts, row + at, col, STEP)

            @pl.when(lo < hi)
            def _():
                target = pl.ds(pl.multiple_of(work[task, PIECE], ROW_ALIGN), frame)
                source = pl.ds(work[task, SHIFT], frame)
                for b in range(2 * across):
                    packed[work[task, ROLE], target, lanes_of(b)] = piece[b, source, :]

        return carry

    lax.fori_loop(0, 2 * cap, one, 0)
    end = start_all([(total.at[:, :, own_rows], total_out)], sems)
    for phase in range(phases):
        upper = parity[0] == phase
        role = jnp.where(upper, 0, 1)
        copy_out_rows(jnp.where(upper, own[KEPT], up[LENT]), packed.at[role], packed_outs[phase], chunk_sems)
    wait_all(end)


def frames_gradient(phases, own, up, parity, tile, edge, middle, frames, probe, tables, as_upper, as_lower):
    cap, frame, _ = frames.shape
    extent = tile.shape[-1]
    modes = probe.shape[0]
    tall = extent + 2 * frame
    blocks = (extent + frame) // LANES
    across = frame // LANES
    rows = as_upper.shape[0]
    kept_rows = cap * KEEP
    return pl.pallas_call(
        lambda *refs: frames_kernel(phases, *refs),
        out_shape=(jax.ShapeDtypeStruct((2, blocks, extent, LANES), F32),)
        + (jax.ShapeDtypeStruct(as_upper.shape, F32),) * phases,
        in_specs=[smem_spec()] * 3 + [hbm_spec()] * 8,
        out_specs=(hbm_spec(),) * (1 + phases),
        scratch_shapes=[
            pltpu.VMEM((2, blocks, tall, LANES), F32),
            pltpu.VMEM((2, blocks, tall, LANES), F32),
            pltpu.VMEM((2 * cap, 2 * across, 2 * frame, LANES), F32),
            pltpu.VMEM((2, kept_rows + frame, 2 * frame), F32),
            pltpu.VMEM((2 * across, 2 * frame, LANES), F32),
            pltpu.VMEM((2 * cap, across, frame, LANES), F32),
            pltpu.VMEM(probe.shape, F32),
            pltpu.VMEM(tables.shape, BF16),
            pltpu.VMEM((2, frame, frame), F32),
            pltpu.VMEM((2, frame // 2, frame), F32),
            pltpu.VMEM((2, modes, frame, frame), BF16),
            pltpu.VMEM((2, modes, frame, frame), BF16),
            pltpu.VMEM((2, modes, frame, frame), F32),
            pltpu.VMEM((2, modes, frame, frame), F32),
            pltpu.SMEM((2 * cap, 16), jnp.int32),
            pltpu.SemaphoreType.DMA((blocks + 2 * across + 2,)),
            pltpu.SemaphoreType.DMA((2 * cap, 2 * across)),
            pltpu.SemaphoreType.DMA((2 * cap, 2 * across)),
            pltpu.SemaphoreType.DMA((rows // CHUNK,)),
        ],
        compiler_params=params(55),
        cost_estimate=kernel_cost(cap, modes, frame),
        name="frames_gradient",
    )(own, up, parity, tile, edge, middle, frames, probe, tables, as_upper, as_lower)


def light_kernel(own, up, beside, probe, light_out, light, sem):
    modes, _, frame, _ = probe.shape
    own_blocks, extent, _ = light_out.shape
    across = frame // LANES
    inside = (pl.ds(across, own_blocks), pl.ds(frame, extent), slice(None))
    light[inside] = jnp.zeros((own_blocks, extent, LANES), F32)
    power = jnp.zeros((frame, frame), F32)
    for mode in range(modes):
        power += probe[mode, 0] * probe[mode, 0] + probe[mode, 1] * probe[mode, 1]
    power = halves(power)
    for table, lead, down, right in ((own, 0, 0, 0), (beside, 0, 0, 1), (up, 0, 1, 0), (beside, TABLE, 1, 1)):

        def lit(slot, carry, table=table, lead=lead, down=down, right=right):
            row = table[lead + ROW + slot] + frame - down * extent
            col = table[lead + COL + slot] + frame - right * extent

            @pl.when((row > 0) & (col > 0))
            def _():
                add_window(light, (), power, row, col, frame)

            return carry

        lax.fori_loop(0, table[lead + COUNT], lit, 0)
    copy = pltpu.make_async_copy(light.at[inside[0], inside[1]], light_out, sem)
    copy.start()
    copy.wait()


def light_plane(own, up, beside, probe, extent):
    frame = probe.shape[-1]
    wide = extent + 2 * frame
    return pl.pallas_call(
        light_kernel,
        out_shape=jax.ShapeDtypeStruct((extent // LANES, extent, LANES), F32),
        in_specs=[smem_spec()] * 3 + [vmem_spec()],
        out_specs=any_spec(),
        scratch_shapes=[pltpu.VMEM((wide // LANES, wide, LANES), F32), pltpu.SemaphoreType.DMA],
        compiler_params=params(9),
        cost_estimate=pl.CostEstimate(flops=0, bytes_accessed=4 * MIB, transcendentals=0),
        name="light_plane",
    )(own, up, beside, probe)


def join_kernel(frame, own, up, as_upper, as_lower, total_in, total_out, right_out, top, bottom, between, held, sems):
    blocks = top.shape[1]
    extent = total_in.shape[2]
    across = frame // LANES
    tail = frame - KEEP
    cap = (held.shape[1] - KEEP) // KEEP
    right = pl.ds(blocks - across, across)
    top_rows, bottom_rows = pl.ds(0, KEEP), pl.ds(extent - tail, tail)
    kept_bottom = bottom.at[:, :, pl.ds(0, tail)]
    middle_rows = pl.ds(KEEP, extent - frame)
    loads = start_all([
        (total_in.at[:, :, bottom_rows], kept_bottom),
        (total_in.at[:, :, top_rows], top),
        (total_in.at[:, right, middle_rows], between),
    ], sems)
    row_index = lax.broadcasted_iota(jnp.int32, (KEEP, LANES), 0)

    def add_pieces(table, needed, field, pieces, band, height, base, load):
        chunks = (needed + CHUNK - 1) // CHUNK

        def copies(chunk):
            at = pl.ds(pl.multiple_of(chunk * CHUNK, CHUNK), CHUNK)
            return [pltpu.make_async_copy(pieces.at[at, lanes_of(b)], held.at[b, at], sems.at[3 + chunk * 2 * across + b])
                    for b in range(2 * across)]

        def begin(chunk, carry):
            for copy in copies(chunk):
                copy.start()
            return carry

        def end(chunk, carry):
            for copy in copies(chunk):
                copy.wait()
            return carry

        def one(slot, carry):
            used = table[field + slot]

            @pl.when(used > 0)
            def _():
                row = table[ROW + slot] - base if base else 0
                at = pl.ds(pl.multiple_of(table[PLACE + slot], ROW_ALIGN), height)
                for plane in range(2):
                    got = [jnp.where(row_index[:height] < used, held[plane * across + b, at, :], 0.0) for b in range(across)]
                    add_window(band, (plane,), got, row, table[COL + slot], height)

            return carry

        lax.fori_loop(0, chunks, begin, 0)
        lax.fori_loop(0, chunks, end, 0)
        load.wait()

        @pl.when(needed > 0)
        def _():
            lax.fori_loop(0, cap, one, 0)

    add_pieces(own, own[LENT], FAR, as_upper, bottom, tail, extent - tail, loads[0])
    add_pieces(up, up[KEPT], NEAR, as_lower, top, KEEP, 0, loads[1])
    loads[2].wait()
    stores = start_all([
        (top.at[:, right], right_out.at[:, :, top_rows]),
        (between, right_out.at[:, :, middle_rows]),
        (bottom.at[:, right, pl.ds(0, tail)], right_out.at[:, :, bottom_rows]),
        (top, total_out.at[:, :, top_rows]),
        (kept_bottom, total_out.at[:, :, bottom_rows]),
    ], sems)
    wait_all(stores)


def join_pieces(own, up, as_upper, as_lower, total, cap):
    frame = as_upper.shape[1] // 2
    _, blocks, extent, _ = total.shape
    across = frame // LANES
    rows = cap * KEEP
    return pl.pallas_call(
        lambda *refs: join_kernel(frame, *refs),
        out_shape=(jax.ShapeDtypeStruct(total.shape, F32), jax.ShapeDtypeStruct((2, across, extent, LANES), F32)),
        in_specs=[smem_spec(), smem_spec(), hbm_spec(), hbm_spec(), hbm_spec()],
        out_specs=(hbm_spec(), any_spec()),
        input_output_aliases={4: 0},
        scratch_shapes=[
            pltpu.VMEM((2, blocks, KEEP, LANES), F32),
            pltpu.VMEM((2, blocks, 2 * (frame - KEEP), LANES), F32),
            pltpu.VMEM((2, across, extent - frame, LANES), F32),
            pltpu.VMEM((2 * across, rows + KEEP, LANES), F32),
            pltpu.SemaphoreType.DMA((max(5, 3 + rows // CHUNK * 2 * across),)),
        ],
        compiler_params=params(56),
        name="join_pieces",
    )(own, up, as_upper, as_lower, total)


def right_half_kernel(tile, total, light, out):
    for b in range(total.shape[1]):
        below = 1.0 / (light[b] + 1.0)
        for plane in range(2):
            out[plane, :, lanes_of(b)] = tile[plane, :, lanes_of(b)] - total[plane, b] * below


def right_half(tile, total, light):
    extent = tile.shape[-1]
    across = total.shape[1] * LANES - extent
    part = (extent - across) // LANES
    tall = 128
    return pl.pallas_call(
        right_half_kernel,
        grid=(extent // tall,),
        out_shape=jax.ShapeDtypeStruct(tile.shape, F32),
        in_specs=[
            pl.BlockSpec((2, tall, extent - across), lambda i: (0, i, 1)),
            pl.BlockSpec((2, part, tall, LANES), lambda i: (0, 1, i, 0)),
            pl.BlockSpec((part, tall, LANES), lambda i: (1, i, 0)),
        ],
        out_specs=pl.BlockSpec((2, tall, extent - across), lambda i: (0, i, 1)),
        compiler_params=params(8),
        name="right_half",
    )(tile, total, light)


def left_half_kernel(tile, total, light, left, begun, out):
    for b in range(total.shape[1]):
        below = 1.0 / (light[b] + 1.0)
        for plane in range(2):
            grad = total[plane, b] + left[plane, b]
            out[plane, :, lanes_of(b)] = tile[plane, :, lanes_of(b)] - grad * below


def left_half(tile, total, light, left, begun):
    extent = tile.shape[-1]
    across = left.shape[1]
    tall = 256
    return pl.pallas_call(
        left_half_kernel,
        grid=(extent // tall,),
        out_shape=jax.ShapeDtypeStruct(tile.shape, F32),
        in_specs=[
            pl.BlockSpec((2, tall, across * LANES), lambda i: (0, i, 0)),
            pl.BlockSpec((2, across, tall, LANES), lambda i: (0, 0, i, 0)),
            pl.BlockSpec((across, tall, LANES), lambda i: (0, i, 0)),
            pl.BlockSpec((2, across, tall, LANES), lambda i: (0, 0, i, 0)),
            any_spec(),
        ],
        out_specs=pl.BlockSpec((2, tall, across * LANES), lambda i: (0, i, 0)),
        input_output_aliases={4: 0},
        compiler_params=params(8),
        name="left_half",
    )(tile, total, light, left, begun)


def body(object_tiles, probe, positions, frames, counts):
    tile = object_tiles[0]
    extent = tile.shape[-1]
    frame = frames.shape[-1]
    cap = frames.shape[1]
    peers = lax.axis_size("scan")
    tile_row = lax.axis_index("scan") // TCOLS
    phases = min(2, peers // TCOLS - 1)
    tables = dft_tables(frame)
    parity = (tile_row % 2).reshape(1)
    even = tile_row % 2 == 0

    own, edge, middle = prepare(positions, counts, tile, frame)
    up = shifted(own, "scan", TCOLS)
    edge = shifted(edge, "scan", -1)
    middle = shifted(middle, "scan", -1)
    beside = shifted(jnp.concatenate([own, up]), "scan", 1)

    def exchange(phase, packed, choice):
        uppers = [k for k in range(peers - TCOLS) if k // TCOLS % 2 == phase]
        pairs = [(k, k + TCOLS) for k in uppers] + [(k + TCOLS, k) for k in uppers]

        def sender(size):
            def run(data):
                return lax.dynamic_update_slice(data, lax.ppermute(data[:size], "scan", pairs), (0, 0))
            return run

        branches = [lambda data: data] + [sender(size) for size in SIZES]
        return lax.switch(choice.reshape(()), branches, packed)

    def by_role(arrays):
        if len(arrays) == 1:
            return arrays[0], arrays[0]
        return jnp.where(even, arrays[0], arrays[1]), jnp.where(even, arrays[1], arrays[0])

    cuts = [cut_pieces(phase, own, up, parity, tile, edge, frames[0]) for phase in range(phases)]
    received = by_role([exchange(phase, cut[0], cut[1]) for phase, cut in enumerate(cuts)])
    received, beside = lax.optimization_barrier((received, beside))
    total, *packed = frames_gradient(
        phases, own, up, parity, tile, edge, middle, frames[0], probe, tables, *received)
    returned = by_role([exchange(phase, packed[phase], cut[2]) for phase, cut in enumerate(cuts)])
    total, right = join_pieces(own, up, *returned, total, cap)
    left = shifted(right, "scan", 1)
    total, beside = lax.optimization_barrier((total, beside))
    light = light_plane(own, up, beside, probe, extent)
    begun = right_half(tile, total, light)
    return left_half(tile, total, light, left, begun)[None]


def solution(mesh):
    return jax.shard_map(
        body,
        mesh=mesh,
        in_specs=(
            P(("grp", "scan"), None, None, None),
            P(),
            P(("grp", "scan"), None, None),
            P(("grp", "scan"), None, None, None),
            P(("grp", "scan")),
        ),
        out_specs=P(("grp", "scan"), None, None, None),
        check_vma=False,
    )
```

```python
import math

import jax
import jax.numpy as jnp
import numpy as np
from jax import lax
from jax.experimental import pallas as pl
from jax.experimental.pallas import tpu as pltpu
from jax.sharding import PartitionSpec as P

TCOLS = 8
LANES = 128
ROW_ALIGN = 8
CHUNK = 64
STEP = 32
TILE_ROWS = 16
SIZES = (32, 64, 96, 128, 160, 192, 224, 256, 320, 384, 448, 512, 640, 768, 960, 1344)
MIB = 1024 * 1024
F32 = jnp.float32
BF16 = jnp.bfloat16

KEEP = 160
ROW, COL, NEAR, FAR, PLACE, SHOT = 0, 8, 16, 24, 32, 40
COUNT, KEPT, LENT, FORTH, BACK = 48, 49, 50, 51, 52
TABLE = 64

ACTIVE, AT_ROW, AT_COL, LO, HI, START, PIECE, SHIFT, ROLE = range(9)


def dft_tables(frame):
    near = np.arange(frame // 2, dtype=np.int64)
    blocks = []
    for odd in range(2):
        phase = (near[:, None] * (2 * near[None, :] + odd) % frame).astype(np.float64) * (2.0 * math.pi / frame)
        c, s = np.cos(phase), np.sin(phase)
        ahead = np.block([[c, -s], [s, c]])
        back = np.block([[c.T, s.T], [-s.T, c.T]])
        blocks.append((ahead, ahead.T, back, back.T))
    order = np.zeros((frame, frame))
    order[2 * near, near] = 1.0
    order[2 * near + 1, near + frame // 2] = 1.0
    tables = [blocks[odd][kind] for kind in range(4) for odd in range(2)] + [order]
    return jnp.asarray(np.stack(tables), F32).astype(BF16)


def shifted(array, axis, by):
    peers = lax.axis_size(axis)
    pairs = [(i, i + by) for i in range(peers) if 0 <= i + by < peers]
    return lax.ppermute(array, axis, pairs)


def any_spec():
    return pl.BlockSpec(memory_space=pl.ANY)


def hbm_spec():
    return pl.BlockSpec(memory_space=pltpu.HBM)


def smem_spec():
    return pl.BlockSpec(memory_space=pltpu.SMEM)


def vmem_spec():
    return pl.BlockSpec(memory_space=pltpu.VMEM)


def params(mebibytes):
    return pltpu.CompilerParams(vmem_limit_bytes=mebibytes * MIB)


def taken_from(blocks, by):
    lane = lax.broadcasted_iota(jnp.int32, blocks[0].shape, 1)
    rolled = [pltpu.roll(block, lax.rem(LANES - by, LANES), axis=1) for block in blocks]
    return [jnp.where(lane < LANES - by, one, two) for one, two in zip(rolled[:-1], rolled[1:])]


def put_into(blocks, by):
    lane = lax.broadcasted_iota(jnp.int32, blocks[0].shape, 1)
    rolled = [pltpu.roll(block, by, axis=1) for block in blocks]
    none = jnp.zeros_like(blocks[0])
    return [jnp.where(lane >= by, one, two) for one, two in zip(rolled + [none], [none] + rolled)]


def start_all(pairs, sems, first=0):
    copies = [pltpu.make_async_copy(source, target, sems.at[first + at]) for at, (source, target) in enumerate(pairs)]
    for copy in copies:
        copy.start()
    return copies


def wait_all(copies):
    for copy in copies:
        copy.wait()


def lanes_of(block):
    return pl.ds(block * LANES, LANES)


def side_by_side(parts):
    return jnp.concatenate(parts, axis=1)


def halves(array):
    return [array[:, :LANES], array[:, LANES:]]


def copy_out_rows(needed, packed, out, sems):
    chunks = (needed + CHUNK - 1) // CHUNK

    def copy(chunk):
        at = pl.ds(pl.multiple_of(chunk * CHUNK, CHUNK), CHUNK)
        return pltpu.make_async_copy(packed.at[at], out.at[at], sems.at[chunk])

    def begin(chunk, carry):
        copy(chunk).start()
        return carry

    def end(chunk, carry):
        copy(chunk).wait()
        return carry

    lax.fori_loop(0, chunks, begin, 0)
    lax.fori_loop(0, chunks, end, 0)


def up_to(value, step):
    return (value + step - 1) // step * step


def size_choice(needed):
    choice = jnp.where(needed > 0, 1, 0)
    for size in SIZES:
        choice = choice + jnp.where(needed > size, 1, 0)
    return choice


def prep_kernel(positions, counts, tile, table, edge, middle, sems):
    cap = positions.shape[2]
    extent = tile.shape[-1]
    frame = edge.shape[-1]
    count = counts[0]
    lanes = pl.ds(0, frame)
    copies = start_all([
        (tile.at[:, pl.ds(0, KEEP), lanes], edge.at[:, pl.ds(0, KEEP)]),
        (tile.at[:, pl.ds(KEEP + extent - frame, frame - KEEP), lanes], edge.at[:, pl.ds(KEEP, frame - KEEP)]),
        (tile.at[:, pl.ds(KEEP, extent - frame), lanes], middle),
    ], sems)
    kept, lent, shots = jnp.int32(0), jnp.int32(0), jnp.int32(0)
    for at in range(TABLE):
        table[at] = 0
    for slot in range(cap):
        row = lax.rem(positions[0, 0, slot], extent)
        col = lax.rem(positions[0, 1, slot], extent)
        below = jnp.where(slot < count, jnp.maximum(row + (frame - extent), 0), 0)
        stays = below <= KEEP
        near = jnp.where(stays, below, 0)
        far = jnp.where(stays, 0, frame - below)
        table[ROW + slot] = row
        table[COL + slot] = col
        table[NEAR + slot] = near
        table[FAR + slot] = far
        table[PLACE + slot] = jnp.where(stays, kept, lent)
        table[SHOT + slot] = shots
        kept = kept + up_to(near, ROW_ALIGN)
        lent = lent + up_to(far, ROW_ALIGN)
        shots = shots + jnp.where(stays, 0, frame // 2)
    for slot in range(cap):
        table[SHOT + slot] = table[SHOT + slot] + lent
    table[COUNT] = count
    table[KEPT] = kept
    table[LENT] = lent
    table[FORTH] = jnp.maximum(kept, lent + shots)
    table[BACK] = jnp.maximum(kept, lent)
    wait_all(copies)


def prepare(positions, counts, tile, frame):
    extent = tile.shape[-1]
    return pl.pallas_call(
        prep_kernel,
        out_shape=(
            jax.ShapeDtypeStruct((TABLE,), jnp.int32),
            jax.ShapeDtypeStruct((2, frame, frame), F32),
            jax.ShapeDtypeStruct((2, extent - frame, frame), F32),
        ),
        in_specs=[smem_spec(), smem_spec(), hbm_spec()],
        out_specs=(smem_spec(), vmem_spec(), vmem_spec()),
        scratch_shapes=[pltpu.SemaphoreType.DMA((3,))],
        compiler_params=params(62),
        name="prepare",
    )(jnp.swapaxes(positions, 1, 2), counts, tile)


def cut_kernel(phase, own, up, parity, tile, edge, frames, out, forth, back, band, packed, sems, chunk_sems):
    cap, frame, _ = frames.shape
    extent = tile.shape[-1]
    across = frame // LANES
    own_blocks = extent // LANES
    upper = parity[0] == phase
    forth[0] = size_choice(jnp.where(upper, own[FORTH], up[FORTH]))
    back[0] = size_choice(jnp.where(upper, own[BACK], up[BACK]))
    lends = jnp.logical_and(upper, own[LENT] > 0)
    gives = jnp.logical_and(jnp.logical_not(upper), up[KEPT] > 0)

    def cut(col, row, place):
        at = pl.ds(pl.multiple_of(place, ROW_ALIGN), frame)
        for plane in range(2):
            packed[at, pl.ds(plane * frame, frame)] = side_by_side(window(band, (plane,), row, col, frame, across))

    @pl.when(jnp.logical_or(lends, gives))
    def _():
        base = jnp.where(upper, extent - frame, 0)
        rows = pl.ds(pl.multiple_of(base, ROW_ALIGN), frame)
        wait_all(start_all(
            [(tile.at[:, rows, lanes_of(b)], band.at[:, b, pl.ds(0, frame)]) for b in range(own_blocks)]
            + [(edge.at[:, :, lanes_of(b)], band.at[:, own_blocks + b, pl.ds(0, frame)]) for b in range(across)], sems))

        def one(slot, carry):
            @pl.when(jnp.logical_and(upper, own[FAR + slot] > 0))
            def _():
                cut(own[COL + slot], own[ROW + slot] - (extent - frame), own[PLACE + slot])

            @pl.when(jnp.logical_and(gives, up[NEAR + slot] > 0))
            def _():
                cut(up[COL + slot], 0, up[PLACE + slot])

            return carry

        lax.fori_loop(0, cap, one, 0)

        def shots(slot):
            at = pl.ds(pl.multiple_of(own[SHOT + slot], ROW_ALIGN), frame // 2)
            return [pltpu.make_async_copy(frames.at[slot, pl.ds(part * frame // 2, frame // 2)],
                                          packed.at[at, pl.ds(part * frame, frame)], sems.at[2 * slot + part])
                    for part in range(2)]

        for wait in range(2):
            for slot in range(cap):
                @pl.when(jnp.logical_and(lends, own[FAR + slot] > 0))
                def _():
                    for copy in shots(slot):
                        if wait:
                            copy.wait()
                        else:
                            copy.start()

        copy_out_rows(jnp.where(upper, own[FORTH], up[KEPT]), packed, out, chunk_sems)


def cut_pieces(phase, own, up, parity, tile, edge, frames):
    cap, frame, _ = frames.shape
    extent = tile.shape[-1]
    blocks = (extent + frame) // LANES
    rows = SIZES[-1]
    return pl.pallas_call(
        lambda *refs: cut_kernel(phase, *refs),
        out_shape=(
            jax.ShapeDtypeStruct((rows, 2 * frame), F32),
            jax.ShapeDtypeStruct((1,), jnp.int32),
            jax.ShapeDtypeStruct((1,), jnp.int32),
        ),
        in_specs=[smem_spec(), smem_spec(), smem_spec(), hbm_spec(), hbm_spec(), hbm_spec()],
        out_specs=(hbm_spec(), smem_spec(), smem_spec()),
        scratch_shapes=[
            pltpu.VMEM((2, blocks, 2 * frame, LANES), F32),
            pltpu.VMEM((rows + frame, 2 * frame), F32),
            pltpu.SemaphoreType.DMA((max(blocks, 2 * cap),)),
            pltpu.SemaphoreType.DMA((rows // CHUNK,)),
        ],
        compiler_params=params(60),
        name="cut_pieces",
    )(own, up, parity, tile, edge, frames)


def dot(one, two):
    return jnp.dot(one, two, preferred_element_type=F32)


def stacked(parts):
    return jnp.concatenate(parts, axis=0)


def lane_parts(array):
    half = array.shape[1] // 2
    return array[:, :half], array[:, half:]


def wave_stage(mode, probe, patch, waves):
    frame = probe.shape[2]
    for at in range(0, frame, STEP):
        rows = pl.ds(at, STEP)
        probe_real, probe_imag = probe[mode, 0, rows], probe[mode, 1, rows]
        patch_real, patch_imag = patch[0, rows], patch[1, rows]
        parts = [lane_parts(part) for part in (
            probe_real * patch_real - probe_imag * patch_imag, probe_real * patch_imag + probe_imag * patch_real)]
        waves[0, mode, rows] = side_by_side([near + far for near, far in parts]).astype(BF16)
        waves[1, mode, rows] = side_by_side([near - far for near, far in parts]).astype(BF16)


def rows_dot(mode, source, tables, first, product):
    for odd in range(2):
        product[odd, mode] = dot(source[odd, mode], tables[first + odd])


def columns_dot(mode, tables, first, source, product):
    for odd in range(2):
        product[odd, mode] = dot(tables[first + odd], source[odd, mode])


def half_stage(mode, product, halfway):
    half = product.shape[2] // 2
    for at in range(0, half, TILE_ROWS):
        near, far = pl.ds(at, TILE_ROWS), pl.ds(half + at, TILE_ROWS)
        upper = [product[odd, mode, near] for odd in range(2)]
        lower = [product[odd, mode, far] for odd in range(2)]
        for odd in range(2):
            mixed = [a + b if not odd else a - b for a, b in zip(upper, lower)]
            real, imag = zip(*[lane_parts(part) for part in mixed])
            halfway[odd, mode, near] = side_by_side(real).astype(BF16)
            halfway[odd, mode, far] = side_by_side(imag).astype(BF16)


def residual_stage(modes, frame, field, amplitude, waves):
    half = frame // 2
    for odd in range(2):
        for at in range(0, half, TILE_ROWS):
            near, far = pl.ds(at, TILE_ROWS), pl.ds(half + at, TILE_ROWS)
            real = [field[odd, mode, near] for mode in range(modes)]
            imag = [field[odd, mode, far] for mode in range(modes)]
            lit = sum(a * a + b * b for a, b in zip(real, imag))
            factor = 1.0 / frame - amplitude[odd, near] * lax.rsqrt(jnp.maximum(lit, float(frame * frame)))
            target = pl.ds(odd * half + at, TILE_ROWS)
            for mode in range(modes):
                parts = [lane_parts(real[mode] * factor), lane_parts(imag[mode] * factor)]
                for column in range(2):
                    waves[column, mode, target] = side_by_side([part[column] for part in parts]).astype(BF16)


def back_stage(mode, product, halfway):
    half = product.shape[2] // 2
    for odd in range(2):
        for at in range(0, half, TILE_ROWS):
            rows = pl.ds(odd * half + at, TILE_ROWS)
            even_part, odd_part = product[0, mode, rows], product[1, mode, rows]
            near, far = lane_parts(even_part + odd_part), lane_parts(even_part - odd_part)
            halfway[odd, mode, pl.ds(at, TILE_ROWS)] = side_by_side([near[0], far[0]]).astype(BF16)
            halfway[odd, mode, pl.ds(half + at, TILE_ROWS)] = side_by_side([near[1], far[1]]).astype(BF16)


def gradient_stage(some_modes, first, product, probe, piece):
    frame = probe.shape[2]
    half = frame // 2
    across = frame // LANES
    for at in range(0, half, TILE_ROWS):
        rows = [pl.ds(at, TILE_ROWS), pl.ds(half + at, TILE_ROWS)]
        grads = [[0.0, 0.0], [0.0, 0.0]]
        for mode in some_modes:
            mixed = [(product[0, mode, part], product[1, mode, part]) for part in rows]
            for side in range(2):
                back_real, back_imag = [a + b if not side else a - b for a, b in mixed]
                probe_real, probe_imag = probe[mode, 0, rows[side]], probe[mode, 1, rows[side]]
                grads[side][0] += probe_real * back_real + probe_imag * back_imag
                grads[side][1] += probe_real * back_imag - probe_imag * back_real
        for side in range(2):
            for plane in range(2):
                grad = grads[side][plane] * (1.0 / frame)
                for b in range(across):
                    where = (plane * across + b, rows[side], slice(None))
                    part = grad[:, b * LANES:(b + 1) * LANES]
                    piece[where] = part if first else piece[where] + part


def frame_step(patch, amplitude, probe, tables, waves, halfway, product, field, piece):
    modes, _, frame, _ = probe.shape
    for step in range(modes + 1):
        if step < modes:
            wave_stage(step, probe, patch, waves)
            rows_dot(step, waves, tables, 0, product)
        if step:
            half_stage(step - 1, product, halfway)
            columns_dot(step - 1, tables, 2, halfway, field)
    residual_stage(modes, frame, field, amplitude, waves)
    for step in range(modes + 1):
        if step < modes:
            rows_dot(step, waves, tables, 4, product)
        if step:
            back_stage(step - 1, product, halfway)
            columns_dot(step - 1, tables, 6, halfway, field)
        if step and step % 2 == 0:
            gradient_stage((step - 2, step - 1), step == 2, field, probe, piece)


def ordered_amplitude(measured, task, order, amplitude):
    frame = measured.shape[2]
    for odd in range(2):
        root = jnp.sqrt(side_by_side(
            [measured[task, b, pl.ds(odd, frame // 2, stride=2), :] for b in range(measured.shape[1])]))
        high = root.astype(BF16)
        low = (root - high.astype(F32)).astype(BF16)
        amplitude[odd] = dot(high, order) + dot(low, order)


def window(band, lead, row, col, height, across):
    return taken_from(
        [band[lead + (col // LANES + b, pl.ds(row, height), slice(None))] for b in range(across + 1)],
        lax.rem(col, LANES),
    )


def add_window(total, lead, parts, row, col, frame):
    for b, moved in enumerate(put_into(parts, lax.rem(col, LANES))):
        at = lead + (col // LANES + b, pl.ds(row, frame), slice(None))
        total[at] = total[at] + moved


def kernel_cost(frames, modes, frame):
    return pl.CostEstimate(
        flops=frames * modes * 4 * 4 * frame ** 3, bytes_accessed=16 * 1024 * 1024, transcendentals=0)


def frames_kernel(phases, own, up, parity, tile, edge, middle, frames, probe_in, tables_in, as_upper, as_lower, total_out, *rest):
    packed_outs = rest[:phases]
    (band, total, held, packed, piece, measured, probe, tables, patch, amplitude, waves, halfway, product, field, work,
     sems, shot_sems, held_sems, chunk_sems) = rest[phases:]
    cap, frame, _ = frames.shape
    extent = tile.shape[-1]
    across = frame // LANES
    own_blocks = extent // LANES
    half = frame // 2
    own_rows = pl.ds(frame, extent)

    first = start_all(
        [(tile.at[:, :, lanes_of(b)], band.at[:, b, own_rows]) for b in range(own_blocks)]
        + [(source.at[:, pl.ds(at, height), lanes_of(b)], band.at[:, own_blocks + b, pl.ds(frame + target, height)])
           for source, at, height, target in (
               (edge, 0, KEEP, 0), (middle, 0, extent - frame, KEEP), (edge, KEEP, frame - KEEP, KEEP + extent - frame))
           for b in range(across)]
        + [(probe_in, probe), (tables_in, tables)], sems)

    def mine(slot):
        return jnp.logical_and(slot < own[COUNT], own[FAR + slot] == 0)

    def borrowed(slot):
        return up[FAR + slot] > 0

    def shot_copies(slot, task, lent):
        if not lent:
            return [pltpu.make_async_copy(frames.at[slot, :, lanes_of(b)], measured.at[task, b], shot_sems.at[task, b])
                    for b in range(across)]
        at = pl.ds(pl.multiple_of(up[SHOT + slot], ROW_ALIGN), half)
        return [
            pltpu.make_async_copy(as_lower.at[at, lanes_of(part * across + b)],
                                  measured.at[task, b, pl.ds(part * half, half)], shot_sems.at[task, part * across + b])
            for part in range(2) for b in range(across)
        ]

    def held_copies(slot, task, lent):
        source, table = (as_lower, up) if lent else (as_upper, own)
        at = pl.ds(pl.multiple_of(table[PLACE + slot], ROW_ALIGN), frame)
        return [
            pltpu.make_async_copy(source.at[at, lanes_of(b)], held.at[task, b, pl.ds(frame, frame)], held_sems.at[task, b])
            for b in range(2 * across)
        ]

    def for_tasks(wait):
        for slot in range(cap):
            def run(copies):
                for copy in copies:
                    if wait:
                        copy.wait()
                    else:
                        copy.start()

            @pl.when(mine(slot))
            def _():
                run(shot_copies(slot, slot, False))

            @pl.when(own[NEAR + slot] > 0)
            def _():
                run(held_copies(slot, slot, False))

            @pl.when(borrowed(slot))
            def _():
                run(shot_copies(slot, cap + slot, True))
                run(held_copies(slot, cap + slot, True))

    for_tasks(False)
    for slot in range(cap):
        near = own[NEAR + slot]
        for field_at, value in (
            (ACTIVE, mine(slot).astype(jnp.int32)), (AT_ROW, own[ROW + slot] + frame), (AT_COL, own[COL + slot]),
            (LO, frame - near), (HI, frame), (START, near), (PIECE, own[PLACE + slot]), (SHIFT, frame - near), (ROLE, 0),
        ):
            work[slot, field_at] = value
        for field_at, value in (
            (ACTIVE, borrowed(slot).astype(jnp.int32)), (AT_ROW, up[ROW + slot] + frame - extent), (AT_COL, up[COL + slot]),
            (LO, 0), (HI, up[FAR + slot]), (START, frame), (PIECE, up[PLACE + slot]), (SHIFT, 0), (ROLE, 1),
        ):
            work[cap + slot, field_at] = value
    total[...] = jnp.zeros_like(total)
    wait_all(first)
    for_tasks(True)
    row_index = lax.broadcasted_iota(jnp.int32, (STEP, LANES), 0)

    def one(task, carry):
        @pl.when(work[task, ACTIVE] > 0)
        def _():
            row, col, start = work[task, AT_ROW], work[task, AT_COL], work[task, START]
            lo, hi = work[task, LO], work[task, HI]
            for at in range(0, frame, STEP):
                theirs = jnp.logical_and(row_index >= lo - at, row_index < hi - at)
                for plane in range(2):
                    near = window(band, (plane,), row + at, col, STEP, across)
                    other = [held[task, plane * across + b, pl.ds(start + at, STEP), :] for b in range(across)]
                    patch[plane, pl.ds(at, STEP)] = side_by_side([jnp.where(theirs, b, a) for a, b in zip(near, other)])
            ordered_amplitude(measured, task, tables[8], amplitude)
            frame_step(patch, amplitude, probe, tables, waves, halfway, product, field, piece)
            for at in range(0, frame, STEP):
                for plane in range(2):
                    parts = [piece[plane * across + b, pl.ds(at, STEP), :] for b in range(across)]
                    add_window(total, (plane,), parts, row + at, col, STEP)

            @pl.when(lo < hi)
            def _():
                target = pl.ds(pl.multiple_of(work[task, PIECE], ROW_ALIGN), frame)
                source = pl.ds(work[task, SHIFT], frame)
                for b in range(2 * across):
                    packed[work[task, ROLE], target, lanes_of(b)] = piece[b, source, :]

        return carry

    lax.fori_loop(0, 2 * cap, one, 0)
    end = start_all([(total.at[:, :, own_rows], total_out)], sems)
    for phase in range(phases):
        upper = parity[0] == phase
        role = jnp.where(upper, 0, 1)
        copy_out_rows(jnp.where(upper, own[KEPT], up[LENT]), packed.at[role], packed_outs[phase], chunk_sems)
    wait_all(end)


def frames_gradient(phases, own, up, parity, tile, edge, middle, frames, probe, tables, as_upper, as_lower):
    cap, frame, _ = frames.shape
    extent = tile.shape[-1]
    modes = probe.shape[0]
    tall = extent + 2 * frame
    blocks = (extent + frame) // LANES
    across = frame // LANES
    rows = as_upper.shape[0]
    kept_rows = cap * KEEP
    return pl.pallas_call(
        lambda *refs: frames_kernel(phases, *refs),
        out_shape=(jax.ShapeDtypeStruct((2, blocks, extent, LANES), F32),)
        + (jax.ShapeDtypeStruct((kept_rows, 2 * frame), F32),) * phases,
        in_specs=[smem_spec()] * 3 + [hbm_spec()] * 8,
        out_specs=(hbm_spec(),) * (1 + phases),
        scratch_shapes=[
            pltpu.VMEM((2, blocks, tall, LANES), F32),
            pltpu.VMEM((2, blocks, tall, LANES), F32),
            pltpu.VMEM((2 * cap, 2 * across, 2 * frame, LANES), F32),
            pltpu.VMEM((2, kept_rows + frame, 2 * frame), F32),
            pltpu.VMEM((2 * across, 2 * frame, LANES), F32),
            pltpu.VMEM((2 * cap, across, frame, LANES), F32),
            pltpu.VMEM(probe.shape, F32),
            pltpu.VMEM(tables.shape, BF16),
            pltpu.VMEM((2, frame, frame), F32),
            pltpu.VMEM((2, frame // 2, frame), F32),
            pltpu.VMEM((2, modes, frame, frame), BF16),
            pltpu.VMEM((2, modes, frame, frame), BF16),
            pltpu.VMEM((2, modes, frame, frame), F32),
            pltpu.VMEM((2, modes, frame, frame), F32),
            pltpu.SMEM((2 * cap, 16), jnp.int32),
            pltpu.SemaphoreType.DMA((blocks + 2 * across + 2,)),
            pltpu.SemaphoreType.DMA((2 * cap, 2 * across)),
            pltpu.SemaphoreType.DMA((2 * cap, 2 * across)),
            pltpu.SemaphoreType.DMA((rows // CHUNK,)),
        ],
        compiler_params=params(54),
        cost_estimate=kernel_cost(cap, modes, frame),
        name="frames_gradient",
    )(own, up, parity, tile, edge, middle, frames, probe, tables, as_upper, as_lower)


def light_kernel(own, up, beside, probe, light_out, light, sem):
    modes, _, frame, _ = probe.shape
    own_blocks, extent, _ = light_out.shape
    across = frame // LANES
    inside = (pl.ds(across, own_blocks), pl.ds(frame, extent), slice(None))
    light[inside] = jnp.zeros((own_blocks, extent, LANES), F32)
    power = jnp.zeros((frame, frame), F32)
    for mode in range(modes):
        power += probe[mode, 0] * probe[mode, 0] + probe[mode, 1] * probe[mode, 1]
    power = halves(power)
    for table, lead, down, right in ((own, 0, 0, 0), (beside, 0, 0, 1), (up, 0, 1, 0), (beside, TABLE, 1, 1)):

        def lit(slot, carry, table=table, lead=lead, down=down, right=right):
            row = table[lead + ROW + slot] + frame - down * extent
            col = table[lead + COL + slot] + frame - right * extent

            @pl.when((row > 0) & (col > 0))
            def _():
                add_window(light, (), power, row, col, frame)

            return carry

        lax.fori_loop(0, table[lead + COUNT], lit, 0)
    copy = pltpu.make_async_copy(light.at[inside[0], inside[1]], light_out, sem)
    copy.start()
    copy.wait()


def light_plane(own, up, beside, probe, extent):
    frame = probe.shape[-1]
    wide = extent + 2 * frame
    return pl.pallas_call(
        light_kernel,
        out_shape=jax.ShapeDtypeStruct((extent // LANES, extent, LANES), F32),
        in_specs=[smem_spec()] * 3 + [vmem_spec()],
        out_specs=any_spec(),
        scratch_shapes=[pltpu.VMEM((wide // LANES, wide, LANES), F32), pltpu.SemaphoreType.DMA],
        compiler_params=params(9),
        cost_estimate=pl.CostEstimate(flops=0, bytes_accessed=4 * MIB, transcendentals=0),
        name="light_plane",
    )(own, up, beside, probe)


def add_pieces(frame, table, needed, field, pieces, band, blocks, height, row_of, held, sems):
    across = frame // LANES
    cap = (held.shape[1] - KEEP) // KEEP
    chunks = (needed + CHUNK - 1) // CHUNK
    row_index = lax.broadcasted_iota(jnp.int32, (height, LANES), 0)

    def copies(chunk):
        at = pl.ds(pl.multiple_of(chunk * CHUNK, CHUNK), CHUNK)
        return [pltpu.make_async_copy(pieces.at[at, lanes_of(b)], held.at[b, at], sems.at[chunk * 2 * across + b])
                for b in range(2 * across)]

    def begin(chunk, carry):
        for copy in copies(chunk):
            copy.start()
        return carry

    def end(chunk, carry):
        for copy in copies(chunk):
            copy.wait()
        return carry

    def one(slot, carry):
        used = table[field + slot]
        first = table[COL + slot] // LANES

        @pl.when(jnp.logical_and(used > 0, jnp.logical_and(first + across >= blocks[0], first < blocks[1])))
        def _():
            at = pl.ds(pl.multiple_of(table[PLACE + slot], ROW_ALIGN), height)
            for plane in range(2):
                got = [jnp.where(row_index < used, held[plane * across + b, at, :], 0.0) for b in range(across)]
                for b, moved in enumerate(put_into(got, lax.rem(table[COL + slot], LANES))):
                    @pl.when(jnp.logical_and(first + b >= blocks[0], first + b < blocks[1]))
                    def _():
                        where = (plane, first + b - blocks[0], pl.ds(row_of(slot), height), slice(None))
                        band[where] = band[where] + moved

        return carry

    lax.fori_loop(0, chunks, begin, 0)
    lax.fori_loop(0, chunks, end, 0)

    @pl.when(needed > 0)
    def _():
        lax.fori_loop(0, cap, one, 0)


def join_right_kernel(frame, own, up, as_upper, as_lower, total, right_out, band, held, sems, piece_sems):
    across = frame // LANES
    blocks, extent = total.shape[1:3]
    rows = pl.ds(0, extent)
    reach = (blocks - across, blocks)
    wait_all(start_all([(total.at[:, pl.ds(blocks - across, across)], band.at[:, :, rows])], sems))
    add_pieces(frame, own, own[LENT], FAR, as_upper, band, reach, frame - KEEP, lambda slot: own[ROW + slot], held, piece_sems)
    add_pieces(frame, up, up[KEPT], NEAR, as_lower, band, reach, KEEP, lambda slot: 0, held, piece_sems)
    wait_all(start_all([(band.at[:, :, rows], right_out)], sems))


def join_right(own, up, as_upper, as_lower, total, cap):
    frame = as_upper.shape[1] // 2
    extent = total.shape[2]
    across = frame // LANES
    rows = cap * KEEP
    return pl.pallas_call(
        lambda *refs: join_right_kernel(frame, *refs),
        out_shape=jax.ShapeDtypeStruct((2, across, extent, LANES), F32),
        in_specs=[smem_spec(), smem_spec(), hbm_spec(), hbm_spec(), hbm_spec()],
        out_specs=any_spec(),
        scratch_shapes=[
            pltpu.VMEM((2, across, extent + frame, LANES), F32),
            pltpu.VMEM((2 * across, rows + KEEP, LANES), F32),
            pltpu.SemaphoreType.DMA((1,)),
            pltpu.SemaphoreType.DMA((rows // CHUNK * 2 * across,)),
        ],
        compiler_params=params(56),
        name="join_right",
    )(own, up, as_upper, as_lower, total)


def join_own_kernel(frame, own, up, as_upper, as_lower, total_in, total_out, top, bottom, held, sems, piece_sems):
    own_blocks = top.shape[1]
    extent = total_in.shape[2]
    tail = frame - KEEP
    mine = pl.ds(0, own_blocks)
    reach = (0, own_blocks)

    def part(needed, rows, band, source, table, field, height, row_of):
        @pl.when(needed > 0)
        def _():
            wait_all(start_all([(total_in.at[:, mine, rows], band)], sems))
            add_pieces(frame, table, needed, field, source, band_of[field], reach, height, row_of, held, piece_sems)
            wait_all(start_all([(band, total_out.at[:, mine, rows])], sems))

    band_of = {FAR: bottom, NEAR: top}
    part(own[LENT], pl.ds(extent - tail, tail), bottom.at[:, :, pl.ds(0, tail)], as_upper, own, FAR, tail,
         lambda slot: own[ROW + slot] - (extent - tail))
    part(up[KEPT], pl.ds(0, KEEP), top, as_lower, up, NEAR, KEEP, lambda slot: 0)


def join_own(own, up, as_upper, as_lower, total, cap):
    frame = as_upper.shape[1] // 2
    own_blocks = total.shape[2] // LANES
    across = frame // LANES
    rows = cap * KEEP
    return pl.pallas_call(
        lambda *refs: join_own_kernel(frame, *refs),
        out_shape=jax.ShapeDtypeStruct(total.shape, F32),
        in_specs=[smem_spec(), smem_spec(), hbm_spec(), hbm_spec(), hbm_spec()],
        out_specs=hbm_spec(),
        input_output_aliases={4: 0},
        scratch_shapes=[
            pltpu.VMEM((2, own_blocks, KEEP, LANES), F32),
            pltpu.VMEM((2, own_blocks, 2 * (frame - KEEP), LANES), F32),
            pltpu.VMEM((2 * across, rows + KEEP, LANES), F32),
            pltpu.SemaphoreType.DMA((1,)),
            pltpu.SemaphoreType.DMA((rows // CHUNK * 2 * across,)),
        ],
        compiler_params=params(56),
        name="join_own",
    )(own, up, as_upper, as_lower, total)


def right_half_kernel(tile, total, light, out):
    for b in range(total.shape[1]):
        below = 1.0 / (light[b] + 1.0)
        for plane in range(2):
            out[plane, :, lanes_of(b)] = tile[plane, :, lanes_of(b)] - total[plane, b] * below


def right_half(tile, total, light):
    extent = tile.shape[-1]
    across = total.shape[1] * LANES - extent
    part = (extent - across) // LANES
    tall = 128
    return pl.pallas_call(
        right_half_kernel,
        grid=(extent // tall,),
        out_shape=jax.ShapeDtypeStruct(tile.shape, F32),
        in_specs=[
            pl.BlockSpec((2, tall, extent - across), lambda i: (0, i, 1)),
            pl.BlockSpec((2, part, tall, LANES), lambda i: (0, 1, i, 0)),
            pl.BlockSpec((part, tall, LANES), lambda i: (1, i, 0)),
        ],
        out_specs=pl.BlockSpec((2, tall, extent - across), lambda i: (0, i, 1)),
        compiler_params=params(8),
        name="right_half",
    )(tile, total, light)


def left_half_kernel(tile, total, light, left, begun, out):
    for b in range(total.shape[1]):
        below = 1.0 / (light[b] + 1.0)
        for plane in range(2):
            grad = total[plane, b] + left[plane, b]
            out[plane, :, lanes_of(b)] = tile[plane, :, lanes_of(b)] - grad * below


def left_half(tile, total, light, left, begun):
    extent = tile.shape[-1]
    across = left.shape[1]
    tall = 256
    return pl.pallas_call(
        left_half_kernel,
        grid=(extent // tall,),
        out_shape=jax.ShapeDtypeStruct(tile.shape, F32),
        in_specs=[
            pl.BlockSpec((2, tall, across * LANES), lambda i: (0, i, 0)),
            pl.BlockSpec((2, across, tall, LANES), lambda i: (0, 0, i, 0)),
            pl.BlockSpec((across, tall, LANES), lambda i: (0, i, 0)),
            pl.BlockSpec((2, across, tall, LANES), lambda i: (0, 0, i, 0)),
            any_spec(),
        ],
        out_specs=pl.BlockSpec((2, tall, across * LANES), lambda i: (0, i, 0)),
        input_output_aliases={4: 0},
        compiler_params=params(8),
        name="left_half",
    )(tile, total, light, left, begun)


def body(object_tiles, probe, positions, frames, counts):
    tile = object_tiles[0]
    extent = tile.shape[-1]
    frame = frames.shape[-1]
    cap = frames.shape[1]
    peers = lax.axis_size("scan")
    tile_row = lax.axis_index("scan") // TCOLS
    phases = min(2, peers // TCOLS - 1)
    tables = dft_tables(frame)
    parity = (tile_row % 2).reshape(1)
    even = tile_row % 2 == 0

    own, edge, middle = prepare(positions, counts, tile, frame)
    up = shifted(own, "scan", TCOLS)
    edge = shifted(edge, "scan", -1)
    middle = shifted(middle, "scan", -1)
    beside = shifted(jnp.concatenate([own, up]), "scan", 1)

    def exchange(phase, packed, choice):
        uppers = [k for k in range(peers - TCOLS) if k // TCOLS % 2 == phase]
        pairs = [(k, k + TCOLS) for k in uppers] + [(k + TCOLS, k) for k in uppers]

        def sender(size):
            def run(data):
                return lax.dynamic_update_slice(data, lax.ppermute(data[:size], "scan", pairs), (0, 0))
            return run

        branches = [lambda data: data] + [sender(size) for size in SIZES if size <= packed.shape[0]]
        return lax.switch(choice.reshape(()), branches, packed)

    def by_role(arrays):
        if len(arrays) == 1:
            return arrays[0], arrays[0]
        return jnp.where(even, arrays[0], arrays[1]), jnp.where(even, arrays[1], arrays[0])

    cuts = [cut_pieces(phase, own, up, parity, tile, edge, frames[0]) for phase in range(phases)]
    received = by_role([exchange(phase, cut[0], cut[1]) for phase, cut in enumerate(cuts)])
    received, beside = lax.optimization_barrier((received, beside))
    total, *packed = frames_gradient(
        phases, own, up, parity, tile, edge, middle, frames[0], probe, tables, *received)
    returned = by_role([exchange(phase, packed[phase], cut[2]) for phase, cut in enumerate(cuts)])
    right = join_right(own, up, *returned, total, cap)
    right, total, beside = lax.optimization_barrier((right, total, beside))
    left = shifted(right, "scan", 1)
    total = join_own(own, up, *returned, total, cap)
    light = light_plane(own, up, beside, probe, extent)
    begun = right_half(tile, total, light)
    return left_half(tile, total, light, left, begun)[None]


def solution(mesh):
    return jax.shard_map(
        body,
        mesh=mesh,
        in_specs=(
            P(("grp", "scan"), None, None, None),
            P(),
            P(("grp", "scan"), None, None),
            P(("grp", "scan"), None, None, None),
            P(("grp", "scan")),
        ),
        out_specs=P(("grp", "scan"), None, None, None),
        check_vma=False,
    )
```

```python
import math

import jax
import jax.numpy as jnp
import numpy as np
from jax import lax
from jax.experimental import pallas as pl
from jax.experimental.pallas import tpu as pltpu
from jax.sharding import PartitionSpec as P

TCOLS = 8
LANES = 128
ROW_ALIGN = 8
CHUNK = 64
STEP = 32
TILE_ROWS = 16
SIZES = (32, 64, 96, 128, 160, 192, 224, 256, 320, 384, 448, 512, 640, 768, 960, 1344)
MIB = 1024 * 1024
F32 = jnp.float32
BF16 = jnp.bfloat16

KEEP = 160
ROW, COL, NEAR, FAR, PLACE, SHOT = 0, 8, 16, 24, 32, 40
COUNT, KEPT, LENT, FORTH, BACK = 48, 49, 50, 51, 52
TABLE = 64

ACTIVE, AT_ROW, AT_COL, LO, HI, START, PIECE, SHIFT, ROLE = range(9)


def dft_tables(frame):
    near = np.arange(frame // 2, dtype=np.int64)
    blocks = []
    for odd in range(2):
        phase = (near[:, None] * (2 * near[None, :] + odd) % frame).astype(np.float64) * (2.0 * math.pi / frame)
        c, s = np.cos(phase), np.sin(phase)
        ahead = np.block([[c, -s], [s, c]])
        back = np.block([[c.T, s.T], [-s.T, c.T]])
        blocks.append((ahead, ahead.T, back, back.T))
    order = np.zeros((frame, frame))
    order[2 * near, near] = 1.0
    order[2 * near + 1, near + frame // 2] = 1.0
    tables = [blocks[odd][kind] for kind in range(4) for odd in range(2)] + [order]
    return jnp.asarray(np.stack(tables), F32).astype(BF16)


def shifted(array, axis, by):
    peers = lax.axis_size(axis)
    pairs = [(i, i + by) for i in range(peers) if 0 <= i + by < peers]
    return lax.ppermute(array, axis, pairs)


def any_spec():
    return pl.BlockSpec(memory_space=pl.ANY)


def hbm_spec():
    return pl.BlockSpec(memory_space=pltpu.HBM)


def smem_spec():
    return pl.BlockSpec(memory_space=pltpu.SMEM)


def vmem_spec():
    return pl.BlockSpec(memory_space=pltpu.VMEM)


def params(mebibytes):
    return pltpu.CompilerParams(vmem_limit_bytes=mebibytes * MIB)


def taken_from(blocks, by):
    lane = lax.broadcasted_iota(jnp.int32, blocks[0].shape, 1)
    rolled = [pltpu.roll(block, lax.rem(LANES - by, LANES), axis=1) for block in blocks]
    return [jnp.where(lane < LANES - by, one, two) for one, two in zip(rolled[:-1], rolled[1:])]


def put_into(blocks, by):
    lane = lax.broadcasted_iota(jnp.int32, blocks[0].shape, 1)
    rolled = [pltpu.roll(block, by, axis=1) for block in blocks]
    none = jnp.zeros_like(blocks[0])
    return [jnp.where(lane >= by, one, two) for one, two in zip(rolled + [none], [none] + rolled)]


def start_all(pairs, sems, first=0):
    copies = [pltpu.make_async_copy(source, target, sems.at[first + at]) for at, (source, target) in enumerate(pairs)]
    for copy in copies:
        copy.start()
    return copies


def wait_all(copies):
    for copy in copies:
        copy.wait()


def lanes_of(block):
    return pl.ds(block * LANES, LANES)


def side_by_side(parts):
    return jnp.concatenate(parts, axis=1)


def halves(array):
    return [array[:, :LANES], array[:, LANES:]]


def copy_out_rows(needed, packed, out, sems):
    chunks = (needed + CHUNK - 1) // CHUNK

    def copy(chunk):
        at = pl.ds(pl.multiple_of(chunk * CHUNK, CHUNK), CHUNK)
        return pltpu.make_async_copy(packed.at[at], out.at[at], sems.at[chunk])

    def begin(chunk, carry):
        copy(chunk).start()
        return carry

    def end(chunk, carry):
        copy(chunk).wait()
        return carry

    lax.fori_loop(0, chunks, begin, 0)
    lax.fori_loop(0, chunks, end, 0)


def up_to(value, step):
    return (value + step - 1) // step * step


def size_choice(needed):
    choice = jnp.where(needed > 0, 1, 0)
    for size in SIZES:
        choice = choice + jnp.where(needed > size, 1, 0)
    return choice


def prep_kernel(positions, counts, tile, table, edge, middle, sems):
    cap = positions.shape[2]
    extent = tile.shape[-1]
    frame = edge.shape[-1]
    count = counts[0]
    lanes = pl.ds(0, frame)
    copies = start_all([
        (tile.at[:, pl.ds(0, KEEP), lanes], edge.at[:, pl.ds(0, KEEP)]),
        (tile.at[:, pl.ds(KEEP + extent - frame, frame - KEEP), lanes], edge.at[:, pl.ds(KEEP, frame - KEEP)]),
        (tile.at[:, pl.ds(KEEP, extent - frame), lanes], middle),
    ], sems)
    kept, lent, shots = jnp.int32(0), jnp.int32(0), jnp.int32(0)
    for at in range(TABLE):
        table[at] = 0
    for slot in range(cap):
        row = lax.rem(positions[0, 0, slot], extent)
        col = lax.rem(positions[0, 1, slot], extent)
        below = jnp.where(slot < count, jnp.maximum(row + (frame - extent), 0), 0)
        stays = below <= KEEP
        near = jnp.where(stays, below, 0)
        far = jnp.where(stays, 0, frame - below)
        table[ROW + slot] = row
        table[COL + slot] = col
        table[NEAR + slot] = near
        table[FAR + slot] = far
        table[PLACE + slot] = jnp.where(stays, kept, lent)
        table[SHOT + slot] = shots
        kept = kept + up_to(near, ROW_ALIGN)
        lent = lent + up_to(far, ROW_ALIGN)
        shots = shots + jnp.where(stays, 0, frame // 2)
    for slot in range(cap):
        table[SHOT + slot] = table[SHOT + slot] + lent
    table[COUNT] = count
    table[KEPT] = kept
    table[LENT] = lent
    table[FORTH] = jnp.maximum(kept, lent + shots)
    table[BACK] = jnp.maximum(kept, lent)
    wait_all(copies)


def prepare(positions, counts, tile, frame):
    extent = tile.shape[-1]
    return pl.pallas_call(
        prep_kernel,
        out_shape=(
            jax.ShapeDtypeStruct((TABLE,), jnp.int32),
            jax.ShapeDtypeStruct((2, frame, frame), F32),
            jax.ShapeDtypeStruct((2, extent - frame, frame), F32),
        ),
        in_specs=[smem_spec(), smem_spec(), hbm_spec()],
        out_specs=(smem_spec(), vmem_spec(), vmem_spec()),
        scratch_shapes=[pltpu.SemaphoreType.DMA((3,))],
        compiler_params=params(62),
        name="prepare",
    )(jnp.swapaxes(positions, 1, 2), counts, tile)


def cut_kernel(phase, own, up, parity, tile, edge, frames, out, forth, back, band, packed, sems, chunk_sems):
    cap, frame, _ = frames.shape
    extent = tile.shape[-1]
    across = frame // LANES
    own_blocks = extent // LANES
    upper = parity[0] == phase
    forth[0] = size_choice(jnp.where(upper, own[FORTH], up[FORTH]))
    back[0] = size_choice(jnp.where(upper, own[BACK], up[BACK]))
    lends = jnp.logical_and(upper, own[LENT] > 0)
    gives = jnp.logical_and(jnp.logical_not(upper), up[KEPT] > 0)

    def cut(col, row, place):
        at = pl.ds(pl.multiple_of(place, ROW_ALIGN), frame)
        for plane in range(2):
            packed[at, pl.ds(plane * frame, frame)] = side_by_side(window(band, (plane,), row, col, frame, across))

    @pl.when(jnp.logical_or(lends, gives))
    def _():
        base = jnp.where(upper, extent - frame, 0)
        rows = pl.ds(pl.multiple_of(base, ROW_ALIGN), frame)
        wait_all(start_all(
            [(tile.at[:, rows, lanes_of(b)], band.at[:, b, pl.ds(0, frame)]) for b in range(own_blocks)]
            + [(edge.at[:, :, lanes_of(b)], band.at[:, own_blocks + b, pl.ds(0, frame)]) for b in range(across)], sems))

        def one(slot, carry):
            @pl.when(jnp.logical_and(upper, own[FAR + slot] > 0))
            def _():
                cut(own[COL + slot], own[ROW + slot] - (extent - frame), own[PLACE + slot])

            @pl.when(jnp.logical_and(gives, up[NEAR + slot] > 0))
            def _():
                cut(up[COL + slot], 0, up[PLACE + slot])

            return carry

        lax.fori_loop(0, cap, one, 0)

        def shots(slot):
            at = pl.ds(pl.multiple_of(own[SHOT + slot], ROW_ALIGN), frame // 2)
            return [pltpu.make_async_copy(frames.at[slot, pl.ds(part * frame // 2, frame // 2)],
                                          packed.at[at, pl.ds(part * frame, frame)], sems.at[2 * slot + part])
                    for part in range(2)]

        for wait in range(2):
            for slot in range(cap):
                @pl.when(jnp.logical_and(lends, own[FAR + slot] > 0))
                def _():
                    for copy in shots(slot):
                        if wait:
                            copy.wait()
                        else:
                            copy.start()

        copy_out_rows(jnp.where(upper, own[FORTH], up[KEPT]), packed, out, chunk_sems)


def cut_pieces(phase, own, up, parity, tile, edge, frames):
    cap, frame, _ = frames.shape
    extent = tile.shape[-1]
    blocks = (extent + frame) // LANES
    rows = SIZES[-1]
    return pl.pallas_call(
        lambda *refs: cut_kernel(phase, *refs),
        out_shape=(
            jax.ShapeDtypeStruct((rows, 2 * frame), F32),
            jax.ShapeDtypeStruct((1,), jnp.int32),
            jax.ShapeDtypeStruct((1,), jnp.int32),
        ),
        in_specs=[smem_spec(), smem_spec(), smem_spec(), hbm_spec(), hbm_spec(), hbm_spec()],
        out_specs=(hbm_spec(), smem_spec(), smem_spec()),
        scratch_shapes=[
            pltpu.VMEM((2, blocks, 2 * frame, LANES), F32),
            pltpu.VMEM((rows + frame, 2 * frame), F32),
            pltpu.SemaphoreType.DMA((max(blocks, 2 * cap),)),
            pltpu.SemaphoreType.DMA((rows // CHUNK,)),
        ],
        compiler_params=params(60),
        name="cut_pieces",
    )(own, up, parity, tile, edge, frames)


def dot(one, two):
    return jnp.dot(one, two, preferred_element_type=F32)


def stacked(parts):
    return jnp.concatenate(parts, axis=0)


def lane_parts(array):
    half = array.shape[1] // 2
    return array[:, :half], array[:, half:]


def wave_stage(mode, probe, patch, waves):
    frame = probe.shape[2]
    for at in range(0, frame, STEP):
        rows = pl.ds(at, STEP)
        probe_real, probe_imag = probe[mode, 0, rows], probe[mode, 1, rows]
        patch_real, patch_imag = patch[0, rows], patch[1, rows]
        parts = [lane_parts(part) for part in (
            probe_real * patch_real - probe_imag * patch_imag, probe_real * patch_imag + probe_imag * patch_real)]
        waves[0, mode, rows] = side_by_side([near + far for near, far in parts]).astype(BF16)
        waves[1, mode, rows] = side_by_side([near - far for near, far in parts]).astype(BF16)


def rows_dot(mode, source, tables, first, product):
    for odd in range(2):
        product[odd, mode] = dot(source[odd, mode], tables[first + odd])


def columns_dot(mode, tables, first, source, product):
    for odd in range(2):
        product[odd, mode] = dot(tables[first + odd], source[odd, mode])


def half_stage(mode, product, halfway):
    half = product.shape[2] // 2
    for at in range(0, half, TILE_ROWS):
        near, far = pl.ds(at, TILE_ROWS), pl.ds(half + at, TILE_ROWS)
        upper = [product[odd, mode, near] for odd in range(2)]
        lower = [product[odd, mode, far] for odd in range(2)]
        for odd in range(2):
            mixed = [a + b if not odd else a - b for a, b in zip(upper, lower)]
            real, imag = zip(*[lane_parts(part) for part in mixed])
            halfway[odd, mode, near] = side_by_side(real).astype(BF16)
            halfway[odd, mode, far] = side_by_side(imag).astype(BF16)


def residual_stage(modes, frame, field, amplitude, waves):
    half = frame // 2
    for odd in range(2):
        for at in range(0, half, TILE_ROWS):
            near, far = pl.ds(at, TILE_ROWS), pl.ds(half + at, TILE_ROWS)
            real = [field[odd, mode, near] for mode in range(modes)]
            imag = [field[odd, mode, far] for mode in range(modes)]
            lit = sum(a * a + b * b for a, b in zip(real, imag))
            factor = 1.0 / frame - amplitude[odd, near] * lax.rsqrt(jnp.maximum(lit, float(frame * frame)))
            target = pl.ds(odd * half + at, TILE_ROWS)
            for mode in range(modes):
                parts = [lane_parts(real[mode] * factor), lane_parts(imag[mode] * factor)]
                for column in range(2):
                    waves[column, mode, target] = side_by_side([part[column] for part in parts]).astype(BF16)


def back_stage(mode, product, halfway):
    half = product.shape[2] // 2
    for odd in range(2):
        for at in range(0, half, TILE_ROWS):
            rows = pl.ds(odd * half + at, TILE_ROWS)
            even_part, odd_part = product[0, mode, rows], product[1, mode, rows]
            near, far = lane_parts(even_part + odd_part), lane_parts(even_part - odd_part)
            halfway[odd, mode, pl.ds(at, TILE_ROWS)] = side_by_side([near[0], far[0]]).astype(BF16)
            halfway[odd, mode, pl.ds(half + at, TILE_ROWS)] = side_by_side([near[1], far[1]]).astype(BF16)


def gradient_stage(some_modes, first, product, probe, piece):
    frame = probe.shape[2]
    half = frame // 2
    across = frame // LANES
    for at in range(0, half, TILE_ROWS):
        rows = [pl.ds(at, TILE_ROWS), pl.ds(half + at, TILE_ROWS)]
        grads = [[0.0, 0.0], [0.0, 0.0]]
        for mode in some_modes:
            mixed = [(product[0, mode, part], product[1, mode, part]) for part in rows]
            for side in range(2):
                back_real, back_imag = [a + b if not side else a - b for a, b in mixed]
                probe_real, probe_imag = probe[mode, 0, rows[side]], probe[mode, 1, rows[side]]
                grads[side][0] += probe_real * back_real + probe_imag * back_imag
                grads[side][1] += probe_real * back_imag - probe_imag * back_real
        for side in range(2):
            for plane in range(2):
                grad = grads[side][plane] * (1.0 / frame)
                for b in range(across):
                    where = (plane * across + b, rows[side], slice(None))
                    part = grad[:, b * LANES:(b + 1) * LANES]
                    piece[where] = part if first else piece[where] + part


def frame_step(patch, amplitude, probe, tables, waves, halfway, product, field, piece):
    modes, _, frame, _ = probe.shape
    for step in range(modes + 1):
        if step < modes:
            wave_stage(step, probe, patch, waves)
            rows_dot(step, waves, tables, 0, product)
        if step:
            half_stage(step - 1, product, halfway)
            columns_dot(step - 1, tables, 2, halfway, field)
    residual_stage(modes, frame, field, amplitude, waves)
    for step in range(modes + 1):
        if step < modes:
            rows_dot(step, waves, tables, 4, product)
        if step:
            back_stage(step - 1, product, halfway)
            columns_dot(step - 1, tables, 6, halfway, field)
        if step and step % 2 == 0:
            gradient_stage((step - 2, step - 1), step == 2, field, probe, piece)


def ordered_amplitude(measured, task, order, amplitude):
    frame = measured.shape[2]
    for odd in range(2):
        root = jnp.sqrt(side_by_side(
            [measured[task, b, pl.ds(odd, frame // 2, stride=2), :] for b in range(measured.shape[1])]))
        high = root.astype(BF16)
        low = (root - high.astype(F32)).astype(BF16)
        amplitude[odd] = dot(high, order) + dot(low, order)


def window(band, lead, row, col, height, across):
    return taken_from(
        [band[lead + (col // LANES + b, pl.ds(row, height), slice(None))] for b in range(across + 1)],
        lax.rem(col, LANES),
    )


def add_window(total, lead, parts, row, col, frame):
    for b, moved in enumerate(put_into(parts, lax.rem(col, LANES))):
        at = lead + (col // LANES + b, pl.ds(row, frame), slice(None))
        total[at] = total[at] + moved


def kernel_cost(frames, modes, frame):
    return pl.CostEstimate(
        flops=frames * modes * 4 * 4 * frame ** 3, bytes_accessed=16 * 1024 * 1024, transcendentals=0)


def frames_kernel(phases, own, up, parity, tile, edge, middle, frames, probe_in, tables_in, as_upper, as_lower, total_out, *rest):
    packed_outs = rest[:phases]
    (band, total, held, packed, piece, measured, probe, tables, patch, amplitude, waves, halfway, product, field, work,
     sems, shot_sems, held_sems, chunk_sems) = rest[phases:]
    cap, frame, _ = frames.shape
    extent = tile.shape[-1]
    across = frame // LANES
    own_blocks = extent // LANES
    half = frame // 2
    own_rows = pl.ds(frame, extent)

    first = start_all(
        [(tile.at[:, :, lanes_of(b)], band.at[:, b, own_rows]) for b in range(own_blocks)]
        + [(source.at[:, pl.ds(at, height), lanes_of(b)], band.at[:, own_blocks + b, pl.ds(frame + target, height)])
           for source, at, height, target in (
               (edge, 0, KEEP, 0), (middle, 0, extent - frame, KEEP), (edge, KEEP, frame - KEEP, KEEP + extent - frame))
           for b in range(across)]
        + [(probe_in, probe), (tables_in, tables)], sems)

    def mine(slot):
        return jnp.logical_and(slot < own[COUNT], own[FAR + slot] == 0)

    def borrowed(slot):
        return up[FAR + slot] > 0

    def shot_copies(slot, task, lent):
        if not lent:
            return [pltpu.make_async_copy(frames.at[slot, :, lanes_of(b)], measured.at[task, b], shot_sems.at[task, b])
                    for b in range(across)]
        at = pl.ds(pl.multiple_of(up[SHOT + slot], ROW_ALIGN), half)
        return [
            pltpu.make_async_copy(as_lower.at[at, lanes_of(part * across + b)],
                                  measured.at[task, b, pl.ds(part * half, half)], shot_sems.at[task, part * across + b])
            for part in range(2) for b in range(across)
        ]

    def held_copies(slot, task, lent):
        source, table = (as_lower, up) if lent else (as_upper, own)
        at = pl.ds(pl.multiple_of(table[PLACE + slot], ROW_ALIGN), frame)
        return [
            pltpu.make_async_copy(source.at[at, lanes_of(b)], held.at[task, b, pl.ds(frame, frame)], held_sems.at[task, b])
            for b in range(2 * across)
        ]

    def for_tasks(wait):
        for slot in range(cap):
            def run(copies):
                for copy in copies:
                    if wait:
                        copy.wait()
                    else:
                        copy.start()

            @pl.when(mine(slot))
            def _():
                run(shot_copies(slot, slot, False))

            @pl.when(own[NEAR + slot] > 0)
            def _():
                run(held_copies(slot, slot, False))

            @pl.when(borrowed(slot))
            def _():
                run(shot_copies(slot, cap + slot, True))
                run(held_copies(slot, cap + slot, True))

    for_tasks(False)
    for slot in range(cap):
        near = own[NEAR + slot]
        for field_at, value in (
            (ACTIVE, mine(slot).astype(jnp.int32)), (AT_ROW, own[ROW + slot] + frame), (AT_COL, own[COL + slot]),
            (LO, frame - near), (HI, frame), (START, near), (PIECE, own[PLACE + slot]), (SHIFT, frame - near), (ROLE, 0),
        ):
            work[slot, field_at] = value
        for field_at, value in (
            (ACTIVE, borrowed(slot).astype(jnp.int32)), (AT_ROW, up[ROW + slot] + frame - extent), (AT_COL, up[COL + slot]),
            (LO, 0), (HI, up[FAR + slot]), (START, frame), (PIECE, up[PLACE + slot]), (SHIFT, 0), (ROLE, 1),
        ):
            work[cap + slot, field_at] = value
    total[:, :, own_rows, :] = jnp.zeros((2, band.shape[1], extent, LANES), F32)
    wait_all(first)
    for_tasks(True)
    row_index = lax.broadcasted_iota(jnp.int32, (STEP, LANES), 0)

    def one(task, carry):
        @pl.when(work[task, ACTIVE] > 0)
        def _():
            row, col, start = work[task, AT_ROW], work[task, AT_COL], work[task, START]
            lo, hi = work[task, LO], work[task, HI]
            for at in range(0, frame, STEP):
                theirs = jnp.logical_and(row_index >= lo - at, row_index < hi - at)
                for plane in range(2):
                    near = window(band, (plane,), row + at, col, STEP, across)
                    other = [held[task, plane * across + b, pl.ds(start + at, STEP), :] for b in range(across)]
                    patch[plane, pl.ds(at, STEP)] = side_by_side([jnp.where(theirs, b, a) for a, b in zip(near, other)])
            ordered_amplitude(measured, task, tables[8], amplitude)
            frame_step(patch, amplitude, probe, tables, waves, halfway, product, field, piece)
            for at in range(0, frame, STEP):
                for plane in range(2):
                    parts = [piece[plane * across + b, pl.ds(at, STEP), :] for b in range(across)]
                    add_window(total, (plane,), parts, row + at, col, STEP)

            @pl.when(lo < hi)
            def _():
                target = pl.ds(pl.multiple_of(work[task, PIECE], ROW_ALIGN), frame)
                source = pl.ds(work[task, SHIFT], frame)
                for b in range(2 * across):
                    packed[work[task, ROLE], target, lanes_of(b)] = piece[b, source, :]

        return carry

    lax.fori_loop(0, 2 * cap, one, 0)
    end = start_all([(total.at[:, :, own_rows], total_out)], sems)
    for phase in range(phases):
        upper = parity[0] == phase
        role = jnp.where(upper, 0, 1)
        copy_out_rows(jnp.where(upper, own[KEPT], up[LENT]), packed.at[role], packed_outs[phase], chunk_sems)
    wait_all(end)


def frames_gradient(phases, own, up, parity, tile, edge, middle, frames, probe, tables, as_upper, as_lower):
    cap, frame, _ = frames.shape
    extent = tile.shape[-1]
    modes = probe.shape[0]
    tall = extent + 2 * frame
    blocks = (extent + frame) // LANES
    across = frame // LANES
    rows = as_upper.shape[0]
    kept_rows = cap * KEEP
    return pl.pallas_call(
        lambda *refs: frames_kernel(phases, *refs),
        out_shape=(jax.ShapeDtypeStruct((2, blocks, extent, LANES), F32),)
        + (jax.ShapeDtypeStruct(as_upper.shape, F32),) * phases,
        in_specs=[smem_spec()] * 3 + [hbm_spec()] * 8,
        out_specs=(hbm_spec(),) * (1 + phases),
        scratch_shapes=[
            pltpu.VMEM((2, blocks, tall, LANES), F32),
            pltpu.VMEM((2, blocks, tall, LANES), F32),
            pltpu.VMEM((2 * cap, 2 * across, 2 * frame, LANES), F32),
            pltpu.VMEM((2, kept_rows + frame, 2 * frame), F32),
            pltpu.VMEM((2 * across, 2 * frame, LANES), F32),
            pltpu.VMEM((2 * cap, across, frame, LANES), F32),
            pltpu.VMEM(probe.shape, F32),
            pltpu.VMEM(tables.shape, BF16),
            pltpu.VMEM((2, frame, frame), F32),
            pltpu.VMEM((2, frame // 2, frame), F32),
            pltpu.VMEM((2, modes, frame, frame), BF16),
            pltpu.VMEM((2, modes, frame, frame), BF16),
            pltpu.VMEM((2, modes, frame, frame), F32),
            pltpu.VMEM((2, modes, frame, frame), F32),
            pltpu.SMEM((2 * cap, 16), jnp.int32),
            pltpu.SemaphoreType.DMA((blocks + 2 * across + 2,)),
            pltpu.SemaphoreType.DMA((2 * cap, 2 * across)),
            pltpu.SemaphoreType.DMA((2 * cap, 2 * across)),
            pltpu.SemaphoreType.DMA((rows // CHUNK,)),
        ],
        compiler_params=params(55),
        cost_estimate=kernel_cost(cap, modes, frame),
        name="frames_gradient",
    )(own, up, parity, tile, edge, middle, frames, probe, tables, as_upper, as_lower)


def light_kernel(place, tables, probe, light_out, light, sem):
    modes, _, frame, _ = probe.shape
    own_blocks, extent, _ = light_out.shape
    across = frame // LANES
    inside = (pl.ds(across, own_blocks), pl.ds(frame, extent), slice(None))
    light[inside] = jnp.zeros((own_blocks, extent, LANES), F32)
    power = jnp.zeros((frame, frame), F32)
    for mode in range(modes):
        power += probe[mode, 0] * probe[mode, 0] + probe[mode, 1] * probe[mode, 1]
    power = halves(power)
    for down, right in ((0, 0), (0, 1), (1, 0), (1, 1)):
        back = down * TCOLS + right
        lead = jnp.maximum(place[0] - back, 0) * TABLE

        def lit(slot, carry, lead=lead, down=down, right=right):
            row = tables[lead + ROW + slot] + frame - down * extent
            col = tables[lead + COL + slot] + frame - right * extent

            @pl.when((row > 0) & (col > 0))
            def _():
                add_window(light, (), power, row, col, frame)

            return carry

        lax.fori_loop(0, jnp.where(place[0] >= back, tables[lead + COUNT], 0), lit, 0)
    copy = pltpu.make_async_copy(light.at[inside[0], inside[1]], light_out, sem)
    copy.start()
    copy.wait()


def light_plane(place, tables, probe, extent):
    frame = probe.shape[-1]
    wide = extent + 2 * frame
    return pl.pallas_call(
        light_kernel,
        out_shape=jax.ShapeDtypeStruct((extent // LANES, extent, LANES), F32),
        in_specs=[smem_spec()] * 2 + [vmem_spec()],
        out_specs=any_spec(),
        scratch_shapes=[pltpu.VMEM((wide // LANES, wide, LANES), F32), pltpu.SemaphoreType.DMA],
        compiler_params=params(9),
        cost_estimate=pl.CostEstimate(flops=0, bytes_accessed=4 * MIB, transcendentals=0),
        name="light_plane",
    )(place, tables, probe)


def add_pieces(frame, table, needed, field, pieces, band, blocks, height, row_of, held, sems, loads=()):
    across = frame // LANES
    cap = (held.shape[1] - KEEP) // KEEP
    chunks = (needed + CHUNK - 1) // CHUNK
    row_index = lax.broadcasted_iota(jnp.int32, (height, LANES), 0)

    def copies(chunk):
        at = pl.ds(pl.multiple_of(chunk * CHUNK, CHUNK), CHUNK)
        return [pltpu.make_async_copy(pieces.at[at, lanes_of(b)], held.at[b, at], sems.at[chunk * 2 * across + b])
                for b in range(2 * across)]

    def begin(chunk, carry):
        for copy in copies(chunk):
            copy.start()
        return carry

    def end(chunk, carry):
        for copy in copies(chunk):
            copy.wait()
        return carry

    def one(slot, carry):
        used = table[field + slot]
        first = table[COL + slot] // LANES

        @pl.when(jnp.logical_and(used > 0, jnp.logical_and(first + across >= blocks[0], first < blocks[1])))
        def _():
            at = pl.ds(pl.multiple_of(table[PLACE + slot], ROW_ALIGN), height)
            for plane in range(2):
                got = [jnp.where(row_index < used, held[plane * across + b, at, :], 0.0) for b in range(across)]
                for b, moved in enumerate(put_into(got, lax.rem(table[COL + slot], LANES))):
                    @pl.when(jnp.logical_and(first + b >= blocks[0], first + b < blocks[1]))
                    def _():
                        where = (plane, first + b - blocks[0], pl.ds(row_of(slot), height), slice(None))
                        band[where] = band[where] + moved

        return carry

    lax.fori_loop(0, chunks, begin, 0)
    lax.fori_loop(0, chunks, end, 0)
    wait_all(loads)

    @pl.when(needed > 0)
    def _():
        lax.fori_loop(0, cap, one, 0)


def join_right_kernel(frame, own, up, as_upper, as_lower, total, right_out, band, held, sems, piece_sems):
    across = frame // LANES
    blocks, extent = total.shape[1:3]
    rows = pl.ds(0, extent)
    reach = (blocks - across, blocks)
    loads = start_all([(total.at[:, pl.ds(blocks - across, across)], band.at[:, :, rows])], sems)
    add_pieces(frame, own, own[LENT], FAR, as_upper, band, reach, frame - KEEP, lambda slot: own[ROW + slot], held, piece_sems,
               loads)
    add_pieces(frame, up, up[KEPT], NEAR, as_lower, band, reach, KEEP, lambda slot: 0, held, piece_sems)
    wait_all(start_all([(band.at[:, :, rows], right_out)], sems))


def join_right(own, up, as_upper, as_lower, total, cap):
    frame = as_upper.shape[1] // 2
    extent = total.shape[2]
    across = frame // LANES
    rows = cap * KEEP
    return pl.pallas_call(
        lambda *refs: join_right_kernel(frame, *refs),
        out_shape=jax.ShapeDtypeStruct((2, across, extent, LANES), F32),
        in_specs=[smem_spec(), smem_spec(), hbm_spec(), hbm_spec(), hbm_spec()],
        out_specs=any_spec(),
        scratch_shapes=[
            pltpu.VMEM((2, across, extent + frame, LANES), F32),
            pltpu.VMEM((2 * across, rows + KEEP, LANES), F32),
            pltpu.SemaphoreType.DMA((1,)),
            pltpu.SemaphoreType.DMA((rows // CHUNK * 2 * across,)),
        ],
        compiler_params=params(56),
        name="join_right",
    )(own, up, as_upper, as_lower, total)


def join_own_kernel(frame, own, up, as_upper, as_lower, total_in, total_out, top, bottom, held, sems, piece_sems):
    own_blocks = top.shape[1]
    extent = total_in.shape[2]
    tail = frame - KEEP
    mine = pl.ds(0, own_blocks)
    reach = (0, own_blocks)

    def part(needed, rows, band, source, table, field, height, row_of):
        @pl.when(needed > 0)
        def _():
            loads = start_all([(total_in.at[:, mine, rows], band)], sems)
            add_pieces(frame, table, needed, field, source, band_of[field], reach, height, row_of, held, piece_sems, loads)
            wait_all(start_all([(band, total_out.at[:, mine, rows])], sems))

    band_of = {FAR: bottom, NEAR: top}
    part(own[LENT], pl.ds(extent - tail, tail), bottom.at[:, :, pl.ds(0, tail)], as_upper, own, FAR, tail,
         lambda slot: own[ROW + slot] - (extent - tail))
    part(up[KEPT], pl.ds(0, KEEP), top, as_lower, up, NEAR, KEEP, lambda slot: 0)


def join_own(own, up, as_upper, as_lower, total, cap):
    frame = as_upper.shape[1] // 2
    own_blocks = total.shape[2] // LANES
    across = frame // LANES
    rows = cap * KEEP
    return pl.pallas_call(
        lambda *refs: join_own_kernel(frame, *refs),
        out_shape=jax.ShapeDtypeStruct(total.shape, F32),
        in_specs=[smem_spec(), smem_spec(), hbm_spec(), hbm_spec(), hbm_spec()],
        out_specs=hbm_spec(),
        input_output_aliases={4: 0},
        scratch_shapes=[
            pltpu.VMEM((2, own_blocks, KEEP, LANES), F32),
            pltpu.VMEM((2, own_blocks, 2 * (frame - KEEP), LANES), F32),
            pltpu.VMEM((2 * across, rows + KEEP, LANES), F32),
            pltpu.SemaphoreType.DMA((1,)),
            pltpu.SemaphoreType.DMA((rows // CHUNK * 2 * across,)),
        ],
        compiler_params=params(56),
        name="join_own",
    )(own, up, as_upper, as_lower, total)


def right_half_kernel(tile, total, light, out):
    for b in range(total.shape[1]):
        below = 1.0 / (light[b] + 1.0)
        for plane in range(2):
            out[plane, :, lanes_of(b)] = tile[plane, :, lanes_of(b)] - total[plane, b] * below


def right_half(tile, total, light):
    extent = tile.shape[-1]
    across = total.shape[1] * LANES - extent
    part = (extent - across) // LANES
    tall = 128
    return pl.pallas_call(
        right_half_kernel,
        grid=(extent // tall,),
        out_shape=jax.ShapeDtypeStruct(tile.shape, F32),
        in_specs=[
            pl.BlockSpec((2, tall, extent - across), lambda i: (0, i, 1)),
            pl.BlockSpec((2, part, tall, LANES), lambda i: (0, 1, i, 0)),
            pl.BlockSpec((part, tall, LANES), lambda i: (1, i, 0)),
        ],
        out_specs=pl.BlockSpec((2, tall, extent - across), lambda i: (0, i, 1)),
        compiler_params=params(8),
        name="right_half",
    )(tile, total, light)


def left_half_kernel(tile, total, light, left, begun, out):
    for b in range(total.shape[1]):
        below = 1.0 / (light[b] + 1.0)
        for plane in range(2):
            grad = total[plane, b] + left[plane, b]
            out[plane, :, lanes_of(b)] = tile[plane, :, lanes_of(b)] - grad * below


def left_half(tile, total, light, left, begun):
    extent = tile.shape[-1]
    across = left.shape[1]
    tall = 256
    return pl.pallas_call(
        left_half_kernel,
        grid=(extent // tall,),
        out_shape=jax.ShapeDtypeStruct(tile.shape, F32),
        in_specs=[
            pl.BlockSpec((2, tall, across * LANES), lambda i: (0, i, 0)),
            pl.BlockSpec((2, across, tall, LANES), lambda i: (0, 0, i, 0)),
            pl.BlockSpec((across, tall, LANES), lambda i: (0, i, 0)),
            pl.BlockSpec((2, across, tall, LANES), lambda i: (0, 0, i, 0)),
            any_spec(),
        ],
        out_specs=pl.BlockSpec((2, tall, across * LANES), lambda i: (0, i, 0)),
        input_output_aliases={4: 0},
        compiler_params=params(8),
        name="left_half",
    )(tile, total, light, left, begun)


def body(object_tiles, probe, positions, frames, counts):
    tile = object_tiles[0]
    extent = tile.shape[-1]
    frame = frames.shape[-1]
    cap = frames.shape[1]
    peers = lax.axis_size("scan")
    place = lax.axis_index("scan").astype(jnp.int32).reshape(1)
    tile_row = lax.axis_index("scan") // TCOLS
    phases = min(2, peers // TCOLS - 1)
    tables = dft_tables(frame)
    parity = (tile_row % 2).reshape(1)
    even = tile_row % 2 == 0

    own, edge, middle = prepare(positions, counts, tile, frame)
    up = shifted(own, "scan", TCOLS)
    edge = shifted(edge, "scan", -1)
    middle = shifted(middle, "scan", -1)
    everyone = lax.all_gather(own, "scan", tiled=True)

    def exchange(phase, packed, choice):
        uppers = [k for k in range(peers - TCOLS) if k // TCOLS % 2 == phase]
        pairs = [(k, k + TCOLS) for k in uppers] + [(k + TCOLS, k) for k in uppers]

        def sender(size):
            def run(data):
                return lax.dynamic_update_slice(data, lax.ppermute(data[:size], "scan", pairs), (0, 0))
            return run

        branches = [lambda data: data] + [sender(size) for size in SIZES if size <= packed.shape[0]]
        return lax.switch(choice.reshape(()), branches, packed)

    def by_role(arrays):
        if len(arrays) == 1:
            return arrays[0], arrays[0]
        return jnp.where(even, arrays[0], arrays[1]), jnp.where(even, arrays[1], arrays[0])

    cuts = [cut_pieces(phase, own, up, parity, tile, edge, frames[0]) for phase in range(phases)]
    received = by_role([exchange(phase, cut[0], cut[1]) for phase, cut in enumerate(cuts)])
    total, *packed = frames_gradient(
        phases, own, up, parity, tile, edge, middle, frames[0], probe, tables, *received)
    returned = by_role([exchange(phase, packed[phase], cut[2]) for phase, cut in enumerate(cuts)])
    right = join_right(own, up, *returned, total, cap)
    right, total, everyone = lax.optimization_barrier((right, total, everyone))
    left = shifted(right, "scan", 1)
    total = join_own(own, up, *returned, total, cap)
    light = light_plane(place, everyone, probe, extent)
    begun = right_half(tile, total, light)
    return left_half(tile, total, light, left, begun)[None]


def solution(mesh):
    return jax.shard_map(
        body,
        mesh=mesh,
        in_specs=(
            P(("grp", "scan"), None, None, None),
            P(),
            P(("grp", "scan"), None, None),
            P(("grp", "scan"), None, None, None),
            P(("grp", "scan")),
        ),
        out_specs=P(("grp", "scan"), None, None, None),
        check_vma=False,
    )
```

```python
import math

import jax
import jax.numpy as jnp
import numpy as np
from jax import lax
from jax.experimental import pallas as pl
from jax.experimental.pallas import tpu as pltpu
from jax.sharding import PartitionSpec as P

TCOLS = 8
LANES = 128
ROW_ALIGN = 8
CHUNK = 64
STEP = 32
TILE_ROWS = 16
SIZES = (32, 64, 96, 128, 160, 192, 224, 256, 320, 384, 448, 512, 640, 768, 960, 1344)
MIB = 1024 * 1024
F32 = jnp.float32
BF16 = jnp.bfloat16

KEEP = 160
ROW, COL, NEAR, FAR, PLACE, SHOT = 0, 8, 16, 24, 32, 40
COUNT, KEPT, LENT, FORTH, BACK = 48, 49, 50, 51, 52
TABLE = 64

ACTIVE, AT_ROW, AT_COL, LO, HI, START, PIECE, SHIFT, ROLE = range(9)


def dft_tables(frame):
    near = np.arange(frame // 2, dtype=np.int64)
    blocks = []
    for odd in range(2):
        phase = (near[:, None] * (2 * near[None, :] + odd) % frame).astype(np.float64) * (2.0 * math.pi / frame)
        c, s = np.cos(phase), np.sin(phase)
        ahead = np.block([[c, -s], [s, c]])
        back = np.block([[c.T, s.T], [-s.T, c.T]])
        blocks.append((ahead, ahead.T, back, back.T))
    order = np.zeros((frame, frame))
    order[2 * near, near] = 1.0
    order[2 * near + 1, near + frame // 2] = 1.0
    tables = [blocks[odd][kind] for kind in range(4) for odd in range(2)] + [order]
    return jnp.asarray(np.stack(tables), F32).astype(BF16)


def shifted(array, axis, by):
    peers = lax.axis_size(axis)
    pairs = [(i, i + by) for i in range(peers) if 0 <= i + by < peers]
    return lax.ppermute(array, axis, pairs)


def any_spec():
    return pl.BlockSpec(memory_space=pl.ANY)


def hbm_spec():
    return pl.BlockSpec(memory_space=pltpu.HBM)


def smem_spec():
    return pl.BlockSpec(memory_space=pltpu.SMEM)


def vmem_spec():
    return pl.BlockSpec(memory_space=pltpu.VMEM)


def params(mebibytes):
    return pltpu.CompilerParams(vmem_limit_bytes=mebibytes * MIB)


def taken_from(blocks, by):
    lane = lax.broadcasted_iota(jnp.int32, blocks[0].shape, 1)
    rolled = [pltpu.roll(block, lax.rem(LANES - by, LANES), axis=1) for block in blocks]
    return [jnp.where(lane < LANES - by, one, two) for one, two in zip(rolled[:-1], rolled[1:])]


def put_into(blocks, by):
    lane = lax.broadcasted_iota(jnp.int32, blocks[0].shape, 1)
    rolled = [pltpu.roll(block, by, axis=1) for block in blocks]
    none = jnp.zeros_like(blocks[0])
    return [jnp.where(lane >= by, one, two) for one, two in zip(rolled + [none], [none] + rolled)]


def start_all(pairs, sems, first=0):
    copies = [pltpu.make_async_copy(source, target, sems.at[first + at]) for at, (source, target) in enumerate(pairs)]
    for copy in copies:
        copy.start()
    return copies


def wait_all(copies):
    for copy in copies:
        copy.wait()


def lanes_of(block):
    return pl.ds(block * LANES, LANES)


def side_by_side(parts):
    return jnp.concatenate(parts, axis=1)


def halves(array):
    return [array[:, :LANES], array[:, LANES:]]


def copy_out_rows(needed, packed, out, sems):
    chunks = (needed + CHUNK - 1) // CHUNK

    def copy(chunk):
        at = pl.ds(pl.multiple_of(chunk * CHUNK, CHUNK), CHUNK)
        return pltpu.make_async_copy(packed.at[at], out.at[at], sems.at[chunk])

    def begin(chunk, carry):
        copy(chunk).start()
        return carry

    def end(chunk, carry):
        copy(chunk).wait()
        return carry

    lax.fori_loop(0, chunks, begin, 0)
    lax.fori_loop(0, chunks, end, 0)


def up_to(value, step):
    return (value + step - 1) // step * step


def size_choice(needed):
    choice = jnp.where(needed > 0, 1, 0)
    for size in SIZES:
        choice = choice + jnp.where(needed > size, 1, 0)
    return choice


def prep_kernel(positions, counts, tile, table, edge, middle, sems):
    cap = positions.shape[2]
    extent = tile.shape[-1]
    frame = edge.shape[-1]
    count = counts[0]
    lanes = pl.ds(0, frame)
    copies = start_all([
        (tile.at[:, pl.ds(0, KEEP), lanes], edge.at[:, pl.ds(0, KEEP)]),
        (tile.at[:, pl.ds(KEEP + extent - frame, frame - KEEP), lanes], edge.at[:, pl.ds(KEEP, frame - KEEP)]),
        (tile.at[:, pl.ds(KEEP, extent - frame), lanes], middle),
    ], sems)
    kept, lent, shots = jnp.int32(0), jnp.int32(0), jnp.int32(0)
    for at in range(TABLE):
        table[at] = 0
    for slot in range(cap):
        row = lax.rem(positions[0, 0, slot], extent)
        col = lax.rem(positions[0, 1, slot], extent)
        below = jnp.where(slot < count, jnp.maximum(row + (frame - extent), 0), 0)
        stays = below <= KEEP
        near = jnp.where(stays, below, 0)
        far = jnp.where(stays, 0, frame - below)
        table[ROW + slot] = row
        table[COL + slot] = col
        table[NEAR + slot] = near
        table[FAR + slot] = far
        table[PLACE + slot] = jnp.where(stays, kept, lent)
        table[SHOT + slot] = shots
        kept = kept + up_to(near, ROW_ALIGN)
        lent = lent + up_to(far, ROW_ALIGN)
        shots = shots + jnp.where(stays, 0, frame // 2)
    for slot in range(cap):
        table[SHOT + slot] = table[SHOT + slot] + lent
    table[COUNT] = count
    table[KEPT] = kept
    table[LENT] = lent
    table[FORTH] = jnp.maximum(kept, lent + shots)
    table[BACK] = jnp.maximum(kept, lent)
    wait_all(copies)


def prepare(positions, counts, tile, frame):
    extent = tile.shape[-1]
    return pl.pallas_call(
        prep_kernel,
        out_shape=(
            jax.ShapeDtypeStruct((TABLE,), jnp.int32),
            jax.ShapeDtypeStruct((2, frame, frame), F32),
            jax.ShapeDtypeStruct((2, extent - frame, frame), F32),
        ),
        in_specs=[smem_spec(), smem_spec(), hbm_spec()],
        out_specs=(smem_spec(), vmem_spec(), vmem_spec()),
        scratch_shapes=[pltpu.SemaphoreType.DMA((3,))],
        compiler_params=params(62),
        name="prepare",
    )(jnp.swapaxes(positions, 1, 2), counts, tile)


def cut_kernel(phase, own, up, parity, tile, edge, frames, out, forth, back, band, packed, sems, chunk_sems):
    cap, frame, _ = frames.shape
    extent = tile.shape[-1]
    across = frame // LANES
    own_blocks = extent // LANES
    upper = parity[0] == phase
    forth[0] = size_choice(jnp.where(upper, own[FORTH], up[FORTH]))
    back[0] = size_choice(jnp.where(upper, own[BACK], up[BACK]))
    lends = jnp.logical_and(upper, own[LENT] > 0)
    gives = jnp.logical_and(jnp.logical_not(upper), up[KEPT] > 0)

    def cut(col, row, place):
        at = pl.ds(pl.multiple_of(place, ROW_ALIGN), frame)
        for plane in range(2):
            packed[at, pl.ds(plane * frame, frame)] = side_by_side(window(band, (plane,), row, col, frame, across))

    @pl.when(jnp.logical_or(lends, gives))
    def _():
        base = jnp.where(upper, extent - frame, 0)
        rows = pl.ds(pl.multiple_of(base, ROW_ALIGN), frame)
        wait_all(start_all(
            [(tile.at[:, rows, lanes_of(b)], band.at[:, b, pl.ds(0, frame)]) for b in range(own_blocks)]
            + [(edge.at[:, :, lanes_of(b)], band.at[:, own_blocks + b, pl.ds(0, frame)]) for b in range(across)], sems))

        def one(slot, carry):
            @pl.when(jnp.logical_and(upper, own[FAR + slot] > 0))
            def _():
                cut(own[COL + slot], own[ROW + slot] - (extent - frame), own[PLACE + slot])

            @pl.when(jnp.logical_and(gives, up[NEAR + slot] > 0))
            def _():
                cut(up[COL + slot], 0, up[PLACE + slot])

            return carry

        lax.fori_loop(0, cap, one, 0)

        def shots(slot):
            at = pl.ds(pl.multiple_of(own[SHOT + slot], ROW_ALIGN), frame // 2)
            return [pltpu.make_async_copy(frames.at[slot, pl.ds(part * frame // 2, frame // 2)],
                                          packed.at[at, pl.ds(part * frame, frame)], sems.at[2 * slot + part])
                    for part in range(2)]

        for wait in range(2):
            for slot in range(cap):
                @pl.when(jnp.logical_and(lends, own[FAR + slot] > 0))
                def _():
                    for copy in shots(slot):
                        if wait:
                            copy.wait()
                        else:
                            copy.start()

        copy_out_rows(jnp.where(upper, own[FORTH], up[KEPT]), packed, out, chunk_sems)


def cut_pieces(phase, own, up, parity, tile, edge, frames):
    cap, frame, _ = frames.shape
    extent = tile.shape[-1]
    blocks = (extent + frame) // LANES
    rows = SIZES[-1]
    return pl.pallas_call(
        lambda *refs: cut_kernel(phase, *refs),
        out_shape=(
            jax.ShapeDtypeStruct((rows, 2 * frame), F32),
            jax.ShapeDtypeStruct((1,), jnp.int32),
            jax.ShapeDtypeStruct((1,), jnp.int32),
        ),
        in_specs=[smem_spec(), smem_spec(), smem_spec(), hbm_spec(), hbm_spec(), hbm_spec()],
        out_specs=(hbm_spec(), smem_spec(), smem_spec()),
        scratch_shapes=[
            pltpu.VMEM((2, blocks, 2 * frame, LANES), F32),
            pltpu.VMEM((rows + frame, 2 * frame), F32),
            pltpu.SemaphoreType.DMA((max(blocks, 2 * cap),)),
            pltpu.SemaphoreType.DMA((rows // CHUNK,)),
        ],
        compiler_params=params(60),
        name="cut_pieces",
    )(own, up, parity, tile, edge, frames)


def dot(one, two):
    return jnp.dot(one, two, preferred_element_type=F32)


def stacked(parts):
    return jnp.concatenate(parts, axis=0)


def lane_parts(array):
    half = array.shape[1] // 2
    return array[:, :half], array[:, half:]


def wave_stage(mode, probe, patch, waves):
    frame = probe.shape[2]
    for at in range(0, frame, STEP):
        rows = pl.ds(at, STEP)
        probe_real, probe_imag = probe[mode, 0, rows], probe[mode, 1, rows]
        patch_real, patch_imag = patch[0, rows], patch[1, rows]
        parts = [lane_parts(part) for part in (
            probe_real * patch_real - probe_imag * patch_imag, probe_real * patch_imag + probe_imag * patch_real)]
        waves[0, mode, rows] = side_by_side([near + far for near, far in parts]).astype(BF16)
        waves[1, mode, rows] = side_by_side([near - far for near, far in parts]).astype(BF16)


def rows_dot(mode, source, tables, first, product):
    for odd in range(2):
        product[odd, mode] = dot(source[odd, mode], tables[first + odd])


def columns_dot(mode, tables, first, source, product):
    for odd in range(2):
        product[odd, mode] = dot(tables[first + odd], source[odd, mode])


def half_stage(mode, product, halfway):
    half = product.shape[2] // 2
    for at in range(0, half, TILE_ROWS):
        near, far = pl.ds(at, TILE_ROWS), pl.ds(half + at, TILE_ROWS)
        upper = [product[odd, mode, near] for odd in range(2)]
        lower = [product[odd, mode, far] for odd in range(2)]
        for odd in range(2):
            mixed = [a + b if not odd else a - b for a, b in zip(upper, lower)]
            real, imag = zip(*[lane_parts(part) for part in mixed])
            halfway[odd, mode, near] = side_by_side(real).astype(BF16)
            halfway[odd, mode, far] = side_by_side(imag).astype(BF16)


def residual_stage(modes, frame, field, amplitude, waves):
    half = frame // 2
    for odd in range(2):
        for at in range(0, half, TILE_ROWS):
            near, far = pl.ds(at, TILE_ROWS), pl.ds(half + at, TILE_ROWS)
            real = [field[odd, mode, near] for mode in range(modes)]
            imag = [field[odd, mode, far] for mode in range(modes)]
            lit = sum(a * a + b * b for a, b in zip(real, imag))
            factor = 1.0 / frame - amplitude[odd, near] * lax.rsqrt(jnp.maximum(lit, float(frame * frame)))
            target = pl.ds(odd * half + at, TILE_ROWS)
            for mode in range(modes):
                parts = [lane_parts(real[mode] * factor), lane_parts(imag[mode] * factor)]
                for column in range(2):
                    waves[column, mode, target] = side_by_side([part[column] for part in parts]).astype(BF16)


def back_stage(mode, product, halfway):
    half = product.shape[2] // 2
    for odd in range(2):
        for at in range(0, half, TILE_ROWS):
            rows = pl.ds(odd * half + at, TILE_ROWS)
            even_part, odd_part = product[0, mode, rows], product[1, mode, rows]
            near, far = lane_parts(even_part + odd_part), lane_parts(even_part - odd_part)
            halfway[odd, mode, pl.ds(at, TILE_ROWS)] = side_by_side([near[0], far[0]]).astype(BF16)
            halfway[odd, mode, pl.ds(half + at, TILE_ROWS)] = side_by_side([near[1], far[1]]).astype(BF16)


def gradient_stage(some_modes, first, product, probe, piece):
    frame = probe.shape[2]
    half = frame // 2
    across = frame // LANES
    for at in range(0, half, TILE_ROWS):
        rows = [pl.ds(at, TILE_ROWS), pl.ds(half + at, TILE_ROWS)]
        grads = [[0.0, 0.0], [0.0, 0.0]]
        for mode in some_modes:
            mixed = [(product[0, mode, part], product[1, mode, part]) for part in rows]
            for side in range(2):
                back_real, back_imag = [a + b if not side else a - b for a, b in mixed]
                probe_real, probe_imag = probe[mode, 0, rows[side]], probe[mode, 1, rows[side]]
                grads[side][0] += probe_real * back_real + probe_imag * back_imag
                grads[side][1] += probe_real * back_imag - probe_imag * back_real
        for side in range(2):
            for plane in range(2):
                grad = grads[side][plane] * (1.0 / frame)
                for b in range(across):
                    where = (plane * across + b, rows[side], slice(None))
                    part = grad[:, b * LANES:(b + 1) * LANES]
                    piece[where] = part if first else piece[where] + part


def frame_step(patch, amplitude, probe, tables, waves, halfway, product, field, piece):
    modes, _, frame, _ = probe.shape
    for step in range(modes + 1):
        if step < modes:
            wave_stage(step, probe, patch, waves)
            rows_dot(step, waves, tables, 0, product)
        if step:
            half_stage(step - 1, product, halfway)
            columns_dot(step - 1, tables, 2, halfway, field)
    residual_stage(modes, frame, field, amplitude, waves)
    for step in range(modes + 1):
        if step < modes:
            rows_dot(step, waves, tables, 4, product)
        if step:
            back_stage(step - 1, product, halfway)
            columns_dot(step - 1, tables, 6, halfway, field)
        if step and step % 2 == 0:
            gradient_stage((step - 2, step - 1), step == 2, field, probe, piece)


def ordered_amplitude(measured, task, order, amplitude):
    frame = measured.shape[2]
    for odd in range(2):
        root = jnp.sqrt(side_by_side(
            [measured[task, b, pl.ds(odd, frame // 2, stride=2), :] for b in range(measured.shape[1])]))
        high = root.astype(BF16)
        low = (root - high.astype(F32)).astype(BF16)
        amplitude[odd] = dot(high, order) + dot(low, order)


def window(band, lead, row, col, height, across):
    return taken_from(
        [band[lead + (col // LANES + b, pl.ds(row, height), slice(None))] for b in range(across + 1)],
        lax.rem(col, LANES),
    )


def add_window(total, lead, parts, row, col, frame):
    for b, moved in enumerate(put_into(parts, lax.rem(col, LANES))):
        at = lead + (col // LANES + b, pl.ds(row, frame), slice(None))
        total[at] = total[at] + moved


def kernel_cost(frames, modes, frame):
    return pl.CostEstimate(
        flops=frames * modes * 4 * 4 * frame ** 3, bytes_accessed=16 * 1024 * 1024, transcendentals=0)


def frames_kernel(phases, own, up, parity, tile, edge, middle, frames, probe_in, tables_in, as_upper, as_lower, total_out, *rest):
    packed_outs = rest[:phases]
    (band, total, held, packed, piece, measured, probe, tables, patch, amplitude, waves, halfway, product, field, work,
     sems, shot_sems, held_sems, chunk_sems) = rest[phases:]
    cap, frame, _ = frames.shape
    extent = tile.shape[-1]
    across = frame // LANES
    own_blocks = extent // LANES
    half = frame // 2
    own_rows = pl.ds(frame, extent)

    first = start_all(
        [(tile.at[:, :, lanes_of(b)], band.at[:, b, own_rows]) for b in range(own_blocks)]
        + [(source.at[:, pl.ds(at, height), lanes_of(b)], band.at[:, own_blocks + b, pl.ds(frame + target, height)])
           for source, at, height, target in (
               (edge, 0, KEEP, 0), (middle, 0, extent - frame, KEEP), (edge, KEEP, frame - KEEP, KEEP + extent - frame))
           for b in range(across)]
        + [(probe_in, probe), (tables_in, tables)], sems)

    def mine(slot):
        return jnp.logical_and(slot < own[COUNT], own[FAR + slot] == 0)

    def borrowed(slot):
        return up[FAR + slot] > 0

    def shot_copies(slot, task, lent):
        if not lent:
            return [pltpu.make_async_copy(frames.at[slot, :, lanes_of(b)], measured.at[task, b], shot_sems.at[task, b])
                    for b in range(across)]
        at = pl.ds(pl.multiple_of(up[SHOT + slot], ROW_ALIGN), half)
        return [
            pltpu.make_async_copy(as_lower.at[at, lanes_of(part * across + b)],
                                  measured.at[task, b, pl.ds(part * half, half)], shot_sems.at[task, part * across + b])
            for part in range(2) for b in range(across)
        ]

    def held_copies(slot, task, lent):
        source, table = (as_lower, up) if lent else (as_upper, own)
        at = pl.ds(pl.multiple_of(table[PLACE + slot], ROW_ALIGN), frame)
        return [
            pltpu.make_async_copy(source.at[at, lanes_of(b)], held.at[task, b, pl.ds(frame, frame)], held_sems.at[task, b])
            for b in range(2 * across)
        ]

    def for_tasks(wait):
        for slot in range(cap):
            def run(copies):
                for copy in copies:
                    if wait:
                        copy.wait()
                    else:
                        copy.start()

            @pl.when(mine(slot))
            def _():
                run(shot_copies(slot, slot, False))

            @pl.when(own[NEAR + slot] > 0)
            def _():
                run(held_copies(slot, slot, False))

            @pl.when(borrowed(slot))
            def _():
                run(shot_copies(slot, cap + slot, True))
                run(held_copies(slot, cap + slot, True))

    for_tasks(False)
    for slot in range(cap):
        near = own[NEAR + slot]
        for field_at, value in (
            (ACTIVE, mine(slot).astype(jnp.int32)), (AT_ROW, own[ROW + slot] + frame), (AT_COL, own[COL + slot]),
            (LO, frame - near), (HI, frame), (START, near), (PIECE, own[PLACE + slot]), (SHIFT, frame - near), (ROLE, 0),
        ):
            work[slot, field_at] = value
        for field_at, value in (
            (ACTIVE, borrowed(slot).astype(jnp.int32)), (AT_ROW, up[ROW + slot] + frame - extent), (AT_COL, up[COL + slot]),
            (LO, 0), (HI, up[FAR + slot]), (START, frame), (PIECE, up[PLACE + slot]), (SHIFT, 0), (ROLE, 1),
        ):
            work[cap + slot, field_at] = value
    total[:, :, own_rows, :] = jnp.zeros((2, band.shape[1], extent, LANES), F32)
    wait_all(first)
    for_tasks(True)
    row_index = lax.broadcasted_iota(jnp.int32, (STEP, LANES), 0)

    def one(task, carry):
        @pl.when(work[task, ACTIVE] > 0)
        def _():
            row, col, start = work[task, AT_ROW], work[task, AT_COL], work[task, START]
            lo, hi = work[task, LO], work[task, HI]
            for at in range(0, frame, STEP):
                theirs = jnp.logical_and(row_index >= lo - at, row_index < hi - at)
                for plane in range(2):
                    near = window(band, (plane,), row + at, col, STEP, across)
                    other = [held[task, plane * across + b, pl.ds(start + at, STEP), :] for b in range(across)]
                    patch[plane, pl.ds(at, STEP)] = side_by_side([jnp.where(theirs, b, a) for a, b in zip(near, other)])
            ordered_amplitude(measured, task, tables[8], amplitude)
            frame_step(patch, amplitude, probe, tables, waves, halfway, product, field, piece)
            for at in range(0, frame, STEP):
                for plane in range(2):
                    parts = [piece[plane * across + b, pl.ds(at, STEP), :] for b in range(across)]
                    add_window(total, (plane,), parts, row + at, col, STEP)

            @pl.when(lo < hi)
            def _():
                target = pl.ds(pl.multiple_of(work[task, PIECE], ROW_ALIGN), frame)
                source = pl.ds(work[task, SHIFT], frame)
                for b in range(2 * across):
                    packed[work[task, ROLE], target, lanes_of(b)] = piece[b, source, :]

        return carry

    lax.fori_loop(0, 2 * cap, one, 0)
    end = start_all([(total.at[:, :, own_rows], total_out)], sems)
    for phase in range(phases):
        upper = parity[0] == phase
        role = jnp.where(upper, 0, 1)
        copy_out_rows(jnp.where(upper, own[KEPT], up[LENT]), packed.at[role], packed_outs[phase], chunk_sems)
    wait_all(end)


def frames_gradient(phases, own, up, parity, tile, edge, middle, frames, probe, tables, as_upper, as_lower):
    cap, frame, _ = frames.shape
    extent = tile.shape[-1]
    modes = probe.shape[0]
    tall = extent + 2 * frame
    blocks = (extent + frame) // LANES
    across = frame // LANES
    rows = as_upper.shape[0]
    kept_rows = cap * KEEP
    return pl.pallas_call(
        lambda *refs: frames_kernel(phases, *refs),
        out_shape=(jax.ShapeDtypeStruct((2, blocks, extent, LANES), F32),)
        + (jax.ShapeDtypeStruct(as_upper.shape, F32),) * phases,
        in_specs=[smem_spec()] * 3 + [hbm_spec()] * 8,
        out_specs=(hbm_spec(),) * (1 + phases),
        scratch_shapes=[
            pltpu.VMEM((2, blocks, tall, LANES), F32),
            pltpu.VMEM((2, blocks, tall, LANES), F32),
            pltpu.VMEM((2 * cap, 2 * across, 2 * frame, LANES), F32),
            pltpu.VMEM((2, kept_rows + frame, 2 * frame), F32),
            pltpu.VMEM((2 * across, 2 * frame, LANES), F32),
            pltpu.VMEM((2 * cap, across, frame, LANES), F32),
            pltpu.VMEM(probe.shape, F32),
            pltpu.VMEM(tables.shape, BF16),
            pltpu.VMEM((2, frame, frame), F32),
            pltpu.VMEM((2, frame // 2, frame), F32),
            pltpu.VMEM((2, modes, frame, frame), BF16),
            pltpu.VMEM((2, modes, frame, frame), BF16),
            pltpu.VMEM((2, modes, frame, frame), F32),
            pltpu.VMEM((2, modes, frame, frame), F32),
            pltpu.SMEM((2 * cap, 16), jnp.int32),
            pltpu.SemaphoreType.DMA((blocks + 2 * across + 2,)),
            pltpu.SemaphoreType.DMA((2 * cap, 2 * across)),
            pltpu.SemaphoreType.DMA((2 * cap, 2 * across)),
            pltpu.SemaphoreType.DMA((rows // CHUNK,)),
        ],
        compiler_params=params(55),
        cost_estimate=kernel_cost(cap, modes, frame),
        name="frames_gradient",
    )(own, up, parity, tile, edge, middle, frames, probe, tables, as_upper, as_lower)


def light_kernel(own, up, beside, probe, light_out, light, sem):
    modes, _, frame, _ = probe.shape
    own_blocks, extent, _ = light_out.shape
    across = frame // LANES
    inside = (pl.ds(across, own_blocks), pl.ds(frame, extent), slice(None))
    light[inside] = jnp.zeros((own_blocks, extent, LANES), F32)
    power = jnp.zeros((frame, frame), F32)
    for mode in range(modes):
        power += probe[mode, 0] * probe[mode, 0] + probe[mode, 1] * probe[mode, 1]
    power = halves(power)
    for table, lead, down, right in ((own, 0, 0, 0), (beside, 0, 0, 1), (up, 0, 1, 0), (beside, TABLE, 1, 1)):

        def lit(slot, carry, table=table, lead=lead, down=down, right=right):
            row = table[lead + ROW + slot] + frame - down * extent
            col = table[lead + COL + slot] + frame - right * extent

            @pl.when((row > 0) & (col > 0))
            def _():
                add_window(light, (), power, row, col, frame)

            return carry

        lax.fori_loop(0, table[lead + COUNT], lit, 0)
    copy = pltpu.make_async_copy(light.at[inside[0], inside[1]], light_out, sem)
    copy.start()
    copy.wait()


def light_plane(own, up, beside, probe, extent):
    frame = probe.shape[-1]
    wide = extent + 2 * frame
    return pl.pallas_call(
        light_kernel,
        out_shape=jax.ShapeDtypeStruct((extent // LANES, extent, LANES), F32),
        in_specs=[smem_spec()] * 3 + [vmem_spec()],
        out_specs=any_spec(),
        scratch_shapes=[pltpu.VMEM((wide // LANES, wide, LANES), F32), pltpu.SemaphoreType.DMA],
        compiler_params=params(9),
        cost_estimate=pl.CostEstimate(flops=0, bytes_accessed=4 * MIB, transcendentals=0),
        name="light_plane",
    )(own, up, beside, probe)


def add_pieces(frame, table, needed, field, pieces, band, blocks, height, row_of, held, sems, loads=()):
    across = frame // LANES
    cap = (held.shape[1] - KEEP) // KEEP
    chunks = (needed + CHUNK - 1) // CHUNK
    row_index = lax.broadcasted_iota(jnp.int32, (height, LANES), 0)

    def copies(chunk):
        at = pl.ds(pl.multiple_of(chunk * CHUNK, CHUNK), CHUNK)
        return [pltpu.make_async_copy(pieces.at[at, lanes_of(b)], held.at[b, at], sems.at[chunk * 2 * across + b])
                for b in range(2 * across)]

    def begin(chunk, carry):
        for copy in copies(chunk):
            copy.start()
        return carry

    def end(chunk, carry):
        for copy in copies(chunk):
            copy.wait()
        return carry

    def one(slot, carry):
        used = table[field + slot]
        first = table[COL + slot] // LANES

        @pl.when(jnp.logical_and(used > 0, jnp.logical_and(first + across >= blocks[0], first < blocks[1])))
        def _():
            at = pl.ds(pl.multiple_of(table[PLACE + slot], ROW_ALIGN), height)
            for plane in range(2):
                got = [jnp.where(row_index < used, held[plane * across + b, at, :], 0.0) for b in range(across)]
                for b, moved in enumerate(put_into(got, lax.rem(table[COL + slot], LANES))):
                    @pl.when(jnp.logical_and(first + b >= blocks[0], first + b < blocks[1]))
                    def _():
                        where = (plane, first + b - blocks[0], pl.ds(row_of(slot), height), slice(None))
                        band[where] = band[where] + moved

        return carry

    lax.fori_loop(0, chunks, begin, 0)
    lax.fori_loop(0, chunks, end, 0)
    wait_all(loads)

    @pl.when(needed > 0)
    def _():
        lax.fori_loop(0, cap, one, 0)


def join_right_kernel(frame, own, up, as_upper, as_lower, total, right_out, band, held, sems, piece_sems):
    across = frame // LANES
    blocks, extent = total.shape[1:3]
    rows = pl.ds(0, extent)
    reach = (blocks - across, blocks)
    loads = start_all([(total.at[:, pl.ds(blocks - across, across)], band.at[:, :, rows])], sems)
    add_pieces(frame, own, own[LENT], FAR, as_upper, band, reach, frame - KEEP, lambda slot: own[ROW + slot], held, piece_sems,
               loads)
    add_pieces(frame, up, up[KEPT], NEAR, as_lower, band, reach, KEEP, lambda slot: 0, held, piece_sems)
    wait_all(start_all([(band.at[:, :, rows], right_out)], sems))


def join_right(own, up, as_upper, as_lower, total, cap):
    frame = as_upper.shape[1] // 2
    extent = total.shape[2]
    across = frame // LANES
    rows = cap * KEEP
    return pl.pallas_call(
        lambda *refs: join_right_kernel(frame, *refs),
        out_shape=jax.ShapeDtypeStruct((2, across, extent, LANES), F32),
        in_specs=[smem_spec(), smem_spec(), hbm_spec(), hbm_spec(), hbm_spec()],
        out_specs=any_spec(),
        scratch_shapes=[
            pltpu.VMEM((2, across, extent + frame, LANES), F32),
            pltpu.VMEM((2 * across, rows + KEEP, LANES), F32),
            pltpu.SemaphoreType.DMA((1,)),
            pltpu.SemaphoreType.DMA((rows // CHUNK * 2 * across,)),
        ],
        compiler_params=params(56),
        name="join_right",
    )(own, up, as_upper, as_lower, total)


def join_own_kernel(frame, own, up, as_upper, as_lower, total_in, total_out, top, bottom, held, sems, piece_sems):
    own_blocks = top.shape[1]
    extent = total_in.shape[2]
    tail = frame - KEEP
    mine = pl.ds(0, own_blocks)
    reach = (0, own_blocks)

    def part(needed, rows, band, source, table, field, height, row_of):
        @pl.when(needed > 0)
        def _():
            loads = start_all([(total_in.at[:, mine, rows], band)], sems)
            add_pieces(frame, table, needed, field, source, band_of[field], reach, height, row_of, held, piece_sems, loads)
            wait_all(start_all([(band, total_out.at[:, mine, rows])], sems))

    band_of = {FAR: bottom, NEAR: top}
    part(own[LENT], pl.ds(extent - tail, tail), bottom.at[:, :, pl.ds(0, tail)], as_upper, own, FAR, tail,
         lambda slot: own[ROW + slot] - (extent - tail))
    part(up[KEPT], pl.ds(0, KEEP), top, as_lower, up, NEAR, KEEP, lambda slot: 0)


def join_own(own, up, as_upper, as_lower, total, cap):
    frame = as_upper.shape[1] // 2
    own_blocks = total.shape[2] // LANES
    across = frame // LANES
    rows = cap * KEEP
    return pl.pallas_call(
        lambda *refs: join_own_kernel(frame, *refs),
        out_shape=jax.ShapeDtypeStruct(total.shape, F32),
        in_specs=[smem_spec(), smem_spec(), hbm_spec(), hbm_spec(), hbm_spec()],
        out_specs=hbm_spec(),
        input_output_aliases={4: 0},
        scratch_shapes=[
            pltpu.VMEM((2, own_blocks, KEEP, LANES), F32),
            pltpu.VMEM((2, own_blocks, 2 * (frame - KEEP), LANES), F32),
            pltpu.VMEM((2 * across, rows + KEEP, LANES), F32),
            pltpu.SemaphoreType.DMA((1,)),
            pltpu.SemaphoreType.DMA((rows // CHUNK * 2 * across,)),
        ],
        compiler_params=params(56),
        name="join_own",
    )(own, up, as_upper, as_lower, total)


def right_half_kernel(tile, total, light, out):
    for b in range(total.shape[1]):
        below = 1.0 / (light[b] + 1.0)
        for plane in range(2):
            out[plane, :, lanes_of(b)] = tile[plane, :, lanes_of(b)] - total[plane, b] * below


def right_half(tile, total, light):
    extent = tile.shape[-1]
    across = total.shape[1] * LANES - extent
    part = (extent - across) // LANES
    tall = 128
    return pl.pallas_call(
        right_half_kernel,
        grid=(extent // tall,),
        out_shape=jax.ShapeDtypeStruct(tile.shape, F32),
        in_specs=[
            pl.BlockSpec((2, tall, extent - across), lambda i: (0, i, 1)),
            pl.BlockSpec((2, part, tall, LANES), lambda i: (0, 1, i, 0)),
            pl.BlockSpec((part, tall, LANES), lambda i: (1, i, 0)),
        ],
        out_specs=pl.BlockSpec((2, tall, extent - across), lambda i: (0, i, 1)),
        compiler_params=params(8),
        name="right_half",
    )(tile, total, light)


def left_half_kernel(tile, total, light, left, begun, out):
    for b in range(total.shape[1]):
        below = 1.0 / (light[b] + 1.0)
        for plane in range(2):
            grad = total[plane, b] + left[plane, b]
            out[plane, :, lanes_of(b)] = tile[plane, :, lanes_of(b)] - grad * below


def left_half(tile, total, light, left, begun):
    extent = tile.shape[-1]
    across = left.shape[1]
    tall = 256
    return pl.pallas_call(
        left_half_kernel,
        grid=(extent // tall,),
        out_shape=jax.ShapeDtypeStruct(tile.shape, F32),
        in_specs=[
            pl.BlockSpec((2, tall, across * LANES), lambda i: (0, i, 0)),
            pl.BlockSpec((2, across, tall, LANES), lambda i: (0, 0, i, 0)),
            pl.BlockSpec((across, tall, LANES), lambda i: (0, i, 0)),
            pl.BlockSpec((2, across, tall, LANES), lambda i: (0, 0, i, 0)),
            any_spec(),
        ],
        out_specs=pl.BlockSpec((2, tall, across * LANES), lambda i: (0, i, 0)),
        input_output_aliases={4: 0},
        compiler_params=params(8),
        name="left_half",
    )(tile, total, light, left, begun)


def body(object_tiles, probe, positions, frames, counts):
    tile = object_tiles[0]
    extent = tile.shape[-1]
    frame = frames.shape[-1]
    cap = frames.shape[1]
    peers = lax.axis_size("scan")
    tile_row = lax.axis_index("scan") // TCOLS
    phases = min(2, peers // TCOLS - 1)
    tables = dft_tables(frame)
    parity = (tile_row % 2).reshape(1)
    even = tile_row % 2 == 0

    own, edge, middle = prepare(positions, counts, tile, frame)
    up = shifted(own, "scan", TCOLS)
    edge = shifted(edge, "scan", -1)
    middle = shifted(middle, "scan", -1)
    beside = shifted(jnp.concatenate([own, up]), "scan", 1)

    def exchange(phase, packed, choice):
        uppers = [k for k in range(peers - TCOLS) if k // TCOLS % 2 == phase]
        pairs = [(k, k + TCOLS) for k in uppers] + [(k + TCOLS, k) for k in uppers]

        def sender(size):
            def run(data):
                return lax.dynamic_update_slice(data, lax.ppermute(data[:size], "scan", pairs), (0, 0))
            return run

        branches = [lambda data: data] + [sender(size) for size in SIZES if size <= packed.shape[0]]
        return lax.switch(choice.reshape(()), branches, packed)

    def by_role(arrays):
        if len(arrays) == 1:
            return arrays[0], arrays[0]
        return jnp.where(even, arrays[0], arrays[1]), jnp.where(even, arrays[1], arrays[0])

    cuts = [cut_pieces(phase, own, up, parity, tile, edge, frames[0]) for phase in range(phases)]
    received = by_role([exchange(phase, cut[0], cut[1]) for phase, cut in enumerate(cuts)])
    received, beside = lax.optimization_barrier((received, beside))
    total, *packed = frames_gradient(
        phases, own, up, parity, tile, edge, middle, frames[0], probe, tables, *received)
    returned = by_role([exchange(phase, packed[phase], cut[2]) for phase, cut in enumerate(cuts)])
    right = join_right(own, up, *returned, total, cap)
    right, total, beside = lax.optimization_barrier((right, total, beside))
    left = shifted(right, "scan", 1)
    total = join_own(own, up, *returned, total, cap)
    light = light_plane(own, up, beside, probe, extent)
    begun = right_half(tile, total, light)
    return left_half(tile, total, light, left, begun)[None]


def solution(mesh):
    return jax.shard_map(
        body,
        mesh=mesh,
        in_specs=(
            P(("grp", "scan"), None, None, None),
            P(),
            P(("grp", "scan"), None, None),
            P(("grp", "scan"), None, None, None),
            P(("grp", "scan")),
        ),
        out_specs=P(("grp", "scan"), None, None, None),
        check_vma=False,
    )
```

```python
import math

import jax
import jax.numpy as jnp
import numpy as np
from jax import lax
from jax.experimental import pallas as pl
from jax.experimental.pallas import tpu as pltpu
from jax.sharding import PartitionSpec as P

TCOLS = 8
LANES = 128
ROW_ALIGN = 8
CHUNK = 64
STEP = 32
TILE_ROWS = 16
SIZES = (32, 64, 96, 128, 160, 192, 224, 256, 320, 384, 448, 512, 640, 768, 960, 1344)
MIB = 1024 * 1024
F32 = jnp.float32
BF16 = jnp.bfloat16

KEEP = 160
ROW, COL, NEAR, FAR, PLACE, SHOT = 0, 8, 16, 24, 32, 40
COUNT, KEPT, LENT, FORTH, BACK = 48, 49, 50, 51, 52
TABLE = 64

ACTIVE, AT_ROW, AT_COL, LO, HI, START, PIECE, SHIFT, ROLE = range(9)


def dft_tables(frame):
    near = np.arange(frame // 2, dtype=np.int64)
    blocks = []
    for odd in range(2):
        phase = (near[:, None] * (2 * near[None, :] + odd) % frame).astype(np.float64) * (2.0 * math.pi / frame)
        c, s = np.cos(phase), np.sin(phase)
        ahead = np.block([[c, -s], [s, c]])
        back = np.block([[c.T, s.T], [-s.T, c.T]])
        blocks.append((ahead, ahead.T, back, back.T))
    order = np.zeros((frame, frame))
    order[2 * near, near] = 1.0
    order[2 * near + 1, near + frame // 2] = 1.0
    tables = [blocks[odd][kind] for kind in range(4) for odd in range(2)] + [order]
    return jnp.asarray(np.stack(tables), F32).astype(BF16)


def shifted(array, axis, by):
    peers = lax.axis_size(axis)
    pairs = [(i, i + by) for i in range(peers) if 0 <= i + by < peers]
    return lax.ppermute(array, axis, pairs)


def any_spec():
    return pl.BlockSpec(memory_space=pl.ANY)


def hbm_spec():
    return pl.BlockSpec(memory_space=pltpu.HBM)


def smem_spec():
    return pl.BlockSpec(memory_space=pltpu.SMEM)


def vmem_spec():
    return pl.BlockSpec(memory_space=pltpu.VMEM)


def params(mebibytes):
    return pltpu.CompilerParams(vmem_limit_bytes=mebibytes * MIB)


def taken_from(blocks, by):
    lane = lax.broadcasted_iota(jnp.int32, blocks[0].shape, 1)
    rolled = [pltpu.roll(block, lax.rem(LANES - by, LANES), axis=1) for block in blocks]
    return [jnp.where(lane < LANES - by, one, two) for one, two in zip(rolled[:-1], rolled[1:])]


def put_into(blocks, by):
    lane = lax.broadcasted_iota(jnp.int32, blocks[0].shape, 1)
    rolled = [pltpu.roll(block, by, axis=1) for block in blocks]
    none = jnp.zeros_like(blocks[0])
    return [jnp.where(lane >= by, one, two) for one, two in zip(rolled + [none], [none] + rolled)]


def start_all(pairs, sems, first=0):
    copies = [pltpu.make_async_copy(source, target, sems.at[first + at]) for at, (source, target) in enumerate(pairs)]
    for copy in copies:
        copy.start()
    return copies


def wait_all(copies):
    for copy in copies:
        copy.wait()


def lanes_of(block):
    return pl.ds(block * LANES, LANES)


def side_by_side(parts):
    return jnp.concatenate(parts, axis=1)


def halves(array):
    return [array[:, :LANES], array[:, LANES:]]


def copy_out_rows(needed, packed, out, sems):
    chunks = (needed + CHUNK - 1) // CHUNK

    def copy(chunk):
        at = pl.ds(pl.multiple_of(chunk * CHUNK, CHUNK), CHUNK)
        return pltpu.make_async_copy(packed.at[at], out.at[at], sems.at[chunk])

    def begin(chunk, carry):
        copy(chunk).start()
        return carry

    def end(chunk, carry):
        copy(chunk).wait()
        return carry

    lax.fori_loop(0, chunks, begin, 0)
    lax.fori_loop(0, chunks, end, 0)


def up_to(value, step):
    return (value + step - 1) // step * step


def size_choice(needed):
    choice = jnp.where(needed > 0, 1, 0)
    for size in SIZES:
        choice = choice + jnp.where(needed > size, 1, 0)
    return choice


def prep_kernel(positions, counts, tile, table, edge, middle, sems):
    cap = positions.shape[2]
    extent = tile.shape[-1]
    frame = edge.shape[-1]
    count = counts[0]
    lanes = pl.ds(0, frame)
    copies = start_all([
        (tile.at[:, pl.ds(0, KEEP), lanes], edge.at[:, pl.ds(0, KEEP)]),
        (tile.at[:, pl.ds(KEEP + extent - frame, frame - KEEP), lanes], edge.at[:, pl.ds(KEEP, frame - KEEP)]),
        (tile.at[:, pl.ds(KEEP, extent - frame), lanes], middle),
    ], sems)
    kept, lent, shots = jnp.int32(0), jnp.int32(0), jnp.int32(0)
    for at in range(TABLE):
        table[at] = 0
    for slot in range(cap):
        row = lax.rem(positions[0, 0, slot], extent)
        col = lax.rem(positions[0, 1, slot], extent)
        below = jnp.where(slot < count, jnp.maximum(row + (frame - extent), 0), 0)
        stays = below <= KEEP
        near = jnp.where(stays, below, 0)
        far = jnp.where(stays, 0, frame - below)
        table[ROW + slot] = row
        table[COL + slot] = col
        table[NEAR + slot] = near
        table[FAR + slot] = far
        table[PLACE + slot] = jnp.where(stays, kept, lent)
        table[SHOT + slot] = shots
        kept = kept + up_to(near, ROW_ALIGN)
        lent = lent + up_to(far, ROW_ALIGN)
        shots = shots + jnp.where(stays, 0, frame // 2)
    for slot in range(cap):
        table[SHOT + slot] = table[SHOT + slot] + lent
    table[COUNT] = count
    table[KEPT] = kept
    table[LENT] = lent
    table[FORTH] = jnp.maximum(kept, lent + shots)
    table[BACK] = jnp.maximum(kept, lent)
    wait_all(copies)


def prepare(positions, counts, tile, frame):
    extent = tile.shape[-1]
    return pl.pallas_call(
        prep_kernel,
        out_shape=(
            jax.ShapeDtypeStruct((TABLE,), jnp.int32),
            jax.ShapeDtypeStruct((2, frame, frame), F32),
            jax.ShapeDtypeStruct((2, extent - frame, frame), F32),
        ),
        in_specs=[smem_spec(), smem_spec(), hbm_spec()],
        out_specs=(smem_spec(), vmem_spec(), vmem_spec()),
        scratch_shapes=[pltpu.SemaphoreType.DMA((3,))],
        compiler_params=params(62),
        name="prepare",
    )(jnp.swapaxes(positions, 1, 2), counts, tile)


def cut_kernel(phase, own, up, parity, tile, edge, frames, out, forth, back, band, packed, sems, chunk_sems):
    cap, frame, _ = frames.shape
    extent = tile.shape[-1]
    across = frame // LANES
    own_blocks = extent // LANES
    upper = parity[0] == phase
    forth[0] = size_choice(jnp.where(upper, own[FORTH], up[FORTH]))
    back[0] = size_choice(jnp.where(upper, own[BACK], up[BACK]))
    lends = jnp.logical_and(upper, own[LENT] > 0)
    gives = jnp.logical_and(jnp.logical_not(upper), up[KEPT] > 0)

    def cut(col, row, place):
        at = pl.ds(pl.multiple_of(place, ROW_ALIGN), frame)
        for plane in range(2):
            packed[at, pl.ds(plane * frame, frame)] = side_by_side(window(band, (plane,), row, col, frame, across))

    @pl.when(jnp.logical_or(lends, gives))
    def _():
        base = jnp.where(upper, extent - frame, 0)
        rows = pl.ds(pl.multiple_of(base, ROW_ALIGN), frame)
        wait_all(start_all(
            [(tile.at[:, rows, lanes_of(b)], band.at[:, b, pl.ds(0, frame)]) for b in range(own_blocks)]
            + [(edge.at[:, :, lanes_of(b)], band.at[:, own_blocks + b, pl.ds(0, frame)]) for b in range(across)], sems))

        def one(slot, carry):
            @pl.when(jnp.logical_and(upper, own[FAR + slot] > 0))
            def _():
                cut(own[COL + slot], own[ROW + slot] - (extent - frame), own[PLACE + slot])

            @pl.when(jnp.logical_and(gives, up[NEAR + slot] > 0))
            def _():
                cut(up[COL + slot], 0, up[PLACE + slot])

            return carry

        lax.fori_loop(0, cap, one, 0)

        def shots(slot):
            at = pl.ds(pl.multiple_of(own[SHOT + slot], ROW_ALIGN), frame // 2)
            return [pltpu.make_async_copy(frames.at[slot, pl.ds(part * frame // 2, frame // 2)],
                                          packed.at[at, pl.ds(part * frame, frame)], sems.at[2 * slot + part])
                    for part in range(2)]

        for wait in range(2):
            for slot in range(cap):
                @pl.when(jnp.logical_and(lends, own[FAR + slot] > 0))
                def _():
                    for copy in shots(slot):
                        if wait:
                            copy.wait()
                        else:
                            copy.start()

        copy_out_rows(jnp.where(upper, own[FORTH], up[KEPT]), packed, out, chunk_sems)


def cut_pieces(phase, own, up, parity, tile, edge, frames):
    cap, frame, _ = frames.shape
    extent = tile.shape[-1]
    blocks = (extent + frame) // LANES
    rows = SIZES[-1]
    return pl.pallas_call(
        lambda *refs: cut_kernel(phase, *refs),
        out_shape=(
            jax.ShapeDtypeStruct((rows, 2 * frame), F32),
            jax.ShapeDtypeStruct((1,), jnp.int32),
            jax.ShapeDtypeStruct((1,), jnp.int32),
        ),
        in_specs=[smem_spec(), smem_spec(), smem_spec(), hbm_spec(), hbm_spec(), hbm_spec()],
        out_specs=(hbm_spec(), smem_spec(), smem_spec()),
        scratch_shapes=[
            pltpu.VMEM((2, blocks, 2 * frame, LANES), F32),
            pltpu.VMEM((rows + frame, 2 * frame), F32),
            pltpu.SemaphoreType.DMA((max(blocks, 2 * cap),)),
            pltpu.SemaphoreType.DMA((rows // CHUNK,)),
        ],
        compiler_params=params(60),
        name="cut_pieces",
    )(own, up, parity, tile, edge, frames)


def dot(one, two):
    return jnp.dot(one, two, preferred_element_type=F32)


def stacked(parts):
    return jnp.concatenate(parts, axis=0)


def lane_parts(array):
    half = array.shape[1] // 2
    return array[:, :half], array[:, half:]


def wave_stage(mode, probe, patch, waves):
    frame = probe.shape[2]
    for at in range(0, frame, TILE_ROWS):
        rows = pl.ds(at, TILE_ROWS)
        probe_real, probe_imag = probe[mode, 0, rows], probe[mode, 1, rows]
        patch_real, patch_imag = patch[0, rows], patch[1, rows]
        parts = [lane_parts(part) for part in (
            probe_real * patch_real - probe_imag * patch_imag, probe_real * patch_imag + probe_imag * patch_real)]
        waves[0, mode, rows] = side_by_side([near + far for near, far in parts]).astype(BF16)
        waves[1, mode, rows] = side_by_side([near - far for near, far in parts]).astype(BF16)


def rows_dot(mode, source, tables, first, product):
    for odd in range(2):
        product[odd, mode] = dot(source[odd, mode], tables[first + odd])


def columns_dot(mode, tables, first, source, product):
    for odd in range(2):
        product[odd, mode] = dot(tables[first + odd], source[odd, mode])


def half_stage(mode, product, halfway):
    half = product.shape[2] // 2
    for at in range(0, half, TILE_ROWS):
        near, far = pl.ds(at, TILE_ROWS), pl.ds(half + at, TILE_ROWS)
        upper = [product[odd, mode, near] for odd in range(2)]
        lower = [product[odd, mode, far] for odd in range(2)]
        for odd in range(2):
            mixed = [a + b if not odd else a - b for a, b in zip(upper, lower)]
            real, imag = zip(*[lane_parts(part) for part in mixed])
            halfway[odd, mode, near] = side_by_side(real).astype(BF16)
            halfway[odd, mode, far] = side_by_side(imag).astype(BF16)


def residual_stage(modes, frame, field, amplitude, waves):
    half = frame // 2
    for odd in range(2):
        for at in range(0, half, TILE_ROWS):
            near, far = pl.ds(at, TILE_ROWS), pl.ds(half + at, TILE_ROWS)
            real = [field[odd, mode, near] for mode in range(modes)]
            imag = [field[odd, mode, far] for mode in range(modes)]
            lit = sum(a * a + b * b for a, b in zip(real, imag))
            factor = 1.0 / frame - amplitude[odd, near] * lax.rsqrt(jnp.maximum(lit, float(frame * frame)))
            target = pl.ds(odd * half + at, TILE_ROWS)
            for mode in range(modes):
                parts = [lane_parts(real[mode] * factor), lane_parts(imag[mode] * factor)]
                for column in range(2):
                    waves[column, mode, target] = side_by_side([part[column] for part in parts]).astype(BF16)


def back_stage(mode, product, halfway):
    half = product.shape[2] // 2
    for odd in range(2):
        for at in range(0, half, TILE_ROWS):
            rows = pl.ds(odd * half + at, TILE_ROWS)
            even_part, odd_part = product[0, mode, rows], product[1, mode, rows]
            near, far = lane_parts(even_part + odd_part), lane_parts(even_part - odd_part)
            halfway[odd, mode, pl.ds(at, TILE_ROWS)] = side_by_side([near[0], far[0]]).astype(BF16)
            halfway[odd, mode, pl.ds(half + at, TILE_ROWS)] = side_by_side([near[1], far[1]]).astype(BF16)


def gradient_stage(some_modes, first, product, probe, piece):
    frame = probe.shape[2]
    half = frame // 2
    across = frame // LANES
    for at in range(0, half, ROW_ALIGN):
        rows = [pl.ds(at, ROW_ALIGN), pl.ds(half + at, ROW_ALIGN)]
        grads = [[0.0, 0.0], [0.0, 0.0]]
        for mode in some_modes:
            mixed = [(product[0, mode, part], product[1, mode, part]) for part in rows]
            for side in range(2):
                back_real, back_imag = [a + b if not side else a - b for a, b in mixed]
                probe_real, probe_imag = probe[mode, 0, rows[side]], probe[mode, 1, rows[side]]
                grads[side][0] += probe_real * back_real + probe_imag * back_imag
                grads[side][1] += probe_real * back_imag - probe_imag * back_real
        for side in range(2):
            for plane in range(2):
                grad = grads[side][plane] * (1.0 / frame)
                for b in range(across):
                    where = (plane * across + b, rows[side], slice(None))
                    part = grad[:, b * LANES:(b + 1) * LANES]
                    piece[where] = part if first else piece[where] + part


def frame_step(patch, amplitude, probe, tables, waves, halfway, product, field, piece):
    modes, _, frame, _ = probe.shape
    for step in range(modes + 1):
        if step < modes:
            wave_stage(step, probe, patch, waves)
            rows_dot(step, waves, tables, 0, product)
        if step:
            half_stage(step - 1, product, halfway)
            columns_dot(step - 1, tables, 2, halfway, field)
    residual_stage(modes, frame, field, amplitude, waves)
    for step in range(modes + 1):
        if step < modes:
            rows_dot(step, waves, tables, 4, product)
        if step:
            back_stage(step - 1, product, halfway)
            columns_dot(step - 1, tables, 6, halfway, field)
        if step and step % 2 == 0:
            gradient_stage((step - 2, step - 1), step == 2, field, probe, piece)


def ordered_amplitude(measured, task, order, amplitude):
    frame = measured.shape[2]
    for odd in range(2):
        root = jnp.sqrt(side_by_side(
            [measured[task, b, pl.ds(odd, frame // 2, stride=2), :] for b in range(measured.shape[1])]))
        high = root.astype(BF16)
        low = (root - high.astype(F32)).astype(BF16)
        amplitude[odd] = dot(high, order) + dot(low, order)


def window(band, lead, row, col, height, across):
    return taken_from(
        [band[lead + (col // LANES + b, pl.ds(row, height), slice(None))] for b in range(across + 1)],
        lax.rem(col, LANES),
    )


def add_window(total, lead, parts, row, col, frame):
    for b, moved in enumerate(put_into(parts, lax.rem(col, LANES))):
        at = lead + (col // LANES + b, pl.ds(row, frame), slice(None))
        total[at] = total[at] + moved


def kernel_cost(frames, modes, frame):
    return pl.CostEstimate(
        flops=frames * modes * 4 * 4 * frame ** 3, bytes_accessed=16 * 1024 * 1024, transcendentals=0)


def frames_kernel(phases, own, up, parity, tile, edge, middle, frames, probe_in, tables_in, as_upper, as_lower, total_out, *rest):
    packed_outs = rest[:phases]
    (band, total, held, packed, piece, measured, probe, tables, patch, amplitude, waves, halfway, product, field, work,
     sems, shot_sems, held_sems, chunk_sems) = rest[phases:]
    cap, frame, _ = frames.shape
    extent = tile.shape[-1]
    across = frame // LANES
    own_blocks = extent // LANES
    half = frame // 2
    own_rows = pl.ds(frame, extent)

    first = start_all(
        [(tile.at[:, :, lanes_of(b)], band.at[:, b, own_rows]) for b in range(own_blocks)]
        + [(source.at[:, pl.ds(at, height), lanes_of(b)], band.at[:, own_blocks + b, pl.ds(frame + target, height)])
           for source, at, height, target in (
               (edge, 0, KEEP, 0), (middle, 0, extent - frame, KEEP), (edge, KEEP, frame - KEEP, KEEP + extent - frame))
           for b in range(across)]
        + [(probe_in, probe), (tables_in, tables)], sems)

    def mine(slot):
        return jnp.logical_and(slot < own[COUNT], own[FAR + slot] == 0)

    def borrowed(slot):
        return up[FAR + slot] > 0

    def shot_copies(slot, task, lent):
        if not lent:
            return [pltpu.make_async_copy(frames.at[slot, :, lanes_of(b)], measured.at[task, b], shot_sems.at[task, b])
                    for b in range(across)]
        at = pl.ds(pl.multiple_of(up[SHOT + slot], ROW_ALIGN), half)
        return [
            pltpu.make_async_copy(as_lower.at[at, lanes_of(part * across + b)],
                                  measured.at[task, b, pl.ds(part * half, half)], shot_sems.at[task, part * across + b])
            for part in range(2) for b in range(across)
        ]

    def held_copies(slot, task, lent):
        source, table = (as_lower, up) if lent else (as_upper, own)
        at = pl.ds(pl.multiple_of(table[PLACE + slot], ROW_ALIGN), frame)
        return [
            pltpu.make_async_copy(source.at[at, lanes_of(b)], held.at[task, b, pl.ds(frame, frame)], held_sems.at[task, b])
            for b in range(2 * across)
        ]

    def for_tasks(wait):
        for slot in range(cap):
            def run(copies):
                for copy in copies:
                    if wait:
                        copy.wait()
                    else:
                        copy.start()

            @pl.when(mine(slot))
            def _():
                run(shot_copies(slot, slot, False))

            @pl.when(own[NEAR + slot] > 0)
            def _():
                run(held_copies(slot, slot, False))

            @pl.when(borrowed(slot))
            def _():
                run(shot_copies(slot, cap + slot, True))
                run(held_copies(slot, cap + slot, True))

    for_tasks(False)
    for slot in range(cap):
        near = own[NEAR + slot]
        for field_at, value in (
            (ACTIVE, mine(slot).astype(jnp.int32)), (AT_ROW, own[ROW + slot] + frame), (AT_COL, own[COL + slot]),
            (LO, frame - near), (HI, frame), (START, near), (PIECE, own[PLACE + slot]), (SHIFT, frame - near), (ROLE, 0),
        ):
            work[slot, field_at] = value
        for field_at, value in (
            (ACTIVE, borrowed(slot).astype(jnp.int32)), (AT_ROW, up[ROW + slot] + frame - extent), (AT_COL, up[COL + slot]),
            (LO, 0), (HI, up[FAR + slot]), (START, frame), (PIECE, up[PLACE + slot]), (SHIFT, 0), (ROLE, 1),
        ):
            work[cap + slot, field_at] = value
    total[:, :, own_rows, :] = jnp.zeros((2, band.shape[1], extent, LANES), F32)
    wait_all(first)
    for_tasks(True)
    row_index = lax.broadcasted_iota(jnp.int32, (STEP, LANES), 0)

    def one(task, carry):
        @pl.when(work[task, ACTIVE] > 0)
        def _():
            row, col, start = work[task, AT_ROW], work[task, AT_COL], work[task, START]
            lo, hi = work[task, LO], work[task, HI]
            for at in range(0, frame, STEP):
                theirs = jnp.logical_and(row_index >= lo - at, row_index < hi - at)
                for plane in range(2):
                    near = window(band, (plane,), row + at, col, STEP, across)
                    other = [held[task, plane * across + b, pl.ds(start + at, STEP), :] for b in range(across)]
                    patch[plane, pl.ds(at, STEP)] = side_by_side([jnp.where(theirs, b, a) for a, b in zip(near, other)])
            ordered_amplitude(measured, task, tables[8], amplitude)
            frame_step(patch, amplitude, probe, tables, waves, halfway, product, field, piece)
            for at in range(0, frame, STEP):
                for plane in range(2):
                    parts = [piece[plane * across + b, pl.ds(at, STEP), :] for b in range(across)]
                    add_window(total, (plane,), parts, row + at, col, STEP)

            @pl.when(lo < hi)
            def _():
                target = pl.ds(pl.multiple_of(work[task, PIECE], ROW_ALIGN), frame)
                source = pl.ds(work[task, SHIFT], frame)
                for b in range(2 * across):
                    packed[work[task, ROLE], target, lanes_of(b)] = piece[b, source, :]

        return carry

    lax.fori_loop(0, 2 * cap, one, 0)
    end = start_all([(total.at[:, :, own_rows], total_out)], sems)
    for phase in range(phases):
        upper = parity[0] == phase
        role = jnp.where(upper, 0, 1)
        copy_out_rows(jnp.where(upper, own[KEPT], up[LENT]), packed.at[role], packed_outs[phase], chunk_sems)
    wait_all(end)


def frames_gradient(phases, own, up, parity, tile, edge, middle, frames, probe, tables, as_upper, as_lower):
    cap, frame, _ = frames.shape
    extent = tile.shape[-1]
    modes = probe.shape[0]
    tall = extent + 2 * frame
    blocks = (extent + frame) // LANES
    across = frame // LANES
    rows = as_upper.shape[0]
    kept_rows = cap * KEEP
    return pl.pallas_call(
        lambda *refs: frames_kernel(phases, *refs),
        out_shape=(jax.ShapeDtypeStruct((2, blocks, extent, LANES), F32),)
        + (jax.ShapeDtypeStruct(as_upper.shape, F32),) * phases,
        in_specs=[smem_spec()] * 3 + [hbm_spec()] * 8,
        out_specs=(hbm_spec(),) * (1 + phases),
        scratch_shapes=[
            pltpu.VMEM((2, blocks, tall, LANES), F32),
            pltpu.VMEM((2, blocks, tall, LANES), F32),
            pltpu.VMEM((2 * cap, 2 * across, 2 * frame, LANES), F32),
            pltpu.VMEM((2, kept_rows + frame, 2 * frame), F32),
            pltpu.VMEM((2 * across, 2 * frame, LANES), F32),
            pltpu.VMEM((2 * cap, across, frame, LANES), F32),
            pltpu.VMEM(probe.shape, F32),
            pltpu.VMEM(tables.shape, BF16),
            pltpu.VMEM((2, frame, frame), F32),
            pltpu.VMEM((2, frame // 2, frame), F32),
            pltpu.VMEM((2, modes, frame, frame), BF16),
            pltpu.VMEM((2, modes, frame, frame), BF16),
            pltpu.VMEM((2, modes, frame, frame), F32),
            pltpu.VMEM((2, modes, frame, frame), F32),
            pltpu.SMEM((2 * cap, 16), jnp.int32),
            pltpu.SemaphoreType.DMA((blocks + 2 * across + 2,)),
            pltpu.SemaphoreType.DMA((2 * cap, 2 * across)),
            pltpu.SemaphoreType.DMA((2 * cap, 2 * across)),
            pltpu.SemaphoreType.DMA((rows // CHUNK,)),
        ],
        compiler_params=params(55),
        cost_estimate=kernel_cost(cap, modes, frame),
        name="frames_gradient",
    )(own, up, parity, tile, edge, middle, frames, probe, tables, as_upper, as_lower)


def light_kernel(own, up, beside, probe, light_out, light, sem):
    modes, _, frame, _ = probe.shape
    own_blocks, extent, _ = light_out.shape
    across = frame // LANES
    inside = (pl.ds(across, own_blocks), pl.ds(frame, extent), slice(None))
    light[inside] = jnp.zeros((own_blocks, extent, LANES), F32)
    power = jnp.zeros((frame, frame), F32)
    for mode in range(modes):
        power += probe[mode, 0] * probe[mode, 0] + probe[mode, 1] * probe[mode, 1]
    power = halves(power)
    for table, lead, down, right in ((own, 0, 0, 0), (beside, 0, 0, 1), (up, 0, 1, 0), (beside, TABLE, 1, 1)):

        def lit(slot, carry, table=table, lead=lead, down=down, right=right):
            row = table[lead + ROW + slot] + frame - down * extent
            col = table[lead + COL + slot] + frame - right * extent

            @pl.when((row > 0) & (col > 0))
            def _():
                add_window(light, (), power, row, col, frame)

            return carry

        lax.fori_loop(0, table[lead + COUNT], lit, 0)
    copy = pltpu.make_async_copy(light.at[inside[0], inside[1]], light_out, sem)
    copy.start()
    copy.wait()


def light_plane(own, up, beside, probe, extent):
    frame = probe.shape[-1]
    wide = extent + 2 * frame
    return pl.pallas_call(
        light_kernel,
        out_shape=jax.ShapeDtypeStruct((extent // LANES, extent, LANES), F32),
        in_specs=[smem_spec()] * 3 + [vmem_spec()],
        out_specs=any_spec(),
        scratch_shapes=[pltpu.VMEM((wide // LANES, wide, LANES), F32), pltpu.SemaphoreType.DMA],
        compiler_params=params(9),
        cost_estimate=pl.CostEstimate(flops=0, bytes_accessed=4 * MIB, transcendentals=0),
        name="light_plane",
    )(own, up, beside, probe)


def add_pieces(frame, table, needed, field, pieces, band, blocks, height, row_of, held, sems, loads=()):
    across = frame // LANES
    cap = (held.shape[1] - KEEP) // KEEP
    chunks = (needed + CHUNK - 1) // CHUNK
    row_index = lax.broadcasted_iota(jnp.int32, (height, LANES), 0)

    def copies(chunk):
        at = pl.ds(pl.multiple_of(chunk * CHUNK, CHUNK), CHUNK)
        return [pltpu.make_async_copy(pieces.at[at, lanes_of(b)], held.at[b, at], sems.at[chunk * 2 * across + b])
                for b in range(2 * across)]

    def begin(chunk, carry):
        for copy in copies(chunk):
            copy.start()
        return carry

    def end(chunk, carry):
        for copy in copies(chunk):
            copy.wait()
        return carry

    def one(slot, carry):
        used = table[field + slot]
        first = table[COL + slot] // LANES

        @pl.when(jnp.logical_and(used > 0, jnp.logical_and(first + across >= blocks[0], first < blocks[1])))
        def _():
            at = pl.ds(pl.multiple_of(table[PLACE + slot], ROW_ALIGN), height)
            for plane in range(2):
                got = [jnp.where(row_index < used, held[plane * across + b, at, :], 0.0) for b in range(across)]
                for b, moved in enumerate(put_into(got, lax.rem(table[COL + slot], LANES))):
                    @pl.when(jnp.logical_and(first + b >= blocks[0], first + b < blocks[1]))
                    def _():
                        where = (plane, first + b - blocks[0], pl.ds(row_of(slot), height), slice(None))
                        band[where] = band[where] + moved

        return carry

    lax.fori_loop(0, chunks, begin, 0)
    lax.fori_loop(0, chunks, end, 0)
    wait_all(loads)

    @pl.when(needed > 0)
    def _():
        lax.fori_loop(0, cap, one, 0)


def join_right_kernel(frame, own, up, as_upper, as_lower, total, right_out, band, held, sems, piece_sems):
    across = frame // LANES
    blocks, extent = total.shape[1:3]
    rows = pl.ds(0, extent)
    reach = (blocks - across, blocks)
    loads = start_all([(total.at[:, pl.ds(blocks - across, across)], band.at[:, :, rows])], sems)
    add_pieces(frame, own, own[LENT], FAR, as_upper, band, reach, frame - KEEP, lambda slot: own[ROW + slot], held, piece_sems,
               loads)
    add_pieces(frame, up, up[KEPT], NEAR, as_lower, band, reach, KEEP, lambda slot: 0, held, piece_sems)
    wait_all(start_all([(band.at[:, :, rows], right_out)], sems))


def join_right(own, up, as_upper, as_lower, total, cap):
    frame = as_upper.shape[1] // 2
    extent = total.shape[2]
    across = frame // LANES
    rows = cap * KEEP
    return pl.pallas_call(
        lambda *refs: join_right_kernel(frame, *refs),
        out_shape=jax.ShapeDtypeStruct((2, across, extent, LANES), F32),
        in_specs=[smem_spec(), smem_spec(), hbm_spec(), hbm_spec(), hbm_spec()],
        out_specs=any_spec(),
        scratch_shapes=[
            pltpu.VMEM((2, across, extent + frame, LANES), F32),
            pltpu.VMEM((2 * across, rows + KEEP, LANES), F32),
            pltpu.SemaphoreType.DMA((1,)),
            pltpu.SemaphoreType.DMA((rows // CHUNK * 2 * across,)),
        ],
        compiler_params=params(56),
        name="join_right",
    )(own, up, as_upper, as_lower, total)


def join_own_kernel(frame, own, up, as_upper, as_lower, total_in, total_out, top, bottom, held, sems, piece_sems):
    own_blocks = top.shape[1]
    extent = total_in.shape[2]
    tail = frame - KEEP
    mine = pl.ds(0, own_blocks)
    reach = (0, own_blocks)

    def part(needed, rows, band, source, table, field, height, row_of):
        @pl.when(needed > 0)
        def _():
            loads = start_all([(total_in.at[:, mine, rows], band)], sems)
            add_pieces(frame, table, needed, field, source, band_of[field], reach, height, row_of, held, piece_sems, loads)
            wait_all(start_all([(band, total_out.at[:, mine, rows])], sems))

    band_of = {FAR: bottom, NEAR: top}
    part(own[LENT], pl.ds(extent - tail, tail), bottom.at[:, :, pl.ds(0, tail)], as_upper, own, FAR, tail,
         lambda slot: own[ROW + slot] - (extent - tail))
    part(up[KEPT], pl.ds(0, KEEP), top, as_lower, up, NEAR, KEEP, lambda slot: 0)


def join_own(own, up, as_upper, as_lower, total, cap):
    frame = as_upper.shape[1] // 2
    own_blocks = total.shape[2] // LANES
    across = frame // LANES
    rows = cap * KEEP
    return pl.pallas_call(
        lambda *refs: join_own_kernel(frame, *refs),
        out_shape=jax.ShapeDtypeStruct(total.shape, F32),
        in_specs=[smem_spec(), smem_spec(), hbm_spec(), hbm_spec(), hbm_spec()],
        out_specs=hbm_spec(),
        input_output_aliases={4: 0},
        scratch_shapes=[
            pltpu.VMEM((2, own_blocks, KEEP, LANES), F32),
            pltpu.VMEM((2, own_blocks, 2 * (frame - KEEP), LANES), F32),
            pltpu.VMEM((2 * across, rows + KEEP, LANES), F32),
            pltpu.SemaphoreType.DMA((1,)),
            pltpu.SemaphoreType.DMA((rows // CHUNK * 2 * across,)),
        ],
        compiler_params=params(56),
        name="join_own",
    )(own, up, as_upper, as_lower, total)


def right_half_kernel(tile, total, light, out):
    for b in range(total.shape[1]):
        below = 1.0 / (light[b] + 1.0)
        for plane in range(2):
            out[plane, :, lanes_of(b)] = tile[plane, :, lanes_of(b)] - total[plane, b] * below


def right_half(tile, total, light):
    extent = tile.shape[-1]
    across = total.shape[1] * LANES - extent
    part = (extent - across) // LANES
    tall = 128
    return pl.pallas_call(
        right_half_kernel,
        grid=(extent // tall,),
        out_shape=jax.ShapeDtypeStruct(tile.shape, F32),
        in_specs=[
            pl.BlockSpec((2, tall, extent - across), lambda i: (0, i, 1)),
            pl.BlockSpec((2, part, tall, LANES), lambda i: (0, 1, i, 0)),
            pl.BlockSpec((part, tall, LANES), lambda i: (1, i, 0)),
        ],
        out_specs=pl.BlockSpec((2, tall, extent - across), lambda i: (0, i, 1)),
        compiler_params=params(8),
        name="right_half",
    )(tile, total, light)


def left_half_kernel(tile, total, light, left, begun, out):
    for b in range(total.shape[1]):
        below = 1.0 / (light[b] + 1.0)
        for plane in range(2):
            grad = total[plane, b] + left[plane, b]
            out[plane, :, lanes_of(b)] = tile[plane, :, lanes_of(b)] - grad * below


def left_half(tile, total, light, left, begun):
    extent = tile.shape[-1]
    across = left.shape[1]
    tall = 256
    return pl.pallas_call(
        left_half_kernel,
        grid=(extent // tall,),
        out_shape=jax.ShapeDtypeStruct(tile.shape, F32),
        in_specs=[
            pl.BlockSpec((2, tall, across * LANES), lambda i: (0, i, 0)),
            pl.BlockSpec((2, across, tall, LANES), lambda i: (0, 0, i, 0)),
            pl.BlockSpec((across, tall, LANES), lambda i: (0, i, 0)),
            pl.BlockSpec((2, across, tall, LANES), lambda i: (0, 0, i, 0)),
            any_spec(),
        ],
        out_specs=pl.BlockSpec((2, tall, across * LANES), lambda i: (0, i, 0)),
        input_output_aliases={4: 0},
        compiler_params=params(8),
        name="left_half",
    )(tile, total, light, left, begun)


def body(object_tiles, probe, positions, frames, counts):
    tile = object_tiles[0]
    extent = tile.shape[-1]
    frame = frames.shape[-1]
    cap = frames.shape[1]
    peers = lax.axis_size("scan")
    tile_row = lax.axis_index("scan") // TCOLS
    phases = min(2, peers // TCOLS - 1)
    tables = dft_tables(frame)
    parity = (tile_row % 2).reshape(1)
    even = tile_row % 2 == 0

    own, edge, middle = prepare(positions, counts, tile, frame)
    up = shifted(own, "scan", TCOLS)
    edge = shifted(edge, "scan", -1)
    middle = shifted(middle, "scan", -1)
    beside = shifted(jnp.concatenate([own, up]), "scan", 1)

    def exchange(phase, packed, choice):
        uppers = [k for k in range(peers - TCOLS) if k // TCOLS % 2 == phase]
        pairs = [(k, k + TCOLS) for k in uppers] + [(k + TCOLS, k) for k in uppers]

        def sender(size):
            def run(data):
                return lax.dynamic_update_slice(data, lax.ppermute(data[:size], "scan", pairs), (0, 0))
            return run

        branches = [lambda data: data] + [sender(size) for size in SIZES if size <= packed.shape[0]]
        return lax.switch(choice.reshape(()), branches, packed)

    def by_role(arrays):
        if len(arrays) == 1:
            return arrays[0], arrays[0]
        return jnp.where(even, arrays[0], arrays[1]), jnp.where(even, arrays[1], arrays[0])

    cuts = [cut_pieces(phase, own, up, parity, tile, edge, frames[0]) for phase in range(phases)]
    received = by_role([exchange(phase, cut[0], cut[1]) for phase, cut in enumerate(cuts)])
    received, beside = lax.optimization_barrier((received, beside))
    total, *packed = frames_gradient(
        phases, own, up, parity, tile, edge, middle, frames[0], probe, tables, *received)
    returned = by_role([exchange(phase, packed[phase], cut[2]) for phase, cut in enumerate(cuts)])
    right = join_right(own, up, *returned, total, cap)
    right, total, beside = lax.optimization_barrier((right, total, beside))
    left = shifted(right, "scan", 1)
    total = join_own(own, up, *returned, total, cap)
    light = light_plane(own, up, beside, probe, extent)
    begun = right_half(tile, total, light)
    return left_half(tile, total, light, left, begun)[None]


def solution(mesh):
    return jax.shard_map(
        body,
        mesh=mesh,
        in_specs=(
            P(("grp", "scan"), None, None, None),
            P(),
            P(("grp", "scan"), None, None),
            P(("grp", "scan"), None, None, None),
            P(("grp", "scan")),
        ),
        out_specs=P(("grp", "scan"), None, None, None),
        check_vma=False,
    )
```

```python
import math

import jax
import jax.numpy as jnp
import numpy as np
from jax import lax
from jax.experimental import pallas as pl
from jax.experimental.pallas import tpu as pltpu
from jax.sharding import PartitionSpec as P

TCOLS = 8
LANES = 128
ROW_ALIGN = 8
CHUNK = 64
STEP = 32
TILE_ROWS = 16
SIZES = (32, 64, 96, 128, 160, 192, 224, 256, 320, 384, 448, 512, 640, 768, 960, 1344)
MIB = 1024 * 1024
F32 = jnp.float32
BF16 = jnp.bfloat16

KEEP = 160
ROW, COL, NEAR, FAR, PLACE, SHOT = 0, 8, 16, 24, 32, 40
COUNT, KEPT, LENT, FORTH, BACK = 48, 49, 50, 51, 52
TABLE = 64

ACTIVE, AT_ROW, AT_COL, LO, HI, START, PIECE, SHIFT, ROLE = range(9)


def dft_tables(frame):
    near = np.arange(frame // 2, dtype=np.int64)
    blocks = []
    for odd in range(2):
        phase = (near[:, None] * (2 * near[None, :] + odd) % frame).astype(np.float64) * (2.0 * math.pi / frame)
        c, s = np.cos(phase), np.sin(phase)
        ahead = np.block([[c, -s], [s, c]])
        back = np.block([[c.T, s.T], [-s.T, c.T]])
        blocks.append((ahead, ahead.T, back, back.T))
    order = np.zeros((frame, frame))
    order[2 * near, near] = 1.0
    order[2 * near + 1, near + frame // 2] = 1.0
    tables = [blocks[odd][kind] for kind in range(4) for odd in range(2)] + [order]
    return jnp.asarray(np.stack(tables), F32).astype(BF16)


def shifted(array, axis, by):
    peers = lax.axis_size(axis)
    pairs = [(i, i + by) for i in range(peers) if 0 <= i + by < peers]
    return lax.ppermute(array, axis, pairs)


def any_spec():
    return pl.BlockSpec(memory_space=pl.ANY)


def hbm_spec():
    return pl.BlockSpec(memory_space=pltpu.HBM)


def smem_spec():
    return pl.BlockSpec(memory_space=pltpu.SMEM)


def vmem_spec():
    return pl.BlockSpec(memory_space=pltpu.VMEM)


def params(mebibytes):
    return pltpu.CompilerParams(vmem_limit_bytes=mebibytes * MIB)


def taken_from(blocks, by):
    lane = lax.broadcasted_iota(jnp.int32, blocks[0].shape, 1)
    rolled = [pltpu.roll(block, lax.rem(LANES - by, LANES), axis=1) for block in blocks]
    return [jnp.where(lane < LANES - by, one, two) for one, two in zip(rolled[:-1], rolled[1:])]


def put_into(blocks, by):
    lane = lax.broadcasted_iota(jnp.int32, blocks[0].shape, 1)
    rolled = [pltpu.roll(block, by, axis=1) for block in blocks]
    none = jnp.zeros_like(blocks[0])
    return [jnp.where(lane >= by, one, two) for one, two in zip(rolled + [none], [none] + rolled)]


def start_all(pairs, sems, first=0):
    copies = [pltpu.make_async_copy(source, target, sems.at[first + at]) for at, (source, target) in enumerate(pairs)]
    for copy in copies:
        copy.start()
    return copies


def wait_all(copies):
    for copy in copies:
        copy.wait()


def lanes_of(block):
    return pl.ds(block * LANES, LANES)


def side_by_side(parts):
    return jnp.concatenate(parts, axis=1)


def halves(array):
    return [array[:, :LANES], array[:, LANES:]]


def copy_out_rows(needed, packed, out, sems):
    chunks = (needed + CHUNK - 1) // CHUNK

    def copy(chunk):
        at = pl.ds(pl.multiple_of(chunk * CHUNK, CHUNK), CHUNK)
        return pltpu.make_async_copy(packed.at[at], out.at[at], sems.at[chunk])

    def begin(chunk, carry):
        copy(chunk).start()
        return carry

    def end(chunk, carry):
        copy(chunk).wait()
        return carry

    lax.fori_loop(0, chunks, begin, 0)
    lax.fori_loop(0, chunks, end, 0)


def up_to(value, step):
    return (value + step - 1) // step * step


def size_choice(needed):
    choice = jnp.where(needed > 0, 1, 0)
    for size in SIZES:
        choice = choice + jnp.where(needed > size, 1, 0)
    return choice


def strip_kernel(tile, edge, middle, sems):
    extent = tile.shape[-1]
    frame = edge.shape[-1]
    lanes = pl.ds(0, frame)
    wait_all(start_all([
        (tile.at[:, pl.ds(0, KEEP), lanes], edge.at[:, pl.ds(0, KEEP)]),
        (tile.at[:, pl.ds(KEEP + extent - frame, frame - KEEP), lanes], edge.at[:, pl.ds(KEEP, frame - KEEP)]),
        (tile.at[:, pl.ds(KEEP, extent - frame), lanes], middle),
    ], sems))


def table_kernel(extent, frame, positions, counts, table):
    cap = positions.shape[2]
    count = counts[0]
    kept, lent, shots = jnp.int32(0), jnp.int32(0), jnp.int32(0)
    for at in range(TABLE):
        table[at] = 0
    for slot in range(cap):
        row = lax.rem(positions[0, 0, slot], extent)
        col = lax.rem(positions[0, 1, slot], extent)
        below = jnp.where(slot < count, jnp.maximum(row + (frame - extent), 0), 0)
        stays = below <= KEEP
        near = jnp.where(stays, below, 0)
        far = jnp.where(stays, 0, frame - below)
        table[ROW + slot] = row
        table[COL + slot] = col
        table[NEAR + slot] = near
        table[FAR + slot] = far
        table[PLACE + slot] = jnp.where(stays, kept, lent)
        table[SHOT + slot] = shots
        kept = kept + up_to(near, ROW_ALIGN)
        lent = lent + up_to(far, ROW_ALIGN)
        shots = shots + jnp.where(stays, 0, frame // 2)
    for slot in range(cap):
        table[SHOT + slot] = table[SHOT + slot] + lent
    table[COUNT] = count
    table[KEPT] = kept
    table[LENT] = lent
    table[FORTH] = jnp.maximum(kept, lent + shots)
    table[BACK] = jnp.maximum(kept, lent)


def slot_table(positions, counts, extent, frame):
    return pl.pallas_call(
        lambda *refs: table_kernel(extent, frame, *refs),
        out_shape=jax.ShapeDtypeStruct((TABLE,), jnp.int32),
        in_specs=[smem_spec(), smem_spec()],
        out_specs=smem_spec(),
        name="slot_table",
    )(jnp.swapaxes(positions, 1, 2), counts)


def strips(tile, frame):
    extent = tile.shape[-1]
    return pl.pallas_call(
        strip_kernel,
        out_shape=(
            jax.ShapeDtypeStruct((2, frame, frame), F32),
            jax.ShapeDtypeStruct((2, extent - frame, frame), F32),
        ),
        in_specs=[hbm_spec()],
        out_specs=(vmem_spec(), vmem_spec()),
        scratch_shapes=[pltpu.SemaphoreType.DMA((3,))],
        compiler_params=params(61),
        name="strips",
    )(tile)


def cut_kernel(phase, own, up, parity, tile, edge, frames, out, forth, back, band, packed, sems, chunk_sems):
    cap, frame, _ = frames.shape
    extent = tile.shape[-1]
    across = frame // LANES
    own_blocks = extent // LANES
    upper = parity[0] == phase
    forth[0] = size_choice(jnp.where(upper, own[FORTH], up[FORTH]))
    back[0] = size_choice(jnp.where(upper, own[BACK], up[BACK]))
    lends = jnp.logical_and(upper, own[LENT] > 0)
    gives = jnp.logical_and(jnp.logical_not(upper), up[KEPT] > 0)

    def cut(col, row, place):
        at = pl.ds(pl.multiple_of(place, ROW_ALIGN), frame)
        for plane in range(2):
            packed[at, pl.ds(plane * frame, frame)] = side_by_side(window(band, (plane,), row, col, frame, across))

    @pl.when(jnp.logical_or(lends, gives))
    def _():
        base = jnp.where(upper, extent - frame, 0)
        rows = pl.ds(pl.multiple_of(base, ROW_ALIGN), frame)
        wait_all(start_all(
            [(tile.at[:, rows, lanes_of(b)], band.at[:, b, pl.ds(0, frame)]) for b in range(own_blocks)]
            + [(edge.at[:, :, lanes_of(b)], band.at[:, own_blocks + b, pl.ds(0, frame)]) for b in range(across)], sems))

        def one(slot, carry):
            @pl.when(jnp.logical_and(upper, own[FAR + slot] > 0))
            def _():
                cut(own[COL + slot], own[ROW + slot] - (extent - frame), own[PLACE + slot])

            @pl.when(jnp.logical_and(gives, up[NEAR + slot] > 0))
            def _():
                cut(up[COL + slot], 0, up[PLACE + slot])

            return carry

        lax.fori_loop(0, cap, one, 0)

        def shots(slot):
            at = pl.ds(pl.multiple_of(own[SHOT + slot], ROW_ALIGN), frame // 2)
            return [pltpu.make_async_copy(frames.at[slot, pl.ds(part * frame // 2, frame // 2)],
                                          packed.at[at, pl.ds(part * frame, frame)], sems.at[2 * slot + part])
                    for part in range(2)]

        for wait in range(2):
            for slot in range(cap):
                @pl.when(jnp.logical_and(lends, own[FAR + slot] > 0))
                def _():
                    for copy in shots(slot):
                        if wait:
                            copy.wait()
                        else:
                            copy.start()

        copy_out_rows(jnp.where(upper, own[FORTH], up[KEPT]), packed, out, chunk_sems)


def cut_pieces(phase, own, up, parity, tile, edge, frames):
    cap, frame, _ = frames.shape
    extent = tile.shape[-1]
    blocks = (extent + frame) // LANES
    rows = SIZES[-1]
    return pl.pallas_call(
        lambda *refs: cut_kernel(phase, *refs),
        out_shape=(
            jax.ShapeDtypeStruct((rows, 2 * frame), F32),
            jax.ShapeDtypeStruct((1,), jnp.int32),
            jax.ShapeDtypeStruct((1,), jnp.int32),
        ),
        in_specs=[smem_spec(), smem_spec(), smem_spec(), hbm_spec(), hbm_spec(), hbm_spec()],
        out_specs=(hbm_spec(), smem_spec(), smem_spec()),
        scratch_shapes=[
            pltpu.VMEM((2, blocks, 2 * frame, LANES), F32),
            pltpu.VMEM((rows + frame, 2 * frame), F32),
            pltpu.SemaphoreType.DMA((max(blocks, 2 * cap),)),
            pltpu.SemaphoreType.DMA((rows // CHUNK,)),
        ],
        compiler_params=params(60),
        name="cut_pieces",
    )(own, up, parity, tile, edge, frames)


def dot(one, two):
    return jnp.dot(one, two, preferred_element_type=F32)


def stacked(parts):
    return jnp.concatenate(parts, axis=0)


def lane_parts(array):
    half = array.shape[1] // 2
    return array[:, :half], array[:, half:]


def wave_stage(mode, probe, patch, waves):
    frame = probe.shape[2]
    for at in range(0, frame, TILE_ROWS):
        rows = pl.ds(at, TILE_ROWS)
        probe_real, probe_imag = probe[mode, 0, rows], probe[mode, 1, rows]
        patch_real, patch_imag = patch[0, rows], patch[1, rows]
        parts = [lane_parts(part) for part in (
            probe_real * patch_real - probe_imag * patch_imag, probe_real * patch_imag + probe_imag * patch_real)]
        waves[0, mode, rows] = side_by_side([near + far for near, far in parts]).astype(BF16)
        waves[1, mode, rows] = side_by_side([near - far for near, far in parts]).astype(BF16)


def rows_dot(pair, source, tables, first, product):
    modes = pl.ds(2 * pair, 2)
    for odd in range(2):
        both = source[odd, modes]
        product[odd, modes] = dot(both.reshape(2 * both.shape[1], both.shape[2]), tables[first + odd]).reshape(both.shape)


def columns_dot(mode, tables, first, source, product):
    for odd in range(2):
        product[odd, mode] = dot(tables[first + odd], source[odd, mode])


def half_stage(mode, product, halfway):
    half = product.shape[2] // 2
    for at in range(0, half, TILE_ROWS):
        near, far = pl.ds(at, TILE_ROWS), pl.ds(half + at, TILE_ROWS)
        upper = [product[odd, mode, near] for odd in range(2)]
        lower = [product[odd, mode, far] for odd in range(2)]
        for odd in range(2):
            mixed = [a + b if not odd else a - b for a, b in zip(upper, lower)]
            real, imag = zip(*[lane_parts(part) for part in mixed])
            halfway[odd, mode, near] = side_by_side(real).astype(BF16)
            halfway[odd, mode, far] = side_by_side(imag).astype(BF16)


def residual_stage(modes, frame, field, amplitude, waves):
    half = frame // 2
    for odd in range(2):
        for at in range(0, half, TILE_ROWS):
            near, far = pl.ds(at, TILE_ROWS), pl.ds(half + at, TILE_ROWS)
            real = [field[odd, mode, near] for mode in range(modes)]
            imag = [field[odd, mode, far] for mode in range(modes)]
            lit = sum(a * a + b * b for a, b in zip(real, imag))
            factor = 1.0 / frame - amplitude[odd, near] * lax.rsqrt(jnp.maximum(lit, float(frame * frame)))
            target = pl.ds(odd * half + at, TILE_ROWS)
            for mode in range(modes):
                parts = [lane_parts(real[mode] * factor), lane_parts(imag[mode] * factor)]
                for column in range(2):
                    waves[column, mode, target] = side_by_side([part[column] for part in parts]).astype(BF16)


def back_stage(mode, product, halfway):
    half = product.shape[2] // 2
    for odd in range(2):
        for at in range(0, half, TILE_ROWS):
            rows = pl.ds(odd * half + at, TILE_ROWS)
            even_part, odd_part = product[0, mode, rows], product[1, mode, rows]
            near, far = lane_parts(even_part + odd_part), lane_parts(even_part - odd_part)
            halfway[odd, mode, pl.ds(at, TILE_ROWS)] = side_by_side([near[0], far[0]]).astype(BF16)
            halfway[odd, mode, pl.ds(half + at, TILE_ROWS)] = side_by_side([near[1], far[1]]).astype(BF16)


def gradient_stage(some_modes, first, product, probe, piece):
    frame = probe.shape[2]
    half = frame // 2
    across = frame // LANES
    for at in range(0, half, ROW_ALIGN):
        rows = [pl.ds(at, ROW_ALIGN), pl.ds(half + at, ROW_ALIGN)]
        grads = [[0.0, 0.0], [0.0, 0.0]]
        for mode in some_modes:
            mixed = [(product[0, mode, part], product[1, mode, part]) for part in rows]
            for side in range(2):
                back_real, back_imag = [a + b if not side else a - b for a, b in mixed]
                probe_real, probe_imag = probe[mode, 0, rows[side]], probe[mode, 1, rows[side]]
                grads[side][0] += probe_real * back_real + probe_imag * back_imag
                grads[side][1] += probe_real * back_imag - probe_imag * back_real
        for side in range(2):
            for plane in range(2):
                grad = grads[side][plane] * (1.0 / frame)
                for b in range(across):
                    where = (plane * across + b, rows[side], slice(None))
                    part = grad[:, b * LANES:(b + 1) * LANES]
                    piece[where] = part if first else piece[where] + part


def frame_step(patch, amplitude, probe, tables, waves, halfway, product, field, piece):
    modes, _, frame, _ = probe.shape
    pairs = modes // 2
    for step in range(pairs + 1):
        if step < pairs:
            for mode in (2 * step, 2 * step + 1):
                wave_stage(mode, probe, patch, waves)
            rows_dot(step, waves, tables, 0, product)
        if step:
            for mode in (2 * step - 2, 2 * step - 1):
                half_stage(mode, product, halfway)
                columns_dot(mode, tables, 2, halfway, field)
    residual_stage(modes, frame, field, amplitude, waves)
    for step in range(pairs + 1):
        if step < pairs:
            rows_dot(step, waves, tables, 4, product)
        if step:
            for mode in (2 * step - 2, 2 * step - 1):
                back_stage(mode, product, halfway)
                columns_dot(mode, tables, 6, halfway, field)
            gradient_stage((2 * step - 2, 2 * step - 1), step == 1, field, probe, piece)


def ordered_amplitude(measured, task, order, amplitude):
    frame = measured.shape[2]
    for odd in range(2):
        root = jnp.sqrt(side_by_side(
            [measured[task, b, pl.ds(odd, frame // 2, stride=2), :] for b in range(measured.shape[1])]))
        high = root.astype(BF16)
        low = (root - high.astype(F32)).astype(BF16)
        amplitude[odd] = dot(high, order) + dot(low, order)


def window(band, lead, row, col, height, across):
    return taken_from(
        [band[lead + (col // LANES + b, pl.ds(row, height), slice(None))] for b in range(across + 1)],
        lax.rem(col, LANES),
    )


def add_window(total, lead, parts, row, col, frame):
    for b, moved in enumerate(put_into(parts, lax.rem(col, LANES))):
        at = lead + (col // LANES + b, pl.ds(row, frame), slice(None))
        total[at] = total[at] + moved


def kernel_cost(frames, modes, frame):
    return pl.CostEstimate(
        flops=frames * modes * 4 * 4 * frame ** 3, bytes_accessed=16 * 1024 * 1024, transcendentals=0)


def frames_kernel(phases, own, up, parity, tile, edge, middle, frames, probe_in, tables_in, as_upper, as_lower, total_out, *rest):
    packed_outs = rest[:phases]
    (band, total, held, packed, piece, measured, probe, tables, patch, amplitude, waves, halfway, product, field, work,
     sems, shot_sems, held_sems, chunk_sems) = rest[phases:]
    cap, frame, _ = frames.shape
    extent = tile.shape[-1]
    across = frame // LANES
    own_blocks = extent // LANES
    half = frame // 2
    own_rows = pl.ds(frame, extent)

    first = start_all(
        [(tile.at[:, :, lanes_of(b)], band.at[:, b, own_rows]) for b in range(own_blocks)]
        + [(source.at[:, pl.ds(at, height), lanes_of(b)], band.at[:, own_blocks + b, pl.ds(frame + target, height)])
           for source, at, height, target in (
               (edge, 0, KEEP, 0), (middle, 0, extent - frame, KEEP), (edge, KEEP, frame - KEEP, KEEP + extent - frame))
           for b in range(across)]
        + [(probe_in, probe), (tables_in, tables)], sems)

    def mine(slot):
        return jnp.logical_and(slot < own[COUNT], own[FAR + slot] == 0)

    def borrowed(slot):
        return up[FAR + slot] > 0

    def shot_copies(slot, task, lent):
        if not lent:
            return [pltpu.make_async_copy(frames.at[slot, :, lanes_of(b)], measured.at[task, b], shot_sems.at[task, b])
                    for b in range(across)]
        at = pl.ds(pl.multiple_of(up[SHOT + slot], ROW_ALIGN), half)
        return [
            pltpu.make_async_copy(as_lower.at[at, lanes_of(part * across + b)],
                                  measured.at[task, b, pl.ds(part * half, half)], shot_sems.at[task, part * across + b])
            for part in range(2) for b in range(across)
        ]

    def held_copies(slot, task, lent):
        source, table = (as_lower, up) if lent else (as_upper, own)
        at = pl.ds(pl.multiple_of(table[PLACE + slot], ROW_ALIGN), frame)
        return [
            pltpu.make_async_copy(source.at[at, lanes_of(b)], held.at[task, b, pl.ds(frame, frame)], held_sems.at[task, b])
            for b in range(2 * across)
        ]

    def for_tasks(wait):
        for slot in range(cap):
            def run(copies):
                for copy in copies:
                    if wait:
                        copy.wait()
                    else:
                        copy.start()

            @pl.when(mine(slot))
            def _():
                run(shot_copies(slot, slot, False))

            @pl.when(own[NEAR + slot] > 0)
            def _():
                run(held_copies(slot, slot, False))

            @pl.when(borrowed(slot))
            def _():
                run(shot_copies(slot, cap + slot, True))
                run(held_copies(slot, cap + slot, True))

    for_tasks(False)
    for slot in range(cap):
        near = own[NEAR + slot]
        for field_at, value in (
            (ACTIVE, mine(slot).astype(jnp.int32)), (AT_ROW, own[ROW + slot] + frame), (AT_COL, own[COL + slot]),
            (LO, frame - near), (HI, frame), (START, near), (PIECE, own[PLACE + slot]), (SHIFT, frame - near), (ROLE, 0),
        ):
            work[slot, field_at] = value
        for field_at, value in (
            (ACTIVE, borrowed(slot).astype(jnp.int32)), (AT_ROW, up[ROW + slot] + frame - extent), (AT_COL, up[COL + slot]),
            (LO, 0), (HI, up[FAR + slot]), (START, frame), (PIECE, up[PLACE + slot]), (SHIFT, 0), (ROLE, 1),
        ):
            work[cap + slot, field_at] = value
    total[:, :, own_rows, :] = jnp.zeros((2, band.shape[1], extent, LANES), F32)
    wait_all(first)
    for_tasks(True)
    row_index = lax.broadcasted_iota(jnp.int32, (STEP, LANES), 0)

    def one(task, carry):
        @pl.when(work[task, ACTIVE] > 0)
        def _():
            row, col, start = work[task, AT_ROW], work[task, AT_COL], work[task, START]
            lo, hi = work[task, LO], work[task, HI]
            for at in range(0, frame, STEP):
                theirs = jnp.logical_and(row_index >= lo - at, row_index < hi - at)
                for plane in range(2):
                    near = window(band, (plane,), row + at, col, STEP, across)
                    other = [held[task, plane * across + b, pl.ds(start + at, STEP), :] for b in range(across)]
                    patch[plane, pl.ds(at, STEP)] = side_by_side([jnp.where(theirs, b, a) for a, b in zip(near, other)])
            ordered_amplitude(measured, task, tables[8], amplitude)
            frame_step(patch, amplitude, probe, tables, waves, halfway, product, field, piece)
            for at in range(0, frame, STEP):
                for plane in range(2):
                    parts = [piece[plane * across + b, pl.ds(at, STEP), :] for b in range(across)]
                    add_window(total, (plane,), parts, row + at, col, STEP)

            @pl.when(lo < hi)
            def _():
                target = pl.ds(pl.multiple_of(work[task, PIECE], ROW_ALIGN), frame)
                source = pl.ds(work[task, SHIFT], frame)
                for b in range(2 * across):
                    packed[work[task, ROLE], target, lanes_of(b)] = piece[b, source, :]

        return carry

    lax.fori_loop(0, 2 * cap, one, 0)
    end = start_all([(total.at[:, :, own_rows], total_out)], sems)
    for phase in range(phases):
        upper = parity[0] == phase
        role = jnp.where(upper, 0, 1)
        copy_out_rows(jnp.where(upper, own[KEPT], up[LENT]), packed.at[role], packed_outs[phase], chunk_sems)
    wait_all(end)


def frames_gradient(phases, own, up, parity, tile, edge, middle, frames, probe, tables, as_upper, as_lower):
    cap, frame, _ = frames.shape
    extent = tile.shape[-1]
    modes = probe.shape[0]
    tall = extent + 2 * frame
    blocks = (extent + frame) // LANES
    across = frame // LANES
    rows = as_upper.shape[0]
    kept_rows = cap * KEEP
    return pl.pallas_call(
        lambda *refs: frames_kernel(phases, *refs),
        out_shape=(jax.ShapeDtypeStruct((2, blocks, extent, LANES), F32),)
        + (jax.ShapeDtypeStruct(as_upper.shape, F32),) * phases,
        in_specs=[smem_spec()] * 3 + [hbm_spec()] * 8,
        out_specs=(hbm_spec(),) * (1 + phases),
        scratch_shapes=[
            pltpu.VMEM((2, blocks, tall, LANES), F32),
            pltpu.VMEM((2, blocks, tall, LANES), F32),
            pltpu.VMEM((2 * cap, 2 * across, 2 * frame, LANES), F32),
            pltpu.VMEM((2, kept_rows + frame, 2 * frame), F32),
            pltpu.VMEM((2 * across, 2 * frame, LANES), F32),
            pltpu.VMEM((2 * cap, across, frame, LANES), F32),
            pltpu.VMEM(probe.shape, F32),
            pltpu.VMEM(tables.shape, BF16),
            pltpu.VMEM((2, frame, frame), F32),
            pltpu.VMEM((2, frame // 2, frame), F32),
            pltpu.VMEM((2, modes, frame, frame), BF16),
            pltpu.VMEM((2, modes, frame, frame), BF16),
            pltpu.VMEM((2, modes, frame, frame), F32),
            pltpu.VMEM((2, modes, frame, frame), F32),
            pltpu.SMEM((2 * cap, 16), jnp.int32),
            pltpu.SemaphoreType.DMA((blocks + 2 * across + 2,)),
            pltpu.SemaphoreType.DMA((2 * cap, 2 * across)),
            pltpu.SemaphoreType.DMA((2 * cap, 2 * across)),
            pltpu.SemaphoreType.DMA((rows // CHUNK,)),
        ],
        compiler_params=params(55),
        cost_estimate=kernel_cost(cap, modes, frame),
        name="frames_gradient",
    )(own, up, parity, tile, edge, middle, frames, probe, tables, as_upper, as_lower)


def light_kernel(own, up, beside, probe, light_out, light, sem):
    modes, _, frame, _ = probe.shape
    own_blocks, extent, _ = light_out.shape
    across = frame // LANES
    inside = (pl.ds(across, own_blocks), pl.ds(frame, extent), slice(None))
    light[inside] = jnp.zeros((own_blocks, extent, LANES), F32)
    power = jnp.zeros((frame, frame), F32)
    for mode in range(modes):
        power += probe[mode, 0] * probe[mode, 0] + probe[mode, 1] * probe[mode, 1]
    power = halves(power)
    for table, lead, down, right in ((own, 0, 0, 0), (beside, 0, 0, 1), (up, 0, 1, 0), (beside, TABLE, 1, 1)):

        def lit(slot, carry, table=table, lead=lead, down=down, right=right):
            row = table[lead + ROW + slot] + frame - down * extent
            col = table[lead + COL + slot] + frame - right * extent

            @pl.when((row > 0) & (col > 0))
            def _():
                add_window(light, (), power, row, col, frame)

            return carry

        lax.fori_loop(0, table[lead + COUNT], lit, 0)
    copy = pltpu.make_async_copy(light.at[inside[0], inside[1]], light_out, sem)
    copy.start()
    copy.wait()


def light_plane(own, up, beside, probe, extent):
    frame = probe.shape[-1]
    wide = extent + 2 * frame
    return pl.pallas_call(
        light_kernel,
        out_shape=jax.ShapeDtypeStruct((extent // LANES, extent, LANES), F32),
        in_specs=[smem_spec()] * 3 + [vmem_spec()],
        out_specs=any_spec(),
        scratch_shapes=[pltpu.VMEM((wide // LANES, wide, LANES), F32), pltpu.SemaphoreType.DMA],
        compiler_params=params(9),
        cost_estimate=pl.CostEstimate(flops=0, bytes_accessed=4 * MIB, transcendentals=0),
        name="light_plane",
    )(own, up, beside, probe)


def add_pieces(frame, table, needed, field, pieces, band, blocks, height, row_of, held, sems, loads=()):
    across = frame // LANES
    cap = (held.shape[1] - KEEP) // KEEP
    chunks = (needed + CHUNK - 1) // CHUNK
    row_index = lax.broadcasted_iota(jnp.int32, (height, LANES), 0)

    def copies(chunk):
        at = pl.ds(pl.multiple_of(chunk * CHUNK, CHUNK), CHUNK)
        return [pltpu.make_async_copy(pieces.at[at, lanes_of(b)], held.at[b, at], sems.at[chunk * 2 * across + b])
                for b in range(2 * across)]

    def begin(chunk, carry):
        for copy in copies(chunk):
            copy.start()
        return carry

    def end(chunk, carry):
        for copy in copies(chunk):
            copy.wait()
        return carry

    def one(slot, carry):
        used = table[field + slot]
        first = table[COL + slot] // LANES

        @pl.when(jnp.logical_and(used > 0, jnp.logical_and(first + across >= blocks[0], first < blocks[1])))
        def _():
            at = pl.ds(pl.multiple_of(table[PLACE + slot], ROW_ALIGN), height)
            for plane in range(2):
                got = [jnp.where(row_index < used, held[plane * across + b, at, :], 0.0) for b in range(across)]
                for b, moved in enumerate(put_into(got, lax.rem(table[COL + slot], LANES))):
                    @pl.when(jnp.logical_and(first + b >= blocks[0], first + b < blocks[1]))
                    def _():
                        where = (plane, first + b - blocks[0], pl.ds(row_of(slot), height), slice(None))
                        band[where] = band[where] + moved

        return carry

    lax.fori_loop(0, chunks, begin, 0)
    lax.fori_loop(0, chunks, end, 0)
    wait_all(loads)

    @pl.when(needed > 0)
    def _():
        lax.fori_loop(0, cap, one, 0)


def join_right_kernel(frame, own, up, as_upper, as_lower, total, right_out, band, held, sems, piece_sems):
    across = frame // LANES
    blocks, extent = total.shape[1:3]
    rows = pl.ds(0, extent)
    reach = (blocks - across, blocks)
    loads = start_all([(total.at[:, pl.ds(blocks - across, across)], band.at[:, :, rows])], sems)
    add_pieces(frame, own, own[LENT], FAR, as_upper, band, reach, frame - KEEP, lambda slot: own[ROW + slot], held, piece_sems,
               loads)
    add_pieces(frame, up, up[KEPT], NEAR, as_lower, band, reach, KEEP, lambda slot: 0, held, piece_sems)
    wait_all(start_all([(band.at[:, :, rows], right_out)], sems))


def join_right(own, up, as_upper, as_lower, total, cap):
    frame = as_upper.shape[1] // 2
    extent = total.shape[2]
    across = frame // LANES
    rows = cap * KEEP
    return pl.pallas_call(
        lambda *refs: join_right_kernel(frame, *refs),
        out_shape=jax.ShapeDtypeStruct((2, across, extent, LANES), F32),
        in_specs=[smem_spec(), smem_spec(), hbm_spec(), hbm_spec(), hbm_spec()],
        out_specs=any_spec(),
        scratch_shapes=[
            pltpu.VMEM((2, across, extent + frame, LANES), F32),
            pltpu.VMEM((2 * across, rows + KEEP, LANES), F32),
            pltpu.SemaphoreType.DMA((1,)),
            pltpu.SemaphoreType.DMA((rows // CHUNK * 2 * across,)),
        ],
        compiler_params=params(56),
        name="join_right",
    )(own, up, as_upper, as_lower, total)


def join_own_kernel(frame, own, up, as_upper, as_lower, total_in, total_out, top, bottom, held, sems, piece_sems):
    own_blocks = top.shape[1]
    extent = total_in.shape[2]
    tail = frame - KEEP
    mine = pl.ds(0, own_blocks)
    reach = (0, own_blocks)

    def part(needed, rows, band, source, table, field, height, row_of):
        @pl.when(needed > 0)
        def _():
            loads = start_all([(total_in.at[:, mine, rows], band)], sems)
            add_pieces(frame, table, needed, field, source, band_of[field], reach, height, row_of, held, piece_sems, loads)
            wait_all(start_all([(band, total_out.at[:, mine, rows])], sems))

    band_of = {FAR: bottom, NEAR: top}
    part(own[LENT], pl.ds(extent - tail, tail), bottom.at[:, :, pl.ds(0, tail)], as_upper, own, FAR, tail,
         lambda slot: own[ROW + slot] - (extent - tail))
    part(up[KEPT], pl.ds(0, KEEP), top, as_lower, up, NEAR, KEEP, lambda slot: 0)


def join_own(own, up, as_upper, as_lower, total, cap):
    frame = as_upper.shape[1] // 2
    own_blocks = total.shape[2] // LANES
    across = frame // LANES
    rows = cap * KEEP
    return pl.pallas_call(
        lambda *refs: join_own_kernel(frame, *refs),
        out_shape=jax.ShapeDtypeStruct(total.shape, F32),
        in_specs=[smem_spec(), smem_spec(), hbm_spec(), hbm_spec(), hbm_spec()],
        out_specs=hbm_spec(),
        input_output_aliases={4: 0},
        scratch_shapes=[
            pltpu.VMEM((2, own_blocks, KEEP, LANES), F32),
            pltpu.VMEM((2, own_blocks, 2 * (frame - KEEP), LANES), F32),
            pltpu.VMEM((2 * across, rows + KEEP, LANES), F32),
            pltpu.SemaphoreType.DMA((1,)),
            pltpu.SemaphoreType.DMA((rows // CHUNK * 2 * across,)),
        ],
        compiler_params=params(56),
        name="join_own",
    )(own, up, as_upper, as_lower, total)


def right_half_kernel(tile, total, light, out):
    for b in range(total.shape[1]):
        below = 1.0 / (light[b] + 1.0)
        for plane in range(2):
            out[plane, :, lanes_of(b)] = tile[plane, :, lanes_of(b)] - total[plane, b] * below


def right_half(tile, total, light):
    extent = tile.shape[-1]
    across = total.shape[1] * LANES - extent
    part = (extent - across) // LANES
    tall = 128
    return pl.pallas_call(
        right_half_kernel,
        grid=(extent // tall,),
        out_shape=jax.ShapeDtypeStruct(tile.shape, F32),
        in_specs=[
            pl.BlockSpec((2, tall, extent - across), lambda i: (0, i, 1)),
            pl.BlockSpec((2, part, tall, LANES), lambda i: (0, 1, i, 0)),
            pl.BlockSpec((part, tall, LANES), lambda i: (1, i, 0)),
        ],
        out_specs=pl.BlockSpec((2, tall, extent - across), lambda i: (0, i, 1)),
        compiler_params=params(8),
        name="right_half",
    )(tile, total, light)


def left_half_kernel(tile, total, light, left, begun, out):
    for b in range(total.shape[1]):
        below = 1.0 / (light[b] + 1.0)
        for plane in range(2):
            grad = total[plane, b] + left[plane, b]
            out[plane, :, lanes_of(b)] = tile[plane, :, lanes_of(b)] - grad * below


def left_half(tile, total, light, left, begun):
    extent = tile.shape[-1]
    across = left.shape[1]
    tall = 256
    return pl.pallas_call(
        left_half_kernel,
        grid=(extent // tall,),
        out_shape=jax.ShapeDtypeStruct(tile.shape, F32),
        in_specs=[
            pl.BlockSpec((2, tall, across * LANES), lambda i: (0, i, 0)),
            pl.BlockSpec((2, across, tall, LANES), lambda i: (0, 0, i, 0)),
            pl.BlockSpec((across, tall, LANES), lambda i: (0, i, 0)),
            pl.BlockSpec((2, across, tall, LANES), lambda i: (0, 0, i, 0)),
            any_spec(),
        ],
        out_specs=pl.BlockSpec((2, tall, across * LANES), lambda i: (0, i, 0)),
        input_output_aliases={4: 0},
        compiler_params=params(8),
        name="left_half",
    )(tile, total, light, left, begun)


def body(object_tiles, probe, positions, frames, counts):
    tile = object_tiles[0]
    extent = tile.shape[-1]
    frame = frames.shape[-1]
    cap = frames.shape[1]
    peers = lax.axis_size("scan")
    tile_row = lax.axis_index("scan") // TCOLS
    phases = min(2, peers // TCOLS - 1)
    tables = dft_tables(frame)
    parity = (tile_row % 2).reshape(1)
    even = tile_row % 2 == 0

    own = slot_table(positions, counts, extent, frame)
    up = shifted(own, "scan", TCOLS)
    edge, middle, up = lax.optimization_barrier((*strips(tile, frame), up))
    edge = shifted(edge, "scan", -1)
    middle = shifted(middle, "scan", -1)
    beside = shifted(jnp.concatenate([own, up]), "scan", 1)

    def exchange(phase, packed, choice):
        uppers = [k for k in range(peers - TCOLS) if k // TCOLS % 2 == phase]
        pairs = [(k, k + TCOLS) for k in uppers] + [(k + TCOLS, k) for k in uppers]

        def sender(size):
            def run(data):
                return lax.dynamic_update_slice(data, lax.ppermute(data[:size], "scan", pairs), (0, 0))
            return run

        branches = [lambda data: data] + [sender(size) for size in SIZES if size <= packed.shape[0]]
        return lax.switch(choice.reshape(()), branches, packed)

    def by_role(arrays):
        if len(arrays) == 1:
            return arrays[0], arrays[0]
        return jnp.where(even, arrays[0], arrays[1]), jnp.where(even, arrays[1], arrays[0])

    cuts = [cut_pieces(phase, own, up, parity, tile, edge, frames[0]) for phase in range(phases)]
    received = by_role([exchange(phase, cut[0], cut[1]) for phase, cut in enumerate(cuts)])
    received, beside = lax.optimization_barrier((received, beside))
    total, *packed = frames_gradient(
        phases, own, up, parity, tile, edge, middle, frames[0], probe, tables, *received)
    returned = by_role([exchange(phase, packed[phase], cut[2]) for phase, cut in enumerate(cuts)])
    right = join_right(own, up, *returned, total, cap)
    right, total, beside = lax.optimization_barrier((right, total, beside))
    left = shifted(right, "scan", 1)
    total = join_own(own, up, *returned, total, cap)
    light = light_plane(own, up, beside, probe, extent)
    begun = right_half(tile, total, light)
    return left_half(tile, total, light, left, begun)[None]


def solution(mesh):
    return jax.shard_map(
        body,
        mesh=mesh,
        in_specs=(
            P(("grp", "scan"), None, None, None),
            P(),
            P(("grp", "scan"), None, None),
            P(("grp", "scan"), None, None, None),
            P(("grp", "scan")),
        ),
        out_specs=P(("grp", "scan"), None, None, None),
        check_vma=False,
    )
```

```python
import math

import jax
import jax.numpy as jnp
import numpy as np
from jax import lax
from jax.experimental import pallas as pl
from jax.experimental.pallas import tpu as pltpu
from jax.sharding import PartitionSpec as P

TCOLS = 8
LANES = 128
ROW_ALIGN = 8
CHUNK = 64
STEP = 32
TILE_ROWS = 16
SIZES = (32, 64, 96, 128, 160, 192, 224, 256, 320, 384, 448, 512, 640, 768, 960, 1344)
MIB = 1024 * 1024
F32 = jnp.float32
BF16 = jnp.bfloat16

KEEP = 160
ROW, COL, NEAR, FAR, PLACE, SHOT = 0, 8, 16, 24, 32, 40
COUNT, KEPT, LENT, FORTH, BACK = 48, 49, 50, 51, 52
TABLE = 64

ACTIVE, AT_ROW, AT_COL, LO, HI, START, PIECE, SHIFT, ROLE = range(9)


def dft_tables(frame):
    near = np.arange(frame // 2, dtype=np.int64)
    blocks = []
    for odd in range(2):
        phase = (near[:, None] * (2 * near[None, :] + odd) % frame).astype(np.float64) * (2.0 * math.pi / frame)
        c, s = np.cos(phase), np.sin(phase)
        ahead = np.block([[c, -s], [s, c]])
        back = np.block([[c.T, s.T], [-s.T, c.T]])
        blocks.append((ahead, ahead.T, back, back.T))
    order = np.zeros((frame, frame))
    order[2 * near, near] = 1.0
    order[2 * near + 1, near + frame // 2] = 1.0
    tables = [blocks[odd][kind] for kind in range(4) for odd in range(2)] + [order]
    return jnp.asarray(np.stack(tables), F32).astype(BF16)


def shifted(array, axis, by):
    peers = lax.axis_size(axis)
    pairs = [(i, i + by) for i in range(peers) if 0 <= i + by < peers]
    return lax.ppermute(array, axis, pairs)


def any_spec():
    return pl.BlockSpec(memory_space=pl.ANY)


def hbm_spec():
    return pl.BlockSpec(memory_space=pltpu.HBM)


def smem_spec():
    return pl.BlockSpec(memory_space=pltpu.SMEM)


def vmem_spec():
    return pl.BlockSpec(memory_space=pltpu.VMEM)


def params(mebibytes):
    return pltpu.CompilerParams(vmem_limit_bytes=mebibytes * MIB)


def taken_from(blocks, by):
    lane = lax.broadcasted_iota(jnp.int32, blocks[0].shape, 1)
    rolled = [pltpu.roll(block, lax.rem(LANES - by, LANES), axis=1) for block in blocks]
    return [jnp.where(lane < LANES - by, one, two) for one, two in zip(rolled[:-1], rolled[1:])]


def put_into(blocks, by):
    lane = lax.broadcasted_iota(jnp.int32, blocks[0].shape, 1)
    rolled = [pltpu.roll(block, by, axis=1) for block in blocks]
    none = jnp.zeros_like(blocks[0])
    return [jnp.where(lane >= by, one, two) for one, two in zip(rolled + [none], [none] + rolled)]


def start_all(pairs, sems, first=0):
    copies = [pltpu.make_async_copy(source, target, sems.at[first + at]) for at, (source, target) in enumerate(pairs)]
    for copy in copies:
        copy.start()
    return copies


def wait_all(copies):
    for copy in copies:
        copy.wait()


def lanes_of(block):
    return pl.ds(block * LANES, LANES)


def side_by_side(parts):
    return jnp.concatenate(parts, axis=1)


def halves(array):
    return [array[:, :LANES], array[:, LANES:]]


def copy_out_rows(needed, packed, out, sems):
    chunks = (needed + CHUNK - 1) // CHUNK

    def copy(chunk):
        at = pl.ds(pl.multiple_of(chunk * CHUNK, CHUNK), CHUNK)
        return pltpu.make_async_copy(packed.at[at], out.at[at], sems.at[chunk])

    def begin(chunk, carry):
        copy(chunk).start()
        return carry

    def end(chunk, carry):
        copy(chunk).wait()
        return carry

    lax.fori_loop(0, chunks, begin, 0)
    lax.fori_loop(0, chunks, end, 0)


def up_to(value, step):
    return (value + step - 1) // step * step


def size_choice(needed):
    choice = jnp.where(needed > 0, 1, 0)
    for size in SIZES:
        choice = choice + jnp.where(needed > size, 1, 0)
    return choice


def strip_kernel(tile, edge, middle, sems):
    extent = tile.shape[-1]
    frame = edge.shape[-1]
    lanes = pl.ds(0, frame)
    wait_all(start_all([
        (tile.at[:, pl.ds(0, KEEP), lanes], edge.at[:, pl.ds(0, KEEP)]),
        (tile.at[:, pl.ds(KEEP + extent - frame, frame - KEEP), lanes], edge.at[:, pl.ds(KEEP, frame - KEEP)]),
        (tile.at[:, pl.ds(KEEP, extent - frame), lanes], middle),
    ], sems))


def table_kernel(extent, frame, positions, counts, table):
    cap = positions.shape[2]
    count = counts[0]
    kept, lent, shots = jnp.int32(0), jnp.int32(0), jnp.int32(0)
    for at in range(TABLE):
        table[at] = 0
    for slot in range(cap):
        row = lax.rem(positions[0, 0, slot], extent)
        col = lax.rem(positions[0, 1, slot], extent)
        below = jnp.where(slot < count, jnp.maximum(row + (frame - extent), 0), 0)
        stays = below <= KEEP
        near = jnp.where(stays, below, 0)
        far = jnp.where(stays, 0, frame - below)
        table[ROW + slot] = row
        table[COL + slot] = col
        table[NEAR + slot] = near
        table[FAR + slot] = far
        table[PLACE + slot] = jnp.where(stays, kept, lent)
        table[SHOT + slot] = shots
        kept = kept + up_to(near, ROW_ALIGN)
        lent = lent + up_to(far, ROW_ALIGN)
        shots = shots + jnp.where(stays, 0, frame // 2)
    for slot in range(cap):
        table[SHOT + slot] = table[SHOT + slot] + lent
    table[COUNT] = count
    table[KEPT] = kept
    table[LENT] = lent
    table[FORTH] = jnp.maximum(kept, lent + shots)
    table[BACK] = jnp.maximum(kept, lent)


def slot_table(positions, counts, extent, frame):
    return pl.pallas_call(
        lambda *refs: table_kernel(extent, frame, *refs),
        out_shape=jax.ShapeDtypeStruct((TABLE,), jnp.int32),
        in_specs=[smem_spec(), smem_spec()],
        out_specs=smem_spec(),
        name="slot_table",
    )(jnp.swapaxes(positions, 1, 2), counts)


def strips(tile, frame):
    extent = tile.shape[-1]
    return pl.pallas_call(
        strip_kernel,
        out_shape=(
            jax.ShapeDtypeStruct((2, frame, frame), F32),
            jax.ShapeDtypeStruct((2, extent - frame, frame), F32),
        ),
        in_specs=[hbm_spec()],
        out_specs=(vmem_spec(), vmem_spec()),
        scratch_shapes=[pltpu.SemaphoreType.DMA((3,))],
        compiler_params=params(61),
        name="strips",
    )(tile)


def cut_kernel(phase, own, up, parity, tile, edge, frames, out, forth, back, band, packed, sems, chunk_sems):
    cap, frame, _ = frames.shape
    extent = tile.shape[-1]
    across = frame // LANES
    own_blocks = extent // LANES
    upper = parity[0] == phase
    forth[0] = size_choice(jnp.where(upper, own[FORTH], up[FORTH]))
    back[0] = size_choice(jnp.where(upper, own[BACK], up[BACK]))
    lends = jnp.logical_and(upper, own[LENT] > 0)
    gives = jnp.logical_and(jnp.logical_not(upper), up[KEPT] > 0)

    def cut(col, row, place):
        at = pl.ds(pl.multiple_of(place, ROW_ALIGN), frame)
        for plane in range(2):
            packed[at, pl.ds(plane * frame, frame)] = side_by_side(window(band, (plane,), row, col, frame, across))

    @pl.when(jnp.logical_or(lends, gives))
    def _():
        base = jnp.where(upper, extent - frame, 0)
        rows = pl.ds(pl.multiple_of(base, ROW_ALIGN), frame)
        wait_all(start_all(
            [(tile.at[:, rows, lanes_of(b)], band.at[:, b, pl.ds(0, frame)]) for b in range(own_blocks)]
            + [(edge.at[:, :, lanes_of(b)], band.at[:, own_blocks + b, pl.ds(0, frame)]) for b in range(across)], sems))

        def one(slot, carry):
            @pl.when(jnp.logical_and(upper, own[FAR + slot] > 0))
            def _():
                cut(own[COL + slot], own[ROW + slot] - (extent - frame), own[PLACE + slot])

            @pl.when(jnp.logical_and(gives, up[NEAR + slot] > 0))
            def _():
                cut(up[COL + slot], 0, up[PLACE + slot])

            return carry

        lax.fori_loop(0, cap, one, 0)

        def shots(slot):
            at = pl.ds(pl.multiple_of(own[SHOT + slot], ROW_ALIGN), frame // 2)
            return [pltpu.make_async_copy(frames.at[slot, pl.ds(part * frame // 2, frame // 2)],
                                          packed.at[at, pl.ds(part * frame, frame)], sems.at[2 * slot + part])
                    for part in range(2)]

        for wait in range(2):
            for slot in range(cap):
                @pl.when(jnp.logical_and(lends, own[FAR + slot] > 0))
                def _():
                    for copy in shots(slot):
                        if wait:
                            copy.wait()
                        else:
                            copy.start()

        copy_out_rows(jnp.where(upper, own[FORTH], up[KEPT]), packed, out, chunk_sems)


def cut_pieces(phase, own, up, parity, tile, edge, frames):
    cap, frame, _ = frames.shape
    extent = tile.shape[-1]
    blocks = (extent + frame) // LANES
    rows = SIZES[-1]
    return pl.pallas_call(
        lambda *refs: cut_kernel(phase, *refs),
        out_shape=(
            jax.ShapeDtypeStruct((rows, 2 * frame), F32),
            jax.ShapeDtypeStruct((1,), jnp.int32),
            jax.ShapeDtypeStruct((1,), jnp.int32),
        ),
        in_specs=[smem_spec(), smem_spec(), smem_spec(), hbm_spec(), hbm_spec(), hbm_spec()],
        out_specs=(hbm_spec(), smem_spec(), smem_spec()),
        scratch_shapes=[
            pltpu.VMEM((2, blocks, 2 * frame, LANES), F32),
            pltpu.VMEM((rows + frame, 2 * frame), F32),
            pltpu.SemaphoreType.DMA((max(blocks, 2 * cap),)),
            pltpu.SemaphoreType.DMA((rows // CHUNK,)),
        ],
        compiler_params=params(60),
        name="cut_pieces",
    )(own, up, parity, tile, edge, frames)


def dot(one, two):
    return jnp.dot(one, two, preferred_element_type=F32)


def stacked(parts):
    return jnp.concatenate(parts, axis=0)


def lane_parts(array):
    half = array.shape[1] // 2
    return array[:, :half], array[:, half:]


def wave_stage(mode, probe, patch, waves):
    frame = probe.shape[2]
    for at in range(0, frame, TILE_ROWS):
        rows = pl.ds(at, TILE_ROWS)
        probe_real, probe_imag = probe[mode, 0, rows], probe[mode, 1, rows]
        patch_real, patch_imag = patch[0, rows], patch[1, rows]
        parts = [lane_parts(part) for part in (
            probe_real * patch_real - probe_imag * patch_imag, probe_real * patch_imag + probe_imag * patch_real)]
        waves[0, mode, rows] = side_by_side([near + far for near, far in parts]).astype(BF16)
        waves[1, mode, rows] = side_by_side([near - far for near, far in parts]).astype(BF16)


def rows_dot(start, count, source, tables, first, product):
    modes = pl.ds(start, count)
    for odd in range(2):
        both = source[odd, modes]
        product[odd, modes] = dot(both.reshape(count * both.shape[1], both.shape[2]), tables[first + odd]).reshape(both.shape)


def columns_dot(mode, tables, first, source, product):
    for odd in range(2):
        product[odd, mode] = dot(tables[first + odd], source[odd, mode])


def half_stage(mode, product, halfway):
    half = product.shape[2] // 2
    for at in range(0, half, TILE_ROWS):
        near, far = pl.ds(at, TILE_ROWS), pl.ds(half + at, TILE_ROWS)
        upper = [product[odd, mode, near] for odd in range(2)]
        lower = [product[odd, mode, far] for odd in range(2)]
        for odd in range(2):
            mixed = [a + b if not odd else a - b for a, b in zip(upper, lower)]
            real, imag = zip(*[lane_parts(part) for part in mixed])
            halfway[odd, mode, near] = side_by_side(real).astype(BF16)
            halfway[odd, mode, far] = side_by_side(imag).astype(BF16)


def residual_stage(modes, frame, field, amplitude, waves):
    half = frame // 2
    for odd in range(2):
        for at in range(0, half, TILE_ROWS):
            near, far = pl.ds(at, TILE_ROWS), pl.ds(half + at, TILE_ROWS)
            real = [field[odd, mode, near] for mode in range(modes)]
            imag = [field[odd, mode, far] for mode in range(modes)]
            lit = sum(a * a + b * b for a, b in zip(real, imag))
            factor = 1.0 / frame - amplitude[odd, near] * lax.rsqrt(jnp.maximum(lit, float(frame * frame)))
            target = pl.ds(odd * half + at, TILE_ROWS)
            for mode in range(modes):
                parts = [lane_parts(real[mode] * factor), lane_parts(imag[mode] * factor)]
                for column in range(2):
                    waves[column, mode, target] = side_by_side([part[column] for part in parts]).astype(BF16)


def back_stage(mode, product, halfway):
    half = product.shape[2] // 2
    for odd in range(2):
        for at in range(0, half, TILE_ROWS):
            rows = pl.ds(odd * half + at, TILE_ROWS)
            even_part, odd_part = product[0, mode, rows], product[1, mode, rows]
            near, far = lane_parts(even_part + odd_part), lane_parts(even_part - odd_part)
            halfway[odd, mode, pl.ds(at, TILE_ROWS)] = side_by_side([near[0], far[0]]).astype(BF16)
            halfway[odd, mode, pl.ds(half + at, TILE_ROWS)] = side_by_side([near[1], far[1]]).astype(BF16)


def gradient_stage(some_modes, first, product, probe, piece):
    frame = probe.shape[2]
    half = frame // 2
    across = frame // LANES
    for at in range(0, half, ROW_ALIGN):
        rows = [pl.ds(at, ROW_ALIGN), pl.ds(half + at, ROW_ALIGN)]
        grads = [[0.0, 0.0], [0.0, 0.0]]
        for mode in some_modes:
            mixed = [(product[0, mode, part], product[1, mode, part]) for part in rows]
            for side in range(2):
                back_real, back_imag = [a + b if not side else a - b for a, b in mixed]
                probe_real, probe_imag = probe[mode, 0, rows[side]], probe[mode, 1, rows[side]]
                grads[side][0] += probe_real * back_real + probe_imag * back_imag
                grads[side][1] += probe_real * back_imag - probe_imag * back_real
        for side in range(2):
            for plane in range(2):
                grad = grads[side][plane] * (1.0 / frame)
                for b in range(across):
                    where = (plane * across + b, rows[side], slice(None))
                    part = grad[:, b * LANES:(b + 1) * LANES]
                    piece[where] = part if first else piece[where] + part


def frame_step(patch, amplitude, probe, tables, waves, halfway, product, field, piece):
    modes, _, frame, _ = probe.shape
    pairs = modes // 2
    for step in range(pairs + 1):
        if step < pairs:
            for mode in (2 * step, 2 * step + 1):
                wave_stage(mode, probe, patch, waves)
            rows_dot(2 * step, 2, waves, tables, 0, product)
        if step:
            for mode in (2 * step - 2, 2 * step - 1):
                half_stage(mode, product, halfway)
                columns_dot(mode, tables, 2, halfway, field)
    residual_stage(modes, frame, field, amplitude, waves)
    rows_dot(0, modes, waves, tables, 4, product)
    for step in range(pairs):
        for mode in (2 * step, 2 * step + 1):
            back_stage(mode, product, halfway)
            columns_dot(mode, tables, 6, halfway, field)
        gradient_stage((2 * step, 2 * step + 1), step == 0, field, probe, piece)


def ordered_amplitude(measured, task, order, amplitude):
    frame = measured.shape[2]
    for odd in range(2):
        root = jnp.sqrt(side_by_side(
            [measured[task, b, pl.ds(odd, frame // 2, stride=2), :] for b in range(measured.shape[1])]))
        high = root.astype(BF16)
        low = (root - high.astype(F32)).astype(BF16)
        amplitude[odd] = dot(high, order) + dot(low, order)


def window(band, lead, row, col, height, across):
    return taken_from(
        [band[lead + (col // LANES + b, pl.ds(row, height), slice(None))] for b in range(across + 1)],
        lax.rem(col, LANES),
    )


def add_window(total, lead, parts, row, col, frame):
    for b, moved in enumerate(put_into(parts, lax.rem(col, LANES))):
        at = lead + (col // LANES + b, pl.ds(row, frame), slice(None))
        total[at] = total[at] + moved


def kernel_cost(frames, modes, frame):
    return pl.CostEstimate(
        flops=frames * modes * 4 * 4 * frame ** 3, bytes_accessed=16 * 1024 * 1024, transcendentals=0)


def frames_kernel(phases, own, up, parity, tile, edge, middle, frames, probe_in, tables_in, as_upper, as_lower, total_out, *rest):
    packed_outs = rest[:phases]
    (band, total, held, packed, piece, measured, probe, tables, patch, amplitude, waves, halfway, product, field, work,
     sems, shot_sems, held_sems, chunk_sems) = rest[phases:]
    cap, frame, _ = frames.shape
    extent = tile.shape[-1]
    across = frame // LANES
    own_blocks = extent // LANES
    half = frame // 2
    own_rows = pl.ds(frame, extent)

    first = start_all(
        [(tile.at[:, :, lanes_of(b)], band.at[:, b, own_rows]) for b in range(own_blocks)]
        + [(source.at[:, pl.ds(at, height), lanes_of(b)], band.at[:, own_blocks + b, pl.ds(frame + target, height)])
           for source, at, height, target in (
               (edge, 0, KEEP, 0), (middle, 0, extent - frame, KEEP), (edge, KEEP, frame - KEEP, KEEP + extent - frame))
           for b in range(across)]
        + [(probe_in, probe), (tables_in, tables)], sems)

    def mine(slot):
        return jnp.logical_and(slot < own[COUNT], own[FAR + slot] == 0)

    def borrowed(slot):
        return up[FAR + slot] > 0

    def shot_copies(slot, task, lent):
        if not lent:
            return [pltpu.make_async_copy(frames.at[slot, :, lanes_of(b)], measured.at[task, b], shot_sems.at[task, b])
                    for b in range(across)]
        at = pl.ds(pl.multiple_of(up[SHOT + slot], ROW_ALIGN), half)
        return [
            pltpu.make_async_copy(as_lower.at[at, lanes_of(part * across + b)],
                                  measured.at[task, b, pl.ds(part * half, half)], shot_sems.at[task, part * across + b])
            for part in range(2) for b in range(across)
        ]

    def held_copies(slot, task, lent):
        source, table = (as_lower, up) if lent else (as_upper, own)
        at = pl.ds(pl.multiple_of(table[PLACE + slot], ROW_ALIGN), frame)
        return [
            pltpu.make_async_copy(source.at[at, lanes_of(b)], held.at[task, b, pl.ds(frame, frame)], held_sems.at[task, b])
            for b in range(2 * across)
        ]

    def for_tasks(wait):
        for slot in range(cap):
            def run(copies):
                for copy in copies:
                    if wait:
                        copy.wait()
                    else:
                        copy.start()

            @pl.when(mine(slot))
            def _():
                run(shot_copies(slot, slot, False))

            @pl.when(own[NEAR + slot] > 0)
            def _():
                run(held_copies(slot, slot, False))

            @pl.when(borrowed(slot))
            def _():
                run(shot_copies(slot, cap + slot, True))
                run(held_copies(slot, cap + slot, True))

    for_tasks(False)
    for slot in range(cap):
        near = own[NEAR + slot]
        for field_at, value in (
            (ACTIVE, mine(slot).astype(jnp.int32)), (AT_ROW, own[ROW + slot] + frame), (AT_COL, own[COL + slot]),
            (LO, frame - near), (HI, frame), (START, near), (PIECE, own[PLACE + slot]), (SHIFT, frame - near), (ROLE, 0),
        ):
            work[slot, field_at] = value
        for field_at, value in (
            (ACTIVE, borrowed(slot).astype(jnp.int32)), (AT_ROW, up[ROW + slot] + frame - extent), (AT_COL, up[COL + slot]),
            (LO, 0), (HI, up[FAR + slot]), (START, frame), (PIECE, up[PLACE + slot]), (SHIFT, 0), (ROLE, 1),
        ):
            work[cap + slot, field_at] = value
    total[:, :, own_rows, :] = jnp.zeros((2, band.shape[1], extent, LANES), F32)
    wait_all(first)
    for_tasks(True)
    row_index = lax.broadcasted_iota(jnp.int32, (STEP, LANES), 0)

    def one(task, carry):
        @pl.when(work[task, ACTIVE] > 0)
        def _():
            row, col, start = work[task, AT_ROW], work[task, AT_COL], work[task, START]
            lo, hi = work[task, LO], work[task, HI]
            for at in range(0, frame, STEP):
                theirs = jnp.logical_and(row_index >= lo - at, row_index < hi - at)
                for plane in range(2):
                    near = window(band, (plane,), row + at, col, STEP, across)
                    other = [held[task, plane * across + b, pl.ds(start + at, STEP), :] for b in range(across)]
                    patch[plane, pl.ds(at, STEP)] = side_by_side([jnp.where(theirs, b, a) for a, b in zip(near, other)])
            ordered_amplitude(measured, task, tables[8], amplitude)
            frame_step(patch, amplitude, probe, tables, waves, halfway, product, field, piece)
            for at in range(0, frame, STEP):
                for plane in range(2):
                    parts = [piece[plane * across + b, pl.ds(at, STEP), :] for b in range(across)]
                    add_window(total, (plane,), parts, row + at, col, STEP)

            @pl.when(lo < hi)
            def _():
                target = pl.ds(pl.multiple_of(work[task, PIECE], ROW_ALIGN), frame)
                source = pl.ds(work[task, SHIFT], frame)
                for b in range(2 * across):
                    packed[work[task, ROLE], target, lanes_of(b)] = piece[b, source, :]

        return carry

    lax.fori_loop(0, 2 * cap, one, 0)
    end = start_all([(total.at[:, :, own_rows], total_out)], sems)
    for phase in range(phases):
        upper = parity[0] == phase
        role = jnp.where(upper, 0, 1)
        copy_out_rows(jnp.where(upper, own[KEPT], up[LENT]), packed.at[role], packed_outs[phase], chunk_sems)
    wait_all(end)


def frames_gradient(phases, own, up, parity, tile, edge, middle, frames, probe, tables, as_upper, as_lower):
    cap, frame, _ = frames.shape
    extent = tile.shape[-1]
    modes = probe.shape[0]
    tall = extent + 2 * frame
    blocks = (extent + frame) // LANES
    across = frame // LANES
    rows = as_upper.shape[0]
    kept_rows = cap * KEEP
    return pl.pallas_call(
        lambda *refs: frames_kernel(phases, *refs),
        out_shape=(jax.ShapeDtypeStruct((2, blocks, extent, LANES), F32),)
        + (jax.ShapeDtypeStruct(as_upper.shape, F32),) * phases,
        in_specs=[smem_spec()] * 3 + [hbm_spec()] * 8,
        out_specs=(hbm_spec(),) * (1 + phases),
        scratch_shapes=[
            pltpu.VMEM((2, blocks, tall, LANES), F32),
            pltpu.VMEM((2, blocks, tall, LANES), F32),
            pltpu.VMEM((2 * cap, 2 * across, 2 * frame, LANES), F32),
            pltpu.VMEM((2, kept_rows + frame, 2 * frame), F32),
            pltpu.VMEM((2 * across, 2 * frame, LANES), F32),
            pltpu.VMEM((2 * cap, across, frame, LANES), F32),
            pltpu.VMEM(probe.shape, F32),
            pltpu.VMEM(tables.shape, BF16),
            pltpu.VMEM((2, frame, frame), F32),
            pltpu.VMEM((2, frame // 2, frame), F32),
            pltpu.VMEM((2, modes, frame, frame), BF16),
            pltpu.VMEM((2, modes, frame, frame), BF16),
            pltpu.VMEM((2, modes, frame, frame), F32),
            pltpu.VMEM((2, modes, frame, frame), F32),
            pltpu.SMEM((2 * cap, 16), jnp.int32),
            pltpu.SemaphoreType.DMA((blocks + 2 * across + 2,)),
            pltpu.SemaphoreType.DMA((2 * cap, 2 * across)),
            pltpu.SemaphoreType.DMA((2 * cap, 2 * across)),
            pltpu.SemaphoreType.DMA((rows // CHUNK,)),
        ],
        compiler_params=params(55),
        cost_estimate=kernel_cost(cap, modes, frame),
        name="frames_gradient",
    )(own, up, parity, tile, edge, middle, frames, probe, tables, as_upper, as_lower)


def light_kernel(own, up, beside, probe, light_out, light, sem):
    modes, _, frame, _ = probe.shape
    own_blocks, extent, _ = light_out.shape
    across = frame // LANES
    inside = (pl.ds(across, own_blocks), pl.ds(frame, extent), slice(None))
    light[inside] = jnp.zeros((own_blocks, extent, LANES), F32)
    power = jnp.zeros((frame, frame), F32)
    for mode in range(modes):
        power += probe[mode, 0] * probe[mode, 0] + probe[mode, 1] * probe[mode, 1]
    power = halves(power)
    for table, lead, down, right in ((own, 0, 0, 0), (beside, 0, 0, 1), (up, 0, 1, 0), (beside, TABLE, 1, 1)):

        def lit(slot, carry, table=table, lead=lead, down=down, right=right):
            row = table[lead + ROW + slot] + frame - down * extent
            col = table[lead + COL + slot] + frame - right * extent

            @pl.when((row > 0) & (col > 0))
            def _():
                add_window(light, (), power, row, col, frame)

            return carry

        lax.fori_loop(0, table[lead + COUNT], lit, 0)
    copy = pltpu.make_async_copy(light.at[inside[0], inside[1]], light_out, sem)
    copy.start()
    copy.wait()


def light_plane(own, up, beside, probe, extent):
    frame = probe.shape[-1]
    wide = extent + 2 * frame
    return pl.pallas_call(
        light_kernel,
        out_shape=jax.ShapeDtypeStruct((extent // LANES, extent, LANES), F32),
        in_specs=[smem_spec()] * 3 + [vmem_spec()],
        out_specs=any_spec(),
        scratch_shapes=[pltpu.VMEM((wide // LANES, wide, LANES), F32), pltpu.SemaphoreType.DMA],
        compiler_params=params(9),
        cost_estimate=pl.CostEstimate(flops=0, bytes_accessed=4 * MIB, transcendentals=0),
        name="light_plane",
    )(own, up, beside, probe)


def add_pieces(frame, table, needed, field, pieces, band, blocks, height, row_of, held, sems, loads=()):
    across = frame // LANES
    cap = (held.shape[1] - KEEP) // KEEP
    chunks = (needed + CHUNK - 1) // CHUNK
    row_index = lax.broadcasted_iota(jnp.int32, (height, LANES), 0)

    def copies(chunk):
        at = pl.ds(pl.multiple_of(chunk * CHUNK, CHUNK), CHUNK)
        return [pltpu.make_async_copy(pieces.at[at, lanes_of(b)], held.at[b, at], sems.at[chunk * 2 * across + b])
                for b in range(2 * across)]

    def begin(chunk, carry):
        for copy in copies(chunk):
            copy.start()
        return carry

    def end(chunk, carry):
        for copy in copies(chunk):
            copy.wait()
        return carry

    def one(slot, carry):
        used = table[field + slot]
        first = table[COL + slot] // LANES

        @pl.when(jnp.logical_and(used > 0, jnp.logical_and(first + across >= blocks[0], first < blocks[1])))
        def _():
            at = pl.ds(pl.multiple_of(table[PLACE + slot], ROW_ALIGN), height)
            for plane in range(2):
                got = [jnp.where(row_index < used, held[plane * across + b, at, :], 0.0) for b in range(across)]
                for b, moved in enumerate(put_into(got, lax.rem(table[COL + slot], LANES))):
                    @pl.when(jnp.logical_and(first + b >= blocks[0], first + b < blocks[1]))
                    def _():
                        where = (plane, first + b - blocks[0], pl.ds(row_of(slot), height), slice(None))
                        band[where] = band[where] + moved

        return carry

    lax.fori_loop(0, chunks, begin, 0)
    lax.fori_loop(0, chunks, end, 0)
    wait_all(loads)

    @pl.when(needed > 0)
    def _():
        lax.fori_loop(0, cap, one, 0)


def join_right_kernel(frame, own, up, as_upper, as_lower, total, right_out, band, held, sems, piece_sems):
    across = frame // LANES
    blocks, extent = total.shape[1:3]
    rows = pl.ds(0, extent)
    reach = (blocks - across, blocks)
    loads = start_all([(total.at[:, pl.ds(blocks - across, across)], band.at[:, :, rows])], sems)
    add_pieces(frame, own, own[LENT], FAR, as_upper, band, reach, frame - KEEP, lambda slot: own[ROW + slot], held, piece_sems,
               loads)
    add_pieces(frame, up, up[KEPT], NEAR, as_lower, band, reach, KEEP, lambda slot: 0, held, piece_sems)
    wait_all(start_all([(band.at[:, :, rows], right_out)], sems))


def join_right(own, up, as_upper, as_lower, total, cap):
    frame = as_upper.shape[1] // 2
    extent = total.shape[2]
    across = frame // LANES
    rows = cap * KEEP
    return pl.pallas_call(
        lambda *refs: join_right_kernel(frame, *refs),
        out_shape=jax.ShapeDtypeStruct((2, across, extent, LANES), F32),
        in_specs=[smem_spec(), smem_spec(), hbm_spec(), hbm_spec(), hbm_spec()],
        out_specs=any_spec(),
        scratch_shapes=[
            pltpu.VMEM((2, across, extent + frame, LANES), F32),
            pltpu.VMEM((2 * across, rows + KEEP, LANES), F32),
            pltpu.SemaphoreType.DMA((1,)),
            pltpu.SemaphoreType.DMA((rows // CHUNK * 2 * across,)),
        ],
        compiler_params=params(56),
        name="join_right",
    )(own, up, as_upper, as_lower, total)


def join_own_kernel(frame, own, up, as_upper, as_lower, total_in, total_out, top, bottom, held, sems, piece_sems):
    own_blocks = top.shape[1]
    extent = total_in.shape[2]
    tail = frame - KEEP
    mine = pl.ds(0, own_blocks)
    reach = (0, own_blocks)

    def part(needed, rows, band, source, table, field, height, row_of):
        @pl.when(needed > 0)
        def _():
            loads = start_all([(total_in.at[:, mine, rows], band)], sems)
            add_pieces(frame, table, needed, field, source, band_of[field], reach, height, row_of, held, piece_sems, loads)
            wait_all(start_all([(band, total_out.at[:, mine, rows])], sems))

    band_of = {FAR: bottom, NEAR: top}
    part(own[LENT], pl.ds(extent - tail, tail), bottom.at[:, :, pl.ds(0, tail)], as_upper, own, FAR, tail,
         lambda slot: own[ROW + slot] - (extent - tail))
    part(up[KEPT], pl.ds(0, KEEP), top, as_lower, up, NEAR, KEEP, lambda slot: 0)


def join_own(own, up, as_upper, as_lower, total, cap):
    frame = as_upper.shape[1] // 2
    own_blocks = total.shape[2] // LANES
    across = frame // LANES
    rows = cap * KEEP
    return pl.pallas_call(
        lambda *refs: join_own_kernel(frame, *refs),
        out_shape=jax.ShapeDtypeStruct(total.shape, F32),
        in_specs=[smem_spec(), smem_spec(), hbm_spec(), hbm_spec(), hbm_spec()],
        out_specs=hbm_spec(),
        input_output_aliases={4: 0},
        scratch_shapes=[
            pltpu.VMEM((2, own_blocks, KEEP, LANES), F32),
            pltpu.VMEM((2, own_blocks, 2 * (frame - KEEP), LANES), F32),
            pltpu.VMEM((2 * across, rows + KEEP, LANES), F32),
            pltpu.SemaphoreType.DMA((1,)),
            pltpu.SemaphoreType.DMA((rows // CHUNK * 2 * across,)),
        ],
        compiler_params=params(56),
        name="join_own",
    )(own, up, as_upper, as_lower, total)


def right_half_kernel(tile, total, light, out):
    for b in range(total.shape[1]):
        below = 1.0 / (light[b] + 1.0)
        for plane in range(2):
            out[plane, :, lanes_of(b)] = tile[plane, :, lanes_of(b)] - total[plane, b] * below


def right_half(tile, total, light):
    extent = tile.shape[-1]
    across = total.shape[1] * LANES - extent
    part = (extent - across) // LANES
    tall = 128
    return pl.pallas_call(
        right_half_kernel,
        grid=(extent // tall,),
        out_shape=jax.ShapeDtypeStruct(tile.shape, F32),
        in_specs=[
            pl.BlockSpec((2, tall, extent - across), lambda i: (0, i, 1)),
            pl.BlockSpec((2, part, tall, LANES), lambda i: (0, 1, i, 0)),
            pl.BlockSpec((part, tall, LANES), lambda i: (1, i, 0)),
        ],
        out_specs=pl.BlockSpec((2, tall, extent - across), lambda i: (0, i, 1)),
        compiler_params=params(8),
        name="right_half",
    )(tile, total, light)


def left_half_kernel(tile, total, light, left, begun, out):
    for b in range(total.shape[1]):
        below = 1.0 / (light[b] + 1.0)
        for plane in range(2):
            grad = total[plane, b] + left[plane, b]
            out[plane, :, lanes_of(b)] = tile[plane, :, lanes_of(b)] - grad * below


def left_half(tile, total, light, left, begun):
    extent = tile.shape[-1]
    across = left.shape[1]
    tall = 256
    return pl.pallas_call(
        left_half_kernel,
        grid=(extent // tall,),
        out_shape=jax.ShapeDtypeStruct(tile.shape, F32),
        in_specs=[
            pl.BlockSpec((2, tall, across * LANES), lambda i: (0, i, 0)),
            pl.BlockSpec((2, across, tall, LANES), lambda i: (0, 0, i, 0)),
            pl.BlockSpec((across, tall, LANES), lambda i: (0, i, 0)),
            pl.BlockSpec((2, across, tall, LANES), lambda i: (0, 0, i, 0)),
            any_spec(),
        ],
        out_specs=pl.BlockSpec((2, tall, across * LANES), lambda i: (0, i, 0)),
        input_output_aliases={4: 0},
        compiler_params=params(8),
        name="left_half",
    )(tile, total, light, left, begun)


def body(object_tiles, probe, positions, frames, counts):
    tile = object_tiles[0]
    extent = tile.shape[-1]
    frame = frames.shape[-1]
    cap = frames.shape[1]
    peers = lax.axis_size("scan")
    tile_row = lax.axis_index("scan") // TCOLS
    phases = min(2, peers // TCOLS - 1)
    tables = dft_tables(frame)
    parity = (tile_row % 2).reshape(1)
    even = tile_row % 2 == 0

    own = slot_table(positions, counts, extent, frame)
    up = shifted(own, "scan", TCOLS)
    edge, middle, up = lax.optimization_barrier((*strips(tile, frame), up))
    edge = shifted(edge, "scan", -1)
    middle = shifted(middle, "scan", -1)
    beside = shifted(jnp.concatenate([own, up]), "scan", 1)

    def exchange(phase, packed, choice):
        uppers = [k for k in range(peers - TCOLS) if k // TCOLS % 2 == phase]
        pairs = [(k, k + TCOLS) for k in uppers] + [(k + TCOLS, k) for k in uppers]

        def sender(size):
            def run(data):
                return lax.dynamic_update_slice(data, lax.ppermute(data[:size], "scan", pairs), (0, 0))
            return run

        branches = [lambda data: data] + [sender(size) for size in SIZES if size <= packed.shape[0]]
        return lax.switch(choice.reshape(()), branches, packed)

    def by_role(arrays):
        if len(arrays) == 1:
            return arrays[0], arrays[0]
        return jnp.where(even, arrays[0], arrays[1]), jnp.where(even, arrays[1], arrays[0])

    cuts = [cut_pieces(phase, own, up, parity, tile, edge, frames[0]) for phase in range(phases)]
    received = by_role([exchange(phase, cut[0], cut[1]) for phase, cut in enumerate(cuts)])
    received, beside = lax.optimization_barrier((received, beside))
    total, *packed = frames_gradient(
        phases, own, up, parity, tile, edge, middle, frames[0], probe, tables, *received)
    returned = by_role([exchange(phase, packed[phase], cut[2]) for phase, cut in enumerate(cuts)])
    right = join_right(own, up, *returned, total, cap)
    right, total, beside = lax.optimization_barrier((right, total, beside))
    left = shifted(right, "scan", 1)
    total = join_own(own, up, *returned, total, cap)
    light = light_plane(own, up, beside, probe, extent)
    begun = right_half(tile, total, light)
    return left_half(tile, total, light, left, begun)[None]


def solution(mesh):
    return jax.shard_map(
        body,
        mesh=mesh,
        in_specs=(
            P(("grp", "scan"), None, None, None),
            P(),
            P(("grp", "scan"), None, None),
            P(("grp", "scan"), None, None, None),
            P(("grp", "scan")),
        ),
        out_specs=P(("grp", "scan"), None, None, None),
        check_vma=False,
    )
```

```python
import math

import jax
import jax.numpy as jnp
import numpy as np
from jax import lax
from jax.experimental import pallas as pl
from jax.experimental.pallas import tpu as pltpu
from jax.sharding import PartitionSpec as P

TCOLS = 8
LANES = 128
ROW_ALIGN = 8
CHUNK = 64
STEP = 32
TILE_ROWS = 16
SIZES = (32, 64, 96, 128, 160, 192, 224, 256, 288, 320, 352, 384, 416, 448, 480, 512, 576, 640, 704, 768, 832, 960, 1344)
MIB = 1024 * 1024
F32 = jnp.float32
BF16 = jnp.bfloat16

KEEP = 160
ROW, COL, NEAR, FAR, PLACE, SHOT = 0, 8, 16, 24, 32, 40
COUNT, KEPT, LENT, FORTH, BACK = 48, 49, 50, 51, 52
TABLE = 64

ACTIVE, AT_ROW, AT_COL, LO, HI, START, PIECE, SHIFT, ROLE = range(9)


def dft_tables(frame):
    near = np.arange(frame // 2, dtype=np.int64)
    blocks = []
    for odd in range(2):
        phase = (near[:, None] * (2 * near[None, :] + odd) % frame).astype(np.float64) * (2.0 * math.pi / frame)
        c, s = np.cos(phase), np.sin(phase)
        ahead = np.block([[c, -s], [s, c]])
        back = np.block([[c.T, s.T], [-s.T, c.T]])
        blocks.append((ahead, ahead.T, back, back.T))
    order = np.zeros((frame, frame))
    order[2 * near, near] = 1.0
    order[2 * near + 1, near + frame // 2] = 1.0
    tables = [blocks[odd][kind] for kind in range(4) for odd in range(2)] + [order]
    return jnp.asarray(np.stack(tables), F32).astype(BF16)


def shifted(array, axis, by):
    peers = lax.axis_size(axis)
    pairs = [(i, i + by) for i in range(peers) if 0 <= i + by < peers]
    return lax.ppermute(array, axis, pairs)


def any_spec():
    return pl.BlockSpec(memory_space=pl.ANY)


def hbm_spec():
    return pl.BlockSpec(memory_space=pltpu.HBM)


def smem_spec():
    return pl.BlockSpec(memory_space=pltpu.SMEM)


def vmem_spec():
    return pl.BlockSpec(memory_space=pltpu.VMEM)


def params(mebibytes):
    return pltpu.CompilerParams(vmem_limit_bytes=mebibytes * MIB)


def taken_from(blocks, by):
    lane = lax.broadcasted_iota(jnp.int32, blocks[0].shape, 1)
    rolled = [pltpu.roll(block, lax.rem(LANES - by, LANES), axis=1) for block in blocks]
    return [jnp.where(lane < LANES - by, one, two) for one, two in zip(rolled[:-1], rolled[1:])]


def put_into(blocks, by):
    lane = lax.broadcasted_iota(jnp.int32, blocks[0].shape, 1)
    rolled = [pltpu.roll(block, by, axis=1) for block in blocks]
    none = jnp.zeros_like(blocks[0])
    return [jnp.where(lane >= by, one, two) for one, two in zip(rolled + [none], [none] + rolled)]


def start_all(pairs, sems, first=0):
    copies = [pltpu.make_async_copy(source, target, sems.at[first + at]) for at, (source, target) in enumerate(pairs)]
    for copy in copies:
        copy.start()
    return copies


def wait_all(copies):
    for copy in copies:
        copy.wait()


def lanes_of(block):
    return pl.ds(block * LANES, LANES)


def side_by_side(parts):
    return jnp.concatenate(parts, axis=1)


def halves(array):
    return [array[:, :LANES], array[:, LANES:]]


def copy_out_rows(needed, packed, out, sems):
    chunks = (needed + CHUNK - 1) // CHUNK

    def copy(chunk):
        at = pl.ds(pl.multiple_of(chunk * CHUNK, CHUNK), CHUNK)
        return pltpu.make_async_copy(packed.at[at], out.at[at], sems.at[chunk])

    def begin(chunk, carry):
        copy(chunk).start()
        return carry

    def end(chunk, carry):
        copy(chunk).wait()
        return carry

    lax.fori_loop(0, chunks, begin, 0)
    lax.fori_loop(0, chunks, end, 0)


def up_to(value, step):
    return (value + step - 1) // step * step


def size_choice(needed):
    choice = jnp.where(needed > 0, 1, 0)
    for size in SIZES:
        choice = choice + jnp.where(needed > size, 1, 0)
    return choice


def strip_kernel(tile, edge, middle, sems):
    extent = tile.shape[-1]
    frame = edge.shape[-1]
    lanes = pl.ds(0, frame)
    wait_all(start_all([
        (tile.at[:, pl.ds(0, KEEP), lanes], edge.at[:, pl.ds(0, KEEP)]),
        (tile.at[:, pl.ds(KEEP + extent - frame, frame - KEEP), lanes], edge.at[:, pl.ds(KEEP, frame - KEEP)]),
        (tile.at[:, pl.ds(KEEP, extent - frame), lanes], middle),
    ], sems))


def table_kernel(extent, frame, positions, counts, table):
    cap = positions.shape[2]
    count = counts[0]
    kept, lent, shots = jnp.int32(0), jnp.int32(0), jnp.int32(0)
    for at in range(TABLE):
        table[at] = 0
    for slot in range(cap):
        row = lax.rem(positions[0, 0, slot], extent)
        col = lax.rem(positions[0, 1, slot], extent)
        below = jnp.where(slot < count, jnp.maximum(row + (frame - extent), 0), 0)
        stays = below <= KEEP
        near = jnp.where(stays, below, 0)
        far = jnp.where(stays, 0, frame - below)
        table[ROW + slot] = row
        table[COL + slot] = col
        table[NEAR + slot] = near
        table[FAR + slot] = far
        table[PLACE + slot] = jnp.where(stays, kept, lent)
        table[SHOT + slot] = shots
        kept = kept + up_to(near, ROW_ALIGN)
        lent = lent + up_to(far, ROW_ALIGN)
        shots = shots + jnp.where(stays, 0, frame // 2)
    for slot in range(cap):
        table[SHOT + slot] = table[SHOT + slot] + lent
    table[COUNT] = count
    table[KEPT] = kept
    table[LENT] = lent
    table[FORTH] = jnp.maximum(kept, lent + shots)
    table[BACK] = jnp.maximum(kept, lent)


def slot_table(positions, counts, extent, frame):
    return pl.pallas_call(
        lambda *refs: table_kernel(extent, frame, *refs),
        out_shape=jax.ShapeDtypeStruct((TABLE,), jnp.int32),
        in_specs=[smem_spec(), smem_spec()],
        out_specs=smem_spec(),
        name="slot_table",
    )(jnp.swapaxes(positions, 1, 2), counts)


def strips(tile, frame):
    extent = tile.shape[-1]
    return pl.pallas_call(
        strip_kernel,
        out_shape=(
            jax.ShapeDtypeStruct((2, frame, frame), F32),
            jax.ShapeDtypeStruct((2, extent - frame, frame), F32),
        ),
        in_specs=[hbm_spec()],
        out_specs=(vmem_spec(), vmem_spec()),
        scratch_shapes=[pltpu.SemaphoreType.DMA((3,))],
        compiler_params=params(61),
        name="strips",
    )(tile)


def cut_kernel(phase, own, up, parity, tile, edge, frames, out, forth, back, band, packed, sems, chunk_sems):
    cap, frame, _ = frames.shape
    extent = tile.shape[-1]
    across = frame // LANES
    own_blocks = extent // LANES
    upper = parity[0] == phase
    forth[0] = size_choice(jnp.where(upper, own[FORTH], up[FORTH]))
    back[0] = size_choice(jnp.where(upper, own[BACK], up[BACK]))
    lends = jnp.logical_and(upper, own[LENT] > 0)
    gives = jnp.logical_and(jnp.logical_not(upper), up[KEPT] > 0)

    def cut(col, row, place):
        at = pl.ds(pl.multiple_of(place, ROW_ALIGN), frame)
        for plane in range(2):
            packed[at, pl.ds(plane * frame, frame)] = side_by_side(window(band, (plane,), row, col, frame, across))

    @pl.when(jnp.logical_or(lends, gives))
    def _():
        base = jnp.where(upper, extent - frame, 0)
        rows = pl.ds(pl.multiple_of(base, ROW_ALIGN), frame)
        wait_all(start_all(
            [(tile.at[:, rows, lanes_of(b)], band.at[:, b, pl.ds(0, frame)]) for b in range(own_blocks)]
            + [(edge.at[:, :, lanes_of(b)], band.at[:, own_blocks + b, pl.ds(0, frame)]) for b in range(across)], sems))

        def one(slot, carry):
            @pl.when(jnp.logical_and(upper, own[FAR + slot] > 0))
            def _():
                cut(own[COL + slot], own[ROW + slot] - (extent - frame), own[PLACE + slot])

            @pl.when(jnp.logical_and(gives, up[NEAR + slot] > 0))
            def _():
                cut(up[COL + slot], 0, up[PLACE + slot])

            return carry

        lax.fori_loop(0, cap, one, 0)

        def shots(slot):
            at = pl.ds(pl.multiple_of(own[SHOT + slot], ROW_ALIGN), frame // 2)
            return [pltpu.make_async_copy(frames.at[slot, pl.ds(part * frame // 2, frame // 2)],
                                          packed.at[at, pl.ds(part * frame, frame)], sems.at[2 * slot + part])
                    for part in range(2)]

        for wait in range(2):
            for slot in range(cap):
                @pl.when(jnp.logical_and(lends, own[FAR + slot] > 0))
                def _():
                    for copy in shots(slot):
                        if wait:
                            copy.wait()
                        else:
                            copy.start()

        copy_out_rows(jnp.where(upper, own[FORTH], up[KEPT]), packed, out, chunk_sems)


def cut_pieces(phase, own, up, parity, tile, edge, frames):
    cap, frame, _ = frames.shape
    extent = tile.shape[-1]
    blocks = (extent + frame) // LANES
    rows = SIZES[-1]
    return pl.pallas_call(
        lambda *refs: cut_kernel(phase, *refs),
        out_shape=(
            jax.ShapeDtypeStruct((rows, 2 * frame), F32),
            jax.ShapeDtypeStruct((1,), jnp.int32),
            jax.ShapeDtypeStruct((1,), jnp.int32),
        ),
        in_specs=[smem_spec(), smem_spec(), smem_spec(), hbm_spec(), hbm_spec(), hbm_spec()],
        out_specs=(hbm_spec(), smem_spec(), smem_spec()),
        scratch_shapes=[
            pltpu.VMEM((2, blocks, 2 * frame, LANES), F32),
            pltpu.VMEM((rows + frame, 2 * frame), F32),
            pltpu.SemaphoreType.DMA((max(blocks, 2 * cap),)),
            pltpu.SemaphoreType.DMA((rows // CHUNK,)),
        ],
        compiler_params=params(60),
        name="cut_pieces",
    )(own, up, parity, tile, edge, frames)


def dot(one, two):
    return jnp.dot(one, two, preferred_element_type=F32)


def stacked(parts):
    return jnp.concatenate(parts, axis=0)


def lane_parts(array):
    half = array.shape[1] // 2
    return array[:, :half], array[:, half:]


def wave_stage(mode, probe, patch, waves):
    frame = probe.shape[2]
    for at in range(0, frame, TILE_ROWS):
        rows = pl.ds(at, TILE_ROWS)
        probe_real, probe_imag = probe[mode, 0, rows], probe[mode, 1, rows]
        patch_real, patch_imag = patch[0, rows], patch[1, rows]
        parts = [lane_parts(part) for part in (
            probe_real * patch_real - probe_imag * patch_imag, probe_real * patch_imag + probe_imag * patch_real)]
        waves[0, mode, rows] = side_by_side([near + far for near, far in parts]).astype(BF16)
        waves[1, mode, rows] = side_by_side([near - far for near, far in parts]).astype(BF16)


def rows_dot(pair, source, tables, first, product):
    modes = pl.ds(2 * pair, 2)
    for odd in range(2):
        both = source[odd, modes]
        product[odd, modes] = dot(both.reshape(2 * both.shape[1], both.shape[2]), tables[first + odd]).reshape(both.shape)


def columns_dot(mode, tables, first, source, product):
    for odd in range(2):
        product[odd, mode] = dot(tables[first + odd], source[odd, mode])


def half_stage(mode, product, halfway):
    half = product.shape[2] // 2
    for at in range(0, half, TILE_ROWS):
        near, far = pl.ds(at, TILE_ROWS), pl.ds(half + at, TILE_ROWS)
        upper = [product[odd, mode, near] for odd in range(2)]
        lower = [product[odd, mode, far] for odd in range(2)]
        for odd in range(2):
            mixed = [a + b if not odd else a - b for a, b in zip(upper, lower)]
            real, imag = zip(*[lane_parts(part) for part in mixed])
            halfway[odd, mode, near] = side_by_side(real).astype(BF16)
            halfway[odd, mode, far] = side_by_side(imag).astype(BF16)


def residual_stage(modes, frame, field, amplitude, waves):
    half = frame // 2
    for odd in range(2):
        for at in range(0, half, TILE_ROWS):
            near, far = pl.ds(at, TILE_ROWS), pl.ds(half + at, TILE_ROWS)
            real = [field[odd, mode, near] for mode in range(modes)]
            imag = [field[odd, mode, far] for mode in range(modes)]
            lit = sum(a * a + b * b for a, b in zip(real, imag))
            factor = 1.0 / frame - amplitude[odd, near] * lax.rsqrt(jnp.maximum(lit, float(frame * frame)))
            target = pl.ds(odd * half + at, TILE_ROWS)
            for mode in range(modes):
                parts = [lane_parts(real[mode] * factor), lane_parts(imag[mode] * factor)]
                for column in range(2):
                    waves[column, mode, target] = side_by_side([part[column] for part in parts]).astype(BF16)


def back_stage(mode, product, halfway):
    half = product.shape[2] // 2
    for odd in range(2):
        for at in range(0, half, TILE_ROWS):
            rows = pl.ds(odd * half + at, TILE_ROWS)
            even_part, odd_part = product[0, mode, rows], product[1, mode, rows]
            near, far = lane_parts(even_part + odd_part), lane_parts(even_part - odd_part)
            halfway[odd, mode, pl.ds(at, TILE_ROWS)] = side_by_side([near[0], far[0]]).astype(BF16)
            halfway[odd, mode, pl.ds(half + at, TILE_ROWS)] = side_by_side([near[1], far[1]]).astype(BF16)


def gradient_stage(some_modes, first, product, probe, piece):
    frame = probe.shape[2]
    half = frame // 2
    across = frame // LANES
    for at in range(0, half, ROW_ALIGN):
        rows = [pl.ds(at, ROW_ALIGN), pl.ds(half + at, ROW_ALIGN)]
        grads = [[0.0, 0.0], [0.0, 0.0]]
        for mode in some_modes:
            mixed = [(product[0, mode, part], product[1, mode, part]) for part in rows]
            for side in range(2):
                back_real, back_imag = [a + b if not side else a - b for a, b in mixed]
                probe_real, probe_imag = probe[mode, 0, rows[side]], probe[mode, 1, rows[side]]
                grads[side][0] += probe_real * back_real + probe_imag * back_imag
                grads[side][1] += probe_real * back_imag - probe_imag * back_real
        for side in range(2):
            for plane in range(2):
                grad = grads[side][plane] * (1.0 / frame)
                for b in range(across):
                    where = (plane * across + b, rows[side], slice(None))
                    part = grad[:, b * LANES:(b + 1) * LANES]
                    piece[where] = part if first else piece[where] + part


def frame_step(patch, amplitude, probe, tables, waves, halfway, product, field, piece):
    modes, _, frame, _ = probe.shape
    pairs = modes // 2
    for step in range(pairs + 1):
        if step < pairs:
            for mode in (2 * step, 2 * step + 1):
                wave_stage(mode, probe, patch, waves)
            rows_dot(step, waves, tables, 0, product)
        if step:
            for mode in (2 * step - 2, 2 * step - 1):
                half_stage(mode, product, halfway)
                columns_dot(mode, tables, 2, halfway, field)
    residual_stage(modes, frame, field, amplitude, waves)
    for step in range(pairs + 1):
        if step < pairs:
            rows_dot(step, waves, tables, 4, product)
        if step:
            for mode in (2 * step - 2, 2 * step - 1):
                back_stage(mode, product, halfway)
                columns_dot(mode, tables, 6, halfway, field)
            gradient_stage((2 * step - 2, 2 * step - 1), step == 1, field, probe, piece)


def ordered_amplitude(measured, task, order, amplitude):
    frame = measured.shape[2]
    for odd in range(2):
        root = jnp.sqrt(side_by_side(
            [measured[task, b, pl.ds(odd, frame // 2, stride=2), :] for b in range(measured.shape[1])]))
        high = root.astype(BF16)
        low = (root - high.astype(F32)).astype(BF16)
        amplitude[odd] = dot(high, order) + dot(low, order)


def window(band, lead, row, col, height, across):
    return taken_from(
        [band[lead + (col // LANES + b, pl.ds(row, height), slice(None))] for b in range(across + 1)],
        lax.rem(col, LANES),
    )


def add_window(total, lead, parts, row, col, frame):
    for b, moved in enumerate(put_into(parts, lax.rem(col, LANES))):
        at = lead + (col // LANES + b, pl.ds(row, frame), slice(None))
        total[at] = total[at] + moved


def kernel_cost(frames, modes, frame):
    return pl.CostEstimate(
        flops=frames * modes * 4 * 4 * frame ** 3, bytes_accessed=16 * 1024 * 1024, transcendentals=0)


def frames_kernel(phases, own, up, parity, tile, edge, middle, frames, probe_in, tables_in, as_upper, as_lower, total_out, *rest):
    packed_outs = rest[:phases]
    (band, total, held, packed, piece, measured, probe, tables, patch, amplitude, waves, halfway, product, field, work,
     sems, shot_sems, held_sems, chunk_sems) = rest[phases:]
    cap, frame, _ = frames.shape
    extent = tile.shape[-1]
    across = frame // LANES
    own_blocks = extent // LANES
    half = frame // 2
    own_rows = pl.ds(frame, extent)

    first = start_all(
        [(tile.at[:, :, lanes_of(b)], band.at[:, b, own_rows]) for b in range(own_blocks)]
        + [(source.at[:, pl.ds(at, height), lanes_of(b)], band.at[:, own_blocks + b, pl.ds(frame + target, height)])
           for source, at, height, target in (
               (edge, 0, KEEP, 0), (middle, 0, extent - frame, KEEP), (edge, KEEP, frame - KEEP, KEEP + extent - frame))
           for b in range(across)]
        + [(probe_in, probe), (tables_in, tables)], sems)

    def mine(slot):
        return jnp.logical_and(slot < own[COUNT], own[FAR + slot] == 0)

    def borrowed(slot):
        return up[FAR + slot] > 0

    def shot_copies(slot, task, lent):
        if not lent:
            return [pltpu.make_async_copy(frames.at[slot, :, lanes_of(b)], measured.at[task, b], shot_sems.at[task, b])
                    for b in range(across)]
        at = pl.ds(pl.multiple_of(up[SHOT + slot], ROW_ALIGN), half)
        return [
            pltpu.make_async_copy(as_lower.at[at, lanes_of(part * across + b)],
                                  measured.at[task, b, pl.ds(part * half, half)], shot_sems.at[task, part * across + b])
            for part in range(2) for b in range(across)
        ]

    def held_copies(slot, task, lent):
        source, table = (as_lower, up) if lent else (as_upper, own)
        at = pl.ds(pl.multiple_of(table[PLACE + slot], ROW_ALIGN), frame)
        return [
            pltpu.make_async_copy(source.at[at, lanes_of(b)], held.at[task, b, pl.ds(frame, frame)], held_sems.at[task, b])
            for b in range(2 * across)
        ]

    def for_tasks(wait):
        for slot in range(cap):
            def run(copies):
                for copy in copies:
                    if wait:
                        copy.wait()
                    else:
                        copy.start()

            @pl.when(mine(slot))
            def _():
                run(shot_copies(slot, slot, False))

            @pl.when(own[NEAR + slot] > 0)
            def _():
                run(held_copies(slot, slot, False))

            @pl.when(borrowed(slot))
            def _():
                run(shot_copies(slot, cap + slot, True))
                run(held_copies(slot, cap + slot, True))

    for_tasks(False)
    for slot in range(cap):
        near = own[NEAR + slot]
        for field_at, value in (
            (ACTIVE, mine(slot).astype(jnp.int32)), (AT_ROW, own[ROW + slot] + frame), (AT_COL, own[COL + slot]),
            (LO, frame - near), (HI, frame), (START, near), (PIECE, own[PLACE + slot]), (SHIFT, frame - near), (ROLE, 0),
        ):
            work[slot, field_at] = value
        for field_at, value in (
            (ACTIVE, borrowed(slot).astype(jnp.int32)), (AT_ROW, up[ROW + slot] + frame - extent), (AT_COL, up[COL + slot]),
            (LO, 0), (HI, up[FAR + slot]), (START, frame), (PIECE, up[PLACE + slot]), (SHIFT, 0), (ROLE, 1),
        ):
            work[cap + slot, field_at] = value
    total[:, :, own_rows, :] = jnp.zeros((2, band.shape[1], extent, LANES), F32)
    wait_all(first)
    for_tasks(True)
    row_index = lax.broadcasted_iota(jnp.int32, (STEP, LANES), 0)

    def one(task, carry):
        @pl.when(work[task, ACTIVE] > 0)
        def _():
            row, col, start = work[task, AT_ROW], work[task, AT_COL], work[task, START]
            lo, hi = work[task, LO], work[task, HI]
            for at in range(0, frame, STEP):
                theirs = jnp.logical_and(row_index >= lo - at, row_index < hi - at)
                for plane in range(2):
                    near = window(band, (plane,), row + at, col, STEP, across)
                    other = [held[task, plane * across + b, pl.ds(start + at, STEP), :] for b in range(across)]
                    patch[plane, pl.ds(at, STEP)] = side_by_side([jnp.where(theirs, b, a) for a, b in zip(near, other)])
            ordered_amplitude(measured, task, tables[8], amplitude)
            frame_step(patch, amplitude, probe, tables, waves, halfway, product, field, piece)
            for at in range(0, frame, STEP):
                for plane in range(2):
                    parts = [piece[plane * across + b, pl.ds(at, STEP), :] for b in range(across)]
                    add_window(total, (plane,), parts, row + at, col, STEP)

            @pl.when(lo < hi)
            def _():
                target = pl.ds(pl.multiple_of(work[task, PIECE], ROW_ALIGN), frame)
                source = pl.ds(work[task, SHIFT], frame)
                for b in range(2 * across):
                    packed[work[task, ROLE], target, lanes_of(b)] = piece[b, source, :]

        return carry

    lax.fori_loop(0, 2 * cap, one, 0)
    end = start_all([(total.at[:, :, own_rows], total_out)], sems)
    for phase in range(phases):
        upper = parity[0] == phase
        role = jnp.where(upper, 0, 1)
        copy_out_rows(jnp.where(upper, own[KEPT], up[LENT]), packed.at[role], packed_outs[phase], chunk_sems)
    wait_all(end)


def frames_gradient(phases, own, up, parity, tile, edge, middle, frames, probe, tables, as_upper, as_lower):
    cap, frame, _ = frames.shape
    extent = tile.shape[-1]
    modes = probe.shape[0]
    tall = extent + 2 * frame
    blocks = (extent + frame) // LANES
    across = frame // LANES
    rows = as_upper.shape[0]
    kept_rows = cap * KEEP
    return pl.pallas_call(
        lambda *refs: frames_kernel(phases, *refs),
        out_shape=(jax.ShapeDtypeStruct((2, blocks, extent, LANES), F32),)
        + (jax.ShapeDtypeStruct(as_upper.shape, F32),) * phases,
        in_specs=[smem_spec()] * 3 + [hbm_spec()] * 8,
        out_specs=(hbm_spec(),) * (1 + phases),
        scratch_shapes=[
            pltpu.VMEM((2, blocks, tall, LANES), F32),
            pltpu.VMEM((2, blocks, tall, LANES), F32),
            pltpu.VMEM((2 * cap, 2 * across, 2 * frame, LANES), F32),
            pltpu.VMEM((2, kept_rows + frame, 2 * frame), F32),
            pltpu.VMEM((2 * across, 2 * frame, LANES), F32),
            pltpu.VMEM((2 * cap, across, frame, LANES), F32),
            pltpu.VMEM(probe.shape, F32),
            pltpu.VMEM(tables.shape, BF16),
            pltpu.VMEM((2, frame, frame), F32),
            pltpu.VMEM((2, frame // 2, frame), F32),
            pltpu.VMEM((2, modes, frame, frame), BF16),
            pltpu.VMEM((2, modes, frame, frame), BF16),
            pltpu.VMEM((2, modes, frame, frame), F32),
            pltpu.VMEM((2, modes, frame, frame), F32),
            pltpu.SMEM((2 * cap, 16), jnp.int32),
            pltpu.SemaphoreType.DMA((blocks + 2 * across + 2,)),
            pltpu.SemaphoreType.DMA((2 * cap, 2 * across)),
            pltpu.SemaphoreType.DMA((2 * cap, 2 * across)),
            pltpu.SemaphoreType.DMA((rows // CHUNK,)),
        ],
        compiler_params=params(55),
        cost_estimate=kernel_cost(cap, modes, frame),
        name="frames_gradient",
    )(own, up, parity, tile, edge, middle, frames, probe, tables, as_upper, as_lower)


def light_kernel(own, up, beside, probe, light_out, light, sem):
    modes, _, frame, _ = probe.shape
    own_blocks, extent, _ = light_out.shape
    across = frame // LANES
    inside = (pl.ds(across, own_blocks), pl.ds(frame, extent), slice(None))
    light[inside] = jnp.zeros((own_blocks, extent, LANES), F32)
    power = jnp.zeros((frame, frame), F32)
    for mode in range(modes):
        power += probe[mode, 0] * probe[mode, 0] + probe[mode, 1] * probe[mode, 1]
    power = halves(power)
    for table, lead, down, right in ((own, 0, 0, 0), (beside, 0, 0, 1), (up, 0, 1, 0), (beside, TABLE, 1, 1)):

        def lit(slot, carry, table=table, lead=lead, down=down, right=right):
            row = table[lead + ROW + slot] + frame - down * extent
            col = table[lead + COL + slot] + frame - right * extent

            @pl.when((row > 0) & (col > 0))
            def _():
                add_window(light, (), power, row, col, frame)

            return carry

        lax.fori_loop(0, table[lead + COUNT], lit, 0)
    copy = pltpu.make_async_copy(light.at[inside[0], inside[1]], light_out, sem)
    copy.start()
    copy.wait()


def light_plane(own, up, beside, probe, extent):
    frame = probe.shape[-1]
    wide = extent + 2 * frame
    return pl.pallas_call(
        light_kernel,
        out_shape=jax.ShapeDtypeStruct((extent // LANES, extent, LANES), F32),
        in_specs=[smem_spec()] * 3 + [vmem_spec()],
        out_specs=any_spec(),
        scratch_shapes=[pltpu.VMEM((wide // LANES, wide, LANES), F32), pltpu.SemaphoreType.DMA],
        compiler_params=params(9),
        cost_estimate=pl.CostEstimate(flops=0, bytes_accessed=4 * MIB, transcendentals=0),
        name="light_plane",
    )(own, up, beside, probe)


def add_pieces(frame, table, needed, field, pieces, band, blocks, height, row_of, held, sems, loads=()):
    across = frame // LANES
    cap = (held.shape[1] - KEEP) // KEEP
    chunks = (needed + CHUNK - 1) // CHUNK
    row_index = lax.broadcasted_iota(jnp.int32, (height, LANES), 0)

    def copies(chunk):
        at = pl.ds(pl.multiple_of(chunk * CHUNK, CHUNK), CHUNK)
        return [pltpu.make_async_copy(pieces.at[at, lanes_of(b)], held.at[b, at], sems.at[chunk * 2 * across + b])
                for b in range(2 * across)]

    def begin(chunk, carry):
        for copy in copies(chunk):
            copy.start()
        return carry

    def end(chunk, carry):
        for copy in copies(chunk):
            copy.wait()
        return carry

    def one(slot, carry):
        used = table[field + slot]
        first = table[COL + slot] // LANES

        @pl.when(jnp.logical_and(used > 0, jnp.logical_and(first + across >= blocks[0], first < blocks[1])))
        def _():
            at = pl.ds(pl.multiple_of(table[PLACE + slot], ROW_ALIGN), height)
            for plane in range(2):
                got = [jnp.where(row_index < used, held[plane * across + b, at, :], 0.0) for b in range(across)]
                for b, moved in enumerate(put_into(got, lax.rem(table[COL + slot], LANES))):
                    @pl.when(jnp.logical_and(first + b >= blocks[0], first + b < blocks[1]))
                    def _():
                        where = (plane, first + b - blocks[0], pl.ds(row_of(slot), height), slice(None))
                        band[where] = band[where] + moved

        return carry

    lax.fori_loop(0, chunks, begin, 0)
    lax.fori_loop(0, chunks, end, 0)
    wait_all(loads)

    @pl.when(needed > 0)
    def _():
        lax.fori_loop(0, cap, one, 0)


def join_right_kernel(frame, own, up, as_upper, as_lower, total, right_out, band, held, sems, piece_sems):
    across = frame // LANES
    blocks, extent = total.shape[1:3]
    rows = pl.ds(0, extent)
    reach = (blocks - across, blocks)
    loads = start_all([(total.at[:, pl.ds(blocks - across, across)], band.at[:, :, rows])], sems)
    add_pieces(frame, own, own[LENT], FAR, as_upper, band, reach, frame - KEEP, lambda slot: own[ROW + slot], held, piece_sems,
               loads)
    add_pieces(frame, up, up[KEPT], NEAR, as_lower, band, reach, KEEP, lambda slot: 0, held, piece_sems)
    wait_all(start_all([(band.at[:, :, rows], right_out)], sems))


def join_right(own, up, as_upper, as_lower, total, cap):
    frame = as_upper.shape[1] // 2
    extent = total.shape[2]
    across = frame // LANES
    rows = cap * KEEP
    return pl.pallas_call(
        lambda *refs: join_right_kernel(frame, *refs),
        out_shape=jax.ShapeDtypeStruct((2, across, extent, LANES), F32),
        in_specs=[smem_spec(), smem_spec(), hbm_spec(), hbm_spec(), hbm_spec()],
        out_specs=any_spec(),
        scratch_shapes=[
            pltpu.VMEM((2, across, extent + frame, LANES), F32),
            pltpu.VMEM((2 * across, rows + KEEP, LANES), F32),
            pltpu.SemaphoreType.DMA((1,)),
            pltpu.SemaphoreType.DMA((rows // CHUNK * 2 * across,)),
        ],
        compiler_params=params(56),
        name="join_right",
    )(own, up, as_upper, as_lower, total)


def join_own_kernel(frame, own, up, as_upper, as_lower, total_in, total_out, top, bottom, held, sems, piece_sems):
    own_blocks = top.shape[1]
    extent = total_in.shape[2]
    tail = frame - KEEP
    mine = pl.ds(0, own_blocks)
    reach = (0, own_blocks)

    def part(needed, rows, band, source, table, field, height, row_of):
        @pl.when(needed > 0)
        def _():
            loads = start_all([(total_in.at[:, mine, rows], band)], sems)
            add_pieces(frame, table, needed, field, source, band_of[field], reach, height, row_of, held, piece_sems, loads)
            wait_all(start_all([(band, total_out.at[:, mine, rows])], sems))

    band_of = {FAR: bottom, NEAR: top}
    part(own[LENT], pl.ds(extent - tail, tail), bottom.at[:, :, pl.ds(0, tail)], as_upper, own, FAR, tail,
         lambda slot: own[ROW + slot] - (extent - tail))
    part(up[KEPT], pl.ds(0, KEEP), top, as_lower, up, NEAR, KEEP, lambda slot: 0)


def join_own(own, up, as_upper, as_lower, total, cap):
    frame = as_upper.shape[1] // 2
    own_blocks = total.shape[2] // LANES
    across = frame // LANES
    rows = cap * KEEP
    return pl.pallas_call(
        lambda *refs: join_own_kernel(frame, *refs),
        out_shape=jax.ShapeDtypeStruct(total.shape, F32),
        in_specs=[smem_spec(), smem_spec(), hbm_spec(), hbm_spec(), hbm_spec()],
        out_specs=hbm_spec(),
        input_output_aliases={4: 0},
        scratch_shapes=[
            pltpu.VMEM((2, own_blocks, KEEP, LANES), F32),
            pltpu.VMEM((2, own_blocks, 2 * (frame - KEEP), LANES), F32),
            pltpu.VMEM((2 * across, rows + KEEP, LANES), F32),
            pltpu.SemaphoreType.DMA((1,)),
            pltpu.SemaphoreType.DMA((rows // CHUNK * 2 * across,)),
        ],
        compiler_params=params(56),
        name="join_own",
    )(own, up, as_upper, as_lower, total)


def right_half_kernel(tile, total, light, out):
    for b in range(total.shape[1]):
        below = 1.0 / (light[b] + 1.0)
        for plane in range(2):
            out[plane, :, lanes_of(b)] = tile[plane, :, lanes_of(b)] - total[plane, b] * below


def right_half(tile, total, light):
    extent = tile.shape[-1]
    across = total.shape[1] * LANES - extent
    part = (extent - across) // LANES
    tall = 128
    return pl.pallas_call(
        right_half_kernel,
        grid=(extent // tall,),
        out_shape=jax.ShapeDtypeStruct(tile.shape, F32),
        in_specs=[
            pl.BlockSpec((2, tall, extent - across), lambda i: (0, i, 1)),
            pl.BlockSpec((2, part, tall, LANES), lambda i: (0, 1, i, 0)),
            pl.BlockSpec((part, tall, LANES), lambda i: (1, i, 0)),
        ],
        out_specs=pl.BlockSpec((2, tall, extent - across), lambda i: (0, i, 1)),
        compiler_params=params(8),
        name="right_half",
    )(tile, total, light)


def left_half_kernel(tile, total, light, left, begun, out):
    for b in range(total.shape[1]):
        below = 1.0 / (light[b] + 1.0)
        for plane in range(2):
            grad = total[plane, b] + left[plane, b]
            out[plane, :, lanes_of(b)] = tile[plane, :, lanes_of(b)] - grad * below


def left_half(tile, total, light, left, begun):
    extent = tile.shape[-1]
    across = left.shape[1]
    tall = 256
    return pl.pallas_call(
        left_half_kernel,
        grid=(extent // tall,),
        out_shape=jax.ShapeDtypeStruct(tile.shape, F32),
        in_specs=[
            pl.BlockSpec((2, tall, across * LANES), lambda i: (0, i, 0)),
            pl.BlockSpec((2, across, tall, LANES), lambda i: (0, 0, i, 0)),
            pl.BlockSpec((across, tall, LANES), lambda i: (0, i, 0)),
            pl.BlockSpec((2, across, tall, LANES), lambda i: (0, 0, i, 0)),
            any_spec(),
        ],
        out_specs=pl.BlockSpec((2, tall, across * LANES), lambda i: (0, i, 0)),
        input_output_aliases={4: 0},
        compiler_params=params(8),
        name="left_half",
    )(tile, total, light, left, begun)


def body(object_tiles, probe, positions, frames, counts):
    tile = object_tiles[0]
    extent = tile.shape[-1]
    frame = frames.shape[-1]
    cap = frames.shape[1]
    peers = lax.axis_size("scan")
    tile_row = lax.axis_index("scan") // TCOLS
    phases = min(2, peers // TCOLS - 1)
    tables = dft_tables(frame)
    parity = (tile_row % 2).reshape(1)
    even = tile_row % 2 == 0

    own = slot_table(positions, counts, extent, frame)
    up = shifted(own, "scan", TCOLS)
    edge, middle, up = lax.optimization_barrier((*strips(tile, frame), up))
    edge = shifted(edge, "scan", -1)
    middle = shifted(middle, "scan", -1)
    beside = shifted(jnp.concatenate([own, up]), "scan", 1)

    def exchange(phase, packed, choice):
        uppers = [k for k in range(peers - TCOLS) if k // TCOLS % 2 == phase]
        pairs = [(k, k + TCOLS) for k in uppers] + [(k + TCOLS, k) for k in uppers]

        def sender(size):
            def run(data):
                return lax.dynamic_update_slice(data, lax.ppermute(data[:size], "scan", pairs), (0, 0))
            return run

        branches = [lambda data: data] + [sender(size) for size in SIZES if size <= packed.shape[0]]
        return lax.switch(choice.reshape(()), branches, packed)

    def by_role(arrays):
        if len(arrays) == 1:
            return arrays[0], arrays[0]
        return jnp.where(even, arrays[0], arrays[1]), jnp.where(even, arrays[1], arrays[0])

    cuts = [cut_pieces(phase, own, up, parity, tile, edge, frames[0]) for phase in range(phases)]
    received = by_role([exchange(phase, cut[0], cut[1]) for phase, cut in enumerate(cuts)])
    received, beside = lax.optimization_barrier((received, beside))
    total, *packed = frames_gradient(
        phases, own, up, parity, tile, edge, middle, frames[0], probe, tables, *received)
    returned = by_role([exchange(phase, packed[phase], cut[2]) for phase, cut in enumerate(cuts)])
    right = join_right(own, up, *returned, total, cap)
    right, total, beside = lax.optimization_barrier((right, total, beside))
    left = shifted(right, "scan", 1)
    total = join_own(own, up, *returned, total, cap)
    light = light_plane(own, up, beside, probe, extent)
    begun = right_half(tile, total, light)
    return left_half(tile, total, light, left, begun)[None]


def solution(mesh):
    return jax.shard_map(
        body,
        mesh=mesh,
        in_specs=(
            P(("grp", "scan"), None, None, None),
            P(),
            P(("grp", "scan"), None, None),
            P(("grp", "scan"), None, None, None),
            P(("grp", "scan")),
        ),
        out_specs=P(("grp", "scan"), None, None, None),
        check_vma=False,
    )
```
